32 devices in a mesh: dp: 4 (over y, core), ctx: 8 (over z, x).
Axes of the slice: x: 2, y: 2, z: 4, core: 2. Of those that a mesh axis runs over, the one named last changes fastest.
Arguments:
- tokens: bfloat16 [4, 1024, 2048], P('dp', 'ctx'), may hold values from -6 to 6
- document_ids: int32 [4, 1024], P('dp'), may hold values from 0 to 6, as said below
- routes: int32 [4, 1024, 8], P('dp', 'ctx'), may hold values from 0 to 15, all different within a row; in each aligned block of 128 rows (0 to 127, 128 to 255, ..., all dimensions but the last counted through in order) at most 128 rows name the same one
- norm_gains: bfloat16 [2048, 4], P(('dp', 'ctx')), may hold values from 0.5 to 1.5
- project_in: bfloat16 [2048, 6144], P(('dp', 'ctx')), may hold values from -0.125 to 0.125
- project_out: bfloat16 [2048, 2048], P(('dp', 'ctx')), may hold values from -1 to 1
- router_weight: bfloat16 [2048, 16], P(('dp', 'ctx')), may hold values from -0.0625 to 0.0625
- expert_in: bfloat16 [16, 2048, 2048], P('ctx', 'dp'), may hold values from -0.125 to 0.125
- expert_out: bfloat16 [16, 1024, 2048], P('ctx', 'dp'), may hold values from -0.5 to 0.5
- cotangent: bfloat16 [4, 1024, 2048], P('dp', 'ctx'), may hold values from -6 to 6
Outputs:
- layer_output: bfloat16 [4, 1024, 2048], P('dp', 'ctx')
- tokens_gradient: bfloat16 [4, 1024, 2048], P('dp', 'ctx')
- gains_gradient: float32 [2048, 4], P(('dp', 'ctx'))
- project_in_gradient: float32 [2048, 6144], P(('dp', 'ctx'))
- project_out_gradient: float32 [2048, 2048], P(('dp', 'ctx'))
- router_gradient: float32 [2048, 16], P(('dp', 'ctx'))
- expert_in_gradient: float32 [16, 2048, 2048], P('ctx', 'dp')
- expert_out_gradient: float32 [16, 1024, 2048], P('ctx', 'dp')
The draws below stay inside these ranges and needn't reach their ends.
Inputs may be any that keep to these rules, and one draw needn't show every extreme that they name: `document_ids`: each stream's ids start at 0 and rise by one where a document starts; ids never fall along a stream. Every stream holds exactly 7 documents, and one of them covers at least positions 64 to 511. `routes`: each row names 8 different experts. In the rows of one device no expert is named by more than 128 rows.
All inputs are finite; a program needn't handle non-finite values.
Results may differ from the reference program's by a relative error of at most 0.015.
Values may be sent and summed in bfloat16 or wider, within the bound.
A program may use at most 320 MiB of HBM per device.

```python
import math
import jax
import jax.numpy as jnp
import numpy as np
from jax import lax

D = 2048
HEADS = 16
HEAD_DIM = 128
FF = 1024
TOP = 8
TOK_DEV = 128
EXPERTS = 16
SEQ = 1024
STREAMS = 4
CAP = 128
N_CTX = 8


def draw_document_ids(key, part):
    key = jax.random.fold_in(key, 7)
    begin_seed, finish_seed, order_seed = jax.random.split(key, 3)
    half_block = TOK_DEV // 2
    break_count = max(1, TOK_DEV // 32)
    places = jnp.arange(SEQ, dtype=jnp.int32)[None, :]
    first_place = jax.random.randint(begin_seed, (STREAMS, 1), 1, half_block)
    last_place = jax.random.randint(finish_seed, (STREAMS, 1), N_CTX * half_block, SEQ - half_block + 1)
    outside = ((places < first_place) | (places > last_place)) & (places > 0)
    order_keys = jax.random.split(order_seed, STREAMS)
    shuffled = jax.vmap(lambda one_key: jax.random.permutation(one_key, SEQ))(order_keys).astype(jnp.int32)
    ranking = shuffled + jnp.where(outside, SEQ, 0)
    unused_values, picked = lax_top(ranking, break_count)
    picked_flag = jnp.sum((places[:, :, None] == picked[:, None, :]).astype(jnp.int32), axis=-1) > 0
    fresh_start = (places == first_place) | (places == last_place) | picked_flag
    return jnp.cumsum(fresh_start.astype(jnp.int32), axis=1).astype(jnp.int32)


def lax_top(ranking, count):
    return jax.lax.top_k(ranking, count)


def shard_levels(rng, dims, pieces, low, high):
    factor_of, own = 1.0, jax.random.fold_in(rng, 6)
    for axis_at, blocks in pieces:
        heights = jnp.exp(jax.random.uniform(jax.random.fold_in(own, axis_at), (blocks,), jnp.float32, low / len(pieces), high / len(pieces)))
        factor_of = factor_of * jnp.repeat(heights, dims[axis_at] // blocks).reshape([-1 if axis == axis_at else 1 for axis in range(len(dims))])
    return factor_of


def assign_block(key, own, number, rows, number_of, top, most, slope):
    order = jax.random.permutation(key, number_of)
    heavy_load, ordinary = load_shares(number_of, rows * top, most, slope, True), load_shares(number_of, rows * top, most, slope, False)
    places = jnp.arange(number_of)

    def named(sizes, turn):
        used = int((sizes > 0).sum())
        fixed = max(1, used // 4)
        shifted = fixed + (places - fixed + turn * (used - fixed)) % max(1, number_of - fixed)
        return jnp.zeros((number_of,), jnp.int32).at[order[jnp.where(places < fixed, places, shifted)]].set(jnp.asarray(sizes, jnp.int32))

    sizes = jnp.where(number % 4 == 0, named(heavy_load, number // 4), named(ordinary, number - number // 4 - 1))
    mixed = jax.random.permutation(jax.random.fold_in(own, 3), number_of)
    donor, taker = mixed[0:number_of // 2 * 2:2], mixed[1:number_of // 2 * 2:2]
    room = jnp.minimum(sizes[donor] - 1, most - sizes[taker]) // 2
    room = jnp.where((donor == order[0]) | (taker == order[0]) | (sizes[taker] == 0), 0, jnp.maximum(room, 0))
    shifted = jax.random.randint(jax.random.fold_in(own, 4), (number_of // 2,), 0, 1 << 20) % (room + 1)
    sizes = sizes.at[donor].add(-shifted).at[taker].add(shifted)
    members = jnp.searchsorted(jnp.cumsum(sizes), jnp.arange(rows * top), side="right").astype(jnp.int32)
    listing = members.reshape(top, rows).T
    listing = listing[jax.random.permutation(jax.random.fold_in(own, 1), rows)]
    turn = jax.random.randint(jax.random.fold_in(own, 2), (rows, 1), 0, top)
    return jnp.take_along_axis(listing, (jnp.arange(top)[None, :] + turn) % top, axis=1)


def load_shares(count, total, reach, lean, full):
    loads = [(1 << 20) // math.isqrt(standing ** lean) + 1 for standing in range(1, count + 1)]
    largest = reach if full else min(reach, max(-(-total // count), total * loads[0] // sum(loads)))
    least = 1 if total - largest >= count - 1 else 0
    counts, rest = [largest] + [least] * (count - 1), total - largest - least * (count - 1)
    while rest > 0:
        candidates = [i for i in range(1, count) if counts[i] < largest] or [i for i in range(1, count) if counts[i] < reach]
        pool, remaining = sum([loads[i] for i in candidates]), rest
        for i in candidates:
            more = min(reach - counts[i], max(1, remaining * loads[i] // pool), rest)
            counts[i] = counts[i] + more
            rest = rest - more
    return np.array(counts)


def gaussian(key, extent, scale, reach, shards=(), held_as=jnp.bfloat16):
    drawn = scale * jax.random.normal(key, extent, jnp.float32)
    if shards:
        drawn = drawn * shard_levels(key, extent, shards, -0.22, 0.18)
    return jnp.clip(drawn, -reach, reach).astype(held_as)


def setup_inputs(seed: int = 0) -> dict:
    key_of = jax.random.split(jax.random.key(seed), 11)
    tokens = gaussian(key_of[0], (STREAMS, SEQ, D), 1.0, 6.0, ((0, 4), (1, 8)))
    document_ids = draw_document_ids(jax.random.fold_in(key_of[10], 71), 0)
    routes_keys = jax.random.split(jax.random.fold_in(key_of[2], 1), STREAMS * SEQ // TOK_DEV)
    routes_turns = jax.random.permutation(jax.random.fold_in(key_of[2], 3), STREAMS * SEQ // TOK_DEV)
    routes = jax.vmap(lambda own, number: assign_block(jax.random.fold_in(key_of[2], 2), own, number, TOK_DEV, EXPERTS, TOP, CAP, 1))(routes_keys, routes_turns).reshape((STREAMS, SEQ, TOP))
    norm_gains = jnp.clip(1.0 + 0.1 * jax.random.normal(key_of[3], (D, 4), jnp.float32), 0.5, 1.5).astype(jnp.bfloat16)
    project_in = gaussian(key_of[4], (D, 3 * D), D ** -0.5, 0.125, ((0, 32),))
    project_out = gaussian(key_of[5], (D, D), (D // 64) ** -0.5, 1.0, ((0, 32),))
    router_weight = gaussian(key_of[6], (D, EXPERTS), (4 * D) ** -0.5, 0.0625, ((0, 32),))
    expert_in = gaussian(key_of[7], (EXPERTS, D, 2 * FF), D ** -0.5, 0.125, ((0, 8), (1, 4)))
    expert_out = gaussian(key_of[8], (EXPERTS, FF, D), (FF // 8) ** -0.5, 0.5, ((0, 8), (1, 4)))
    cotangent = gaussian(key_of[9], (STREAMS, SEQ, D), 1.0, 6.0, ((0, 4), (1, 8)))
    return {"tokens": tokens, "document_ids": document_ids, "routes": routes, "norm_gains": norm_gains, "project_in": project_in, "project_out": project_out, "router_weight": router_weight, "expert_in": expert_in, "expert_out": expert_out, "cotangent": cotangent}


EPSILON = 1e-05
ROPE_BASE = 10000.0
MASKED = -1e+30
HIGHEST = lax.Precision.HIGHEST

@jax.custom_vjp
def low(v):
    return lax.optimization_barrier(v.astype(jnp.bfloat16)).astype(jnp.float32)

@jax.custom_vjp
def low_back(v):
    return v

def low_keep(v):
    return (low(v), None)

def low_pass(kept, grad):
    return (grad,)

def back_keep(v):
    return (v, None)

def back_low(kept, grad):
    return (low(grad),)
low.defvjp(low_keep, low_pass)
low_back.defvjp(back_keep, back_low)

def inverse_rms(values):
    return lax.rsqrt(lax.optimization_barrier(jnp.mean(values * values, axis=-1, keepdims=True)) + EPSILON)

def rotary_tables(relative, head_dim):
    half_dim = head_dim // 2
    frequency = ROPE_BASE ** (-jnp.arange(half_dim, dtype=jnp.float32) / half_dim)
    angles = relative.astype(jnp.float32)[..., None] * frequency
    return (jnp.cos(angles)[..., None, :], jnp.sin(angles)[..., None, :])

def rotate(values, cosine, sine_table):
    half_dim = values.shape[-1] // 2
    first_half = values[..., :half_dim]
    second_half = values[..., half_dim:]
    return jnp.concatenate([first_half * cosine - second_half * sine_table, second_half * cosine + first_half * sine_table], axis=-1)

def dealt_positions(indices, tok_rows, context_size):
    half_block = tok_rows // 2
    device = indices // tok_rows
    within = indices % tok_rows
    block_index = jnp.where(within < half_block, device, 2 * context_size - 1 - device)
    return block_index * half_block + within % half_block

def document_starts(document_row):
    places = jnp.arange(document_row.shape[-1], dtype=jnp.int32)
    head_flag = jnp.ones(document_row.shape[:-1] + (1,), jnp.bool_)
    fresh_start = jnp.concatenate([head_flag, document_row[..., 1:] != document_row[..., :-1]], axis=-1)
    return lax.cummax(jnp.where(fresh_start, places, 0), axis=document_row.ndim - 1)

def reference(tokens, document_ids, routes, norm_gains, project_in, project_out, router_weight, expert_in, expert_out, cotangent):
    indices = jnp.arange(SEQ, dtype=jnp.int32)
    places = dealt_positions(indices, TOK_DEV, N_CTX)
    documents = jnp.take(document_ids, places, axis=1)
    relative = places[None, :] - jnp.take(document_starts(document_ids), places, axis=1)
    cosine, sine_table = rotary_tables(relative, HEAD_DIM)
    route_onehot = (routes.reshape(-1, TOP)[..., None] == jnp.arange(EXPERTS, dtype=jnp.int32)).astype(jnp.float32)
    score_scale = HEAD_DIM ** (-0.5)
    query_span = min(512, SEQ)
    span_count = SEQ // query_span

    def attend(queries, key_rows, values, document_row):

        def one_block(block_args):
            query_block, query_place, query_document = block_args
            scores = low_back(jnp.einsum('thd,khd->htk', query_block, key_rows, precision=HIGHEST) * score_scale)
            visible = ((document_row[None, :] == query_document[:, None]) & (places[None, :] <= query_place[:, None]))[None]
            masked_scores = jnp.where(visible, scores, MASKED)
            row_peak = lax.optimization_barrier(jnp.max(masked_scores, axis=-1, keepdims=True))
            row_logsum = row_peak + jnp.log(lax.optimization_barrier(jnp.sum(jnp.where(visible, jnp.exp(masked_scores - row_peak), 0.0), axis=-1, keepdims=True)))
            prob_rows = low(jnp.where(visible, jnp.exp(masked_scores - row_logsum), 0.0))
            return jnp.einsum('htk,khd->thd', prob_rows, values, precision=HIGHEST)
        block_args = (queries.reshape(span_count, query_span, HEADS, HEAD_DIM), places.reshape(span_count, query_span), document_row.reshape(span_count, query_span))
        return lax.map(jax.checkpoint(one_block), block_args).reshape(SEQ, HEADS, HEAD_DIM)

    def forward(inputs, gain_table, weight_in, weight_out, weight_router, first_weights, second_weights):
        attend_normed = inputs * inverse_rms(inputs) * gain_table[:, 0]
        projected = low_back(jnp.einsum('srd,df->srf', low(attend_normed), weight_in, precision=HIGHEST))
        raw_query = projected[..., :D]
        raw_key = projected[..., D:2 * D]
        heads_shape = (STREAMS, SEQ, HEADS, HEAD_DIM)
        queries = low(rotate((raw_query * inverse_rms(raw_query) * gain_table[:, 1]).reshape(heads_shape), cosine, sine_table))
        key_rows = low(rotate((raw_key * inverse_rms(raw_key) * gain_table[:, 2]).reshape(heads_shape), cosine, sine_table))
        values = low(projected[..., 2 * D:].reshape(heads_shape))
        attended = jax.vmap(attend)(queries, key_rows, values, documents)
        attended = low(low_back(attended.reshape(STREAMS, SEQ, D)))
        residual = inputs + low_back(jnp.einsum('srd,de->sre', attended, weight_out, precision=HIGHEST))
        mixed_rows = low((residual * inverse_rms(residual) * gain_table[:, 3]).reshape(-1, D))
        logits = low_back(jnp.dot(mixed_rows, weight_router, precision=HIGHEST))
        gate_weights = jax.nn.softmax(lax.optimization_barrier(jnp.sum(route_onehot * logits[:, None, :], axis=-1)), axis=-1)
        coefficient = lax.optimization_barrier(jnp.sum(gate_weights[..., None] * route_onehot, axis=1))

        def expert_step(running, expert_args):
            first_weight, second_weight, column = expert_args
            expert_up = low_back(jnp.dot(low_back(mixed_rows), first_weight, precision=HIGHEST))
            hidden = low(jax.nn.silu(expert_up[:, :FF]) * expert_up[:, FF:])
            result = low(low_back(jnp.dot(hidden, second_weight, precision=HIGHEST)))
            return (running + column[:, None] * result, None)
        mixture, unused = lax.scan(jax.checkpoint(expert_step), jnp.zeros_like(mixed_rows), (first_weights, second_weights, coefficient.T))
        return residual + mixture.reshape(STREAMS, SEQ, D)
    primals = (tokens.astype(jnp.float32), norm_gains.astype(jnp.float32), project_in.astype(jnp.float32), project_out.astype(jnp.float32), router_weight.astype(jnp.float32), expert_in.astype(jnp.float32), expert_out.astype(jnp.float32))
    output, pullback = jax.vjp(forward, *primals)
    gradients = pullback(cotangent.astype(jnp.float32))
    return (output.astype(jnp.bfloat16), gradients[0].astype(jnp.bfloat16), gradients[1], gradients[2], gradients[3], gradients[4], gradients[5], gradients[6])
```

```python
import jax
import jax.numpy as jnp
from jax import lax
from jax.sharding import PartitionSpec as P

HEADS = 16
HEAD_DIM = 128
FF = 1024


EPSILON = 1e-05
ROPE_BASE = 10000.0
MASKED = -1e30


def inverse_rms(values):
    return lax.rsqrt(jnp.mean(values * values, axis=-1, keepdims=True) + EPSILON)


def normalize_back(normed_back, normed, inverse):
    return inverse * (normed_back - normed * jnp.mean(normed_back * normed, axis=-1, keepdims=True))


def rotary_tables(relative, head_dim):
    half_dim = head_dim // 2
    frequency = ROPE_BASE ** (-jnp.arange(half_dim, dtype=jnp.float32) / half_dim)
    angles = relative.astype(jnp.float32)[..., None] * frequency
    return (jnp.cos(angles)[..., None, :], jnp.sin(angles)[..., None, :])


def rotate(values, cosine, sine_table):
    half_dim = values.shape[-1] // 2
    first_half = values[..., :half_dim]
    second_half = values[..., half_dim:]
    return jnp.concatenate(
        [
            first_half * cosine - second_half * sine_table,
            second_half * cosine + first_half * sine_table,
        ],
        axis=-1,
    )


def dealt_positions(indices, tok_rows, context_size):
    half_block = tok_rows // 2
    device = indices // tok_rows
    within = indices % tok_rows
    block_index = jnp.where(within < half_block, device, 2 * context_size - 1 - device)
    return block_index * half_block + within % half_block


def document_starts(document_row):
    places = jnp.arange(document_row.shape[-1], dtype=jnp.int32)
    head_flag = jnp.ones(document_row.shape[:-1] + (1,), jnp.bool_)
    fresh_start = jnp.concatenate(
        [head_flag, document_row[..., 1:] != document_row[..., :-1]], axis=-1
    )
    return lax.cummax(jnp.where(fresh_start, places, 0), axis=document_row.ndim - 1)


def block_scores(
    query_rows, key_block, query_place, query_document, key_place, key_document, score_scale
):
    scores = (
        jnp.einsum("thd,khd->htk", query_rows, key_block, preferred_element_type=jnp.float32)
        * score_scale
    )
    visible = (
        (key_document[None, :] == query_document[:, None])
        & (key_place[None, :] <= query_place[:, None])
    )[None]
    return (jnp.where(visible, scores, MASKED), visible)


def block_backward(
    query_rows,
    output_back,
    row_logsum,
    row_delta,
    key_block,
    value_block,
    query_place,
    query_document,
    key_place,
    key_document,
    score_scale,
):
    scores, visible = block_scores(
        query_rows, key_block, query_place, query_document, key_place, key_document, score_scale
    )
    prob_rows = jnp.where(visible, jnp.exp(scores - row_logsum[..., None]), 0.0)
    prob_back = jnp.einsum(
        "thd,khd->htk", output_back, value_block, preferred_element_type=jnp.float32
    )
    score_back = (prob_rows * (prob_back - row_delta[..., None])).astype(jnp.bfloat16)
    query_part = (
        jnp.einsum("htk,khd->thd", score_back, key_block, preferred_element_type=jnp.float32)
        * score_scale
    )
    key_part = (
        jnp.einsum("htk,thd->khd", score_back, query_rows, preferred_element_type=jnp.float32)
        * score_scale
    )
    value_part = jnp.einsum(
        "htk,thd->khd",
        prob_rows.astype(jnp.bfloat16),
        output_back,
        preferred_element_type=jnp.float32,
    )
    return (query_part, key_part, value_part)


def dispatch_plan(route_rows, expert_count, capacity):
    flat_routes = route_rows.reshape(-1)
    pair_count = flat_routes.shape[0]
    member = (flat_routes[:, None] == jnp.arange(expert_count, dtype=jnp.int32)[None, :]).astype(
        jnp.int32
    )
    earlier = jnp.cumsum(member, axis=0) - member
    target_slot = flat_routes * capacity + jnp.sum(earlier * member, axis=1)
    slot_owner = (
        jnp.full((expert_count * capacity,), pair_count, jnp.int32)
        .at[target_slot]
        .set(jnp.arange(pair_count, dtype=jnp.int32))
    )
    return (target_slot, slot_owner)


def gathered_local(
    tokens,
    document_ids,
    routes,
    norm_gains,
    project_in,
    project_out,
    router_weight,
    expert_in,
    expert_out,
    cotangent,
):
    inputs = tokens[0].astype(jnp.float32)
    tok_rows, model_width = inputs.shape
    context_size = lax.axis_size("ctx")
    sequence_rows = tok_rows * context_size
    local_experts = expert_in.shape[0]
    expert_count = local_experts * context_size
    route_rows = routes[0]
    top_count = route_rows.shape[1]
    capacity = 2 * tok_rows * top_count // expert_count
    score_scale = HEAD_DIM ** (-0.5)
    key_span = min(512, sequence_rows)
    key_blocks = sequence_rows // key_span
    heads_shape = (tok_rows, HEADS, HEAD_DIM)
    block_shape = (key_blocks, key_span, HEADS, HEAD_DIM)
    slot_shape = (context_size, local_experts * capacity, model_width)
    expert_shape = (context_size, local_experts, capacity, model_width)
    gathered_gains, gathered_in, gathered_out, gathered_router = (
        lax.all_gather(norm_gains, ("dp", "ctx"), axis=0, tiled=True),
        lax.all_gather(project_in, ("dp", "ctx"), axis=0, tiled=True),
        lax.all_gather(project_out, ("dp", "ctx"), axis=0, tiled=True),
        lax.all_gather(router_weight, ("dp", "ctx"), axis=0, tiled=True),
    )
    gathered_first, gathered_second = (
        lax.all_gather(expert_in, "dp", axis=1, tiled=True),
        lax.all_gather(expert_out, "dp", axis=1, tiled=True),
    )
    gain_rows = gathered_gains.astype(jnp.float32)
    own_rows = lax.axis_index("ctx") * tok_rows + jnp.arange(tok_rows, dtype=jnp.int32)
    own_place = dealt_positions(own_rows, tok_rows, context_size)
    all_place = dealt_positions(jnp.arange(sequence_rows, dtype=jnp.int32), tok_rows, context_size)
    document_row = document_ids[0]
    own_document = jnp.take(document_row, own_place)
    all_document = jnp.take(document_row, all_place)
    relative = own_place - jnp.take(document_starts(document_row), own_place)
    cosine, sine_table = rotary_tables(relative, HEAD_DIM)
    attend_inverse = inverse_rms(inputs)
    attend_normed = inputs * attend_inverse
    attend_in = (attend_normed * gain_rows[:, 0]).astype(jnp.bfloat16)
    projected = jnp.dot(attend_in, gathered_in, preferred_element_type=jnp.float32)
    raw_query = projected[:, :model_width]
    raw_key = projected[:, model_width : 2 * model_width]
    query_inverse = inverse_rms(raw_query)
    query_normed = raw_query * query_inverse
    key_inverse = inverse_rms(raw_key)
    key_normed = raw_key * key_inverse
    query_low = rotate(
        (query_normed * gain_rows[:, 1]).reshape(heads_shape), cosine, sine_table
    ).astype(jnp.bfloat16)
    key_low = rotate(
        (key_normed * gain_rows[:, 2]).reshape(heads_shape), cosine, sine_table
    ).astype(jnp.bfloat16)
    value_low = projected[:, 2 * model_width :].astype(jnp.bfloat16)
    key_all, value_all = (
        lax.all_gather(key_low.reshape(tok_rows, model_width), "ctx", axis=0, tiled=True),
        lax.all_gather(value_low, "ctx", axis=0, tiled=True),
    )
    key_split = key_all.reshape(block_shape)
    value_split = value_all.reshape(block_shape)
    place_split = all_place.reshape(key_blocks, key_span)
    document_split = all_document.reshape(key_blocks, key_span)

    def total_step(state_pair, block_args):
        row_peak, row_total = state_pair
        key_block, key_place, key_document = block_args
        scores, visible = block_scores(
            query_low, key_block, own_place, own_document, key_place, key_document, score_scale
        )
        new_peak = jnp.maximum(row_peak, jnp.max(scores, axis=-1))
        fresh_total = jnp.sum(
            jnp.where(visible, jnp.exp(scores - new_peak[..., None]), 0.0), axis=-1
        )
        return ((new_peak, row_total * jnp.exp(row_peak - new_peak) + fresh_total), None)

    start_pair = (
        jnp.full((HEADS, tok_rows), MASKED, jnp.float32),
        jnp.zeros((HEADS, tok_rows), jnp.float32),
    )
    (row_peak, row_total), unused = lax.scan(
        total_step, start_pair, (key_split, place_split, document_split)
    )
    row_logsum = row_peak + jnp.log(row_total)

    def value_step(running, block_args):
        key_block, value_block, key_place, key_document = block_args
        scores, visible = block_scores(
            query_low, key_block, own_place, own_document, key_place, key_document, score_scale
        )
        prob_low = jnp.where(visible, jnp.exp(scores - row_logsum[..., None]), 0.0).astype(
            jnp.bfloat16
        )
        return (
            running
            + jnp.einsum("htk,khd->thd", prob_low, value_block, preferred_element_type=jnp.float32),
            None,
        )

    attend_out, unused = lax.scan(
        value_step,
        jnp.zeros(heads_shape, jnp.float32),
        (key_split, value_split, place_split, document_split),
    )
    attend_low = attend_out.reshape(tok_rows, model_width).astype(jnp.bfloat16)
    residual = inputs + jnp.dot(attend_low, gathered_out, preferred_element_type=jnp.float32)
    mixed_inverse = inverse_rms(residual)
    mixed_normed = residual * mixed_inverse
    mixed_low = (mixed_normed * gain_rows[:, 3]).astype(jnp.bfloat16)
    logits = jnp.dot(mixed_low, gathered_router, preferred_element_type=jnp.float32)
    route_onehot = (route_rows[..., None] == jnp.arange(expert_count, dtype=jnp.int32)).astype(
        jnp.float32
    )
    gate_weights = jax.nn.softmax(jnp.sum(route_onehot * logits[:, None, :], axis=-1), axis=-1)
    target_slot, slot_owner = dispatch_plan(route_rows, expert_count, capacity)
    padded_rows = jnp.concatenate([mixed_low, jnp.zeros((1, model_width), jnp.bfloat16)], axis=0)
    send_rows = jnp.take(padded_rows, slot_owner // top_count, axis=0).reshape(slot_shape)
    received = lax.all_to_all(send_rows, "ctx", split_axis=0, concat_axis=0, tiled=True).reshape(
        expert_shape
    )
    expert_up = jnp.einsum(
        "sxcd,xdf->sxcf", received, gathered_first, preferred_element_type=jnp.float32
    )
    gate_part = expert_up[..., :FF]
    up_part = expert_up[..., FF:]
    sigmoid_gate = jax.nn.sigmoid(gate_part)
    swish_gate = gate_part * sigmoid_gate
    hidden_low = (swish_gate * up_part).astype(jnp.bfloat16)
    expert_result = jnp.einsum(
        "sxcf,xfd->sxcd", hidden_low, gathered_second, preferred_element_type=jnp.float32
    ).astype(jnp.bfloat16)
    returned = lax.all_to_all(
        expert_result.reshape(slot_shape), "ctx", split_axis=0, concat_axis=0, tiled=True
    ).reshape(expert_count * capacity, model_width)
    pair_result = jnp.take(returned, target_slot, axis=0).reshape(tok_rows, top_count, model_width)
    mixture = jnp.sum(gate_weights[..., None] * pair_result, axis=1)
    layer_output = (residual + mixture).astype(jnp.bfloat16)
    upstream = cotangent[0].astype(jnp.float32)
    pair_back = (gate_weights[..., None] * upstream[:, None, :]).astype(jnp.bfloat16)
    gate_back = jnp.sum(pair_result * upstream[:, None, :], axis=-1)
    padded_back = jnp.concatenate(
        [
            pair_back.reshape(tok_rows * top_count, model_width),
            jnp.zeros((1, model_width), jnp.bfloat16),
        ],
        axis=0,
    )
    send_back = jnp.take(padded_back, slot_owner, axis=0).reshape(slot_shape)
    received_back = lax.all_to_all(
        send_back, "ctx", split_axis=0, concat_axis=0, tiled=True
    ).reshape(expert_shape)
    first_back, second_back = (gathered_first, gathered_second)
    hidden_back = jnp.einsum(
        "sxcd,xfd->sxcf", received_back, second_back, preferred_element_type=jnp.float32
    )
    second_weight_back = jnp.einsum(
        "sxcf,sxcd->xfd", hidden_low, received_back, preferred_element_type=jnp.float32
    )
    swish_slope = sigmoid_gate * (1.0 + gate_part * (1.0 - sigmoid_gate))
    up_back = jnp.concatenate(
        [hidden_back * up_part * swish_slope, hidden_back * swish_gate], axis=-1
    ).astype(jnp.bfloat16)
    first_weight_back = jnp.einsum(
        "sxcd,sxcf->xdf", received, up_back, preferred_element_type=jnp.float32
    )
    input_back = jnp.einsum(
        "sxcf,xdf->sxcd", up_back, first_back, preferred_element_type=jnp.float32
    ).astype(jnp.bfloat16)
    expert_in_gradient, expert_out_gradient = (
        lax.psum_scatter(
            first_weight_back.astype(jnp.bfloat16), "dp", scatter_dimension=1, tiled=True
        ).astype(jnp.float32),
        lax.psum_scatter(
            second_weight_back.astype(jnp.bfloat16), "dp", scatter_dimension=1, tiled=True
        ).astype(jnp.float32),
    )
    rows_back = lax.all_to_all(
        input_back.reshape(slot_shape), "ctx", split_axis=0, concat_axis=0, tiled=True
    ).reshape(expert_count * capacity, model_width)
    mixed_back = jnp.sum(
        jnp.take(rows_back, target_slot, axis=0)
        .reshape(tok_rows, top_count, model_width)
        .astype(jnp.float32),
        axis=1,
    )
    gains_back, in_back, out_back, router_back = (
        gathered_gains,
        gathered_in,
        gathered_out,
        gathered_router,
    )
    gain_values = gains_back.astype(jnp.float32)
    chosen_back = gate_weights * (
        gate_back - jnp.sum(gate_weights * gate_back, axis=-1, keepdims=True)
    )
    logit_back = jnp.sum(chosen_back[..., None] * route_onehot, axis=1).astype(jnp.bfloat16)
    router_weight_back = jnp.einsum(
        "td,te->de", mixed_low, logit_back, preferred_element_type=jnp.float32
    )
    mixed_back = mixed_back + jnp.einsum(
        "te,de->td", logit_back, router_back, preferred_element_type=jnp.float32
    )
    mixed_gain_back = jnp.sum(mixed_back * mixed_normed, axis=0)
    residual_back = upstream + normalize_back(
        mixed_back * gain_values[:, 3], mixed_normed, mixed_inverse
    )
    residual_low = residual_back.astype(jnp.bfloat16)
    out_weight_back = jnp.einsum(
        "td,te->de", attend_low, residual_low, preferred_element_type=jnp.float32
    )
    attend_back = (
        jnp.einsum("te,de->td", residual_low, out_back, preferred_element_type=jnp.float32)
        .astype(jnp.bfloat16)
        .reshape(heads_shape)
    )
    row_delta = jnp.einsum("thd,thd->ht", attend_back.astype(jnp.float32), attend_out)

    def back_step(query_acc, block_args):
        key_block, value_block, key_place, key_document = block_args
        query_part, key_part, value_part = block_backward(
            query_low,
            attend_back,
            row_logsum,
            row_delta,
            key_block,
            value_block,
            own_place,
            own_document,
            key_place,
            key_document,
            score_scale,
        )
        return (query_acc + query_part, (key_part, value_part))

    query_back, (key_parts, value_parts) = lax.scan(
        back_step,
        jnp.zeros(heads_shape, jnp.float32),
        (key_split, value_split, place_split, document_split),
    )
    key_back, value_back = (
        lax.psum_scatter(
            key_parts.reshape(sequence_rows, model_width).astype(jnp.bfloat16),
            "ctx",
            scatter_dimension=0,
            tiled=True,
        ).astype(jnp.float32),
        lax.psum_scatter(
            value_parts.reshape(sequence_rows, model_width).astype(jnp.bfloat16),
            "ctx",
            scatter_dimension=0,
            tiled=True,
        ).astype(jnp.float32),
    )
    query_flat = rotate(query_back, cosine, -sine_table).reshape(tok_rows, model_width)
    key_flat = rotate(key_back.reshape(heads_shape), cosine, -sine_table).reshape(
        tok_rows, model_width
    )
    query_gain_back = jnp.sum(query_flat * query_normed, axis=0)
    key_gain_back = jnp.sum(key_flat * key_normed, axis=0)
    raw_query_back = normalize_back(query_flat * gain_values[:, 1], query_normed, query_inverse)
    raw_key_back = normalize_back(key_flat * gain_values[:, 2], key_normed, key_inverse)
    raw_back = jnp.concatenate([raw_query_back, raw_key_back, value_back], axis=-1).astype(
        jnp.bfloat16
    )
    in_weight_back = jnp.einsum(
        "td,tf->df", attend_in, raw_back, preferred_element_type=jnp.float32
    )
    attend_in_back = jnp.einsum("tf,df->td", raw_back, in_back, preferred_element_type=jnp.float32)
    attend_gain_back = jnp.sum(attend_in_back * attend_normed, axis=0)
    tokens_back = residual_back + normalize_back(
        attend_in_back * gain_values[:, 0], attend_normed, attend_inverse
    )
    gain_columns = jnp.stack(
        [attend_gain_back, query_gain_back, key_gain_back, mixed_gain_back], axis=1
    )
    gains_gradient, project_in_gradient, project_out_gradient, router_gradient = (
        lax.psum_scatter(gain_columns, ("dp", "ctx"), scatter_dimension=0, tiled=True),
        lax.psum_scatter(in_weight_back, ("dp", "ctx"), scatter_dimension=0, tiled=True),
        lax.psum_scatter(out_weight_back, ("dp", "ctx"), scatter_dimension=0, tiled=True),
        lax.psum_scatter(router_weight_back, ("dp", "ctx"), scatter_dimension=0, tiled=True),
    )
    return (
        layer_output[None],
        tokens_back.astype(jnp.bfloat16)[None],
        gains_gradient,
        project_in_gradient,
        project_out_gradient,
        router_gradient,
        expert_in_gradient,
        expert_out_gradient,
    )


def gather_ctx(block):
    return lax.all_gather(block, "ctx", axis=0, tiled=True)


def scatter_ctx(partial):
    return lax.psum_scatter(
        partial.astype(jnp.bfloat16), "ctx", scatter_dimension=0, tiled=True
    ).astype(jnp.float32)


def heads_local(
    tokens,
    document_ids,
    routes,
    norm_gains,
    project_in,
    project_out,
    router_weight,
    expert_in,
    expert_out,
    cotangent,
):
    bf16, f32 = jnp.bfloat16, jnp.float32
    n = lax.axis_size("ctx")
    n_dp = lax.axis_size("dp")
    me = lax.axis_index("ctx")
    tok_rows, width = tokens.shape[1:]
    rows = tok_rows * n
    weight_rows = project_in.shape[0]
    own_heads = HEADS // n
    cols = own_heads * HEAD_DIM
    local_experts = expert_in.shape[0]
    expert_count = local_experts * n
    score_scale = HEAD_DIM ** (-0.5)

    def own(array, size, axis=0):
        return lax.dynamic_slice_in_dim(array, me * size, size, axis)

    token_all = gather_ctx(tokens[0])
    upstream_all = gather_ctx(cotangent[0])
    route_all = gather_ctx(routes[0])
    in_blocks = project_in.reshape(weight_rows, 3, n, cols).transpose(2, 0, 1, 3)
    in_blocks = in_blocks.reshape(n, weight_rows, 3 * cols)
    in_blocks = lax.all_to_all(in_blocks, "ctx", split_axis=0, concat_axis=0, tiled=True)
    in_own = lax.all_gather(in_blocks, "dp", axis=0, tiled=True).reshape(width, 3 * cols)
    small = jnp.concatenate([norm_gains, router_weight], axis=1)
    small_all = lax.all_gather(small, ("dp", "ctx"), axis=0, tiled=True)
    gains = small_all[:, :4].astype(f32)
    router_all = small_all[:, 4:]
    out_all = lax.all_gather(project_out, ("dp", "ctx"), axis=0, tiled=True)
    first = lax.all_gather(expert_in, "dp", axis=1, tiled=True)
    second = lax.all_gather(expert_out, "dp", axis=1, tiled=True)

    places = dealt_positions(jnp.arange(rows, dtype=jnp.int32), tok_rows, n)
    document_row = document_ids[0]
    documents = jnp.take(document_row, places)
    relative = places - jnp.take(document_starts(document_row), places)
    cosine, sine = rotary_tables(relative, HEAD_DIM)
    visible = (documents[None, :] == documents[:, None]) & (places[None, :] <= places[:, None])

    inputs = token_all.astype(f32)
    attend_inverse = inverse_rms(inputs)
    attend_in = (inputs * attend_inverse * gains[:, 0]).astype(bf16)
    projected = jnp.dot(attend_in, in_own, preferred_element_type=f32)
    raw = projected[:, : 2 * cols].reshape(rows, 2, cols)
    squares = lax.psum(jnp.sum(raw * raw, axis=-1), "ctx")
    inverse = lax.rsqrt(squares / width + EPSILON)[..., None]
    normed = raw * inverse
    pair_gains = own(gains, cols)[:, 1:3].T
    rotated = rotate((normed * pair_gains).reshape(rows, 2 * own_heads, HEAD_DIM), cosine, sine)
    rotated = rotated.reshape(rows, 2, own_heads, HEAD_DIM).astype(bf16)
    query, key = rotated[:, 0], rotated[:, 1]
    value = projected[:, 2 * cols :].astype(bf16).reshape(rows, own_heads, HEAD_DIM)

    scores = jnp.einsum("thd,khd->htk", query, key, preferred_element_type=f32) * score_scale
    scores = jnp.where(visible[None], scores, MASKED)
    peak = jnp.max(scores, axis=-1, keepdims=True)
    powers = jnp.where(visible[None], jnp.exp(scores - peak), 0.0)
    total = jnp.sum(powers, axis=-1, keepdims=True)
    probs = (powers / total).astype(bf16)
    attend_out = jnp.einsum("htk,khd->thd", probs, value, preferred_element_type=f32)
    attend_low = attend_out.reshape(rows, cols).astype(bf16)
    attend_all = lax.all_gather(attend_low, "ctx", axis=1, tiled=True)

    residual = inputs + jnp.dot(attend_all, out_all, preferred_element_type=f32)
    mixed_inverse = inverse_rms(residual)
    mixed_low = (residual * mixed_inverse * gains[:, 3]).astype(bf16)
    logits = jnp.dot(mixed_low, router_all, preferred_element_type=f32)
    named = jnp.any(
        route_all[..., None] == jnp.arange(expert_count, dtype=jnp.int32), axis=1
    )
    chosen = jnp.where(named, logits, MASKED)
    chosen = jnp.where(named, jnp.exp(chosen - jnp.max(chosen, axis=-1, keepdims=True)), 0.0)
    gates = chosen / jnp.sum(chosen, axis=-1, keepdims=True)
    gate_own = own(gates, local_experts, 1).T[..., None]

    expert_up = jnp.einsum("td,xdf->xtf", mixed_low, first, preferred_element_type=f32)
    gate_part, up_part = expert_up[..., :FF], expert_up[..., FF:]
    sigmoid = jax.nn.sigmoid(gate_part)
    swish = gate_part * sigmoid
    hidden = swish * up_part
    hidden_gated = (hidden * gate_own).astype(bf16)
    mixture = jnp.einsum("xtf,xfd->td", hidden_gated, second, preferred_element_type=f32)
    mixture = scatter_ctx(mixture)
    own_residual = own(residual, tok_rows)
    layer_output = (own_residual + mixture).astype(bf16)

    hidden_back = jnp.einsum("td,xfd->xtf", upstream_all, second, preferred_element_type=f32)
    gate_back = jnp.sum(hidden.astype(bf16).astype(f32) * hidden_back, axis=-1)
    hidden_back = hidden_back * gate_own
    slope = sigmoid * (1.0 + gate_part * (1.0 - sigmoid))
    up_back = jnp.concatenate(
        [hidden_back * up_part * slope, hidden_back * swish], axis=-1
    ).astype(bf16)
    second_back = jnp.einsum("xtf,td->xfd", hidden_gated, upstream_all, preferred_element_type=f32)
    first_back = jnp.einsum("td,xtf->xdf", mixed_low, up_back, preferred_element_type=f32)
    expert_in_gradient, expert_out_gradient = (
        lax.psum_scatter(part.astype(bf16), "dp", scatter_dimension=1, tiled=True).astype(f32)
        for part in (first_back, second_back)
    )
    mixed_back = scatter_ctx(
        jnp.einsum("xtf,xdf->td", up_back, first, preferred_element_type=f32)
    )
    gate_back = lax.all_to_all(
        gate_back.reshape(local_experts, n, tok_rows), "ctx", split_axis=1, concat_axis=0, tiled=True
    ).reshape(expert_count, tok_rows).T

    own_gates = own(gates, tok_rows)
    own_mixed = own(mixed_low, tok_rows)
    own_mixed_inverse = own(mixed_inverse, tok_rows)
    own_mixed_normed = own_residual * own_mixed_inverse
    chosen_back = own_gates * (
        gate_back - jnp.sum(own_gates * gate_back, axis=-1, keepdims=True)
    )
    logit_back = chosen_back.astype(bf16)
    router_part = jnp.einsum("td,te->de", own_mixed, logit_back, preferred_element_type=f32)
    mixed_back = mixed_back + jnp.einsum(
        "te,de->td", logit_back, router_all, preferred_element_type=f32
    )
    mixed_gain_back = jnp.sum(mixed_back * own_mixed_normed, axis=0)
    residual_back = cotangent[0].astype(f32) + normalize_back(
        mixed_back * gains[:, 3], own_mixed_normed, own_mixed_inverse
    )
    back_all = gather_ctx(residual_back.astype(bf16))

    out_part = jnp.einsum("td,te->de", attend_low, back_all, preferred_element_type=f32)
    out_part = lax.psum_scatter(
        out_part.astype(bf16), "dp", scatter_dimension=0, tiled=True
    )
    pairs = []
    for d in range(n_dp):
        for c in range(n):
            pairs.append((d * n + c, c * n_dp + d))
    project_out_gradient = lax.ppermute(out_part, ("dp", "ctx"), pairs).astype(f32)
    attend_back = jnp.einsum(
        "td,ed->te", back_all, own(out_all, cols), preferred_element_type=f32
    ).astype(bf16).reshape(rows, own_heads, HEAD_DIM)
    delta = jnp.einsum("thd,thd->ht", attend_back.astype(f32), attend_out)[..., None]
    prob_back = jnp.einsum("thd,khd->htk", attend_back, value, preferred_element_type=f32)
    score_back = (probs.astype(f32) * (prob_back - delta)).astype(bf16)
    query_back = jnp.einsum("htk,khd->thd", score_back, key, preferred_element_type=f32)
    key_back = jnp.einsum("htk,thd->khd", score_back, query, preferred_element_type=f32)
    value_back = jnp.einsum("htk,thd->khd", probs, attend_back, preferred_element_type=f32)
    pair_back = jnp.concatenate([query_back, key_back], axis=1) * score_scale
    pair_back = rotate(pair_back, cosine, -sine).reshape(rows, 2, cols)
    pair_gain_back = jnp.sum(pair_back * normed, axis=0)
    pair_back = pair_back * pair_gains
    means = lax.psum(jnp.sum(pair_back * normed, axis=-1), "ctx")[..., None] / width
    pair_back = inverse * (pair_back - normed * means)
    raw_back = jnp.concatenate(
        [pair_back.reshape(rows, 2 * cols), value_back.reshape(rows, cols)], axis=-1
    ).astype(bf16)
    attend_in_back = scatter_ctx(
        jnp.einsum("tf,df->td", raw_back, in_own, preferred_element_type=f32)
    )
    in_part = jnp.einsum("td,tf->df", attend_in, raw_back, preferred_element_type=f32)
    in_part = lax.psum_scatter(in_part.astype(bf16), "dp", scatter_dimension=0, tiled=True)
    in_part = lax.all_to_all(
        in_part.reshape(n, weight_rows, 3 * cols), "ctx", split_axis=0, concat_axis=0, tiled=True
    ).reshape(n, weight_rows, 3, cols)
    project_in_gradient = in_part.transpose(1, 2, 0, 3).reshape(weight_rows, 3 * width).astype(f32)

    own_inverse = own(attend_inverse, tok_rows)
    own_normed = tokens[0].astype(f32) * own_inverse
    attend_gain_back = jnp.sum(attend_in_back * own_normed, axis=0)
    tokens_back = residual_back + normalize_back(
        attend_in_back * gains[:, 0], own_normed, own_inverse
    )
    pair_columns = lax.dynamic_update_slice_in_dim(
        jnp.zeros((width, 2), f32), pair_gain_back.T, me * cols, 0
    )
    small_part = jnp.concatenate(
        [attend_gain_back[:, None], pair_columns, mixed_gain_back[:, None], router_part], axis=1
    )
    small_gradient = lax.psum_scatter(
        small_part, ("dp", "ctx"), scatter_dimension=0, tiled=True
    )
    return (
        layer_output[None],
        tokens_back.astype(bf16)[None],
        small_gradient[:, :4],
        project_in_gradient,
        project_out_gradient,
        small_gradient[:, 4:],
        expert_in_gradient,
        expert_out_gradient,
    )


def solution(mesh):
    split_heads = HEADS % mesh.shape["ctx"] == 0
    placed = (
        P("dp", "ctx", None),
        P("dp", None),
        P("dp", "ctx", None),
        P(("dp", "ctx"), None),
        P(("dp", "ctx"), None),
        P(("dp", "ctx"), None),
        P(("dp", "ctx"), None),
        P("ctx", "dp", None),
        P("ctx", "dp", None),
        P("dp", "ctx", None),
    )
    return jax.shard_map(
        heads_local if split_heads else gathered_local,
        mesh=mesh,
        in_specs=placed,
        out_specs=(
            P("dp", "ctx", None),
            P("dp", "ctx", None),
            P(("dp", "ctx"), None),
            P(("dp", "ctx"), None),
            P(("dp", "ctx"), None),
            P(("dp", "ctx"), None),
            P("ctx", "dp", None),
            P("ctx", "dp", None),
        ),
        check_vma=False,
    )
```

```python
import jax
import jax.numpy as jnp
from jax import lax
from jax.experimental import pallas as pl
from jax.experimental.pallas import tpu as pltpu
from jax.sharding import PartitionSpec as P

HEADS = 16
HEAD_DIM = 128
FF = 1024


EPSILON = 1e-05
ROPE_BASE = 10000.0
MASKED = -1e30
LANES = 128


def inverse_rms(values):
    return lax.rsqrt(jnp.mean(values * values, axis=-1, keepdims=True) + EPSILON)


def normalize_back(normed_back, normed, inverse):
    return inverse * (normed_back - normed * jnp.mean(normed_back * normed, axis=-1, keepdims=True))


def rotary_tables(relative, head_dim):
    half_dim = head_dim // 2
    frequency = ROPE_BASE ** (-jnp.arange(half_dim, dtype=jnp.float32) / half_dim)
    angles = relative.astype(jnp.float32)[..., None] * frequency
    return (jnp.cos(angles)[..., None, :], jnp.sin(angles)[..., None, :])


def rotate(values, cosine, sine_table):
    half_dim = values.shape[-1] // 2
    first_half = values[..., :half_dim]
    second_half = values[..., half_dim:]
    return jnp.concatenate(
        [
            first_half * cosine - second_half * sine_table,
            second_half * cosine + first_half * sine_table,
        ],
        axis=-1,
    )


def dealt_positions(indices, tok_rows, context_size):
    half_block = tok_rows // 2
    device = indices // tok_rows
    within = indices % tok_rows
    block_index = jnp.where(within < half_block, device, 2 * context_size - 1 - device)
    return block_index * half_block + within % half_block


def document_starts(document_row):
    places = jnp.arange(document_row.shape[-1], dtype=jnp.int32)
    head_flag = jnp.ones(document_row.shape[:-1] + (1,), jnp.bool_)
    fresh_start = jnp.concatenate(
        [head_flag, document_row[..., 1:] != document_row[..., :-1]], axis=-1
    )
    return lax.cummax(jnp.where(fresh_start, places, 0), axis=document_row.ndim - 1)


def block_scores(
    query_rows, key_block, query_place, query_document, key_place, key_document, score_scale
):
    scores = (
        jnp.einsum("thd,khd->htk", query_rows, key_block, preferred_element_type=jnp.float32)
        * score_scale
    )
    visible = (
        (key_document[None, :] == query_document[:, None])
        & (key_place[None, :] <= query_place[:, None])
    )[None]
    return (jnp.where(visible, scores, MASKED), visible)


def block_backward(
    query_rows,
    output_back,
    row_logsum,
    row_delta,
    key_block,
    value_block,
    query_place,
    query_document,
    key_place,
    key_document,
    score_scale,
):
    scores, visible = block_scores(
        query_rows, key_block, query_place, query_document, key_place, key_document, score_scale
    )
    prob_rows = jnp.where(visible, jnp.exp(scores - row_logsum[..., None]), 0.0)
    prob_back = jnp.einsum(
        "thd,khd->htk", output_back, value_block, preferred_element_type=jnp.float32
    )
    score_back = (prob_rows * (prob_back - row_delta[..., None])).astype(jnp.bfloat16)
    query_part = (
        jnp.einsum("htk,khd->thd", score_back, key_block, preferred_element_type=jnp.float32)
        * score_scale
    )
    key_part = (
        jnp.einsum("htk,thd->khd", score_back, query_rows, preferred_element_type=jnp.float32)
        * score_scale
    )
    value_part = jnp.einsum(
        "htk,thd->khd",
        prob_rows.astype(jnp.bfloat16),
        output_back,
        preferred_element_type=jnp.float32,
    )
    return (query_part, key_part, value_part)


def dispatch_plan(route_rows, expert_count, capacity):
    flat_routes = route_rows.reshape(-1)
    pair_count = flat_routes.shape[0]
    member = (flat_routes[:, None] == jnp.arange(expert_count, dtype=jnp.int32)[None, :]).astype(
        jnp.int32
    )
    earlier = jnp.cumsum(member, axis=0) - member
    target_slot = flat_routes * capacity + jnp.sum(earlier * member, axis=1)
    slot_owner = (
        jnp.full((expert_count * capacity,), pair_count, jnp.int32)
        .at[target_slot]
        .set(jnp.arange(pair_count, dtype=jnp.int32))
    )
    return (target_slot, slot_owner)


def gathered_local(
    tokens,
    document_ids,
    routes,
    norm_gains,
    project_in,
    project_out,
    router_weight,
    expert_in,
    expert_out,
    cotangent,
):
    inputs = tokens[0].astype(jnp.float32)
    tok_rows, model_width = inputs.shape
    context_size = lax.axis_size("ctx")
    sequence_rows = tok_rows * context_size
    local_experts = expert_in.shape[0]
    expert_count = local_experts * context_size
    route_rows = routes[0]
    top_count = route_rows.shape[1]
    capacity = 2 * tok_rows * top_count // expert_count
    score_scale = HEAD_DIM ** (-0.5)
    key_span = min(512, sequence_rows)
    key_blocks = sequence_rows // key_span
    heads_shape = (tok_rows, HEADS, HEAD_DIM)
    block_shape = (key_blocks, key_span, HEADS, HEAD_DIM)
    slot_shape = (context_size, local_experts * capacity, model_width)
    expert_shape = (context_size, local_experts, capacity, model_width)
    gathered_gains, gathered_in, gathered_out, gathered_router = (
        lax.all_gather(norm_gains, ("dp", "ctx"), axis=0, tiled=True),
        lax.all_gather(project_in, ("dp", "ctx"), axis=0, tiled=True),
        lax.all_gather(project_out, ("dp", "ctx"), axis=0, tiled=True),
        lax.all_gather(router_weight, ("dp", "ctx"), axis=0, tiled=True),
    )
    gathered_first, gathered_second = (
        lax.all_gather(expert_in, "dp", axis=1, tiled=True),
        lax.all_gather(expert_out, "dp", axis=1, tiled=True),
    )
    gain_rows = gathered_gains.astype(jnp.float32)
    own_rows = lax.axis_index("ctx") * tok_rows + jnp.arange(tok_rows, dtype=jnp.int32)
    own_place = dealt_positions(own_rows, tok_rows, context_size)
    all_place = dealt_positions(jnp.arange(sequence_rows, dtype=jnp.int32), tok_rows, context_size)
    document_row = document_ids[0]
    own_document = jnp.take(document_row, own_place)
    all_document = jnp.take(document_row, all_place)
    relative = own_place - jnp.take(document_starts(document_row), own_place)
    cosine, sine_table = rotary_tables(relative, HEAD_DIM)
    attend_inverse = inverse_rms(inputs)
    attend_normed = inputs * attend_inverse
    attend_in = (attend_normed * gain_rows[:, 0]).astype(jnp.bfloat16)
    projected = jnp.dot(attend_in, gathered_in, preferred_element_type=jnp.float32)
    raw_query = projected[:, :model_width]
    raw_key = projected[:, model_width : 2 * model_width]
    query_inverse = inverse_rms(raw_query)
    query_normed = raw_query * query_inverse
    key_inverse = inverse_rms(raw_key)
    key_normed = raw_key * key_inverse
    query_low = rotate(
        (query_normed * gain_rows[:, 1]).reshape(heads_shape), cosine, sine_table
    ).astype(jnp.bfloat16)
    key_low = rotate(
        (key_normed * gain_rows[:, 2]).reshape(heads_shape), cosine, sine_table
    ).astype(jnp.bfloat16)
    value_low = projected[:, 2 * model_width :].astype(jnp.bfloat16)
    key_all, value_all = (
        lax.all_gather(key_low.reshape(tok_rows, model_width), "ctx", axis=0, tiled=True),
        lax.all_gather(value_low, "ctx", axis=0, tiled=True),
    )
    key_split = key_all.reshape(block_shape)
    value_split = value_all.reshape(block_shape)
    place_split = all_place.reshape(key_blocks, key_span)
    document_split = all_document.reshape(key_blocks, key_span)

    def total_step(state_pair, block_args):
        row_peak, row_total = state_pair
        key_block, key_place, key_document = block_args
        scores, visible = block_scores(
            query_low, key_block, own_place, own_document, key_place, key_document, score_scale
        )
        new_peak = jnp.maximum(row_peak, jnp.max(scores, axis=-1))
        fresh_total = jnp.sum(
            jnp.where(visible, jnp.exp(scores - new_peak[..., None]), 0.0), axis=-1
        )
        return ((new_peak, row_total * jnp.exp(row_peak - new_peak) + fresh_total), None)

    start_pair = (
        jnp.full((HEADS, tok_rows), MASKED, jnp.float32),
        jnp.zeros((HEADS, tok_rows), jnp.float32),
    )
    (row_peak, row_total), unused = lax.scan(
        total_step, start_pair, (key_split, place_split, document_split)
    )
    row_logsum = row_peak + jnp.log(row_total)

    def value_step(running, block_args):
        key_block, value_block, key_place, key_document = block_args
        scores, visible = block_scores(
            query_low, key_block, own_place, own_document, key_place, key_document, score_scale
        )
        prob_low = jnp.where(visible, jnp.exp(scores - row_logsum[..., None]), 0.0).astype(
            jnp.bfloat16
        )
        return (
            running
            + jnp.einsum("htk,khd->thd", prob_low, value_block, preferred_element_type=jnp.float32),
            None,
        )

    attend_out, unused = lax.scan(
        value_step,
        jnp.zeros(heads_shape, jnp.float32),
        (key_split, value_split, place_split, document_split),
    )
    attend_low = attend_out.reshape(tok_rows, model_width).astype(jnp.bfloat16)
    residual = inputs + jnp.dot(attend_low, gathered_out, preferred_element_type=jnp.float32)
    mixed_inverse = inverse_rms(residual)
    mixed_normed = residual * mixed_inverse
    mixed_low = (mixed_normed * gain_rows[:, 3]).astype(jnp.bfloat16)
    logits = jnp.dot(mixed_low, gathered_router, preferred_element_type=jnp.float32)
    route_onehot = (route_rows[..., None] == jnp.arange(expert_count, dtype=jnp.int32)).astype(
        jnp.float32
    )
    gate_weights = jax.nn.softmax(jnp.sum(route_onehot * logits[:, None, :], axis=-1), axis=-1)
    target_slot, slot_owner = dispatch_plan(route_rows, expert_count, capacity)
    padded_rows = jnp.concatenate([mixed_low, jnp.zeros((1, model_width), jnp.bfloat16)], axis=0)
    send_rows = jnp.take(padded_rows, slot_owner // top_count, axis=0).reshape(slot_shape)
    received = lax.all_to_all(send_rows, "ctx", split_axis=0, concat_axis=0, tiled=True).reshape(
        expert_shape
    )
    expert_up = jnp.einsum(
        "sxcd,xdf->sxcf", received, gathered_first, preferred_element_type=jnp.float32
    )
    gate_part = expert_up[..., :FF]
    up_part = expert_up[..., FF:]
    sigmoid_gate = jax.nn.sigmoid(gate_part)
    swish_gate = gate_part * sigmoid_gate
    hidden_low = (swish_gate * up_part).astype(jnp.bfloat16)
    expert_result = jnp.einsum(
        "sxcf,xfd->sxcd", hidden_low, gathered_second, preferred_element_type=jnp.float32
    ).astype(jnp.bfloat16)
    returned = lax.all_to_all(
        expert_result.reshape(slot_shape), "ctx", split_axis=0, concat_axis=0, tiled=True
    ).reshape(expert_count * capacity, model_width)
    pair_result = jnp.take(returned, target_slot, axis=0).reshape(tok_rows, top_count, model_width)
    mixture = jnp.sum(gate_weights[..., None] * pair_result, axis=1)
    layer_output = (residual + mixture).astype(jnp.bfloat16)
    upstream = cotangent[0].astype(jnp.float32)
    pair_back = (gate_weights[..., None] * upstream[:, None, :]).astype(jnp.bfloat16)
    gate_back = jnp.sum(pair_result * upstream[:, None, :], axis=-1)
    padded_back = jnp.concatenate(
        [
            pair_back.reshape(tok_rows * top_count, model_width),
            jnp.zeros((1, model_width), jnp.bfloat16),
        ],
        axis=0,
    )
    send_back = jnp.take(padded_back, slot_owner, axis=0).reshape(slot_shape)
    received_back = lax.all_to_all(
        send_back, "ctx", split_axis=0, concat_axis=0, tiled=True
    ).reshape(expert_shape)
    first_back, second_back = (gathered_first, gathered_second)
    hidden_back = jnp.einsum(
        "sxcd,xfd->sxcf", received_back, second_back, preferred_element_type=jnp.float32
    )
    second_weight_back = jnp.einsum(
        "sxcf,sxcd->xfd", hidden_low, received_back, preferred_element_type=jnp.float32
    )
    swish_slope = sigmoid_gate * (1.0 + gate_part * (1.0 - sigmoid_gate))
    up_back = jnp.concatenate(
        [hidden_back * up_part * swish_slope, hidden_back * swish_gate], axis=-1
    ).astype(jnp.bfloat16)
    first_weight_back = jnp.einsum(
        "sxcd,sxcf->xdf", received, up_back, preferred_element_type=jnp.float32
    )
    input_back = jnp.einsum(
        "sxcf,xdf->sxcd", up_back, first_back, preferred_element_type=jnp.float32
    ).astype(jnp.bfloat16)
    expert_in_gradient, expert_out_gradient = (
        lax.psum_scatter(
            first_weight_back.astype(jnp.bfloat16), "dp", scatter_dimension=1, tiled=True
        ).astype(jnp.float32),
        lax.psum_scatter(
            second_weight_back.astype(jnp.bfloat16), "dp", scatter_dimension=1, tiled=True
        ).astype(jnp.float32),
    )
    rows_back = lax.all_to_all(
        input_back.reshape(slot_shape), "ctx", split_axis=0, concat_axis=0, tiled=True
    ).reshape(expert_count * capacity, model_width)
    mixed_back = jnp.sum(
        jnp.take(rows_back, target_slot, axis=0)
        .reshape(tok_rows, top_count, model_width)
        .astype(jnp.float32),
        axis=1,
    )
    gains_back, in_back, out_back, router_back = (
        gathered_gains,
        gathered_in,
        gathered_out,
        gathered_router,
    )
    gain_values = gains_back.astype(jnp.float32)
    chosen_back = gate_weights * (
        gate_back - jnp.sum(gate_weights * gate_back, axis=-1, keepdims=True)
    )
    logit_back = jnp.sum(chosen_back[..., None] * route_onehot, axis=1).astype(jnp.bfloat16)
    router_weight_back = jnp.einsum(
        "td,te->de", mixed_low, logit_back, preferred_element_type=jnp.float32
    )
    mixed_back = mixed_back + jnp.einsum(
        "te,de->td", logit_back, router_back, preferred_element_type=jnp.float32
    )
    mixed_gain_back = jnp.sum(mixed_back * mixed_normed, axis=0)
    residual_back = upstream + normalize_back(
        mixed_back * gain_values[:, 3], mixed_normed, mixed_inverse
    )
    residual_low = residual_back.astype(jnp.bfloat16)
    out_weight_back = jnp.einsum(
        "td,te->de", attend_low, residual_low, preferred_element_type=jnp.float32
    )
    attend_back = (
        jnp.einsum("te,de->td", residual_low, out_back, preferred_element_type=jnp.float32)
        .astype(jnp.bfloat16)
        .reshape(heads_shape)
    )
    row_delta = jnp.einsum("thd,thd->ht", attend_back.astype(jnp.float32), attend_out)

    def back_step(query_acc, block_args):
        key_block, value_block, key_place, key_document = block_args
        query_part, key_part, value_part = block_backward(
            query_low,
            attend_back,
            row_logsum,
            row_delta,
            key_block,
            value_block,
            own_place,
            own_document,
            key_place,
            key_document,
            score_scale,
        )
        return (query_acc + query_part, (key_part, value_part))

    query_back, (key_parts, value_parts) = lax.scan(
        back_step,
        jnp.zeros(heads_shape, jnp.float32),
        (key_split, value_split, place_split, document_split),
    )
    key_back, value_back = (
        lax.psum_scatter(
            key_parts.reshape(sequence_rows, model_width).astype(jnp.bfloat16),
            "ctx",
            scatter_dimension=0,
            tiled=True,
        ).astype(jnp.float32),
        lax.psum_scatter(
            value_parts.reshape(sequence_rows, model_width).astype(jnp.bfloat16),
            "ctx",
            scatter_dimension=0,
            tiled=True,
        ).astype(jnp.float32),
    )
    query_flat = rotate(query_back, cosine, -sine_table).reshape(tok_rows, model_width)
    key_flat = rotate(key_back.reshape(heads_shape), cosine, -sine_table).reshape(
        tok_rows, model_width
    )
    query_gain_back = jnp.sum(query_flat * query_normed, axis=0)
    key_gain_back = jnp.sum(key_flat * key_normed, axis=0)
    raw_query_back = normalize_back(query_flat * gain_values[:, 1], query_normed, query_inverse)
    raw_key_back = normalize_back(key_flat * gain_values[:, 2], key_normed, key_inverse)
    raw_back = jnp.concatenate([raw_query_back, raw_key_back, value_back], axis=-1).astype(
        jnp.bfloat16
    )
    in_weight_back = jnp.einsum(
        "td,tf->df", attend_in, raw_back, preferred_element_type=jnp.float32
    )
    attend_in_back = jnp.einsum("tf,df->td", raw_back, in_back, preferred_element_type=jnp.float32)
    attend_gain_back = jnp.sum(attend_in_back * attend_normed, axis=0)
    tokens_back = residual_back + normalize_back(
        attend_in_back * gain_values[:, 0], attend_normed, attend_inverse
    )
    gain_columns = jnp.stack(
        [attend_gain_back, query_gain_back, key_gain_back, mixed_gain_back], axis=1
    )
    gains_gradient, project_in_gradient, project_out_gradient, router_gradient = (
        lax.psum_scatter(gain_columns, ("dp", "ctx"), scatter_dimension=0, tiled=True),
        lax.psum_scatter(in_weight_back, ("dp", "ctx"), scatter_dimension=0, tiled=True),
        lax.psum_scatter(out_weight_back, ("dp", "ctx"), scatter_dimension=0, tiled=True),
        lax.psum_scatter(router_weight_back, ("dp", "ctx"), scatter_dimension=0, tiled=True),
    )
    return (
        layer_output[None],
        tokens_back.astype(jnp.bfloat16)[None],
        gains_gradient,
        project_in_gradient,
        project_out_gradient,
        router_gradient,
        expert_in_gradient,
        expert_out_gradient,
    )


MESH = pl.DeviceIdType.MESH
VMEM_LIMIT = 48 * 1024 * 1024


def ring_place(device, n):
    odd = device % 2
    return (1 - odd) * (device // 2) + odd * (n - 1 - device // 2)


def ring_device(place, n):
    far = place // (n // 2)
    return (1 - far) * (2 * place) + far * (2 * (n - 1 - place) + 1)


class Ring:
    def __init__(self, n):
        self.n = n
        self.me = lax.axis_index("ctx")
        self.place = ring_place(self.me, n)

    def at(self, offset):
        return ring_device((self.place + offset + self.n) % self.n, self.n)

    def hops(self, way, half):
        return self.n // 2 if way == half else self.n // 2 - 1

    def barrier(self, others):
        semaphore = pltpu.get_barrier_semaphore()
        for other in others:
            pl.semaphore_signal(semaphore, inc=1, device_id=other, device_id_type=MESH)
        pl.semaphore_wait(semaphore, len(others))

    def neighbours(self):
        return [{"ctx": self.at(1)}, {"ctx": self.at(-1)}]


def remote(source, target, send, receive, device):
    return pltpu.make_async_remote_copy(
        src_ref=source,
        dst_ref=target,
        send_sem=send,
        recv_sem=receive,
        device_id=device,
        device_id_type=MESH,
    )


def gather_steps(ring, source, place, send, receive, arrived=None, ready=None):
    signs = (1, -1)

    def copy(way, half, hop):
        origin = ring.at(-signs[way] * hop)
        spot = place(origin, half)
        return remote(
            source(half) if hop == 0 else spot,
            spot,
            send.at[way, half, hop],
            receive.at[way, half, hop],
            {"ctx": ring.at(signs[way])},
        )

    def landed(way, half, hop):
        spot = place(ring.at(-signs[way] * (hop + 1)), half)
        return remote(
            spot,
            spot,
            send.at[way, half, hop],
            receive.at[way, half, hop],
            {"ctx": ring.at(signs[way])},
        )

    started = []
    for half in (0, 1):
        if ready is not None:
            ready(half)
        for way in (0, 1):
            started.append(copy(way, half, 0))
            started[-1].start()
        yield
    for hop in range(ring.n // 2):
        for half in (0, 1):
            for way in (0, 1):
                if hop < ring.hops(way, half):
                    landed(way, half, hop).wait_recv()
                    if hop + 1 < ring.hops(way, half):
                        started.append(copy(way, half, hop + 1))
                        started[-1].start()
                    if arrived is not None:
                        arrived(way, half, hop, ring.at(-signs[way] * (hop + 1)))
                    yield
    for one in started:
        one.wait_send()


def scatter_steps(ring, part, slots, store, send, receive):
    signs = (1, -1)

    def copy(way, half, hop, source):
        return remote(
            source,
            slots.at[way, half, hop],
            send.at[way, half, hop],
            receive.at[way, half, hop],
            {"ctx": ring.at(signs[way])},
        )

    started = []
    for half in (0, 1):
        for way in (0, 1):
            goal = ring.at(signs[way] * ring.hops(way, half))
            started.append(copy(way, half, 0, part(goal, half)))
            started[-1].start()
        yield
    for hop in range(ring.n // 2):
        for half in (0, 1):
            for way in (0, 1):
                last = ring.hops(way, half) - 1
                if hop <= last:
                    slot = slots.at[way, half, hop]
                    copy(way, half, hop, slot).wait_recv()
                    if hop < last:
                        goal = ring.at(signs[way] * (last - hop))
                        slot[...] = (
                            slot[...].astype(jnp.float32)
                            + part(goal, half)[...].astype(jnp.float32)
                        ).astype(slot.dtype)
                        started.append(copy(way, half, hop + 1, slot))
                        started[-1].start()
                    yield
    for half in (0, 1):
        total = part(ring.me, half)[...].astype(jnp.float32)
        for way in (0, 1):
            total = total + slots[way, half, ring.hops(way, half) - 1].astype(jnp.float32)
        store(half, total)
    for one in started:
        one.wait_send()


def run_steps(*tasks):
    tasks = list(tasks)
    while tasks:
        left = []
        for task in tasks:
            try:
                next(task)
                left.append(task)
            except StopIteration:
                pass
        tasks = left


def sems(*shape):
    return pltpu.SemaphoreType.DMA(shape)


def kernel_call(body, outs, in_specs, out_specs, scratch, identity, name, sent):
    return pl.pallas_call(
        body,
        out_shape=outs,
        in_specs=in_specs,
        out_specs=out_specs,
        scratch_shapes=scratch,
        name=name,
        cost_estimate=pl.CostEstimate(flops=0, bytes_accessed=sent, transcendentals=0),
        compiler_params=pltpu.CompilerParams(
            collective_id=identity, has_side_effects=True, vmem_limit_bytes=VMEM_LIMIT
        ),
    )


ANY = pl.BlockSpec(memory_space=pl.ANY)
VMEM = pl.BlockSpec(memory_space=pltpu.VMEM)


def ring_gather(block, n, identity, name, axis=0):
    rows, width = block.shape
    half_rows = rows // 2
    shape = (rows * n, width) if axis == 0 else (rows, width * n)

    def body(block_ref, all_ref, send, receive, local):
        ring = Ring(n)

        def place(device, half):
            if axis == 0:
                return all_ref.at[pl.ds(pl.multiple_of(device * rows + half * half_rows, 16), half_rows)]
            return all_ref.at[
                pl.ds(half * half_rows, half_rows), pl.ds(pl.multiple_of(device * width, 128), width)
            ]

        whole = (
            all_ref.at[pl.ds(pl.multiple_of(ring.me * rows, 16), rows)]
            if axis == 0
            else all_ref.at[:, pl.ds(pl.multiple_of(ring.me * width, 128), width)]
        )
        own = pltpu.make_async_copy(block_ref, whole, local)
        own.start()
        ring.barrier(ring.neighbours())
        run_steps(
            gather_steps(
                ring,
                lambda half: block_ref.at[pl.ds(half * half_rows, half_rows)],
                place,
                send,
                receive,
            )
        )
        own.wait()

    return kernel_call(
        body,
        jax.ShapeDtypeStruct(shape, block.dtype),
        [ANY],
        ANY,
        [sems(2, 2, n // 2), sems(2, 2, n // 2), pltpu.SemaphoreType.DMA],
        identity,
        name,
        block.size * 2 * n * 32,
    )(block)


def ring_scatter(partial, n, identity, name):
    rows, width = partial.shape[0] // n, partial.shape[1]
    half_rows = rows // 2

    def body(part_ref, sum_ref, slots, send, receive):
        ring = Ring(n)
        ring.barrier(ring.neighbours())

        def part(device, half):
            return part_ref.at[pl.ds(pl.multiple_of(device * rows + half * half_rows, 16), half_rows)]

        def store(half, total):
            sum_ref[pl.ds(half * half_rows, half_rows)] = total

        run_steps(scatter_steps(ring, part, slots, store, send, receive))

    return kernel_call(
        body,
        jax.ShapeDtypeStruct((rows, width), jnp.float32),
        [VMEM],
        VMEM,
        [
            pltpu.VMEM((2, 2, n // 2, half_rows, width), partial.dtype),
            sems(2, 2, n // 2),
            sems(2, 2, n // 2),
        ],
        identity,
        name,
        partial.size * 2 * 32,
    )(partial)


def direct_exchange(blocks, n, identity, name):
    def body(block_ref, got_ref, send, receive):
        me = lax.axis_index("ctx")
        ring = Ring(n)
        ring.barrier([{"ctx": (me + k) % n} for k in range(1, n)])
        got_ref[me] = block_ref[me]
        copies = []
        for k in range(1, n):
            other = (me + k) % n
            copies.append(
                remote(
                    block_ref.at[other],
                    got_ref.at[me],
                    send.at[k - 1],
                    receive.at[k - 1],
                    {"ctx": other},
                )
            )
            copies[-1].start()
        for k in range(1, n):
            spot = got_ref.at[(me - k + n) % n]
            remote(
                spot, spot, send.at[k - 1], receive.at[k - 1], {"ctx": (me + k) % n}
            ).wait_recv()
        for copy in copies:
            copy.wait_send()

    return kernel_call(
        body,
        jax.ShapeDtypeStruct(blocks.shape, blocks.dtype),
        [VMEM],
        VMEM,
        [sems(n - 1), sems(n - 1)],
        identity,
        name,
        blocks.size * 64,
    )(blocks)


def partners():
    dp = lax.axis_index("dp")
    core = dp + 1 - 2 * (dp % 2)
    chip = (dp + 2) % 4
    return dp, core, chip, (core + 2) % 4


def gather_inputs(tokens, named, in_blocks, out_rows, n, n_dp, identity):
    tok_rows, width = tokens.shape
    weight_rows, in_width = in_blocks.shape[1:]

    def body(
        token_ref,
        named_ref,
        in_ref,
        out_ref,
        token_all,
        named_all,
        in_all,
        out_all,
        token_send,
        token_receive,
        out_send,
        out_receive,
        core_send,
        core_receive,
        own_send,
        own_receive,
        named_send,
        named_receive,
        in_send,
        in_receive,
        pass_send,
        pass_receive,
        local,
    ):
        ring = Ring(n)
        me = ring.me
        dp, core, chip, core_chip = partners()
        half_rows = tok_rows // 2

        def token_place(device, half):
            return token_all.at[
                pl.ds(pl.multiple_of(device * tok_rows + half * half_rows, 16), half_rows)
            ]

        def out_place(group, device):
            return out_all.at[
                pl.ds(pl.multiple_of((group * n + device) * weight_rows, 16), weight_rows)
            ]

        locals_ = [
            pltpu.make_async_copy(in_ref.at[me], in_all.at[dp, me], local.at[0]),
            pltpu.make_async_copy(
                token_ref,
                token_all.at[pl.ds(pl.multiple_of(me * tok_rows, 16), tok_rows)],
                local.at[1],
            ),
            pltpu.make_async_copy(named_ref, named_all.at[me], local.at[2]),
            pltpu.make_async_copy(out_ref, out_place(dp, me), local.at[3]),
        ]
        for copy in locals_:
            copy.start()
        others = [(me + k) % n for k in range(1, n)]
        ring.barrier([{"ctx": other} for other in others] + [{"dp": core}, {"dp": chip}])

        out_copies = [
            remote(out_ref, out_place(dp, me), own_send.at[0], own_receive.at[0], {"dp": chip}),
            remote(out_ref, out_place(dp, me), own_send.at[1], own_receive.at[1], {"dp": core}),
        ]
        for copy in out_copies:
            copy.start()
        direct = []
        for k, other in enumerate(others):
            direct.append(
                remote(in_ref.at[other], in_all.at[dp, me], in_send.at[k], in_receive.at[k], {"ctx": other})
            )
            direct.append(
                remote(named_ref, named_all.at[me], named_send.at[k], named_receive.at[k], {"ctx": other})
            )
        for copy in direct:
            copy.start()

        def out_ready(half):
            if half == 1:
                spot = out_place(chip, me)
                remote(spot, spot, own_send.at[0], own_receive.at[0], {"dp": chip}).wait_recv()
                out_copies.append(
                    remote(spot, spot, own_send.at[2], own_receive.at[2], {"dp": core})
                )
                out_copies[-1].start()

        def out_arrived(way, half, hop, origin):
            spot = out_place(chip if half else dp, origin)
            out_copies.append(
                remote(
                    spot,
                    spot,
                    core_send.at[way, half, hop],
                    core_receive.at[way, half, hop],
                    {"dp": core},
                )
            )
            out_copies[-1].start()

        def in_steps():
            for _ in range(2):
                yield
            for k in range(1, n):
                spot = in_all.at[dp, (me - k + n) % n]
                remote(
                    spot, spot, in_send.at[k - 1], in_receive.at[k - 1], {"ctx": others[k - 1]}
                ).wait_recv()
            locals_[0].wait()
            passed = []
            for at, to in ((0, chip), (1, core)):
                passed.append(
                    remote(
                        in_all.at[dp], in_all.at[dp], pass_send.at[at], pass_receive.at[at], {"dp": to}
                    )
                )
                passed[-1].start()
            for _ in range(6):
                yield
            spot = in_all.at[chip]
            remote(spot, spot, pass_send.at[0], pass_receive.at[0], {"dp": chip}).wait_recv()
            passed.append(
                remote(spot, spot, pass_send.at[2], pass_receive.at[2], {"dp": core})
            )
            passed[-1].start()
            for _ in range(6):
                yield
            for at, source in ((1, core), (2, core_chip)):
                spot = in_all.at[source]
                remote(
                    spot, spot, pass_send.at[at], pass_receive.at[at], {"dp": core}
                ).wait_recv()
            for copy in passed:
                copy.wait_send()

        run_steps(
            gather_steps(
                ring,
                lambda half: token_ref.at[pl.ds(half * half_rows, half_rows)],
                token_place,
                token_send,
                token_receive,
            ),
            gather_steps(
                ring,
                lambda half: out_place(chip, me) if half else out_ref,
                lambda device, half: out_place(chip if half else dp, device),
                out_send,
                out_receive,
                out_arrived,
                out_ready,
            ),
            in_steps(),
        )
        for k in range(1, n):
            spot = named_all.at[(me - k + n) % n]
            remote(
                spot, spot, named_send.at[k - 1], named_receive.at[k - 1], {"ctx": others[k - 1]}
            ).wait_recv()
        for at, group in ((1, core), (2, core_chip)):
            spot = out_place(group, me)
            remote(spot, spot, own_send.at[at], own_receive.at[at], {"dp": core}).wait_recv()
        for way, sign in ((0, 1), (1, -1)):
            for half in (0, 1):
                for hop in range(ring.hops(way, half)):
                    spot = out_place(core_chip if half else core, ring.at(-sign * (hop + 1)))
                    remote(
                        spot,
                        spot,
                        core_send.at[way, half, hop],
                        core_receive.at[way, half, hop],
                        {"dp": core},
                    ).wait_recv()
        for copy in direct + out_copies:
            copy.wait_send()
        for copy in locals_[1:]:
            copy.wait()

    return kernel_call(
        body,
        (
            jax.ShapeDtypeStruct((tok_rows * n, width), tokens.dtype),
            jax.ShapeDtypeStruct((n,) + named.shape, named.dtype),
            jax.ShapeDtypeStruct((n_dp,) + in_blocks.shape, in_blocks.dtype),
            jax.ShapeDtypeStruct((weight_rows * n * n_dp, out_rows.shape[1]), out_rows.dtype),
        ),
        [ANY] * 4,
        (ANY,) * 4,
        [sems(2, 2, n // 2)] * 6
        + [sems(3)] * 2
        + [sems(n - 1)] * 4
        + [sems(3)] * 2
        + [sems(4)],
        identity,
        "gather_inputs",
        300_000_000,
    )(tokens, named, in_blocks, out_rows)


def scatter_end(row_part, in_part, out_part, n, identity):
    rows, width = row_part.shape[0] // n, row_part.shape[1]
    half_rows = rows // 2
    f32 = jnp.float32

    def body(
        row_ref,
        in_ref,
        out_ref,
        row_sum,
        in_got,
        out_sum,
        slots,
        in_core,
        in_chip,
        out_core,
        out_chip,
        row_send,
        row_receive,
        pass_send,
        pass_receive,
        in_send,
        in_receive,
    ):
        ring = Ring(n)
        me = ring.me
        dp, core, chip, core_chip = partners()
        others = [(me + k) % n for k in range(1, n)]
        ring.barrier([{"ctx": other} for other in others] + [{"dp": core}, {"dp": chip}])

        def part(device, half):
            return row_ref.at[pl.ds(pl.multiple_of(device * rows + half * half_rows, 16), half_rows)]

        def store(half, total):
            row_sum[pl.ds(half * half_rows, half_rows)] = total

        def passing(at, source, target, to):
            return remote(source, target, pass_send.at[at], pass_receive.at[at], {"dp": to})

        def weight_steps():
            passed = [
                passing(0, in_ref.at[core_chip], in_core.at[1], core),
                passing(1, out_ref.at[core_chip], out_core.at[1], core),
                passing(2, in_ref.at[core], in_core.at[0], core),
                passing(3, out_ref.at[core], out_core.at[0], core),
            ]
            for copy in passed:
                copy.start()
            yield
            passed[0].wait_recv()

            def add_far(k, carry):
                in_core[1, k] = (in_core[1, k].astype(f32) + in_ref[chip, k].astype(f32)).astype(in_ref.dtype)
                return carry

            lax.fori_loop(0, n, add_far, 0)
            passed.append(passing(4, in_core.at[1], in_chip, chip))
            passed[-1].start()
            passed[1].wait_recv()
            out_core[1] = (out_core[1].astype(f32) + out_ref[chip].astype(f32)).astype(out_ref.dtype)
            passed.append(passing(5, out_core.at[1], out_chip, chip))
            passed[-1].start()
            for _ in range(4):
                yield
            passed[2].wait_recv()
            passed[3].wait_recv()
            passed[4].wait_recv()

            def add_near(k, carry):
                in_core[0, k] = (
                    in_core[0, k].astype(f32) + in_ref[dp, k].astype(f32) + in_chip[k].astype(f32)
                ).astype(in_ref.dtype)
                return carry

            lax.fori_loop(0, n, add_near, 0)
            direct = []
            for k, other in enumerate(others):
                direct.append(
                    remote(in_core.at[0, other], in_got.at[me], in_send.at[k], in_receive.at[k], {"ctx": other})
                )
                direct[-1].start()
            in_got[me] = in_core[0, me]
            passed[5].wait_recv()
            out_sum[...] = (
                out_core[0].astype(f32) + out_ref[dp].astype(f32) + out_chip[...].astype(f32)
            ).astype(out_ref.dtype)
            for _ in range(8):
                yield
            for k in range(1, n):
                spot = in_got.at[(me - k + n) % n]
                remote(
                    spot, spot, in_send.at[k - 1], in_receive.at[k - 1], {"ctx": others[k - 1]}
                ).wait_recv()
            for copy in passed + direct:
                copy.wait_send()

        run_steps(scatter_steps(ring, part, slots, store, row_send, row_receive), weight_steps())

    return kernel_call(
        body,
        (
            jax.ShapeDtypeStruct((rows, width), f32),
            jax.ShapeDtypeStruct(in_part.shape[1:], in_part.dtype),
            jax.ShapeDtypeStruct(out_part.shape[1:], out_part.dtype),
        ),
        [VMEM] * 3,
        (VMEM,) * 3,
        [
            pltpu.VMEM((2, 2, n // 2, half_rows, width), row_part.dtype),
            pltpu.VMEM((2,) + in_part.shape[1:], in_part.dtype),
            pltpu.VMEM(in_part.shape[1:], in_part.dtype),
            pltpu.VMEM((2,) + out_part.shape[1:], out_part.dtype),
            pltpu.VMEM(out_part.shape[1:], out_part.dtype),
            sems(2, 2, n // 2),
            sems(2, 2, n // 2),
            sems(6),
            sems(6),
            sems(n - 1),
            sems(n - 1),
        ],
        identity,
        "scatter_end",
        200_000_000,
    )(row_part, in_part, out_part)


def small_scatter(parts, n, n_dp, identity):
    def body(part_ref, sum_ref, got, send, receive):
        me, dp = lax.axis_index("ctx"), lax.axis_index("dp")
        flat = dp * n + me
        count = n * n_dp
        semaphore = pltpu.get_barrier_semaphore()

        def spot(at):
            return (at // n, at % n)

        for k in range(1, count):
            pl.semaphore_signal(
                semaphore, inc=1, device_id=spot((flat + k) % count), device_id_type=MESH
            )
        pl.semaphore_wait(semaphore, count - 1)
        copies = []
        for k in range(1, count):
            to = (flat + k) % count
            copies.append(
                remote(
                    part_ref.at[to // n, to % n], got.at[k], send.at[k], receive.at[k], spot(to)
                )
            )
            copies[-1].start()
        total = part_ref[dp, me]
        for k in range(1, count):
            copies[k - 1].wait_recv()
            total = total + got[k]
        sum_ref[...] = total
        for copy in copies:
            copy.wait_send()

    shape = parts.shape[2:]
    return kernel_call(
        body,
        jax.ShapeDtypeStruct(shape, parts.dtype),
        [VMEM],
        VMEM,
        [pltpu.VMEM((n * n_dp,) + shape, parts.dtype), sems(n * n_dp), sems(n * n_dp)],
        identity,
        "small_scatter",
        40_000_000,
    )(parts)


def gather_ctx(block):
    return lax.all_gather(block, "ctx", axis=0, tiled=True)


def scatter_ctx(partial):
    return lax.psum_scatter(
        partial.astype(jnp.bfloat16), "ctx", scatter_dimension=0, tiled=True
    ).astype(jnp.float32)


def heads_local(
    tokens,
    document_ids,
    routes,
    norm_gains,
    project_in,
    project_out,
    router_weight,
    expert_in,
    expert_out,
    cotangent,
):
    bf16, f32 = jnp.bfloat16, jnp.float32
    n = lax.axis_size("ctx")
    n_dp = lax.axis_size("dp")
    me = lax.axis_index("ctx")
    tok_rows, width = tokens.shape[1:]
    rows = tok_rows * n
    weight_rows = project_in.shape[0]
    own_heads = HEADS // n
    cols = own_heads * HEAD_DIM
    local_experts = expert_in.shape[0]
    expert_count = local_experts * n
    score_scale = HEAD_DIM ** (-0.5)

    def own(array, size, axis=0):
        return lax.dynamic_slice_in_dim(array, me * size, size, axis)

    named = jnp.any(routes[0][..., None] == jnp.arange(LANES, dtype=jnp.int32), axis=1).astype(bf16)
    small = jnp.concatenate(
        [norm_gains, router_weight, jnp.zeros((weight_rows, LANES - 4 - expert_count), bf16)], axis=1
    )
    in_blocks = project_in.reshape(weight_rows, 3, n, cols).transpose(2, 0, 1, 3)
    in_blocks = jnp.concatenate(
        [
            in_blocks.reshape(n, weight_rows, 3 * cols),
            jnp.broadcast_to(small[None], (n, weight_rows, LANES)),
        ],
        axis=2,
    )
    token_all, named_all, in_all, out_all = gather_inputs(
        tokens[0], named, in_blocks, project_out, n, n_dp, 1
    )
    named_all = named_all.reshape(rows, LANES)[:, :expert_count] > 0
    in_all = in_all.reshape(width, 3 * cols + LANES)
    in_own, small_all = in_all[:, : 3 * cols], in_all[:, 3 * cols :]
    gains = small_all[:, :4].astype(f32)
    router_all = small_all[:, 4 : 4 + expert_count]
    first = lax.all_gather(expert_in, "dp", axis=1, tiled=True)
    second = lax.all_gather(expert_out, "dp", axis=1, tiled=True)
    upstream_all = gather_ctx(cotangent[0])

    def sum_ctx(values):
        shape = values.shape
        block = values.reshape(-1, LANES)
        got = direct_exchange(
            jnp.broadcast_to(block[None], (n,) + block.shape), n, 2, "exchange"
        )
        return jnp.sum(got, axis=0).reshape(shape)

    places = dealt_positions(jnp.arange(rows, dtype=jnp.int32), tok_rows, n)
    document_row = document_ids[0]
    documents = jnp.take(document_row, places)
    relative = places - jnp.take(document_starts(document_row), places)
    cosine, sine = rotary_tables(relative, HEAD_DIM)
    visible = (documents[None, :] == documents[:, None]) & (places[None, :] <= places[:, None])

    inputs = token_all.astype(f32)
    attend_inverse = inverse_rms(inputs)
    attend_in = (inputs * attend_inverse * gains[:, 0]).astype(bf16)
    projected = jnp.dot(attend_in, in_own, preferred_element_type=f32)
    raw = projected[:, : 2 * cols].reshape(rows, 2, cols)
    squares = sum_ctx(jnp.sum(raw * raw, axis=-1))
    inverse = lax.rsqrt(squares / width + EPSILON)[..., None]
    normed = raw * inverse
    pair_gains = own(gains, cols)[:, 1:3].T
    rotated = rotate((normed * pair_gains).reshape(rows, 2 * own_heads, HEAD_DIM), cosine, sine)
    rotated = rotated.reshape(rows, 2, own_heads, HEAD_DIM).astype(bf16)
    query, key = rotated[:, 0], rotated[:, 1]
    value = projected[:, 2 * cols :].astype(bf16).reshape(rows, own_heads, HEAD_DIM)

    scores = jnp.einsum("thd,khd->htk", query, key, preferred_element_type=f32) * score_scale
    scores = jnp.where(visible[None], scores, MASKED)
    peak = jnp.max(scores, axis=-1, keepdims=True)
    powers = jnp.where(visible[None], jnp.exp(scores - peak), 0.0)
    total = jnp.sum(powers, axis=-1, keepdims=True)
    probs = (powers / total).astype(bf16)
    attend_out = jnp.einsum("htk,khd->thd", probs, value, preferred_element_type=f32)
    attend_low = attend_out.reshape(rows, cols).astype(bf16)
    attend_all = ring_gather(attend_low, n, 3, "gather_attention", axis=1)

    residual = inputs + jnp.dot(attend_all, out_all, preferred_element_type=f32)
    mixed_inverse = inverse_rms(residual)
    mixed_low = (residual * mixed_inverse * gains[:, 3]).astype(bf16)
    logits = jnp.dot(mixed_low, router_all, preferred_element_type=f32)
    chosen = jnp.where(named_all, logits, MASKED)
    chosen = jnp.where(named_all, jnp.exp(chosen - jnp.max(chosen, axis=-1, keepdims=True)), 0.0)
    gates = chosen / jnp.sum(chosen, axis=-1, keepdims=True)
    gate_own = own(gates, local_experts, 1).T[..., None]

    expert_up = jnp.einsum("td,xdf->xtf", mixed_low, first, preferred_element_type=f32)
    gate_part, up_part = expert_up[..., :FF], expert_up[..., FF:]
    sigmoid = jax.nn.sigmoid(gate_part)
    swish = gate_part * sigmoid
    hidden = swish * up_part
    hidden_gated = (hidden * gate_own).astype(bf16)
    mixture = jnp.einsum("xtf,xfd->td", hidden_gated, second, preferred_element_type=f32)
    mixture = scatter_ctx(mixture)
    own_residual = own(residual, tok_rows)
    layer_output = (own_residual + mixture).astype(bf16)

    hidden_back = jnp.einsum("td,xfd->xtf", upstream_all, second, preferred_element_type=f32)
    gate_back = jnp.sum(hidden.astype(bf16).astype(f32) * hidden_back, axis=-1)
    hidden_back = hidden_back * gate_own
    slope = sigmoid * (1.0 + gate_part * (1.0 - sigmoid))
    up_back = jnp.concatenate(
        [hidden_back * up_part * slope, hidden_back * swish], axis=-1
    ).astype(bf16)
    second_back = jnp.einsum("xtf,td->xfd", hidden_gated, upstream_all, preferred_element_type=f32)
    first_back = jnp.einsum("td,xtf->xdf", mixed_low, up_back, preferred_element_type=f32)
    first_back, second_back, up_back = lax.optimization_barrier(
        (first_back.astype(bf16), second_back.astype(bf16), up_back)
    )
    expert_in_gradient, expert_out_gradient = (
        lax.psum_scatter(part, "dp", scatter_dimension=1, tiled=True).astype(f32)
        for part in (first_back, second_back)
    )
    mixed_back = ring_scatter(
        jnp.einsum("xtf,xdf->td", up_back, first, preferred_element_type=f32).astype(bf16),
        n,
        4,
        "scatter_rows",
    )
    gate_blocks = gate_back.reshape(local_experts, n, tok_rows).transpose(1, 0, 2)
    gate_blocks = jnp.pad(gate_blocks, ((0, 0), (0, 2 * rows // LANES - local_experts), (0, 0)))
    gate_back = direct_exchange(gate_blocks, n, 2, "exchange")[:, :local_experts]
    gate_back = gate_back.reshape(expert_count, tok_rows).T

    own_gates = own(gates, tok_rows)
    own_mixed = own(mixed_low, tok_rows)
    own_mixed_inverse = own(mixed_inverse, tok_rows)
    own_mixed_normed = own_residual * own_mixed_inverse
    chosen_back = own_gates * (
        gate_back - jnp.sum(own_gates * gate_back, axis=-1, keepdims=True)
    )
    logit_back = chosen_back.astype(bf16)
    router_part = jnp.einsum("td,te->de", own_mixed, logit_back, preferred_element_type=f32)
    mixed_back = mixed_back + jnp.einsum(
        "te,de->td", logit_back, router_all, preferred_element_type=f32
    )
    mixed_gain_back = jnp.sum(mixed_back * own_mixed_normed, axis=0)
    residual_back = cotangent[0].astype(f32) + normalize_back(
        mixed_back * gains[:, 3], own_mixed_normed, own_mixed_inverse
    )
    back_all = ring_gather(residual_back.astype(bf16), n, 5, "gather_back")

    out_part = jnp.einsum("td,te->de", attend_low, back_all, preferred_element_type=f32)
    attend_back = jnp.einsum(
        "td,ed->te", back_all, own(out_all, cols), preferred_element_type=f32
    ).astype(bf16).reshape(rows, own_heads, HEAD_DIM)
    delta = jnp.einsum("thd,thd->ht", attend_back.astype(f32), attend_out)[..., None]
    prob_back = jnp.einsum("thd,khd->htk", attend_back, value, preferred_element_type=f32)
    score_back = (probs.astype(f32) * (prob_back - delta)).astype(bf16)
    query_back = jnp.einsum("htk,khd->thd", score_back, key, preferred_element_type=f32)
    key_back = jnp.einsum("htk,thd->khd", score_back, query, preferred_element_type=f32)
    value_back = jnp.einsum("htk,thd->khd", probs, attend_back, preferred_element_type=f32)
    pair_back = jnp.concatenate([query_back, key_back], axis=1) * score_scale
    pair_back = rotate(pair_back, cosine, -sine).reshape(rows, 2, cols)
    pair_gain_back = jnp.sum(pair_back * normed, axis=0)
    pair_back = pair_back * pair_gains
    means = sum_ctx(jnp.sum(pair_back * normed, axis=-1))[..., None] / width
    pair_back = inverse * (pair_back - normed * means)
    raw_back = jnp.concatenate(
        [pair_back.reshape(rows, 2 * cols), value_back.reshape(rows, cols)], axis=-1
    ).astype(bf16)
    row_part = jnp.einsum("tf,df->td", raw_back, in_own, preferred_element_type=f32).astype(bf16)
    in_part = jnp.einsum("td,tf->df", attend_in, raw_back, preferred_element_type=f32).astype(bf16)
    attend_in_back, in_part, out_part = scatter_end(
        row_part,
        in_part.reshape(n_dp, n, weight_rows, 3 * cols),
        out_part.astype(bf16).reshape(n_dp, weight_rows, width),
        n,
        6,
    )
    pairs = [(d * n + c, c * n_dp + d) for d in range(n_dp) for c in range(n)]
    project_out_gradient = lax.ppermute(out_part, ("dp", "ctx"), pairs).astype(f32)
    in_part = in_part.reshape(n, weight_rows, 3, cols)
    project_in_gradient = in_part.transpose(1, 2, 0, 3).reshape(weight_rows, 3 * width).astype(f32)

    own_inverse = own(attend_inverse, tok_rows)
    own_normed = tokens[0].astype(f32) * own_inverse
    attend_gain_back = jnp.sum(attend_in_back * own_normed, axis=0)
    tokens_back = residual_back + normalize_back(
        attend_in_back * gains[:, 0], own_normed, own_inverse
    )
    pair_columns = lax.dynamic_update_slice_in_dim(
        jnp.zeros((width, 2), f32), pair_gain_back.T, me * cols, 0
    )
    small_part = jnp.concatenate(
        [attend_gain_back[:, None], pair_columns, mixed_gain_back[:, None], router_part], axis=1
    )
    small_width = small_part.shape[1]
    small_rows = -(-weight_rows * small_width // (8 * LANES)) * 8
    small_part = jnp.pad(
        small_part.reshape(n_dp * n, weight_rows * small_width),
        ((0, 0), (0, small_rows * LANES - weight_rows * small_width)),
    )
    small_gradient = small_scatter(small_part.reshape(n_dp, n, small_rows, LANES), n, n_dp, 7)
    small_gradient = small_gradient.reshape(-1)[: weight_rows * small_width]
    small_gradient = small_gradient.reshape(weight_rows, small_width)
    return (
        layer_output[None],
        tokens_back.astype(bf16)[None],
        small_gradient[:, :4],
        project_in_gradient,
        project_out_gradient,
        small_gradient[:, 4:],
        expert_in_gradient,
        expert_out_gradient,
    )


def solution(mesh):
    n = mesh.shape["ctx"]
    split_heads = HEADS % n == 0 and n % 4 == 0 and mesh.shape["dp"] == 4
    placed = (
        P("dp", "ctx", None),
        P("dp", None),
        P("dp", "ctx", None),
        P(("dp", "ctx"), None),
        P(("dp", "ctx"), None),
        P(("dp", "ctx"), None),
        P(("dp", "ctx"), None),
        P("ctx", "dp", None),
        P("ctx", "dp", None),
        P("dp", "ctx", None),
    )
    return jax.shard_map(
        heads_local if split_heads else gathered_local,
        mesh=mesh,
        in_specs=placed,
        out_specs=(
            P("dp", "ctx", None),
            P("dp", "ctx", None),
            P(("dp", "ctx"), None),
            P(("dp", "ctx"), None),
            P(("dp", "ctx"), None),
            P(("dp", "ctx"), None),
            P("ctx", "dp", None),
            P("ctx", "dp", None),
        ),
        check_vma=False,
    )
```

```python
import jax
import jax.numpy as jnp
from jax import lax
from jax.experimental import pallas as pl
from jax.experimental.pallas import tpu as pltpu
from jax.sharding import PartitionSpec as P

HEADS = 16
HEAD_DIM = 128
FF = 1024


EPSILON = 1e-05
ROPE_BASE = 10000.0
MASKED = -1e30
LANES = 128


def inverse_rms(values):
    return lax.rsqrt(jnp.mean(values * values, axis=-1, keepdims=True) + EPSILON)


def normalize_back(normed_back, normed, inverse):
    return inverse * (normed_back - normed * jnp.mean(normed_back * normed, axis=-1, keepdims=True))


def rotary_tables(relative, head_dim):
    half_dim = head_dim // 2
    frequency = ROPE_BASE ** (-jnp.arange(half_dim, dtype=jnp.float32) / half_dim)
    angles = relative.astype(jnp.float32)[..., None] * frequency
    return (jnp.cos(angles)[..., None, :], jnp.sin(angles)[..., None, :])


def rotate(values, cosine, sine_table):
    half_dim = values.shape[-1] // 2
    first_half = values[..., :half_dim]
    second_half = values[..., half_dim:]
    return jnp.concatenate(
        [
            first_half * cosine - second_half * sine_table,
            second_half * cosine + first_half * sine_table,
        ],
        axis=-1,
    )


def dealt_positions(indices, tok_rows, context_size):
    half_block = tok_rows // 2
    device = indices // tok_rows
    within = indices % tok_rows
    block_index = jnp.where(within < half_block, device, 2 * context_size - 1 - device)
    return block_index * half_block + within % half_block


def document_starts(document_row):
    places = jnp.arange(document_row.shape[-1], dtype=jnp.int32)
    head_flag = jnp.ones(document_row.shape[:-1] + (1,), jnp.bool_)
    fresh_start = jnp.concatenate(
        [head_flag, document_row[..., 1:] != document_row[..., :-1]], axis=-1
    )
    return lax.cummax(jnp.where(fresh_start, places, 0), axis=document_row.ndim - 1)


def block_scores(
    query_rows, key_block, query_place, query_document, key_place, key_document, score_scale
):
    scores = (
        jnp.einsum("thd,khd->htk", query_rows, key_block, preferred_element_type=jnp.float32)
        * score_scale
    )
    visible = (
        (key_document[None, :] == query_document[:, None])
        & (key_place[None, :] <= query_place[:, None])
    )[None]
    return (jnp.where(visible, scores, MASKED), visible)


def block_backward(
    query_rows,
    output_back,
    row_logsum,
    row_delta,
    key_block,
    value_block,
    query_place,
    query_document,
    key_place,
    key_document,
    score_scale,
):
    scores, visible = block_scores(
        query_rows, key_block, query_place, query_document, key_place, key_document, score_scale
    )
    prob_rows = jnp.where(visible, jnp.exp(scores - row_logsum[..., None]), 0.0)
    prob_back = jnp.einsum(
        "thd,khd->htk", output_back, value_block, preferred_element_type=jnp.float32
    )
    score_back = (prob_rows * (prob_back - row_delta[..., None])).astype(jnp.bfloat16)
    query_part = (
        jnp.einsum("htk,khd->thd", score_back, key_block, preferred_element_type=jnp.float32)
        * score_scale
    )
    key_part = (
        jnp.einsum("htk,thd->khd", score_back, query_rows, preferred_element_type=jnp.float32)
        * score_scale
    )
    value_part = jnp.einsum(
        "htk,thd->khd",
        prob_rows.astype(jnp.bfloat16),
        output_back,
        preferred_element_type=jnp.float32,
    )
    return (query_part, key_part, value_part)


def dispatch_plan(route_rows, expert_count, capacity):
    flat_routes = route_rows.reshape(-1)
    pair_count = flat_routes.shape[0]
    member = (flat_routes[:, None] == jnp.arange(expert_count, dtype=jnp.int32)[None, :]).astype(
        jnp.int32
    )
    earlier = jnp.cumsum(member, axis=0) - member
    target_slot = flat_routes * capacity + jnp.sum(earlier * member, axis=1)
    slot_owner = (
        jnp.full((expert_count * capacity,), pair_count, jnp.int32)
        .at[target_slot]
        .set(jnp.arange(pair_count, dtype=jnp.int32))
    )
    return (target_slot, slot_owner)


def gathered_local(
    tokens,
    document_ids,
    routes,
    norm_gains,
    project_in,
    project_out,
    router_weight,
    expert_in,
    expert_out,
    cotangent,
):
    inputs = tokens[0].astype(jnp.float32)
    tok_rows, model_width = inputs.shape
    context_size = lax.axis_size("ctx")
    sequence_rows = tok_rows * context_size
    local_experts = expert_in.shape[0]
    expert_count = local_experts * context_size
    route_rows = routes[0]
    top_count = route_rows.shape[1]
    capacity = 2 * tok_rows * top_count // expert_count
    score_scale = HEAD_DIM ** (-0.5)
    key_span = min(512, sequence_rows)
    key_blocks = sequence_rows // key_span
    heads_shape = (tok_rows, HEADS, HEAD_DIM)
    block_shape = (key_blocks, key_span, HEADS, HEAD_DIM)
    slot_shape = (context_size, local_experts * capacity, model_width)
    expert_shape = (context_size, local_experts, capacity, model_width)
    gathered_gains, gathered_in, gathered_out, gathered_router = (
        lax.all_gather(norm_gains, ("dp", "ctx"), axis=0, tiled=True),
        lax.all_gather(project_in, ("dp", "ctx"), axis=0, tiled=True),
        lax.all_gather(project_out, ("dp", "ctx"), axis=0, tiled=True),
        lax.all_gather(router_weight, ("dp", "ctx"), axis=0, tiled=True),
    )
    gathered_first, gathered_second = (
        lax.all_gather(expert_in, "dp", axis=1, tiled=True),
        lax.all_gather(expert_out, "dp", axis=1, tiled=True),
    )
    gain_rows = gathered_gains.astype(jnp.float32)
    own_rows = lax.axis_index("ctx") * tok_rows + jnp.arange(tok_rows, dtype=jnp.int32)
    own_place = dealt_positions(own_rows, tok_rows, context_size)
    all_place = dealt_positions(jnp.arange(sequence_rows, dtype=jnp.int32), tok_rows, context_size)
    document_row = document_ids[0]
    own_document = jnp.take(document_row, own_place)
    all_document = jnp.take(document_row, all_place)
    relative = own_place - jnp.take(document_starts(document_row), own_place)
    cosine, sine_table = rotary_tables(relative, HEAD_DIM)
    attend_inverse = inverse_rms(inputs)
    attend_normed = inputs * attend_inverse
    attend_in = (attend_normed * gain_rows[:, 0]).astype(jnp.bfloat16)
    projected = jnp.dot(attend_in, gathered_in, preferred_element_type=jnp.float32)
    raw_query = projected[:, :model_width]
    raw_key = projected[:, model_width : 2 * model_width]
    query_inverse = inverse_rms(raw_query)
    query_normed = raw_query * query_inverse
    key_inverse = inverse_rms(raw_key)
    key_normed = raw_key * key_inverse
    query_low = rotate(
        (query_normed * gain_rows[:, 1]).reshape(heads_shape), cosine, sine_table
    ).astype(jnp.bfloat16)
    key_low = rotate(
        (key_normed * gain_rows[:, 2]).reshape(heads_shape), cosine, sine_table
    ).astype(jnp.bfloat16)
    value_low = projected[:, 2 * model_width :].astype(jnp.bfloat16)
    key_all, value_all = (
        lax.all_gather(key_low.reshape(tok_rows, model_width), "ctx", axis=0, tiled=True),
        lax.all_gather(value_low, "ctx", axis=0, tiled=True),
    )
    key_split = key_all.reshape(block_shape)
    value_split = value_all.reshape(block_shape)
    place_split = all_place.reshape(key_blocks, key_span)
    document_split = all_document.reshape(key_blocks, key_span)

    def total_step(state_pair, block_args):
        row_peak, row_total = state_pair
        key_block, key_place, key_document = block_args
        scores, visible = block_scores(
            query_low, key_block, own_place, own_document, key_place, key_document, score_scale
        )
        new_peak = jnp.maximum(row_peak, jnp.max(scores, axis=-1))
        fresh_total = jnp.sum(
            jnp.where(visible, jnp.exp(scores - new_peak[..., None]), 0.0), axis=-1
        )
        return ((new_peak, row_total * jnp.exp(row_peak - new_peak) + fresh_total), None)

    start_pair = (
        jnp.full((HEADS, tok_rows), MASKED, jnp.float32),
        jnp.zeros((HEADS, tok_rows), jnp.float32),
    )
    (row_peak, row_total), unused = lax.scan(
        total_step, start_pair, (key_split, place_split, document_split)
    )
    row_logsum = row_peak + jnp.log(row_total)

    def value_step(running, block_args):
        key_block, value_block, key_place, key_document = block_args
        scores, visible = block_scores(
            query_low, key_block, own_place, own_document, key_place, key_document, score_scale
        )
        prob_low = jnp.where(visible, jnp.exp(scores - row_logsum[..., None]), 0.0).astype(
            jnp.bfloat16
        )
        return (
            running
            + jnp.einsum("htk,khd->thd", prob_low, value_block, preferred_element_type=jnp.float32),
            None,
        )

    attend_out, unused = lax.scan(
        value_step,
        jnp.zeros(heads_shape, jnp.float32),
        (key_split, value_split, place_split, document_split),
    )
    attend_low = attend_out.reshape(tok_rows, model_width).astype(jnp.bfloat16)
    residual = inputs + jnp.dot(attend_low, gathered_out, preferred_element_type=jnp.float32)
    mixed_inverse = inverse_rms(residual)
    mixed_normed = residual * mixed_inverse
    mixed_low = (mixed_normed * gain_rows[:, 3]).astype(jnp.bfloat16)
    logits = jnp.dot(mixed_low, gathered_router, preferred_element_type=jnp.float32)
    route_onehot = (route_rows[..., None] == jnp.arange(expert_count, dtype=jnp.int32)).astype(
        jnp.float32
    )
    gate_weights = jax.nn.softmax(jnp.sum(route_onehot * logits[:, None, :], axis=-1), axis=-1)
    target_slot, slot_owner = dispatch_plan(route_rows, expert_count, capacity)
    padded_rows = jnp.concatenate([mixed_low, jnp.zeros((1, model_width), jnp.bfloat16)], axis=0)
    send_rows = jnp.take(padded_rows, slot_owner // top_count, axis=0).reshape(slot_shape)
    received = lax.all_to_all(send_rows, "ctx", split_axis=0, concat_axis=0, tiled=True).reshape(
        expert_shape
    )
    expert_up = jnp.einsum(
        "sxcd,xdf->sxcf", received, gathered_first, preferred_element_type=jnp.float32
    )
    gate_part = expert_up[..., :FF]
    up_part = expert_up[..., FF:]
    sigmoid_gate = jax.nn.sigmoid(gate_part)
    swish_gate = gate_part * sigmoid_gate
    hidden_low = (swish_gate * up_part).astype(jnp.bfloat16)
    expert_result = jnp.einsum(
        "sxcf,xfd->sxcd", hidden_low, gathered_second, preferred_element_type=jnp.float32
    ).astype(jnp.bfloat16)
    returned = lax.all_to_all(
        expert_result.reshape(slot_shape), "ctx", split_axis=0, concat_axis=0, tiled=True
    ).reshape(expert_count * capacity, model_width)
    pair_result = jnp.take(returned, target_slot, axis=0).reshape(tok_rows, top_count, model_width)
    mixture = jnp.sum(gate_weights[..., None] * pair_result, axis=1)
    layer_output = (residual + mixture).astype(jnp.bfloat16)
    upstream = cotangent[0].astype(jnp.float32)
    pair_back = (gate_weights[..., None] * upstream[:, None, :]).astype(jnp.bfloat16)
    gate_back = jnp.sum(pair_result * upstream[:, None, :], axis=-1)
    padded_back = jnp.concatenate(
        [
            pair_back.reshape(tok_rows * top_count, model_width),
            jnp.zeros((1, model_width), jnp.bfloat16),
        ],
        axis=0,
    )
    send_back = jnp.take(padded_back, slot_owner, axis=0).reshape(slot_shape)
    received_back = lax.all_to_all(
        send_back, "ctx", split_axis=0, concat_axis=0, tiled=True
    ).reshape(expert_shape)
    first_back, second_back = (gathered_first, gathered_second)
    hidden_back = jnp.einsum(
        "sxcd,xfd->sxcf", received_back, second_back, preferred_element_type=jnp.float32
    )
    second_weight_back = jnp.einsum(
        "sxcf,sxcd->xfd", hidden_low, received_back, preferred_element_type=jnp.float32
    )
    swish_slope = sigmoid_gate * (1.0 + gate_part * (1.0 - sigmoid_gate))
    up_back = jnp.concatenate(
        [hidden_back * up_part * swish_slope, hidden_back * swish_gate], axis=-1
    ).astype(jnp.bfloat16)
    first_weight_back = jnp.einsum(
        "sxcd,sxcf->xdf", received, up_back, preferred_element_type=jnp.float32
    )
    input_back = jnp.einsum(
        "sxcf,xdf->sxcd", up_back, first_back, preferred_element_type=jnp.float32
    ).astype(jnp.bfloat16)
    expert_in_gradient, expert_out_gradient = (
        lax.psum_scatter(
            first_weight_back.astype(jnp.bfloat16), "dp", scatter_dimension=1, tiled=True
        ).astype(jnp.float32),
        lax.psum_scatter(
            second_weight_back.astype(jnp.bfloat16), "dp", scatter_dimension=1, tiled=True
        ).astype(jnp.float32),
    )
    rows_back = lax.all_to_all(
        input_back.reshape(slot_shape), "ctx", split_axis=0, concat_axis=0, tiled=True
    ).reshape(expert_count * capacity, model_width)
    mixed_back = jnp.sum(
        jnp.take(rows_back, target_slot, axis=0)
        .reshape(tok_rows, top_count, model_width)
        .astype(jnp.float32),
        axis=1,
    )
    gains_back, in_back, out_back, router_back = (
        gathered_gains,
        gathered_in,
        gathered_out,
        gathered_router,
    )
    gain_values = gains_back.astype(jnp.float32)
    chosen_back = gate_weights * (
        gate_back - jnp.sum(gate_weights * gate_back, axis=-1, keepdims=True)
    )
    logit_back = jnp.sum(chosen_back[..., None] * route_onehot, axis=1).astype(jnp.bfloat16)
    router_weight_back = jnp.einsum(
        "td,te->de", mixed_low, logit_back, preferred_element_type=jnp.float32
    )
    mixed_back = mixed_back + jnp.einsum(
        "te,de->td", logit_back, router_back, preferred_element_type=jnp.float32
    )
    mixed_gain_back = jnp.sum(mixed_back * mixed_normed, axis=0)
    residual_back = upstream + normalize_back(
        mixed_back * gain_values[:, 3], mixed_normed, mixed_inverse
    )
    residual_low = residual_back.astype(jnp.bfloat16)
    out_weight_back = jnp.einsum(
        "td,te->de", attend_low, residual_low, preferred_element_type=jnp.float32
    )
    attend_back = (
        jnp.einsum("te,de->td", residual_low, out_back, preferred_element_type=jnp.float32)
        .astype(jnp.bfloat16)
        .reshape(heads_shape)
    )
    row_delta = jnp.einsum("thd,thd->ht", attend_back.astype(jnp.float32), attend_out)

    def back_step(query_acc, block_args):
        key_block, value_block, key_place, key_document = block_args
        query_part, key_part, value_part = block_backward(
            query_low,
            attend_back,
            row_logsum,
            row_delta,
            key_block,
            value_block,
            own_place,
            own_document,
            key_place,
            key_document,
            score_scale,
        )
        return (query_acc + query_part, (key_part, value_part))

    query_back, (key_parts, value_parts) = lax.scan(
        back_step,
        jnp.zeros(heads_shape, jnp.float32),
        (key_split, value_split, place_split, document_split),
    )
    key_back, value_back = (
        lax.psum_scatter(
            key_parts.reshape(sequence_rows, model_width).astype(jnp.bfloat16),
            "ctx",
            scatter_dimension=0,
            tiled=True,
        ).astype(jnp.float32),
        lax.psum_scatter(
            value_parts.reshape(sequence_rows, model_width).astype(jnp.bfloat16),
            "ctx",
            scatter_dimension=0,
            tiled=True,
        ).astype(jnp.float32),
    )
    query_flat = rotate(query_back, cosine, -sine_table).reshape(tok_rows, model_width)
    key_flat = rotate(key_back.reshape(heads_shape), cosine, -sine_table).reshape(
        tok_rows, model_width
    )
    query_gain_back = jnp.sum(query_flat * query_normed, axis=0)
    key_gain_back = jnp.sum(key_flat * key_normed, axis=0)
    raw_query_back = normalize_back(query_flat * gain_values[:, 1], query_normed, query_inverse)
    raw_key_back = normalize_back(key_flat * gain_values[:, 2], key_normed, key_inverse)
    raw_back = jnp.concatenate([raw_query_back, raw_key_back, value_back], axis=-1).astype(
        jnp.bfloat16
    )
    in_weight_back = jnp.einsum(
        "td,tf->df", attend_in, raw_back, preferred_element_type=jnp.float32
    )
    attend_in_back = jnp.einsum("tf,df->td", raw_back, in_back, preferred_element_type=jnp.float32)
    attend_gain_back = jnp.sum(attend_in_back * attend_normed, axis=0)
    tokens_back = residual_back + normalize_back(
        attend_in_back * gain_values[:, 0], attend_normed, attend_inverse
    )
    gain_columns = jnp.stack(
        [attend_gain_back, query_gain_back, key_gain_back, mixed_gain_back], axis=1
    )
    gains_gradient, project_in_gradient, project_out_gradient, router_gradient = (
        lax.psum_scatter(gain_columns, ("dp", "ctx"), scatter_dimension=0, tiled=True),
        lax.psum_scatter(in_weight_back, ("dp", "ctx"), scatter_dimension=0, tiled=True),
        lax.psum_scatter(out_weight_back, ("dp", "ctx"), scatter_dimension=0, tiled=True),
        lax.psum_scatter(router_weight_back, ("dp", "ctx"), scatter_dimension=0, tiled=True),
    )
    return (
        layer_output[None],
        tokens_back.astype(jnp.bfloat16)[None],
        gains_gradient,
        project_in_gradient,
        project_out_gradient,
        router_gradient,
        expert_in_gradient,
        expert_out_gradient,
    )


MESH = pl.DeviceIdType.MESH
VMEM_LIMIT = 48 * 1024 * 1024


def ring_place(device, n):
    odd = device % 2
    return (1 - odd) * (device // 2) + odd * (n - 1 - device // 2)


def ring_device(place, n):
    far = place // (n // 2)
    return (1 - far) * (2 * place) + far * (2 * (n - 1 - place) + 1)


class Ring:
    def __init__(self, n):
        self.n = n
        self.me = lax.axis_index("ctx")
        self.place = ring_place(self.me, n)

    def at(self, offset):
        return ring_device((self.place + offset + self.n) % self.n, self.n)

    def hops(self, way, half):
        return self.n // 2 if way == half else self.n // 2 - 1

    def barrier(self, others):
        semaphore = pltpu.get_barrier_semaphore()
        for other in others:
            pl.semaphore_signal(semaphore, inc=1, device_id=other, device_id_type=MESH)
        pl.semaphore_wait(semaphore, len(others))

    def neighbours(self):
        return [{"ctx": self.at(1)}, {"ctx": self.at(-1)}]


def remote(source, target, send, receive, device):
    return pltpu.make_async_remote_copy(
        src_ref=source,
        dst_ref=target,
        send_sem=send,
        recv_sem=receive,
        device_id=device,
        device_id_type=MESH,
    )


def gather_steps(ring, source, place, send, receive, arrived=None, ready=None):
    signs = (1, -1)

    def copy(way, half, hop):
        origin = ring.at(-signs[way] * hop)
        spot = place(origin, half)
        return remote(
            source(half) if hop == 0 else spot,
            spot,
            send.at[way, half, hop],
            receive.at[way, half, hop],
            {"ctx": ring.at(signs[way])},
        )

    def landed(way, half, hop):
        spot = place(ring.at(-signs[way] * (hop + 1)), half)
        return remote(
            spot,
            spot,
            send.at[way, half, hop],
            receive.at[way, half, hop],
            {"ctx": ring.at(signs[way])},
        )

    started = []
    for half in (0, 1):
        if ready is not None:
            ready(half)
        for way in (0, 1):
            started.append(copy(way, half, 0))
            started[-1].start()
        yield
    for hop in range(ring.n // 2):
        for half in (0, 1):
            for way in (0, 1):
                if hop < ring.hops(way, half):
                    landed(way, half, hop).wait_recv()
                    if hop + 1 < ring.hops(way, half):
                        started.append(copy(way, half, hop + 1))
                        started[-1].start()
                    if arrived is not None:
                        arrived(way, half, hop, ring.at(-signs[way] * (hop + 1)))
                    yield
    for one in started:
        one.wait_send()


def scatter_steps(ring, part, slots, store, send, receive):
    signs = (1, -1)

    def copy(way, half, hop, source):
        return remote(
            source,
            slots.at[way, half, hop],
            send.at[way, half, hop],
            receive.at[way, half, hop],
            {"ctx": ring.at(signs[way])},
        )

    started = []
    for half in (0, 1):
        for way in (0, 1):
            goal = ring.at(signs[way] * ring.hops(way, half))
            started.append(copy(way, half, 0, part(goal, half)))
            started[-1].start()
        yield
    for hop in range(ring.n // 2):
        for half in (0, 1):
            for way in (0, 1):
                last = ring.hops(way, half) - 1
                if hop <= last:
                    slot = slots.at[way, half, hop]
                    copy(way, half, hop, slot).wait_recv()
                    if hop < last:
                        goal = ring.at(signs[way] * (last - hop))
                        slot[...] = (
                            slot[...].astype(jnp.float32)
                            + part(goal, half)[...].astype(jnp.float32)
                        ).astype(slot.dtype)
                        started.append(copy(way, half, hop + 1, slot))
                        started[-1].start()
                    yield
    for half in (0, 1):
        total = part(ring.me, half)[...].astype(jnp.float32)
        for way in (0, 1):
            total = total + slots[way, half, ring.hops(way, half) - 1].astype(jnp.float32)
        store(half, total)
    for one in started:
        one.wait_send()


def run_steps(*tasks):
    tasks = list(tasks)
    while tasks:
        left = []
        for task in tasks:
            try:
                next(task)
                left.append(task)
            except StopIteration:
                pass
        tasks = left


def sems(*shape):
    return pltpu.SemaphoreType.DMA(shape)


def kernel_call(body, outs, in_specs, out_specs, scratch, identity, name, sent):
    return pl.pallas_call(
        body,
        out_shape=outs,
        in_specs=in_specs,
        out_specs=out_specs,
        scratch_shapes=scratch,
        name=name,
        cost_estimate=pl.CostEstimate(flops=0, bytes_accessed=sent, transcendentals=0),
        compiler_params=pltpu.CompilerParams(
            collective_id=identity, has_side_effects=True, vmem_limit_bytes=VMEM_LIMIT
        ),
    )


ANY = pl.BlockSpec(memory_space=pl.ANY)
VMEM = pl.BlockSpec(memory_space=pltpu.VMEM)


def ring_gather(block, n, identity, name, axis=0):
    rows, width = block.shape
    half_rows = rows // 2
    shape = (rows * n, width) if axis == 0 else (rows, width * n)

    def body(block_ref, all_ref, send, receive, local):
        ring = Ring(n)

        def place(device, half):
            if axis == 0:
                return all_ref.at[pl.ds(pl.multiple_of(device * rows + half * half_rows, 16), half_rows)]
            return all_ref.at[
                pl.ds(half * half_rows, half_rows), pl.ds(pl.multiple_of(device * width, 128), width)
            ]

        whole = (
            all_ref.at[pl.ds(pl.multiple_of(ring.me * rows, 16), rows)]
            if axis == 0
            else all_ref.at[:, pl.ds(pl.multiple_of(ring.me * width, 128), width)]
        )
        own = pltpu.make_async_copy(block_ref, whole, local)
        own.start()
        ring.barrier(ring.neighbours())
        run_steps(
            gather_steps(
                ring,
                lambda half: block_ref.at[pl.ds(half * half_rows, half_rows)],
                place,
                send,
                receive,
            )
        )
        own.wait()

    return kernel_call(
        body,
        jax.ShapeDtypeStruct(shape, block.dtype),
        [ANY],
        ANY,
        [sems(2, 2, n // 2), sems(2, 2, n // 2), pltpu.SemaphoreType.DMA],
        identity,
        name,
        block.size * 2 * n * 32,
    )(block)


def ring_scatter(partial, n, identity, name):
    rows, width = partial.shape[0] // n, partial.shape[1]
    half_rows = rows // 2

    def body(part_ref, sum_ref, slots, send, receive):
        ring = Ring(n)
        ring.barrier(ring.neighbours())

        def part(device, half):
            return part_ref.at[pl.ds(pl.multiple_of(device * rows + half * half_rows, 16), half_rows)]

        def store(half, total):
            sum_ref[pl.ds(half * half_rows, half_rows)] = total

        run_steps(scatter_steps(ring, part, slots, store, send, receive))

    return kernel_call(
        body,
        jax.ShapeDtypeStruct((rows, width), jnp.float32),
        [VMEM],
        VMEM,
        [
            pltpu.VMEM((2, 2, n // 2, half_rows, width), partial.dtype),
            sems(2, 2, n // 2),
            sems(2, 2, n // 2),
        ],
        identity,
        name,
        partial.size * 2 * 32,
    )(partial)


def direct_exchange(blocks, n, identity, name):
    def body(block_ref, got_ref, send, receive):
        me = lax.axis_index("ctx")
        ring = Ring(n)
        ring.barrier([{"ctx": (me + k) % n} for k in range(1, n)])
        got_ref[me] = block_ref[me]
        copies = []
        for k in range(1, n):
            other = (me + k) % n
            copies.append(
                remote(
                    block_ref.at[other],
                    got_ref.at[me],
                    send.at[k - 1],
                    receive.at[k - 1],
                    {"ctx": other},
                )
            )
            copies[-1].start()
        for k in range(1, n):
            spot = got_ref.at[(me - k + n) % n]
            remote(
                spot, spot, send.at[k - 1], receive.at[k - 1], {"ctx": (me + k) % n}
            ).wait_recv()
        for copy in copies:
            copy.wait_send()

    return kernel_call(
        body,
        jax.ShapeDtypeStruct(blocks.shape, blocks.dtype),
        [VMEM],
        VMEM,
        [sems(n - 1), sems(n - 1)],
        identity,
        name,
        blocks.size * 64,
    )(blocks)


def partners():
    dp = lax.axis_index("dp")
    core = dp + 1 - 2 * (dp % 2)
    chip = (dp + 2) % 4
    return dp, core, chip, (core + 2) % 4


def gather_inputs(tokens, named, in_blocks, out_rows, n, n_dp, identity):
    tok_rows, width = tokens.shape
    weight_rows, in_width = in_blocks.shape[1:]

    def body(
        token_ref,
        named_ref,
        in_ref,
        out_ref,
        token_all,
        named_all,
        in_all,
        out_all,
        token_send,
        token_receive,
        out_send,
        out_receive,
        core_send,
        core_receive,
        own_send,
        own_receive,
        named_send,
        named_receive,
        in_send,
        in_receive,
        pass_send,
        pass_receive,
        local,
    ):
        ring = Ring(n)
        me = ring.me
        dp, core, chip, core_chip = partners()
        half_rows = tok_rows // 2

        def token_place(device, half):
            return token_all.at[
                pl.ds(pl.multiple_of(device * tok_rows + half * half_rows, 16), half_rows)
            ]

        def out_place(group, device):
            return out_all.at[
                pl.ds(pl.multiple_of((group * n + device) * weight_rows, 16), weight_rows)
            ]

        locals_ = [
            pltpu.make_async_copy(in_ref.at[me], in_all.at[dp, me], local.at[0]),
            pltpu.make_async_copy(
                token_ref,
                token_all.at[pl.ds(pl.multiple_of(me * tok_rows, 16), tok_rows)],
                local.at[1],
            ),
            pltpu.make_async_copy(named_ref, named_all.at[me], local.at[2]),
            pltpu.make_async_copy(out_ref, out_place(dp, me), local.at[3]),
        ]
        for copy in locals_:
            copy.start()
        others = [(me + k) % n for k in range(1, n)]
        ring.barrier([{"ctx": other} for other in others] + [{"dp": core}, {"dp": chip}])

        out_copies = [
            remote(out_ref, out_place(dp, me), own_send.at[0], own_receive.at[0], {"dp": chip}),
            remote(out_ref, out_place(dp, me), own_send.at[1], own_receive.at[1], {"dp": core}),
        ]
        for copy in out_copies:
            copy.start()
        direct = []
        for k, other in enumerate(others):
            direct.append(
                remote(in_ref.at[other], in_all.at[dp, me], in_send.at[k], in_receive.at[k], {"ctx": other})
            )
            direct.append(
                remote(named_ref, named_all.at[me], named_send.at[k], named_receive.at[k], {"ctx": other})
            )
        for copy in direct:
            copy.start()

        def out_ready(half):
            if half == 1:
                spot = out_place(chip, me)
                remote(spot, spot, own_send.at[0], own_receive.at[0], {"dp": chip}).wait_recv()
                out_copies.append(
                    remote(spot, spot, own_send.at[2], own_receive.at[2], {"dp": core})
                )
                out_copies[-1].start()

        def out_arrived(way, half, hop, origin):
            spot = out_place(chip if half else dp, origin)
            out_copies.append(
                remote(
                    spot,
                    spot,
                    core_send.at[way, half, hop],
                    core_receive.at[way, half, hop],
                    {"dp": core},
                )
            )
            out_copies[-1].start()

        def in_steps():
            for _ in range(2):
                yield
            for k in range(1, n):
                spot = in_all.at[dp, (me - k + n) % n]
                remote(
                    spot, spot, in_send.at[k - 1], in_receive.at[k - 1], {"ctx": others[k - 1]}
                ).wait_recv()
            locals_[0].wait()
            passed = []
            for at, to in ((0, chip), (1, core)):
                passed.append(
                    remote(
                        in_all.at[dp], in_all.at[dp], pass_send.at[at], pass_receive.at[at], {"dp": to}
                    )
                )
                passed[-1].start()
            for _ in range(6):
                yield
            spot = in_all.at[chip]
            remote(spot, spot, pass_send.at[0], pass_receive.at[0], {"dp": chip}).wait_recv()
            passed.append(
                remote(spot, spot, pass_send.at[2], pass_receive.at[2], {"dp": core})
            )
            passed[-1].start()
            for _ in range(6):
                yield
            for at, source in ((1, core), (2, core_chip)):
                spot = in_all.at[source]
                remote(
                    spot, spot, pass_send.at[at], pass_receive.at[at], {"dp": core}
                ).wait_recv()
            for copy in passed:
                copy.wait_send()

        run_steps(
            gather_steps(
                ring,
                lambda half: token_ref.at[pl.ds(half * half_rows, half_rows)],
                token_place,
                token_send,
                token_receive,
            ),
            gather_steps(
                ring,
                lambda half: out_place(chip, me) if half else out_ref,
                lambda device, half: out_place(chip if half else dp, device),
                out_send,
                out_receive,
                out_arrived,
                out_ready,
            ),
            in_steps(),
        )
        for k in range(1, n):
            spot = named_all.at[(me - k + n) % n]
            remote(
                spot, spot, named_send.at[k - 1], named_receive.at[k - 1], {"ctx": others[k - 1]}
            ).wait_recv()
        for at, group in ((1, core), (2, core_chip)):
            spot = out_place(group, me)
            remote(spot, spot, own_send.at[at], own_receive.at[at], {"dp": core}).wait_recv()
        for way, sign in ((0, 1), (1, -1)):
            for half in (0, 1):
                for hop in range(ring.hops(way, half)):
                    spot = out_place(core_chip if half else core, ring.at(-sign * (hop + 1)))
                    remote(
                        spot,
                        spot,
                        core_send.at[way, half, hop],
                        core_receive.at[way, half, hop],
                        {"dp": core},
                    ).wait_recv()
        for copy in direct + out_copies:
            copy.wait_send()
        for copy in locals_[1:]:
            copy.wait()

    return kernel_call(
        body,
        (
            jax.ShapeDtypeStruct((tok_rows * n, width), tokens.dtype),
            jax.ShapeDtypeStruct((n,) + named.shape, named.dtype),
            jax.ShapeDtypeStruct((n_dp,) + in_blocks.shape, in_blocks.dtype),
            jax.ShapeDtypeStruct((weight_rows * n * n_dp, out_rows.shape[1]), out_rows.dtype),
        ),
        [ANY] * 4,
        (ANY,) * 4,
        [sems(2, 2, n // 2)] * 6
        + [sems(3)] * 2
        + [sems(n - 1)] * 4
        + [sems(3)] * 2
        + [sems(4)],
        identity,
        "gather_inputs",
        300_000_000,
    )(tokens, named, in_blocks, out_rows)


def scatter_end(row_part, in_part, out_part, n, identity):
    rows, width = row_part.shape[0] // n, row_part.shape[1]
    half_rows = rows // 2
    f32 = jnp.float32

    def body(
        row_ref,
        in_ref,
        out_ref,
        row_sum,
        in_got,
        out_sum,
        slots,
        in_core,
        in_chip,
        out_core,
        out_chip,
        row_send,
        row_receive,
        pass_send,
        pass_receive,
        in_send,
        in_receive,
    ):
        ring = Ring(n)
        me = ring.me
        dp, core, chip, core_chip = partners()
        others = [(me + k) % n for k in range(1, n)]
        ring.barrier([{"ctx": other} for other in others] + [{"dp": core}, {"dp": chip}])

        def part(device, half):
            return row_ref.at[pl.ds(pl.multiple_of(device * rows + half * half_rows, 16), half_rows)]

        def store(half, total):
            row_sum[pl.ds(half * half_rows, half_rows)] = total

        def passing(at, source, target, to):
            return remote(source, target, pass_send.at[at], pass_receive.at[at], {"dp": to})

        def weight_steps():
            passed = [
                passing(0, in_ref.at[core_chip], in_core.at[1], core),
                passing(1, out_ref.at[core_chip], out_core.at[1], core),
                passing(2, in_ref.at[core], in_core.at[0], core),
                passing(3, out_ref.at[core], out_core.at[0], core),
            ]
            for copy in passed:
                copy.start()
            yield
            passed[0].wait_recv()

            def add_far(k, carry):
                in_core[1, k] = (in_core[1, k].astype(f32) + in_ref[chip, k].astype(f32)).astype(in_ref.dtype)
                return carry

            lax.fori_loop(0, n, add_far, 0)
            passed.append(passing(4, in_core.at[1], in_chip, chip))
            passed[-1].start()
            passed[1].wait_recv()
            out_core[1] = (out_core[1].astype(f32) + out_ref[chip].astype(f32)).astype(out_ref.dtype)
            passed.append(passing(5, out_core.at[1], out_chip, chip))
            passed[-1].start()
            for _ in range(4):
                yield
            passed[2].wait_recv()
            passed[3].wait_recv()
            passed[4].wait_recv()

            def add_near(k, carry):
                in_core[0, k] = (
                    in_core[0, k].astype(f32) + in_ref[dp, k].astype(f32) + in_chip[k].astype(f32)
                ).astype(in_ref.dtype)
                return carry

            lax.fori_loop(0, n, add_near, 0)
            direct = []
            for k, other in enumerate(others):
                direct.append(
                    remote(in_core.at[0, other], in_got.at[me], in_send.at[k], in_receive.at[k], {"ctx": other})
                )
                direct[-1].start()
            in_got[me] = in_core[0, me]
            passed[5].wait_recv()
            out_sum[...] = (
                out_core[0].astype(f32) + out_ref[dp].astype(f32) + out_chip[...].astype(f32)
            ).astype(out_ref.dtype)
            for _ in range(8):
                yield
            for k in range(1, n):
                spot = in_got.at[(me - k + n) % n]
                remote(
                    spot, spot, in_send.at[k - 1], in_receive.at[k - 1], {"ctx": others[k - 1]}
                ).wait_recv()
            for copy in passed + direct:
                copy.wait_send()

        run_steps(scatter_steps(ring, part, slots, store, row_send, row_receive), weight_steps())

    return kernel_call(
        body,
        (
            jax.ShapeDtypeStruct((rows, width), f32),
            jax.ShapeDtypeStruct(in_part.shape[1:], in_part.dtype),
            jax.ShapeDtypeStruct(out_part.shape[1:], out_part.dtype),
        ),
        [VMEM] * 3,
        (VMEM,) * 3,
        [
            pltpu.VMEM((2, 2, n // 2, half_rows, width), row_part.dtype),
            pltpu.VMEM((2,) + in_part.shape[1:], in_part.dtype),
            pltpu.VMEM(in_part.shape[1:], in_part.dtype),
            pltpu.VMEM((2,) + out_part.shape[1:], out_part.dtype),
            pltpu.VMEM(out_part.shape[1:], out_part.dtype),
            sems(2, 2, n // 2),
            sems(2, 2, n // 2),
            sems(6),
            sems(6),
            sems(n - 1),
            sems(n - 1),
        ],
        identity,
        "scatter_end",
        200_000_000,
    )(row_part, in_part, out_part)


def small_scatter(parts, n, n_dp, identity):
    def body(part_ref, sum_ref, got, send, receive):
        me, dp = lax.axis_index("ctx"), lax.axis_index("dp")
        flat = dp * n + me
        count = n * n_dp
        semaphore = pltpu.get_barrier_semaphore()

        def spot(at):
            return (at // n, at % n)

        for k in range(1, count):
            pl.semaphore_signal(
                semaphore, inc=1, device_id=spot((flat + k) % count), device_id_type=MESH
            )
        pl.semaphore_wait(semaphore, count - 1)
        copies = []
        for k in range(1, count):
            to = (flat + k) % count
            copies.append(
                remote(
                    part_ref.at[to // n, to % n], got.at[k], send.at[k], receive.at[k], spot(to)
                )
            )
            copies[-1].start()
        total = part_ref[dp, me]
        for k in range(1, count):
            copies[k - 1].wait_recv()
            total = total + got[k]
        sum_ref[...] = total
        for copy in copies:
            copy.wait_send()

    shape = parts.shape[2:]
    return kernel_call(
        body,
        jax.ShapeDtypeStruct(shape, parts.dtype),
        [VMEM],
        VMEM,
        [pltpu.VMEM((n * n_dp,) + shape, parts.dtype), sems(n * n_dp), sems(n * n_dp)],
        identity,
        "small_scatter",
        40_000_000,
    )(parts)


def slot_offsets(n):
    offsets = [0]
    for k in range(1, n // 2):
        offsets += [k, -k]
    return offsets + [n // 2]


def slot_of(offset, n):
    if abs(offset) == n // 2:
        return n - 1
    return 2 * offset - 1 if offset > 0 else -2 * offset


def slot_gather_steps(ring, first, slots, send, receive):
    signs = (1, -1)
    half_rows = slots.shape[1] // 2

    def copy(way, half, hop):
        rows = pl.ds(half * half_rows, half_rows)
        held = slot_of(-signs[way] * hop, ring.n)
        return remote(
            first.at[rows] if hop == 0 else slots.at[held, rows],
            slots.at[slot_of(-signs[way] * (hop + 1), ring.n), rows],
            send.at[way, half, hop],
            receive.at[way, half, hop],
            {"ctx": ring.at(signs[way])},
        )

    started = []
    for half in (0, 1):
        for way in (0, 1):
            started.append(copy(way, half, 0))
            started[-1].start()
    yield
    for hop in range(ring.n // 2):
        for half in (0, 1):
            for way in (0, 1):
                if hop < ring.hops(way, half):
                    copy(way, half, hop).wait_recv()
                    if hop + 1 < ring.hops(way, half):
                        started.append(copy(way, half, hop + 1))
                        started[-1].start()
                    yield
    for one in started:
        one.wait_send()


def advance(steps, count):
    for _ in range(count):
        next(steps, None)


def dot(a, b):
    return jnp.dot(a, b, preferred_element_type=jnp.float32)


def dot_across(a, b):
    return lax.dot_general(a, b, (((1,), (1,)), ((), ())), preferred_element_type=jnp.float32)


def experts_in(
    attend_all, token_all, cotangent, out_all, first, second, gain, router, named, n, identity
):
    tok_rows, width = cotangent.shape
    local_experts, ff = first.shape[0], second.shape[0] // first.shape[0]
    rows = tok_rows * n
    pair = 2 * tok_rows
    part = 4 * tok_rows
    tile, wide = 256, 512
    bf16, f32 = jnp.bfloat16, jnp.float32
    offsets = slot_offsets(n)

    def body(
        attend_ref,
        token_ref,
        back_ref,
        out_ref,
        first_ref,
        second_ref,
        gain_ref,
        router_ref,
        named_ref,
        back_all,
        mixed_all,
        gated_all,
        up_all,
        own_gates,
        gate_back,
        own_residual,
        out_s,
        first_s,
        second_s,
        mixed_s,
        back_s,
        attend_s,
        token_s,
        residual_s,
        gate_s,
        sum_s,
        send,
        receive,
        load,
        weight_load,
        save,
        local,
    ):
        ring = Ring(n)
        lanes = lax.broadcasted_iota(jnp.int32, (pair, LANES), 1)
        part_lanes = lax.broadcasted_iota(jnp.int32, (part, LANES), 1)
        loads = [pltpu.make_async_copy(out_ref, out_s, weight_load.at[0])]
        for x in range(local_experts):
            loads.append(pltpu.make_async_copy(first_ref.at[x], first_s.at[x], weight_load.at[1 + x]))
        loads.append(pltpu.make_async_copy(second_ref, second_s, weight_load.at[1 + local_experts]))

        def row_loads(j):
            copies = []
            for k in range(2):
                device = ring.at(offsets[2 * j + k])
                source = pl.ds(pl.multiple_of(device * tok_rows, 16), tok_rows)
                target = pl.ds(k * tok_rows, tok_rows)
                for at, (array, held) in enumerate(((attend_ref, attend_s), (token_ref, token_s))):
                    copies.append(
                        pltpu.make_async_copy(
                            array.at[source], held.at[j % 2, target], load.at[j % 2, k, at]
                        )
                    )
            return copies

        pending = row_loads(0)
        for copy in pending:
            copy.start()
        loads[0].start()
        own = pltpu.make_async_copy(back_ref, back_s.at[0], local)
        own.start()
        ring.barrier(ring.neighbours())
        steps = slot_gather_steps(ring, back_ref, back_s, send, receive)
        advance(steps, 1)
        loads[0].wait()
        for copy in loads[1:]:
            copy.start()

        saves = []
        for j in range(n // 2):
            for copy in pending:
                copy.wait()
            if j + 1 < n // 2:
                pending = row_loads(j + 1)
                for copy in pending:
                    copy.start()

            def project(t, carry, j=j):
                columns = pl.ds(pl.multiple_of(t * wide, wide), wide)
                residual_s[:, columns] = token_s[j % 2, :, columns].astype(f32) + dot(
                    attend_s[j % 2], out_s[:, columns]
                )
                return carry

            lax.fori_loop(0, width // wide, project, 0)
            residual = residual_s[...]
            if j == 0:
                own_residual[...] = residual[:tok_rows]
            inverse = lax.rsqrt(jnp.mean(residual * residual, axis=-1, keepdims=True) + EPSILON)
            mixed = (residual * inverse * gain_ref[0:1, :]).astype(bf16)
            for k in range(2):
                mixed_s[2 * j + k] = mixed[k * tok_rows : (k + 1) * tok_rows]
            logits = dot(mixed, router_ref[...])
            marks = jnp.concatenate(
                [
                    named_ref[pl.ds(pl.multiple_of(ring.at(offsets[2 * j + k]) * tok_rows, 16), tok_rows)]
                    for k in range(2)
                ],
                axis=0,
            ).astype(f32)
            logits = jnp.where(marks > 0, logits, MASKED)
            powers = jnp.where(
                marks > 0, jnp.exp(logits - jnp.max(logits, axis=-1, keepdims=True)), 0.0
            )
            gates = powers / jnp.sum(powers, axis=-1, keepdims=True)
            if j == 0:
                own_gates[...] = gates[:tok_rows]
            held = jnp.zeros((pair, LANES), f32)
            for x in range(local_experts):
                mine = jnp.sum(
                    jnp.where(lanes == ring.me * local_experts + x, gates, 0.0), axis=-1, keepdims=True
                )
                held = jnp.where(lanes == x, mine, held)
            gate_s[pl.ds(j * pair, pair)] = held
            saves.append(
                pltpu.make_async_copy(
                    mixed_s.at[pl.ds(2 * j, 2)], mixed_all.at[pl.ds(2 * j, 2)], save.at[j]
                )
            )
            saves[-1].start()
            advance(steps, 2)

        counts = rows // part
        outgoing = []
        base = n // 2
        for s in range(counts):
            slots = pl.ds(s * 4, 4)
            part_rows = pl.ds(s * part, part)
            advance(steps, 8 if s < counts - 1 else 64)
            if s == 0:
                own.wait()
            sum_s[part_rows] = jnp.zeros((part, LANES), f32)
            for copy in outgoing:
                copy.wait()
            outgoing = []
            for x in range(local_experts):
                if s == 0:
                    loads[1 + x].wait()
                    if x == 0:
                        loads[1 + local_experts].wait()

                def hidden(t, carry, s=s, x=x, slots=slots, part_rows=part_rows):
                    at = pl.multiple_of(t * tile, tile)
                    mixed = mixed_s[slots].reshape(part, width)
                    back = back_s[slots].reshape(part, width)
                    gate_part = dot(mixed, first_s[x, :, pl.ds(at, tile)])
                    up_part = dot(mixed, first_s[x, :, pl.ds(pl.multiple_of(ff + at, tile), tile)])
                    hidden_back = dot_across(
                        back, second_s[pl.ds(pl.multiple_of(x * ff + at, tile), tile), :]
                    )
                    gate = gate_s[part_rows, x : x + 1]
                    sigmoid = jax.nn.sigmoid(gate_part)
                    swish = gate_part * sigmoid
                    value = swish * up_part
                    out_s[pl.ds(0, part), pl.ds(pl.multiple_of(x * ff + at, tile), tile)] = (
                        value * gate
                    ).astype(bf16)
                    sums = jnp.sum(value * hidden_back, axis=-1, keepdims=True)
                    sum_s[part_rows] = sum_s[part_rows] + jnp.where(part_lanes == x, sums, 0.0)
                    hidden_back = hidden_back * gate
                    slope = sigmoid * (1.0 + gate_part * (1.0 - sigmoid))
                    up_rows = pl.ds((1 + x) * part, part)
                    out_s[up_rows, pl.ds(at, tile)] = (hidden_back * up_part * slope).astype(bf16)
                    out_s[up_rows, pl.ds(pl.multiple_of(ff + at, tile), tile)] = (
                        hidden_back * swish
                    ).astype(bf16)
                    return carry

                quarters = ff // tile
                lax.fori_loop(0, quarters // 2, hidden, 0)
                advance(steps, 2)
                lax.fori_loop(quarters // 2, quarters, hidden, 0)
                advance(steps, 2)
                outgoing.append(
                    pltpu.make_async_copy(
                        out_s.at[pl.ds((1 + x) * part, part)],
                        up_all.at[x, part_rows],
                        save.at[base + 1 + x],
                    )
                )
                outgoing[-1].start()
            outgoing.append(
                pltpu.make_async_copy(out_s.at[pl.ds(0, part)], gated_all.at[part_rows], save.at[base])
            )
            outgoing[-1].start()
        spread = pltpu.make_async_copy(back_s, back_all, local)
        spread.start()
        for k in range(n):
            gate_back[k] = jnp.transpose(sum_s[pl.ds(k * tok_rows, tok_rows)])[:8]
        for copy in saves + outgoing:
            copy.wait()
        spread.wait()

    return pl.pallas_call(
        body,
        out_shape=(
            jax.ShapeDtypeStruct((n, tok_rows, width), bf16),
            jax.ShapeDtypeStruct((n, tok_rows, width), bf16),
            jax.ShapeDtypeStruct((rows, local_experts * ff), bf16),
            jax.ShapeDtypeStruct((local_experts, rows, 2 * ff), bf16),
            jax.ShapeDtypeStruct((tok_rows, LANES), f32),
            jax.ShapeDtypeStruct((n, 8, LANES), f32),
            jax.ShapeDtypeStruct((tok_rows, width), f32),
        ),
        in_specs=[ANY] * 6 + [VMEM] * 3,
        out_specs=(ANY,) * 4 + (VMEM,) * 3,
        scratch_shapes=[
            pltpu.VMEM(out_all.shape, bf16),
            pltpu.VMEM(first.shape, bf16),
            pltpu.VMEM(second.shape, bf16),
            pltpu.VMEM((n, tok_rows, width), bf16),
            pltpu.VMEM((n, tok_rows, width), bf16),
            pltpu.VMEM((2, pair, width), bf16),
            pltpu.VMEM((2, pair, width), bf16),
            pltpu.VMEM((pair, width), f32),
            pltpu.VMEM((rows, LANES), f32),
            pltpu.VMEM((rows, LANES), f32),
            sems(2, 2, n // 2),
            sems(2, 2, n // 2),
            sems(2, 2, 2),
            sems(2 + local_experts),
            sems(n // 2 + 1 + local_experts),
            pltpu.SemaphoreType.DMA,
        ],
        name="experts_in",
        cost_estimate=pl.CostEstimate(
            flops=2 * rows * width * (width + 3 * ff * local_experts),
            bytes_accessed=60_000_000,
            transcendentals=0,
        ),
        compiler_params=pltpu.CompilerParams(
            collective_id=identity, has_side_effects=True, vmem_limit_bytes=BIG_VMEM
        ),
    )(attend_all, token_all, cotangent, out_all, first, second, gain, router, named)


BIG_VMEM = 60 * 1024 * 1024


def slot_scatter_steps(ring, parts, slots, store, send, receive, need):
    signs = (1, -1)
    half_rows = parts.shape[1] // 2
    f32 = jnp.float32

    def part(offset, half):
        return parts.at[slot_of(offset, ring.n), pl.ds(half * half_rows, half_rows)]

    def copy(way, half, hop, source):
        return remote(
            source,
            slots.at[way, half, hop],
            send.at[way, half, hop],
            receive.at[way, half, hop],
            {"ctx": ring.at(signs[way])},
        )

    started = []
    firsts = [(way, half) for half in (0, 1) for way in (0, 1)]
    firsts.sort(key=lambda one: -slot_of(signs[one[0]] * ring.hops(*one), ring.n))
    for way, half in firsts:
        goal = signs[way] * ring.hops(way, half)
        need(slot_of(goal, ring.n))
        started.append(copy(way, half, 0, part(goal, half)))
        started[-1].start()
    for hop in range(ring.n // 2):
        for way, half in firsts:
            last = ring.hops(way, half) - 1
            if hop <= last:
                slot = slots.at[way, half, hop]
                if hop < last:
                    goal = signs[way] * (last - hop)
                    need(slot_of(goal, ring.n))
                copy(way, half, hop, slot).wait_recv()
                if hop < last:
                    slot[...] = (
                        slot[...].astype(f32) + part(goal, half)[...].astype(f32)
                    ).astype(slot.dtype)
                    started.append(copy(way, half, hop + 1, slot))
                    started[-1].start()
                yield
    need(0)
    for half in (0, 1):
        total = part(0, half)[...].astype(f32)
        for way in (0, 1):
            total = total + slots[way, half, ring.hops(way, half) - 1].astype(f32)
        store(half, total)
    for one in started:
        one.wait_send()


def experts_out(up_all, gated_all, first, second, gate_back, n, identity):
    local_experts, rows, inner = up_all.shape
    width = first.shape[1]
    tok_rows = rows // n
    half_rows = tok_rows // 2
    pair = 2 * tok_rows
    wide = 512
    count = width // wide
    bf16, f32 = jnp.bfloat16, jnp.float32
    offsets = slot_offsets(n)

    def body(
        up_ref,
        gated_ref,
        first_ref,
        second_ref,
        gate_ref,
        row_sum,
        result_all,
        gate_got,
        first_s,
        second_s,
        up_s,
        gated_s,
        part_s,
        result_s,
        slots,
        send,
        receive,
        gate_send,
        gate_receive,
        load,
        first_load,
        other_load,
        save,
    ):
        ring = Ring(n)

        def up_load(j):
            return pltpu.make_async_copy(
                up_ref.at[:, pl.ds(j * pair, pair)], up_s.at[:, pl.ds(j * pair, pair)], load.at[j]
            )

        def weight_load(t):
            return pltpu.make_async_copy(
                first_ref.at[:, pl.ds(t * wide, wide)],
                first_s.at[:, pl.ds(t * wide, wide)],
                first_load.at[t],
            )

        groups = n // 2
        up_load(groups - 1).start()
        for t in range(count):
            weight_load(t).start()
        for j in range(groups - 1):
            up_load(groups - 2 - j).start()
        others = [
            pltpu.make_async_copy(gated_ref, gated_s, other_load.at[0]),
            pltpu.make_async_copy(second_ref, second_s, other_load.at[1]),
        ]
        for copy in others:
            copy.start()
        ring.barrier([{"ctx": ring.at(k)} for k in range(1, n)])
        gate_copies = []
        for k in range(1, n):
            offset = k if k <= n // 2 else k - n
            back = -offset if offset < n // 2 else offset
            gate_copies.append(
                remote(
                    gate_ref.at[slot_of(offset, n)],
                    gate_got.at[slot_of(back, n)],
                    gate_send.at[slot_of(back, n)],
                    gate_receive.at[slot_of(back, n)],
                    {"ctx": ring.at(k)},
                )
            )
            gate_copies[-1].start()
        gate_got[0] = gate_ref[0]

        done = set()

        def product(j):
            rows_j = pl.ds(j * pair, pair)
            up_load(j).wait()

            def columns(t):
                at = pl.ds(pl.multiple_of(t * wide, wide), wide)
                value = dot_across(up_s[0, rows_j], first_s[0, at, :])
                for x in range(1, local_experts):
                    value = value + dot_across(up_s[x, rows_j], first_s[x, at, :])
                value = value.astype(bf16)
                for k in range(2):
                    part_s[2 * j + k, :, at] = value[k * tok_rows : (k + 1) * tok_rows]

            if not done:
                for t in range(count):
                    weight_load(t).wait()
                    columns(t)
            else:

                def step(t, carry):
                    columns(t)
                    return carry

                lax.fori_loop(0, count, step, 0)
            done.add(j)

        def need(slot):
            if slot // 2 not in done:
                product(slot // 2)

        def store(half, total):
            row_sum[pl.ds(half * half_rows, half_rows)] = total

        steps = slot_scatter_steps(ring, part_s, slots, store, send, receive, need)
        for j in reversed(range(groups)):
            need(2 * j)
            advance(steps, 3)
        for copy in others:
            copy.wait()
        saves = []
        chunk = 2
        for j in range(n // chunk):
            rows_j = pl.ds(j * chunk * tok_rows, chunk * tok_rows)

            def result(t, carry, rows_j=rows_j, j=j):
                at = pl.ds(pl.multiple_of(t * wide, wide), wide)
                value = dot(gated_s[rows_j], second_s[:, at]).astype(bf16)
                for k in range(chunk):
                    result_s[chunk * j + k, :, at] = value[k * tok_rows : (k + 1) * tok_rows]
                return carry

            lax.fori_loop(0, count, result, 0)
            for k in range(chunk):
                slot = chunk * j + k
                device = ring.at(offsets[slot])
                saves.append(
                    pltpu.make_async_copy(
                        result_s.at[slot],
                        result_all.at[pl.ds(pl.multiple_of(device * tok_rows, 16), tok_rows)],
                        save.at[slot],
                    )
                )
                saves[-1].start()
            advance(steps, 2)
        advance(steps, 64)
        for copy in saves:
            copy.wait()
        for copy in gate_copies:
            copy.wait()

    return pl.pallas_call(
        body,
        out_shape=(
            jax.ShapeDtypeStruct((tok_rows, width), f32),
            jax.ShapeDtypeStruct((rows, width), bf16),
            jax.ShapeDtypeStruct(gate_back.shape, f32),
        ),
        in_specs=[ANY] * 4 + [VMEM],
        out_specs=(VMEM, ANY, VMEM),
        scratch_shapes=[
            pltpu.VMEM(first.shape, bf16),
            pltpu.VMEM(second.shape, bf16),
            pltpu.VMEM(up_all.shape, bf16),
            pltpu.VMEM(gated_all.shape, bf16),
            pltpu.VMEM((n, tok_rows, width), bf16),
            pltpu.VMEM((n, tok_rows, width), bf16),
            pltpu.VMEM((2, 2, n // 2, half_rows, width), bf16),
            sems(2, 2, n // 2),
            sems(2, 2, n // 2),
            sems(n),
            sems(n),
            sems(n // 2),
            sems(count),
            sems(2),
            sems(n),
        ],
        name="experts_out",
        cost_estimate=pl.CostEstimate(
            flops=2 * rows * width * 3 * inner // 2 * local_experts,
            bytes_accessed=60_000_000,
            transcendentals=0,
        ),
        compiler_params=pltpu.CompilerParams(
            collective_id=identity, has_side_effects=True, vmem_limit_bytes=BIG_VMEM
        ),
    )(up_all, gated_all, first, second, gate_back)


def gather_and_scatter(block, partial, n, identity):
    rows, width = block.shape
    half_rows = rows // 2

    def body(block_ref, part_ref, all_ref, sum_ref, slots, send, receive, sum_send, sum_receive, local):
        ring = Ring(n)

        def half_of(ref, device, half):
            return ref.at[pl.ds(pl.multiple_of(device * rows + half * half_rows, 16), half_rows)]

        def store(half, total):
            sum_ref[pl.ds(half * half_rows, half_rows)] = total

        own = pltpu.make_async_copy(
            block_ref, all_ref.at[pl.ds(pl.multiple_of(ring.me * rows, 16), rows)], local
        )
        own.start()
        ring.barrier(ring.neighbours())
        run_steps(
            gather_steps(
                ring,
                lambda half: block_ref.at[pl.ds(half * half_rows, half_rows)],
                lambda device, half: half_of(all_ref, device, half),
                send,
                receive,
            ),
            scatter_steps(
                ring,
                lambda device, half: half_of(part_ref, device, half),
                slots,
                store,
                sum_send,
                sum_receive,
            ),
        )
        own.wait()

    return kernel_call(
        body,
        (
            jax.ShapeDtypeStruct((rows * n, width), block.dtype),
            jax.ShapeDtypeStruct((rows, width), jnp.float32),
        ),
        [ANY, VMEM],
        (ANY, VMEM),
        [pltpu.VMEM((2, 2, n // 2, half_rows, width), partial.dtype)]
        + [sems(2, 2, n // 2)] * 4
        + [pltpu.SemaphoreType.DMA],
        identity,
        "gather_and_scatter",
        200_000_000,
    )(block, partial)


def gather_ctx(block):
    return lax.all_gather(block, "ctx", axis=0, tiled=True)


def scatter_ctx(partial):
    return lax.psum_scatter(
        partial.astype(jnp.bfloat16), "ctx", scatter_dimension=0, tiled=True
    ).astype(jnp.float32)


def heads_local(
    tokens,
    document_ids,
    routes,
    norm_gains,
    project_in,
    project_out,
    router_weight,
    expert_in,
    expert_out,
    cotangent,
):
    bf16, f32 = jnp.bfloat16, jnp.float32
    n = lax.axis_size("ctx")
    n_dp = lax.axis_size("dp")
    me = lax.axis_index("ctx")
    tok_rows, width = tokens.shape[1:]
    rows = tok_rows * n
    weight_rows = project_in.shape[0]
    own_heads = HEADS // n
    cols = own_heads * HEAD_DIM
    local_experts = expert_in.shape[0]
    expert_count = local_experts * n
    score_scale = HEAD_DIM ** (-0.5)

    def own(array, size, axis=0):
        return lax.dynamic_slice_in_dim(array, me * size, size, axis)

    named = jnp.any(routes[0][..., None] == jnp.arange(LANES, dtype=jnp.int32), axis=1).astype(bf16)
    small = jnp.concatenate(
        [norm_gains, router_weight, jnp.zeros((weight_rows, LANES - 4 - expert_count), bf16)], axis=1
    )
    in_blocks = project_in.reshape(weight_rows, 3, n, cols).transpose(2, 0, 1, 3)
    in_blocks = jnp.concatenate(
        [
            in_blocks.reshape(n, weight_rows, 3 * cols),
            jnp.broadcast_to(small[None], (n, weight_rows, LANES)),
        ],
        axis=2,
    )
    token_all, named_all, in_all, out_all = gather_inputs(
        tokens[0], named, in_blocks, project_out, n, n_dp, 1
    )
    named_all = named_all.reshape(rows, LANES)
    in_all = in_all.reshape(width, 3 * cols + LANES)
    in_own, small_all = in_all[:, : 3 * cols], in_all[:, 3 * cols :]
    gains = small_all[:, :4].astype(f32)
    router_all = small_all[:, 4 : 4 + expert_count]
    router_wide = jnp.pad(router_all, ((0, 0), (0, LANES - expert_count)))
    first = lax.all_gather(expert_in, "dp", axis=1, tiled=True)
    second = lax.all_gather(expert_out, "dp", axis=1, tiled=True).reshape(local_experts * FF, width)

    def sum_ctx(values):
        shape = values.shape
        block = values.reshape(-1, LANES)
        got = direct_exchange(
            jnp.broadcast_to(block[None], (n,) + block.shape), n, 2, "exchange"
        )
        return jnp.sum(got, axis=0).reshape(shape)

    half_rows = tok_rows // 2

    def dealt(row):
        blocks = row.reshape(2 * n, half_rows)
        return jnp.stack([blocks[:n], blocks[n:][::-1]], axis=1).reshape(rows)

    places = dealt(jnp.arange(rows, dtype=jnp.int32))
    document_row = document_ids[0]
    documents = dealt(document_row)
    relative = places - dealt(document_starts(document_row))
    cosine, sine = rotary_tables(relative, HEAD_DIM)
    visible = (documents[None, :] == documents[:, None]) & (places[None, :] <= places[:, None])

    inputs = token_all.astype(f32)
    attend_inverse = inverse_rms(inputs)
    attend_in = (inputs * attend_inverse * gains[:, 0]).astype(bf16)
    projected = jnp.dot(attend_in, in_own, preferred_element_type=f32)
    raw = projected[:, : 2 * cols].reshape(rows, 2, cols)
    squares = sum_ctx(jnp.sum(raw * raw, axis=-1))
    inverse = lax.rsqrt(squares / width + EPSILON)[..., None]
    normed = raw * inverse
    pair_gains = own(gains, cols)[:, 1:3].T
    rotated = rotate((normed * pair_gains).reshape(rows, 2 * own_heads, HEAD_DIM), cosine, sine)
    rotated = rotated.reshape(rows, 2, own_heads, HEAD_DIM).astype(bf16)
    query, key = rotated[:, 0], rotated[:, 1]
    value = projected[:, 2 * cols :].astype(bf16).reshape(rows, own_heads, HEAD_DIM)

    scores = jnp.einsum("thd,khd->htk", query, key, preferred_element_type=f32) * score_scale
    scores = jnp.where(visible[None], scores, MASKED)
    peak = jnp.max(scores, axis=-1, keepdims=True)
    powers = jnp.where(visible[None], jnp.exp(scores - peak), 0.0)
    total = jnp.sum(powers, axis=-1, keepdims=True)
    probs = (powers / total).astype(bf16)
    attend_out = jnp.einsum("htk,khd->thd", probs, value, preferred_element_type=f32)
    attend_low = attend_out.reshape(rows, cols).astype(bf16)
    attend_all = ring_gather(attend_low, n, 3, "gather_attention", axis=1)

    upstream_all, mixed_all, gated_all, up_all, own_gates, gate_back, own_residual = experts_in(
        attend_all,
        token_all,
        cotangent[0],
        out_all,
        first,
        second,
        jnp.broadcast_to(gains[:, 3][None], (8, width)),
        router_wide,
        named_all,
        n,
        8,
    )
    mixed_slots = mixed_all.reshape(rows, width)
    second_back = jnp.einsum(
        "tf,td->fd", gated_all, upstream_all.reshape(rows, width), preferred_element_type=f32
    ).astype(bf16)
    first_backs = [
        jnp.einsum("td,tf->df", mixed_slots, up_all[x], preferred_element_type=f32).astype(bf16)
        for x in range(local_experts)
    ]
    second_back, first_backs, up_all = lax.optimization_barrier(
        (second_back, first_backs, up_all)
    )
    expert_out_gradient = lax.psum_scatter(
        second_back.reshape(local_experts, FF, width), "dp", scatter_dimension=1, tiled=True
    ).astype(f32)
    expert_in_gradient = jnp.stack(
        [lax.psum_scatter(one, "dp", scatter_dimension=0, tiled=True) for one in first_backs]
    ).astype(f32)
    mixed_back, mixture, gate_back = experts_out(up_all, gated_all, first, second, gate_back, n, 9)
    gate_back = gate_back[:, :local_experts]
    place = ring_place(me, n)
    gate_back = sum(
        jnp.where(
            (jnp.arange(n) == ring_device((place + offset + n) % n, n))[:, None, None],
            gate_back[slot],
            0.0,
        )
        for slot, offset in enumerate(slot_offsets(n))
    )
    gate_back = gate_back.reshape(expert_count, tok_rows).T

    own_gates = own_gates[:, :expert_count]
    own_mixed = mixed_all[0]
    own_mixed_inverse = inverse_rms(own_residual)
    own_mixed_normed = own_residual * own_mixed_inverse
    chosen_back = own_gates * (
        gate_back - jnp.sum(own_gates * gate_back, axis=-1, keepdims=True)
    )
    logit_back = chosen_back.astype(bf16)
    router_part = jnp.einsum("td,te->de", own_mixed, logit_back, preferred_element_type=f32)
    mixed_back = mixed_back + jnp.einsum(
        "te,de->td", logit_back, router_all, preferred_element_type=f32
    )
    mixed_gain_back = jnp.sum(mixed_back * own_mixed_normed, axis=0)
    residual_back = cotangent[0].astype(f32) + normalize_back(
        mixed_back * gains[:, 3], own_mixed_normed, own_mixed_inverse
    )
    back_all, mixture = gather_and_scatter(residual_back.astype(bf16), mixture, n, 5)
    layer_output = (own_residual + mixture).astype(bf16)

    out_part = jnp.einsum("td,te->de", attend_low, back_all, preferred_element_type=f32)
    attend_back = jnp.einsum(
        "td,ed->te", back_all, own(out_all, cols), preferred_element_type=f32
    ).astype(bf16).reshape(rows, own_heads, HEAD_DIM)
    delta = jnp.einsum("thd,thd->ht", attend_back.astype(f32), attend_out)[..., None]
    prob_back = jnp.einsum("thd,khd->htk", attend_back, value, preferred_element_type=f32)
    score_back = (probs.astype(f32) * (prob_back - delta)).astype(bf16)
    query_back = jnp.einsum("htk,khd->thd", score_back, key, preferred_element_type=f32)
    key_back = jnp.einsum("htk,thd->khd", score_back, query, preferred_element_type=f32)
    value_back = jnp.einsum("htk,thd->khd", probs, attend_back, preferred_element_type=f32)
    pair_back = jnp.concatenate([query_back, key_back], axis=1) * score_scale
    pair_back = rotate(pair_back, cosine, -sine).reshape(rows, 2, cols)
    pair_gain_back = jnp.sum(pair_back * normed, axis=0)
    pair_back = pair_back * pair_gains
    means = sum_ctx(jnp.sum(pair_back * normed, axis=-1))[..., None] / width
    pair_back = inverse * (pair_back - normed * means)
    raw_back = jnp.concatenate(
        [pair_back.reshape(rows, 2 * cols), value_back.reshape(rows, cols)], axis=-1
    ).astype(bf16)
    row_part = jnp.einsum("tf,df->td", raw_back, in_own, preferred_element_type=f32).astype(bf16)
    in_part = jnp.einsum("td,tf->df", attend_in, raw_back, preferred_element_type=f32).astype(bf16)
    attend_in_back, in_part, out_part = scatter_end(
        row_part,
        in_part.reshape(n_dp, n, weight_rows, 3 * cols),
        out_part.astype(bf16).reshape(n_dp, weight_rows, width),
        n,
        6,
    )
    pairs = [(d * n + c, c * n_dp + d) for d in range(n_dp) for c in range(n)]
    project_out_gradient = lax.ppermute(out_part, ("dp", "ctx"), pairs).astype(f32)
    in_part = in_part.reshape(n, weight_rows, 3, cols)
    project_in_gradient = in_part.transpose(1, 2, 0, 3).reshape(weight_rows, 3 * width).astype(f32)

    own_inverse = own(attend_inverse, tok_rows)
    own_normed = tokens[0].astype(f32) * own_inverse
    attend_gain_back = jnp.sum(attend_in_back * own_normed, axis=0)
    tokens_back = residual_back + normalize_back(
        attend_in_back * gains[:, 0], own_normed, own_inverse
    )
    pair_columns = lax.dynamic_update_slice_in_dim(
        jnp.zeros((width, 2), f32), pair_gain_back.T, me * cols, 0
    )
    small_part = jnp.concatenate(
        [attend_gain_back[:, None], pair_columns, mixed_gain_back[:, None], router_part], axis=1
    )
    small_width = small_part.shape[1]
    small_rows = -(-weight_rows * small_width // (8 * LANES)) * 8
    small_part = jnp.pad(
        small_part.reshape(n_dp * n, weight_rows * small_width),
        ((0, 0), (0, small_rows * LANES - weight_rows * small_width)),
    )
    small_gradient = small_scatter(small_part.reshape(n_dp, n, small_rows, LANES), n, n_dp, 7)
    small_gradient = small_gradient.reshape(-1)[: weight_rows * small_width]
    small_gradient = small_gradient.reshape(weight_rows, small_width)
    return (
        layer_output[None],
        tokens_back.astype(bf16)[None],
        small_gradient[:, :4],
        project_in_gradient,
        project_out_gradient,
        small_gradient[:, 4:],
        expert_in_gradient,
        expert_out_gradient,
    )


def solution(mesh):
    n = mesh.shape["ctx"]
    split_heads = HEADS % n == 0 and n % 4 == 0 and mesh.shape["dp"] == 4
    placed = (
        P("dp", "ctx", None),
        P("dp", None),
        P("dp", "ctx", None),
        P(("dp", "ctx"), None),
        P(("dp", "ctx"), None),
        P(("dp", "ctx"), None),
        P(("dp", "ctx"), None),
        P("ctx", "dp", None),
        P("ctx", "dp", None),
        P("dp", "ctx", None),
    )
    return jax.shard_map(
        heads_local if split_heads else gathered_local,
        mesh=mesh,
        in_specs=placed,
        out_specs=(
            P("dp", "ctx", None),
            P("dp", "ctx", None),
            P(("dp", "ctx"), None),
            P(("dp", "ctx"), None),
            P(("dp", "ctx"), None),
            P(("dp", "ctx"), None),
            P("ctx", "dp", None),
            P("ctx", "dp", None),
        ),
        check_vma=False,
    )
```

```python
import jax
import jax.numpy as jnp
from jax import lax
from jax.experimental import pallas as pl
from jax.experimental.pallas import tpu as pltpu
from jax.sharding import PartitionSpec as P

HEADS = 16
HEAD_DIM = 128
FF = 1024


EPSILON = 1e-05
ROPE_BASE = 10000.0
MASKED = -1e30
LANES = 128
TILE = 512
WIDE = 1024


def inverse_rms(values):
    return lax.rsqrt(jnp.mean(values * values, axis=-1, keepdims=True) + EPSILON)


def normalize_back(normed_back, normed, inverse):
    return inverse * (normed_back - normed * jnp.mean(normed_back * normed, axis=-1, keepdims=True))


def rotary_tables(relative, head_dim):
    half_dim = head_dim // 2
    frequency = ROPE_BASE ** (-jnp.arange(half_dim, dtype=jnp.float32) / half_dim)
    angles = relative.astype(jnp.float32)[..., None] * frequency
    return (jnp.cos(angles)[..., None, :], jnp.sin(angles)[..., None, :])


def rotate(values, cosine, sine_table):
    half_dim = values.shape[-1] // 2
    first_half = values[..., :half_dim]
    second_half = values[..., half_dim:]
    return jnp.concatenate(
        [
            first_half * cosine - second_half * sine_table,
            second_half * cosine + first_half * sine_table,
        ],
        axis=-1,
    )


def dealt_positions(indices, tok_rows, context_size):
    half_block = tok_rows // 2
    device = indices // tok_rows
    within = indices % tok_rows
    block_index = jnp.where(within < half_block, device, 2 * context_size - 1 - device)
    return block_index * half_block + within % half_block


def document_starts(document_row):
    places = jnp.arange(document_row.shape[-1], dtype=jnp.int32)
    head_flag = jnp.ones(document_row.shape[:-1] + (1,), jnp.bool_)
    fresh_start = jnp.concatenate(
        [head_flag, document_row[..., 1:] != document_row[..., :-1]], axis=-1
    )
    return lax.cummax(jnp.where(fresh_start, places, 0), axis=document_row.ndim - 1)


def block_scores(
    query_rows, key_block, query_place, query_document, key_place, key_document, score_scale
):
    scores = (
        jnp.einsum("thd,khd->htk", query_rows, key_block, preferred_element_type=jnp.float32)
        * score_scale
    )
    visible = (
        (key_document[None, :] == query_document[:, None])
        & (key_place[None, :] <= query_place[:, None])
    )[None]
    return (jnp.where(visible, scores, MASKED), visible)


def block_backward(
    query_rows,
    output_back,
    row_logsum,
    row_delta,
    key_block,
    value_block,
    query_place,
    query_document,
    key_place,
    key_document,
    score_scale,
):
    scores, visible = block_scores(
        query_rows, key_block, query_place, query_document, key_place, key_document, score_scale
    )
    prob_rows = jnp.where(visible, jnp.exp(scores - row_logsum[..., None]), 0.0)
    prob_back = jnp.einsum(
        "thd,khd->htk", output_back, value_block, preferred_element_type=jnp.float32
    )
    score_back = (prob_rows * (prob_back - row_delta[..., None])).astype(jnp.bfloat16)
    query_part = (
        jnp.einsum("htk,khd->thd", score_back, key_block, preferred_element_type=jnp.float32)
        * score_scale
    )
    key_part = (
        jnp.einsum("htk,thd->khd", score_back, query_rows, preferred_element_type=jnp.float32)
        * score_scale
    )
    value_part = jnp.einsum(
        "htk,thd->khd",
        prob_rows.astype(jnp.bfloat16),
        output_back,
        preferred_element_type=jnp.float32,
    )
    return (query_part, key_part, value_part)


def dispatch_plan(route_rows, expert_count, capacity):
    flat_routes = route_rows.reshape(-1)
    pair_count = flat_routes.shape[0]
    member = (flat_routes[:, None] == jnp.arange(expert_count, dtype=jnp.int32)[None, :]).astype(
        jnp.int32
    )
    earlier = jnp.cumsum(member, axis=0) - member
    target_slot = flat_routes * capacity + jnp.sum(earlier * member, axis=1)
    slot_owner = (
        jnp.full((expert_count * capacity,), pair_count, jnp.int32)
        .at[target_slot]
        .set(jnp.arange(pair_count, dtype=jnp.int32))
    )
    return (target_slot, slot_owner)


def gathered_local(
    tokens,
    document_ids,
    routes,
    norm_gains,
    project_in,
    project_out,
    router_weight,
    expert_in,
    expert_out,
    cotangent,
):
    inputs = tokens[0].astype(jnp.float32)
    tok_rows, model_width = inputs.shape
    context_size = lax.axis_size("ctx")
    sequence_rows = tok_rows * context_size
    local_experts = expert_in.shape[0]
    expert_count = local_experts * context_size
    route_rows = routes[0]
    top_count = route_rows.shape[1]
    capacity = 2 * tok_rows * top_count // expert_count
    score_scale = HEAD_DIM ** (-0.5)
    key_span = min(512, sequence_rows)
    key_blocks = sequence_rows // key_span
    heads_shape = (tok_rows, HEADS, HEAD_DIM)
    block_shape = (key_blocks, key_span, HEADS, HEAD_DIM)
    slot_shape = (context_size, local_experts * capacity, model_width)
    expert_shape = (context_size, local_experts, capacity, model_width)
    gathered_gains, gathered_in, gathered_out, gathered_router = (
        lax.all_gather(norm_gains, ("dp", "ctx"), axis=0, tiled=True),
        lax.all_gather(project_in, ("dp", "ctx"), axis=0, tiled=True),
        lax.all_gather(project_out, ("dp", "ctx"), axis=0, tiled=True),
        lax.all_gather(router_weight, ("dp", "ctx"), axis=0, tiled=True),
    )
    gathered_first, gathered_second = (
        lax.all_gather(expert_in, "dp", axis=1, tiled=True),
        lax.all_gather(expert_out, "dp", axis=1, tiled=True),
    )
    gain_rows = gathered_gains.astype(jnp.float32)
    own_rows = lax.axis_index("ctx") * tok_rows + jnp.arange(tok_rows, dtype=jnp.int32)
    own_place = dealt_positions(own_rows, tok_rows, context_size)
    all_place = dealt_positions(jnp.arange(sequence_rows, dtype=jnp.int32), tok_rows, context_size)
    document_row = document_ids[0]
    own_document = jnp.take(document_row, own_place)
    all_document = jnp.take(document_row, all_place)
    relative = own_place - jnp.take(document_starts(document_row), own_place)
    cosine, sine_table = rotary_tables(relative, HEAD_DIM)
    attend_inverse = inverse_rms(inputs)
    attend_normed = inputs * attend_inverse
    attend_in = (attend_normed * gain_rows[:, 0]).astype(jnp.bfloat16)
    projected = jnp.dot(attend_in, gathered_in, preferred_element_type=jnp.float32)
    raw_query = projected[:, :model_width]
    raw_key = projected[:, model_width : 2 * model_width]
    query_inverse = inverse_rms(raw_query)
    query_normed = raw_query * query_inverse
    key_inverse = inverse_rms(raw_key)
    key_normed = raw_key * key_inverse
    query_low = rotate(
        (query_normed * gain_rows[:, 1]).reshape(heads_shape), cosine, sine_table
    ).astype(jnp.bfloat16)
    key_low = rotate(
        (key_normed * gain_rows[:, 2]).reshape(heads_shape), cosine, sine_table
    ).astype(jnp.bfloat16)
    value_low = projected[:, 2 * model_width :].astype(jnp.bfloat16)
    key_all, value_all = (
        lax.all_gather(key_low.reshape(tok_rows, model_width), "ctx", axis=0, tiled=True),
        lax.all_gather(value_low, "ctx", axis=0, tiled=True),
    )
    key_split = key_all.reshape(block_shape)
    value_split = value_all.reshape(block_shape)
    place_split = all_place.reshape(key_blocks, key_span)
    document_split = all_document.reshape(key_blocks, key_span)

    def total_step(state_pair, block_args):
        row_peak, row_total = state_pair
        key_block, key_place, key_document = block_args
        scores, visible = block_scores(
            query_low, key_block, own_place, own_document, key_place, key_document, score_scale
        )
        new_peak = jnp.maximum(row_peak, jnp.max(scores, axis=-1))
        fresh_total = jnp.sum(
            jnp.where(visible, jnp.exp(scores - new_peak[..., None]), 0.0), axis=-1
        )
        return ((new_peak, row_total * jnp.exp(row_peak - new_peak) + fresh_total), None)

    start_pair = (
        jnp.full((HEADS, tok_rows), MASKED, jnp.float32),
        jnp.zeros((HEADS, tok_rows), jnp.float32),
    )
    (row_peak, row_total), unused = lax.scan(
        total_step, start_pair, (key_split, place_split, document_split)
    )
    row_logsum = row_peak + jnp.log(row_total)

    def value_step(running, block_args):
        key_block, value_block, key_place, key_document = block_args
        scores, visible = block_scores(
            query_low, key_block, own_place, own_document, key_place, key_document, score_scale
        )
        prob_low = jnp.where(visible, jnp.exp(scores - row_logsum[..., None]), 0.0).astype(
            jnp.bfloat16
        )
        return (
            running
            + jnp.einsum("htk,khd->thd", prob_low, value_block, preferred_element_type=jnp.float32),
            None,
        )

    attend_out, unused = lax.scan(
        value_step,
        jnp.zeros(heads_shape, jnp.float32),
        (key_split, value_split, place_split, document_split),
    )
    attend_low = attend_out.reshape(tok_rows, model_width).astype(jnp.bfloat16)
    residual = inputs + jnp.dot(attend_low, gathered_out, preferred_element_type=jnp.float32)
    mixed_inverse = inverse_rms(residual)
    mixed_normed = residual * mixed_inverse
    mixed_low = (mixed_normed * gain_rows[:, 3]).astype(jnp.bfloat16)
    logits = jnp.dot(mixed_low, gathered_router, preferred_element_type=jnp.float32)
    route_onehot = (route_rows[..., None] == jnp.arange(expert_count, dtype=jnp.int32)).astype(
        jnp.float32
    )
    gate_weights = jax.nn.softmax(jnp.sum(route_onehot * logits[:, None, :], axis=-1), axis=-1)
    target_slot, slot_owner = dispatch_plan(route_rows, expert_count, capacity)
    padded_rows = jnp.concatenate([mixed_low, jnp.zeros((1, model_width), jnp.bfloat16)], axis=0)
    send_rows = jnp.take(padded_rows, slot_owner // top_count, axis=0).reshape(slot_shape)
    received = lax.all_to_all(send_rows, "ctx", split_axis=0, concat_axis=0, tiled=True).reshape(
        expert_shape
    )
    expert_up = jnp.einsum(
        "sxcd,xdf->sxcf", received, gathered_first, preferred_element_type=jnp.float32
    )
    gate_part = expert_up[..., :FF]
    up_part = expert_up[..., FF:]
    sigmoid_gate = jax.nn.sigmoid(gate_part)
    swish_gate = gate_part * sigmoid_gate
    hidden_low = (swish_gate * up_part).astype(jnp.bfloat16)
    expert_result = jnp.einsum(
        "sxcf,xfd->sxcd", hidden_low, gathered_second, preferred_element_type=jnp.float32
    ).astype(jnp.bfloat16)
    returned = lax.all_to_all(
        expert_result.reshape(slot_shape), "ctx", split_axis=0, concat_axis=0, tiled=True
    ).reshape(expert_count * capacity, model_width)
    pair_result = jnp.take(returned, target_slot, axis=0).reshape(tok_rows, top_count, model_width)
    mixture = jnp.sum(gate_weights[..., None] * pair_result, axis=1)
    layer_output = (residual + mixture).astype(jnp.bfloat16)
    upstream = cotangent[0].astype(jnp.float32)
    pair_back = (gate_weights[..., None] * upstream[:, None, :]).astype(jnp.bfloat16)
    gate_back = jnp.sum(pair_result * upstream[:, None, :], axis=-1)
    padded_back = jnp.concatenate(
        [
            pair_back.reshape(tok_rows * top_count, model_width),
            jnp.zeros((1, model_width), jnp.bfloat16),
        ],
        axis=0,
    )
    send_back = jnp.take(padded_back, slot_owner, axis=0).reshape(slot_shape)
    received_back = lax.all_to_all(
        send_back, "ctx", split_axis=0, concat_axis=0, tiled=True
    ).reshape(expert_shape)
    first_back, second_back = (gathered_first, gathered_second)
    hidden_back = jnp.einsum(
        "sxcd,xfd->sxcf", received_back, second_back, preferred_element_type=jnp.float32
    )
    second_weight_back = jnp.einsum(
        "sxcf,sxcd->xfd", hidden_low, received_back, preferred_element_type=jnp.float32
    )
    swish_slope = sigmoid_gate * (1.0 + gate_part * (1.0 - sigmoid_gate))
    up_back = jnp.concatenate(
        [hidden_back * up_part * swish_slope, hidden_back * swish_gate], axis=-1
    ).astype(jnp.bfloat16)
    first_weight_back = jnp.einsum(
        "sxcd,sxcf->xdf", received, up_back, preferred_element_type=jnp.float32
    )
    input_back = jnp.einsum(
        "sxcf,xdf->sxcd", up_back, first_back, preferred_element_type=jnp.float32
    ).astype(jnp.bfloat16)
    expert_in_gradient, expert_out_gradient = (
        lax.psum_scatter(
            first_weight_back.astype(jnp.bfloat16), "dp", scatter_dimension=1, tiled=True
        ).astype(jnp.float32),
        lax.psum_scatter(
            second_weight_back.astype(jnp.bfloat16), "dp", scatter_dimension=1, tiled=True
        ).astype(jnp.float32),
    )
    rows_back = lax.all_to_all(
        input_back.reshape(slot_shape), "ctx", split_axis=0, concat_axis=0, tiled=True
    ).reshape(expert_count * capacity, model_width)
    mixed_back = jnp.sum(
        jnp.take(rows_back, target_slot, axis=0)
        .reshape(tok_rows, top_count, model_width)
        .astype(jnp.float32),
        axis=1,
    )
    gains_back, in_back, out_back, router_back = (
        gathered_gains,
        gathered_in,
        gathered_out,
        gathered_router,
    )
    gain_values = gains_back.astype(jnp.float32)
    chosen_back = gate_weights * (
        gate_back - jnp.sum(gate_weights * gate_back, axis=-1, keepdims=True)
    )
    logit_back = jnp.sum(chosen_back[..., None] * route_onehot, axis=1).astype(jnp.bfloat16)
    router_weight_back = jnp.einsum(
        "td,te->de", mixed_low, logit_back, preferred_element_type=jnp.float32
    )
    mixed_back = mixed_back + jnp.einsum(
        "te,de->td", logit_back, router_back, preferred_element_type=jnp.float32
    )
    mixed_gain_back = jnp.sum(mixed_back * mixed_normed, axis=0)
    residual_back = upstream + normalize_back(
        mixed_back * gain_values[:, 3], mixed_normed, mixed_inverse
    )
    residual_low = residual_back.astype(jnp.bfloat16)
    out_weight_back = jnp.einsum(
        "td,te->de", attend_low, residual_low, preferred_element_type=jnp.float32
    )
    attend_back = (
        jnp.einsum("te,de->td", residual_low, out_back, preferred_element_type=jnp.float32)
        .astype(jnp.bfloat16)
        .reshape(heads_shape)
    )
    row_delta = jnp.einsum("thd,thd->ht", attend_back.astype(jnp.float32), attend_out)

    def back_step(query_acc, block_args):
        key_block, value_block, key_place, key_document = block_args
        query_part, key_part, value_part = block_backward(
            query_low,
            attend_back,
            row_logsum,
            row_delta,
            key_block,
            value_block,
            own_place,
            own_document,
            key_place,
            key_document,
            score_scale,
        )
        return (query_acc + query_part, (key_part, value_part))

    query_back, (key_parts, value_parts) = lax.scan(
        back_step,
        jnp.zeros(heads_shape, jnp.float32),
        (key_split, value_split, place_split, document_split),
    )
    key_back, value_back = (
        lax.psum_scatter(
            key_parts.reshape(sequence_rows, model_width).astype(jnp.bfloat16),
            "ctx",
            scatter_dimension=0,
            tiled=True,
        ).astype(jnp.float32),
        lax.psum_scatter(
            value_parts.reshape(sequence_rows, model_width).astype(jnp.bfloat16),
            "ctx",
            scatter_dimension=0,
            tiled=True,
        ).astype(jnp.float32),
    )
    query_flat = rotate(query_back, cosine, -sine_table).reshape(tok_rows, model_width)
    key_flat = rotate(key_back.reshape(heads_shape), cosine, -sine_table).reshape(
        tok_rows, model_width
    )
    query_gain_back = jnp.sum(query_flat * query_normed, axis=0)
    key_gain_back = jnp.sum(key_flat * key_normed, axis=0)
    raw_query_back = normalize_back(query_flat * gain_values[:, 1], query_normed, query_inverse)
    raw_key_back = normalize_back(key_flat * gain_values[:, 2], key_normed, key_inverse)
    raw_back = jnp.concatenate([raw_query_back, raw_key_back, value_back], axis=-1).astype(
        jnp.bfloat16
    )
    in_weight_back = jnp.einsum(
        "td,tf->df", attend_in, raw_back, preferred_element_type=jnp.float32
    )
    attend_in_back = jnp.einsum("tf,df->td", raw_back, in_back, preferred_element_type=jnp.float32)
    attend_gain_back = jnp.sum(attend_in_back * attend_normed, axis=0)
    tokens_back = residual_back + normalize_back(
        attend_in_back * gain_values[:, 0], attend_normed, attend_inverse
    )
    gain_columns = jnp.stack(
        [attend_gain_back, query_gain_back, key_gain_back, mixed_gain_back], axis=1
    )
    gains_gradient, project_in_gradient, project_out_gradient, router_gradient = (
        lax.psum_scatter(gain_columns, ("dp", "ctx"), scatter_dimension=0, tiled=True),
        lax.psum_scatter(in_weight_back, ("dp", "ctx"), scatter_dimension=0, tiled=True),
        lax.psum_scatter(out_weight_back, ("dp", "ctx"), scatter_dimension=0, tiled=True),
        lax.psum_scatter(router_weight_back, ("dp", "ctx"), scatter_dimension=0, tiled=True),
    )
    return (
        layer_output[None],
        tokens_back.astype(jnp.bfloat16)[None],
        gains_gradient,
        project_in_gradient,
        project_out_gradient,
        router_gradient,
        expert_in_gradient,
        expert_out_gradient,
    )


MESH = pl.DeviceIdType.MESH
VMEM_LIMIT = 48 * 1024 * 1024


def ring_place(device, n):
    odd = device % 2
    return (1 - odd) * (device // 2) + odd * (n - 1 - device // 2)


def ring_device(place, n):
    far = place // (n // 2)
    return (1 - far) * (2 * place) + far * (2 * (n - 1 - place) + 1)


class Ring:
    def __init__(self, n):
        self.n = n
        self.me = lax.axis_index("ctx")
        self.place = ring_place(self.me, n)

    def at(self, offset):
        return ring_device((self.place + offset + self.n) % self.n, self.n)

    def hops(self, way, half):
        return self.n // 2 if way == half else self.n // 2 - 1

    def barrier(self, others):
        semaphore = pltpu.get_barrier_semaphore()
        for other in others:
            pl.semaphore_signal(semaphore, inc=1, device_id=other, device_id_type=MESH)
        pl.semaphore_wait(semaphore, len(others))

    def neighbours(self):
        return [{"ctx": self.at(1)}, {"ctx": self.at(-1)}]


def remote(source, target, send, receive, device):
    return pltpu.make_async_remote_copy(
        src_ref=source,
        dst_ref=target,
        send_sem=send,
        recv_sem=receive,
        device_id=device,
        device_id_type=MESH,
    )


def gather_steps(ring, source, place, send, receive, arrived=None, ready=None):
    signs = (1, -1)

    def copy(way, half, hop):
        origin = ring.at(-signs[way] * hop)
        spot = place(origin, half)
        return remote(
            source(half) if hop == 0 else spot,
            spot,
            send.at[way, half, hop],
            receive.at[way, half, hop],
            {"ctx": ring.at(signs[way])},
        )

    def landed(way, half, hop):
        spot = place(ring.at(-signs[way] * (hop + 1)), half)
        return remote(
            spot,
            spot,
            send.at[way, half, hop],
            receive.at[way, half, hop],
            {"ctx": ring.at(signs[way])},
        )

    started = []
    for half in (0, 1):
        if ready is not None:
            ready(half)
        for way in (0, 1):
            started.append(copy(way, half, 0))
            started[-1].start()
        yield
    for hop in range(ring.n // 2):
        for half in (0, 1):
            for way in (0, 1):
                if hop < ring.hops(way, half):
                    landed(way, half, hop).wait_recv()
                    if hop + 1 < ring.hops(way, half):
                        started.append(copy(way, half, hop + 1))
                        started[-1].start()
                    if arrived is not None:
                        arrived(way, half, hop, ring.at(-signs[way] * (hop + 1)))
                    yield
    for one in started:
        one.wait_send()


def scatter_steps(ring, part, slots, store, send, receive):
    signs = (1, -1)

    def copy(way, half, hop, source):
        return remote(
            source,
            slots.at[way, half, hop],
            send.at[way, half, hop],
            receive.at[way, half, hop],
            {"ctx": ring.at(signs[way])},
        )

    started = []
    for half in (0, 1):
        for way in (0, 1):
            goal = ring.at(signs[way] * ring.hops(way, half))
            started.append(copy(way, half, 0, part(goal, half)))
            started[-1].start()
        yield
    for hop in range(ring.n // 2):
        for half in (0, 1):
            for way in (0, 1):
                last = ring.hops(way, half) - 1
                if hop <= last:
                    slot = slots.at[way, half, hop]
                    copy(way, half, hop, slot).wait_recv()
                    if hop < last:
                        goal = ring.at(signs[way] * (last - hop))
                        slot[...] = (
                            slot[...].astype(jnp.float32)
                            + part(goal, half)[...].astype(jnp.float32)
                        ).astype(slot.dtype)
                        started.append(copy(way, half, hop + 1, slot))
                        started[-1].start()
                    yield
    for half in (0, 1):
        total = part(ring.me, half)[...].astype(jnp.float32)
        for way in (0, 1):
            total = total + slots[way, half, ring.hops(way, half) - 1].astype(jnp.float32)
        store(half, total)
    for one in started:
        one.wait_send()


def run_steps(*tasks):
    tasks = list(tasks)
    while tasks:
        left = []
        for task in tasks:
            try:
                next(task)
                left.append(task)
            except StopIteration:
                pass
        tasks = left


def sems(*shape):
    return pltpu.SemaphoreType.DMA(shape)


def kernel_call(body, outs, in_specs, out_specs, scratch, identity, name, sent):
    return pl.pallas_call(
        body,
        out_shape=outs,
        in_specs=in_specs,
        out_specs=out_specs,
        scratch_shapes=scratch,
        name=name,
        cost_estimate=pl.CostEstimate(flops=0, bytes_accessed=sent, transcendentals=0),
        compiler_params=pltpu.CompilerParams(
            collective_id=identity, has_side_effects=True, vmem_limit_bytes=VMEM_LIMIT
        ),
    )


ANY = pl.BlockSpec(memory_space=pl.ANY)
VMEM = pl.BlockSpec(memory_space=pltpu.VMEM)


def ring_gather(block, n, identity, name, axis=0):
    rows, width = block.shape
    half_rows = rows // 2
    shape = (rows * n, width) if axis == 0 else (rows, width * n)

    def body(block_ref, all_ref, send, receive, local):
        ring = Ring(n)

        def place(device, half):
            if axis == 0:
                return all_ref.at[pl.ds(pl.multiple_of(device * rows + half * half_rows, 16), half_rows)]
            return all_ref.at[
                pl.ds(half * half_rows, half_rows), pl.ds(pl.multiple_of(device * width, 128), width)
            ]

        whole = (
            all_ref.at[pl.ds(pl.multiple_of(ring.me * rows, 16), rows)]
            if axis == 0
            else all_ref.at[:, pl.ds(pl.multiple_of(ring.me * width, 128), width)]
        )
        own = pltpu.make_async_copy(block_ref, whole, local)
        own.start()
        ring.barrier(ring.neighbours())
        run_steps(
            gather_steps(
                ring,
                lambda half: block_ref.at[pl.ds(half * half_rows, half_rows)],
                place,
                send,
                receive,
            )
        )
        own.wait()

    return kernel_call(
        body,
        jax.ShapeDtypeStruct(shape, block.dtype),
        [ANY],
        ANY,
        [sems(2, 2, n // 2), sems(2, 2, n // 2), pltpu.SemaphoreType.DMA],
        identity,
        name,
        block.size * 2 * n * 32,
    )(block)


def ring_scatter(partial, n, identity, name):
    rows, width = partial.shape[0] // n, partial.shape[1]
    half_rows = rows // 2

    def body(part_ref, sum_ref, slots, send, receive):
        ring = Ring(n)
        ring.barrier(ring.neighbours())

        def part(device, half):
            return part_ref.at[pl.ds(pl.multiple_of(device * rows + half * half_rows, 16), half_rows)]

        def store(half, total):
            sum_ref[pl.ds(half * half_rows, half_rows)] = total

        run_steps(scatter_steps(ring, part, slots, store, send, receive))

    return kernel_call(
        body,
        jax.ShapeDtypeStruct((rows, width), jnp.float32),
        [VMEM],
        VMEM,
        [
            pltpu.VMEM((2, 2, n // 2, half_rows, width), partial.dtype),
            sems(2, 2, n // 2),
            sems(2, 2, n // 2),
        ],
        identity,
        name,
        partial.size * 2 * 32,
    )(partial)


def partners():
    dp = lax.axis_index("dp")
    core = dp + 1 - 2 * (dp % 2)
    chip = (dp + 2) % 4
    return dp, core, chip, (core + 2) % 4


def gather_inputs(tokens, named, in_blocks, n, n_dp, identity):
    tok_rows, width = tokens.shape

    def body(
        token_ref,
        named_ref,
        in_ref,
        token_all,
        named_all,
        in_all,
        token_send,
        token_receive,
        named_send,
        named_receive,
        in_send,
        in_receive,
        pass_send,
        pass_receive,
        local,
    ):
        ring = Ring(n)
        me = ring.me
        dp, core, chip, core_chip = partners()
        half_rows = tok_rows // 2

        def token_place(device, half):
            return token_all.at[
                pl.ds(pl.multiple_of(device * tok_rows + half * half_rows, 16), half_rows)
            ]

        locals_ = [
            pltpu.make_async_copy(in_ref.at[me], in_all.at[dp, me], local.at[0]),
            pltpu.make_async_copy(
                token_ref,
                token_all.at[pl.ds(pl.multiple_of(me * tok_rows, 16), tok_rows)],
                local.at[1],
            ),
            pltpu.make_async_copy(named_ref, named_all.at[me], local.at[2]),
        ]
        for copy in locals_:
            copy.start()
        others = [(me + k) % n for k in range(1, n)]
        ring.barrier([{"ctx": other} for other in others] + [{"dp": core}, {"dp": chip}])

        direct = []
        for k, other in enumerate(others):
            direct.append(
                remote(in_ref.at[other], in_all.at[dp, me], in_send.at[k], in_receive.at[k], {"ctx": other})
            )
            direct.append(
                remote(named_ref, named_all.at[me], named_send.at[k], named_receive.at[k], {"ctx": other})
            )
        for copy in direct:
            copy.start()

        def in_steps():
            for _ in range(2):
                yield
            for k in range(1, n):
                spot = in_all.at[dp, (me - k + n) % n]
                remote(
                    spot, spot, in_send.at[k - 1], in_receive.at[k - 1], {"ctx": others[k - 1]}
                ).wait_recv()
            locals_[0].wait()
            passed = []
            for at, to in ((0, chip), (1, core)):
                passed.append(
                    remote(
                        in_all.at[dp], in_all.at[dp], pass_send.at[at], pass_receive.at[at], {"dp": to}
                    )
                )
                passed[-1].start()
            for _ in range(8):
                yield
            spot = in_all.at[chip]
            remote(spot, spot, pass_send.at[0], pass_receive.at[0], {"dp": chip}).wait_recv()
            passed.append(
                remote(spot, spot, pass_send.at[2], pass_receive.at[2], {"dp": core})
            )
            passed[-1].start()
            for _ in range(4):
                yield
            for at, source in ((1, core), (2, core_chip)):
                spot = in_all.at[source]
                remote(
                    spot, spot, pass_send.at[at], pass_receive.at[at], {"dp": core}
                ).wait_recv()
            for copy in passed:
                copy.wait_send()

        run_steps(
            gather_steps(
                ring,
                lambda half: token_ref.at[pl.ds(half * half_rows, half_rows)],
                token_place,
                token_send,
                token_receive,
            ),
            in_steps(),
        )
        for k in range(1, n):
            spot = named_all.at[(me - k + n) % n]
            remote(
                spot, spot, named_send.at[k - 1], named_receive.at[k - 1], {"ctx": others[k - 1]}
            ).wait_recv()
        for copy in direct:
            copy.wait_send()
        for copy in locals_[1:]:
            copy.wait()

    return kernel_call(
        body,
        (
            jax.ShapeDtypeStruct((tok_rows * n, width), tokens.dtype),
            jax.ShapeDtypeStruct((n,) + named.shape, named.dtype),
            jax.ShapeDtypeStruct((n_dp,) + in_blocks.shape, in_blocks.dtype),
        ),
        [ANY] * 3,
        (ANY,) * 3,
        [sems(2, 2, n // 2)] * 2
        + [sems(n - 1)] * 4
        + [sems(3)] * 2
        + [sems(3)],
        identity,
        "gather_inputs",
        200_000_000,
    )(tokens, named, in_blocks)


def sum_small_steps(ring, small, core_s, chip_s, quarter, got, total, sem):
    pass_send, pass_receive, send, receive = sem
    dp, core, chip, core_chip = partners()
    n, me = ring.n, ring.me
    lanes = quarter.shape[1]
    per_tile = LANES * n // lanes

    def group(at):
        return small.at[:, pl.ds(pl.multiple_of(at * lanes, LANES), lanes)]

    copies = [
        remote(group(core_chip), core_s.at[1], pass_send.at[0], pass_receive.at[0], {"dp": core}),
        remote(group(core), core_s.at[0], pass_send.at[1], pass_receive.at[1], {"dp": core}),
    ]
    for copy in copies:
        copy.start()
    copies[0].wait_recv()
    core_s[1] = core_s[1] + group(chip)[...]
    copies.append(
        remote(core_s.at[1], chip_s, pass_send.at[2], pass_receive.at[2], {"dp": chip})
    )
    copies[-1].start()
    copies[1].wait_recv()
    copies[2].wait_recv()
    quarter[...] = group(dp)[...] + core_s[0] + chip_s[...]

    def tile(device):
        return quarter.at[:, pl.ds(pl.multiple_of(device // per_tile * LANES, LANES), LANES)]

    for k in range(1, n):
        other = (me + k) % n
        copies.append(
            remote(tile(other), got.at[k - 1], send.at[k - 1], receive.at[k - 1], {"ctx": other})
        )
        copies[-1].start()
    value = tile(me)[...]
    for k in range(1, n):
        copies[2 + k].wait_recv()
        value = value + got[k - 1]
    total[...] = value
    for copy in copies:
        copy.wait_send()


def scatter_end(
    row_part, attend_in, raw_back, tokens, residual_back, gain, small, pair_sum, n, n_dp, identity
):
    rows, width = row_part.shape[0] // n, row_part.shape[1]
    half_rows = rows // 2
    span = width // n_dp
    weight_rows = span // n
    in_cols = raw_back.shape[1]
    cols = in_cols // 3
    small_rows = small.shape[0]
    bf16, f32 = jnp.bfloat16, jnp.float32

    def body(
        row_ref,
        attend_ref,
        raw_ref,
        token_ref,
        back_ref,
        gain_ref,
        small_ref,
        pair_ref,
        token_back,
        in_sum,
        small_sum,
        slots,
        row_s,
        attend_s,
        in_part,
        in_core,
        in_chip,
        in_got,
        small_s,
        small_core,
        small_chip,
        small_quarter,
        small_got,
        row_send,
        row_receive,
        pass_send,
        pass_receive,
        in_send,
        in_receive,
        small_pass_send,
        small_pass_receive,
        small_send,
        small_receive,
        load,
    ):
        ring = Ring(n)
        me = ring.me
        dp, core, chip, core_chip = partners()
        others = [(me + k) % n for k in range(1, n)]
        loaded = pltpu.make_async_copy(attend_ref, attend_s, load)
        loaded.start()
        ring.barrier([{"ctx": other} for other in others] + [{"dp": core}, {"dp": chip}])

        def part(device, half):
            return row_ref.at[pl.ds(pl.multiple_of(device * rows + half * half_rows, 16), half_rows)]

        def store(half, total):
            row_s[pl.ds(half * half_rows, half_rows)] = total

        def passing(at, source, target, to):
            return remote(source, target, pass_send.at[at], pass_receive.at[at], {"dp": to})

        def product(group):
            value = lax.dot_general(
                attend_s[:, pl.ds(pl.multiple_of(group * span, LANES), span)],
                raw_ref[...],
                (((0,), (0,)), ((), ())),
                preferred_element_type=f32,
            )
            in_part[group] = value.astype(bf16).reshape(n, weight_rows, in_cols)

        def weight_steps():
            loaded.wait()
            product(core_chip)
            passed = [passing(0, in_part.at[core_chip], in_core.at[1], core)]
            passed[-1].start()
            yield
            product(core)
            passed.append(passing(1, in_part.at[core], in_core.at[0], core))
            passed[-1].start()
            yield
            product(chip)
            passed[0].wait_recv()

            def add_far(k, carry):
                in_core[1, k] = (in_core[1, k].astype(f32) + in_part[chip, k].astype(f32)).astype(bf16)
                return carry

            lax.fori_loop(0, n, add_far, 0)
            passed.append(passing(2, in_core.at[1], in_chip, chip))
            passed[-1].start()
            yield
            product(dp)
            passed[1].wait_recv()
            for _ in range(4):
                yield
            passed[2].wait_recv()

            def add_near(k, carry):
                in_core[0, k] = (
                    in_core[0, k].astype(f32) + in_part[dp, k].astype(f32) + in_chip[k].astype(f32)
                ).astype(bf16)
                return carry

            lax.fori_loop(0, n, add_near, 0)
            direct = []
            for k, other in enumerate(others):
                direct.append(
                    remote(in_core.at[0, other], in_got.at[me], in_send.at[k], in_receive.at[k], {"ctx": other})
                )
                direct[-1].start()
            in_got[me] = in_core[0, me]
            for _ in range(8):
                yield
            for k in range(1, n):
                spot = in_got.at[(me - k + n) % n]
                remote(
                    spot, spot, in_send.at[k - 1], in_receive.at[k - 1], {"ctx": others[k - 1]}
                ).wait_recv()
            for device in range(n):
                for which in range(3):
                    in_sum[:, pl.ds(which * width + device * cols, cols)] = in_got[
                        device, :, pl.ds(which * cols, cols)
                    ].astype(f32)
            for copy in passed + direct:
                copy.wait_send()

        def row_steps():
            yield from scatter_steps(ring, part, slots, store, row_send, row_receive)
            values = token_ref[...].astype(f32)
            inverse = lax.rsqrt(jnp.mean(values * values, axis=-1, keepdims=True) + EPSILON)
            normed = values * inverse
            back = row_s[...]
            small_s[...] = small_ref[...]
            small_s[0:1, :] = jnp.sum(back * normed, axis=0, keepdims=True)
            own = pl.ds(pl.multiple_of(me * cols, LANES), cols)
            small_s[1:2, own] = pair_ref[0:1, :cols]
            small_s[2:3, own] = pair_ref[0:1, cols:]
            back = back * gain_ref[0:1, :]
            token_back[...] = (
                back_ref[...]
                + inverse * (back - normed * jnp.mean(back * normed, axis=-1, keepdims=True))
            ).astype(bf16)
            sum_small_steps(
                ring,
                small_s,
                small_core,
                small_chip,
                small_quarter,
                small_got,
                small_sum,
                (small_pass_send, small_pass_receive, small_send, small_receive),
            )

        run_steps(row_steps(), weight_steps())

    block = (n, weight_rows, in_cols)
    return kernel_call(
        body,
        (
            jax.ShapeDtypeStruct((rows, width), bf16),
            jax.ShapeDtypeStruct((weight_rows, 3 * width), f32),
            jax.ShapeDtypeStruct((small_rows, LANES), f32),
        ),
        [VMEM, ANY] + [VMEM] * 6,
        (VMEM,) * 3,
        [
            pltpu.VMEM((2, 2, n // 2, half_rows, width), row_part.dtype),
            pltpu.VMEM((rows, width), f32),
            pltpu.VMEM(attend_in.shape, bf16),
            pltpu.VMEM((n_dp,) + block, bf16),
            pltpu.VMEM((2,) + block, bf16),
            pltpu.VMEM(block, bf16),
            pltpu.VMEM(block, bf16),
            pltpu.VMEM((small_rows, width), f32),
            pltpu.VMEM((2, small_rows, span), f32),
            pltpu.VMEM((small_rows, span), f32),
            pltpu.VMEM((small_rows, span), f32),
            pltpu.VMEM((n - 1, small_rows, LANES), f32),
            sems(2, 2, n // 2),
            sems(2, 2, n // 2),
            sems(3),
            sems(3),
            sems(n - 1),
            sems(n - 1),
            sems(3),
            sems(3),
            sems(n - 1),
            sems(n - 1),
            pltpu.SemaphoreType.DMA,
        ],
        identity,
        "scatter_end",
        200_000_000,
    )(row_part, attend_in, raw_back, tokens, residual_back, gain, small, pair_sum)


def slot_offsets(n):
    offsets = [0]
    for k in range(1, n // 2):
        offsets += [k, -k]
    return offsets + [n // 2]


def slot_of(offset, n):
    if abs(offset) == n // 2:
        return n - 1
    return 2 * offset - 1 if offset > 0 else -2 * offset


def slot_gather_steps(ring, first, slots, send, receive):
    signs = (1, -1)
    half_rows = slots.shape[1] // 2

    def copy(way, half, hop):
        rows = pl.ds(half * half_rows, half_rows)
        held = slot_of(-signs[way] * hop, ring.n)
        return remote(
            first.at[rows] if hop == 0 else slots.at[held, rows],
            slots.at[slot_of(-signs[way] * (hop + 1), ring.n), rows],
            send.at[way, half, hop],
            receive.at[way, half, hop],
            {"ctx": ring.at(signs[way])},
        )

    started = []
    for half in (0, 1):
        for way in (0, 1):
            started.append(copy(way, half, 0))
            started[-1].start()
    yield
    for hop in range(ring.n // 2):
        for half in (0, 1):
            for way in (0, 1):
                if hop < ring.hops(way, half):
                    copy(way, half, hop).wait_recv()
                    if hop + 1 < ring.hops(way, half):
                        started.append(copy(way, half, hop + 1))
                        started[-1].start()
                    yield
    for one in started:
        one.wait_send()


def advance(steps, count):
    for _ in range(count):
        next(steps, None)


def dot(a, b):
    return jnp.dot(a, b, preferred_element_type=jnp.float32)


def dot_across(a, b):
    return lax.dot_general(a, b, (((1,), (1,)), ((), ())), preferred_element_type=jnp.float32)


def experts_in(
    attend_all, token_all, cotangent, out_all, first, second, gain, router, named, n, identity
):
    tok_rows, width = cotangent.shape
    local_experts, ff = first.shape[0], second.shape[0] // first.shape[0]
    rows = tok_rows * n
    pair = 2 * tok_rows
    part = 4 * tok_rows
    tile, wide = TILE, WIDE
    bf16, f32 = jnp.bfloat16, jnp.float32
    offsets = slot_offsets(n)

    def body(
        attend_ref,
        token_ref,
        back_ref,
        out_ref,
        first_ref,
        second_ref,
        gain_ref,
        router_ref,
        named_ref,
        back_all,
        mixed_all,
        gated_all,
        up_all,
        own_gates,
        gate_back,
        own_residual,
        out_s,
        first_s,
        second_s,
        mixed_s,
        back_s,
        attend_s,
        token_s,
        residual_s,
        gate_s,
        sum_s,
        send,
        receive,
        load,
        weight_load,
        save,
        local,
    ):
        ring = Ring(n)
        lanes = lax.broadcasted_iota(jnp.int32, (pair, LANES), 1)
        part_lanes = lax.broadcasted_iota(jnp.int32, (part, LANES), 1)
        loads = [pltpu.make_async_copy(out_ref, out_s, weight_load.at[0])]
        for x in range(local_experts):
            loads.append(pltpu.make_async_copy(first_ref.at[x], first_s.at[x], weight_load.at[1 + x]))
        loads.append(pltpu.make_async_copy(second_ref, second_s, weight_load.at[1 + local_experts]))

        def row_loads(j):
            copies = []
            for k in range(2):
                device = ring.at(offsets[2 * j + k])
                source = pl.ds(pl.multiple_of(device * tok_rows, 16), tok_rows)
                target = pl.ds(k * tok_rows, tok_rows)
                for at, (array, held) in enumerate(((attend_ref, attend_s), (token_ref, token_s))):
                    copies.append(
                        pltpu.make_async_copy(
                            array.at[source], held.at[j % 2, target], load.at[j % 2, k, at]
                        )
                    )
            return copies

        pending = row_loads(0)
        for copy in pending:
            copy.start()
        loads[0].start()
        own = pltpu.make_async_copy(back_ref, back_s.at[0], local)
        own.start()
        ring.barrier(ring.neighbours())
        steps = slot_gather_steps(ring, back_ref, back_s, send, receive)
        advance(steps, 1)
        loads[0].wait()
        for copy in loads[1:]:
            copy.start()

        saves = []
        for j in range(n // 2):
            for copy in pending:
                copy.wait()
            if j + 1 < n // 2:
                pending = row_loads(j + 1)
                for copy in pending:
                    copy.start()

            def project(t, carry, j=j):
                columns = pl.ds(pl.multiple_of(t * wide, wide), wide)
                residual_s[:, columns] = token_s[j % 2, :, columns].astype(f32) + dot(
                    attend_s[j % 2], out_s[:, columns]
                )
                return carry

            lax.fori_loop(0, width // wide, project, 0)
            residual = residual_s[...]
            if j == 0:
                own_residual[...] = residual[:tok_rows]
            inverse = lax.rsqrt(jnp.mean(residual * residual, axis=-1, keepdims=True) + EPSILON)
            mixed = (residual * inverse * gain_ref[0:1, :]).astype(bf16)
            for k in range(2):
                mixed_s[2 * j + k] = mixed[k * tok_rows : (k + 1) * tok_rows]
            logits = dot(mixed, router_ref[...])
            marks = jnp.concatenate(
                [
                    named_ref[pl.ds(pl.multiple_of(ring.at(offsets[2 * j + k]) * tok_rows, 16), tok_rows)]
                    for k in range(2)
                ],
                axis=0,
            ).astype(f32)
            logits = jnp.where(marks > 0, logits, MASKED)
            powers = jnp.where(
                marks > 0, jnp.exp(logits - jnp.max(logits, axis=-1, keepdims=True)), 0.0
            )
            gates = powers / jnp.sum(powers, axis=-1, keepdims=True)
            if j == 0:
                own_gates[...] = gates[:tok_rows]
            held = jnp.zeros((pair, LANES), f32)
            for x in range(local_experts):
                mine = jnp.sum(
                    jnp.where(lanes == ring.me * local_experts + x, gates, 0.0), axis=-1, keepdims=True
                )
                held = jnp.where(lanes == x, mine, held)
            gate_s[pl.ds(j * pair, pair)] = held
            saves.append(
                pltpu.make_async_copy(
                    mixed_s.at[pl.ds(2 * j, 2)], mixed_all.at[pl.ds(2 * j, 2)], save.at[j]
                )
            )
            saves[-1].start()
            advance(steps, 2)

        counts = rows // part
        outgoing = []
        base = n // 2
        for s in range(counts):
            slots = pl.ds(s * 4, 4)
            part_rows = pl.ds(s * part, part)
            advance(steps, 0 if s < counts - 1 else 64)
            if s == 0:
                own.wait()
            sum_s[part_rows] = jnp.zeros((part, LANES), f32)
            for copy in outgoing:
                copy.wait()
            outgoing = []
            for x in range(local_experts):
                if s == 0:
                    loads[1 + x].wait()
                    if x == 0:
                        loads[1 + local_experts].wait()

                def hidden(t, carry, s=s, x=x, slots=slots, part_rows=part_rows):
                    at = pl.multiple_of(t * tile, tile)
                    mixed = mixed_s[slots].reshape(part, width)
                    back = back_s[slots].reshape(part, width)
                    gate_part = dot(mixed, first_s[x, :, pl.ds(at, tile)])
                    up_part = dot(mixed, first_s[x, :, pl.ds(pl.multiple_of(ff + at, tile), tile)])
                    hidden_back = dot_across(
                        back, second_s[pl.ds(pl.multiple_of(x * ff + at, tile), tile), :]
                    )
                    gate = gate_s[part_rows, x : x + 1]
                    sigmoid = jax.nn.sigmoid(gate_part)
                    swish = gate_part * sigmoid
                    value = swish * up_part
                    out_s[pl.ds(0, part), pl.ds(pl.multiple_of(x * ff + at, tile), tile)] = (
                        value * gate
                    ).astype(bf16)
                    sums = jnp.sum(value * hidden_back, axis=-1, keepdims=True)
                    sum_s[part_rows] = sum_s[part_rows] + jnp.where(part_lanes == x, sums, 0.0)
                    hidden_back = hidden_back * gate
                    slope = sigmoid * (1.0 + gate_part * (1.0 - sigmoid))
                    up_rows = pl.ds((1 + x) * part, part)
                    out_s[up_rows, pl.ds(at, tile)] = (hidden_back * up_part * slope).astype(bf16)
                    out_s[up_rows, pl.ds(pl.multiple_of(ff + at, tile), tile)] = (
                        hidden_back * swish
                    ).astype(bf16)
                    return carry

                pieces = ff // tile
                lax.fori_loop(0, pieces // 2, hidden, 0)
                advance(steps, 2)
                lax.fori_loop(pieces // 2, pieces, hidden, 0)
                advance(steps, 2)
                outgoing.append(
                    pltpu.make_async_copy(
                        out_s.at[pl.ds((1 + x) * part, part)],
                        up_all.at[x, part_rows],
                        save.at[base + 1 + x],
                    )
                )
                outgoing[-1].start()
            outgoing.append(
                pltpu.make_async_copy(out_s.at[pl.ds(0, part)], gated_all.at[part_rows], save.at[base])
            )
            outgoing[-1].start()
        spread = pltpu.make_async_copy(back_s, back_all, local)
        spread.start()
        for k in range(n):
            gate_back[k] = jnp.transpose(sum_s[pl.ds(k * tok_rows, tok_rows)])[:8]
        for copy in saves + outgoing:
            copy.wait()
        spread.wait()

    return pl.pallas_call(
        body,
        out_shape=(
            jax.ShapeDtypeStruct((n, tok_rows, width), bf16),
            jax.ShapeDtypeStruct((n, tok_rows, width), bf16),
            jax.ShapeDtypeStruct((rows, local_experts * ff), bf16),
            jax.ShapeDtypeStruct((local_experts, rows, 2 * ff), bf16),
            jax.ShapeDtypeStruct((tok_rows, LANES), f32),
            jax.ShapeDtypeStruct((n, 8, LANES), f32),
            jax.ShapeDtypeStruct((tok_rows, width), f32),
        ),
        in_specs=[ANY] * 6 + [VMEM] * 3,
        out_specs=(ANY,) * 4 + (VMEM,) * 3,
        scratch_shapes=[
            pltpu.VMEM(out_all.shape, bf16),
            pltpu.VMEM(first.shape, bf16),
            pltpu.VMEM(second.shape, bf16),
            pltpu.VMEM((n, tok_rows, width), bf16),
            pltpu.VMEM((n, tok_rows, width), bf16),
            pltpu.VMEM((2, pair, width), bf16),
            pltpu.VMEM((2, pair, width), bf16),
            pltpu.VMEM((pair, width), f32),
            pltpu.VMEM((rows, LANES), f32),
            pltpu.VMEM((rows, LANES), f32),
            sems(2, 2, n // 2),
            sems(2, 2, n // 2),
            sems(2, 2, 2),
            sems(2 + local_experts),
            sems(n // 2 + 1 + local_experts),
            pltpu.SemaphoreType.DMA,
        ],
        name="experts_in",
        cost_estimate=pl.CostEstimate(
            flops=2 * rows * width * (width + 3 * ff * local_experts),
            bytes_accessed=60_000_000,
            transcendentals=0,
        ),
        compiler_params=pltpu.CompilerParams(
            collective_id=identity, has_side_effects=True, vmem_limit_bytes=BIG_VMEM
        ),
    )(attend_all, token_all, cotangent, out_all, first, second, gain, router, named)


BIG_VMEM = 60 * 1024 * 1024


def slot_scatter_steps(ring, parts, slots, store, send, receive, need):
    signs = (1, -1)
    half_rows = parts.shape[1] // 2
    f32 = jnp.float32

    def part(offset, half):
        return parts.at[slot_of(offset, ring.n), pl.ds(half * half_rows, half_rows)]

    def copy(way, half, hop, source):
        return remote(
            source,
            slots.at[way, half, hop],
            send.at[way, half, hop],
            receive.at[way, half, hop],
            {"ctx": ring.at(signs[way])},
        )

    started = []
    firsts = [(way, half) for half in (0, 1) for way in (0, 1)]
    firsts.sort(key=lambda one: -slot_of(signs[one[0]] * ring.hops(*one), ring.n))
    for way, half in firsts:
        goal = signs[way] * ring.hops(way, half)
        need(slot_of(goal, ring.n))
        started.append(copy(way, half, 0, part(goal, half)))
        started[-1].start()
    for hop in range(ring.n // 2):
        for way, half in firsts:
            last = ring.hops(way, half) - 1
            if hop <= last:
                slot = slots.at[way, half, hop]
                if hop < last:
                    goal = signs[way] * (last - hop)
                    need(slot_of(goal, ring.n))
                copy(way, half, hop, slot).wait_recv()
                if hop < last:
                    slot[...] = (
                        slot[...].astype(f32) + part(goal, half)[...].astype(f32)
                    ).astype(slot.dtype)
                    started.append(copy(way, half, hop + 1, slot))
                    started[-1].start()
                yield
    need(0)
    for half in (0, 1):
        total = part(0, half)[...].astype(f32)
        for way in (0, 1):
            total = total + slots[way, half, ring.hops(way, half) - 1].astype(f32)
        store(half, total)
    for one in started:
        one.wait_send()


def experts_out(up_all, gated_all, first, second, gate_back, n, identity):
    local_experts, rows, inner = up_all.shape
    width = first.shape[1]
    tok_rows = rows // n
    half_rows = tok_rows // 2
    pair = 2 * tok_rows
    wide = 512
    count = width // wide
    bf16, f32 = jnp.bfloat16, jnp.float32
    offsets = slot_offsets(n)

    def body(
        up_ref,
        gated_ref,
        first_ref,
        second_ref,
        gate_ref,
        row_sum,
        result_all,
        gate_got,
        first_s,
        second_s,
        up_s,
        gated_s,
        part_s,
        result_s,
        slots,
        send,
        receive,
        gate_send,
        gate_receive,
        load,
        first_load,
        other_load,
        save,
    ):
        ring = Ring(n)

        def up_load(j):
            return pltpu.make_async_copy(
                up_ref.at[:, pl.ds(j * pair, pair)], up_s.at[:, pl.ds(j * pair, pair)], load.at[j]
            )

        def weight_load(t):
            return pltpu.make_async_copy(
                first_ref.at[:, pl.ds(t * wide, wide)],
                first_s.at[:, pl.ds(t * wide, wide)],
                first_load.at[t],
            )

        groups = n // 2
        up_load(groups - 1).start()
        for t in range(count):
            weight_load(t).start()
        for j in range(groups - 1):
            up_load(groups - 2 - j).start()
        others = [
            pltpu.make_async_copy(gated_ref, gated_s, other_load.at[0]),
            pltpu.make_async_copy(second_ref, second_s, other_load.at[1]),
        ]
        for copy in others:
            copy.start()
        ring.barrier([{"ctx": ring.at(k)} for k in range(1, n)])
        gate_copies = []
        for k in range(1, n):
            offset = k if k <= n // 2 else k - n
            back = -offset if offset < n // 2 else offset
            gate_copies.append(
                remote(
                    gate_ref.at[slot_of(offset, n)],
                    gate_got.at[slot_of(back, n)],
                    gate_send.at[slot_of(back, n)],
                    gate_receive.at[slot_of(back, n)],
                    {"ctx": ring.at(k)},
                )
            )
            gate_copies[-1].start()
        gate_got[0] = gate_ref[0]

        done = set()

        def product(j):
            rows_j = pl.ds(j * pair, pair)
            up_load(j).wait()

            def columns(t):
                at = pl.ds(pl.multiple_of(t * wide, wide), wide)
                value = dot_across(up_s[0, rows_j], first_s[0, at, :])
                for x in range(1, local_experts):
                    value = value + dot_across(up_s[x, rows_j], first_s[x, at, :])
                value = value.astype(bf16)
                for k in range(2):
                    part_s[2 * j + k, :, at] = value[k * tok_rows : (k + 1) * tok_rows]

            if not done:
                for t in range(count):
                    weight_load(t).wait()
                    columns(t)
            else:

                def step(t, carry):
                    columns(t)
                    return carry

                lax.fori_loop(0, count, step, 0)
            done.add(j)

        def need(slot):
            if slot // 2 not in done:
                product(slot // 2)

        def store(half, total):
            row_sum[pl.ds(half * half_rows, half_rows)] = total

        steps = slot_scatter_steps(ring, part_s, slots, store, send, receive, need)
        for j in reversed(range(groups)):
            need(2 * j)
            advance(steps, 1 if j in (0, groups - 1) else 2)
        for copy in others:
            copy.wait()
        saves = []
        chunk = 2
        for j in range(n // chunk):
            rows_j = pl.ds(j * chunk * tok_rows, chunk * tok_rows)

            def result(t, carry, rows_j=rows_j, j=j):
                at = pl.ds(pl.multiple_of(t * wide, wide), wide)
                value = dot(gated_s[rows_j], second_s[:, at]).astype(bf16)
                for k in range(chunk):
                    result_s[chunk * j + k, :, at] = value[k * tok_rows : (k + 1) * tok_rows]
                return carry

            lax.fori_loop(0, count, result, 0)
            for k in range(chunk):
                slot = chunk * j + k
                device = ring.at(offsets[slot])
                saves.append(
                    pltpu.make_async_copy(
                        result_s.at[slot],
                        result_all.at[pl.ds(pl.multiple_of(device * tok_rows, 16), tok_rows)],
                        save.at[slot],
                    )
                )
                saves[-1].start()
            advance(steps, 2)
        advance(steps, 64)
        for copy in saves:
            copy.wait()
        for copy in gate_copies:
            copy.wait()

    return pl.pallas_call(
        body,
        out_shape=(
            jax.ShapeDtypeStruct((tok_rows, width), f32),
            jax.ShapeDtypeStruct((rows, width), bf16),
            jax.ShapeDtypeStruct(gate_back.shape, f32),
        ),
        in_specs=[ANY] * 4 + [VMEM],
        out_specs=(VMEM, ANY, VMEM),
        scratch_shapes=[
            pltpu.VMEM(first.shape, bf16),
            pltpu.VMEM(second.shape, bf16),
            pltpu.VMEM(up_all.shape, bf16),
            pltpu.VMEM(gated_all.shape, bf16),
            pltpu.VMEM((n, tok_rows, width), bf16),
            pltpu.VMEM((n, tok_rows, width), bf16),
            pltpu.VMEM((2, 2, n // 2, half_rows, width), bf16),
            sems(2, 2, n // 2),
            sems(2, 2, n // 2),
            sems(n),
            sems(n),
            sems(n // 2),
            sems(count),
            sems(2),
            sems(n),
        ],
        name="experts_out",
        cost_estimate=pl.CostEstimate(
            flops=2 * rows * width * 3 * inner // 2 * local_experts,
            bytes_accessed=60_000_000,
            transcendentals=0,
        ),
        compiler_params=pltpu.CompilerParams(
            collective_id=identity, has_side_effects=True, vmem_limit_bytes=BIG_VMEM
        ),
    )(up_all, gated_all, first, second, gate_back)


def exchange_rows(ring, sums, flat, got, send, receive, steps):
    n, rows = ring.n, sums.shape[0]
    for k in range(rows // LANES):
        flat[:, pl.ds(k * LANES, LANES)] = jnp.transpose(sums[pl.ds(k * LANES, LANES)])[:8]
    copies = []
    for k in range(1, n):
        copies.append(
            remote(
                flat,
                got.at[k - 1],
                send.at[k - 1],
                receive.at[k - 1],
                {"ctx": (ring.me + k) % n},
            )
        )
        copies[-1].start()
    advance(steps, 1)
    for copy in copies:
        copy.wait_recv()
    total = flat[...]
    for k in range(n - 1):
        total = total + got[k]
    for k in range(rows // LANES):
        block = total[:, k * LANES : (k + 1) * LANES]
        block = jnp.concatenate([block, jnp.zeros((LANES - 8, LANES), jnp.float32)], axis=0)
        sums[pl.ds(k * LANES, LANES)] = jnp.transpose(block)
    for copy in copies:
        copy.wait_send()


def turn(values, cosine, sine):
    return values * cosine + pltpu.roll(values, HEAD_DIM // 2, 1) * sine


def out_gather_steps(ring, out_ref, out_all, sem):
    own_send, own_receive, ring_send, ring_receive, core_send, core_receive, local = sem
    dp, core, chip, core_chip = partners()
    weight_rows, n, me = out_ref.shape[0], ring.n, ring.me

    def place(group, device):
        return out_all.at[pl.ds(pl.multiple_of((group * n + device) * weight_rows, 16), weight_rows)]

    own = pltpu.make_async_copy(out_ref, place(dp, me), local)
    own.start()
    copies = [
        remote(out_ref, place(dp, me), own_send.at[0], own_receive.at[0], {"dp": chip}),
        remote(out_ref, place(dp, me), own_send.at[1], own_receive.at[1], {"dp": core}),
    ]
    for copy in copies:
        copy.start()

    def ready(half):
        if half == 1:
            spot = place(chip, me)
            remote(spot, spot, own_send.at[0], own_receive.at[0], {"dp": chip}).wait_recv()
            copies.append(remote(spot, spot, own_send.at[2], own_receive.at[2], {"dp": core}))
            copies[-1].start()

    def arrived(way, half, hop, origin):
        spot = place(chip if half else dp, origin)
        copies.append(
            remote(
                spot, spot, core_send.at[way, half, hop], core_receive.at[way, half, hop], {"dp": core}
            )
        )
        copies[-1].start()

    yield from gather_steps(
        ring,
        lambda half: place(chip, me) if half else out_ref,
        lambda device, half: place(chip if half else dp, device),
        ring_send,
        ring_receive,
        arrived,
        ready,
    )
    for at, group in ((1, core), (2, core_chip)):
        spot = place(group, me)
        remote(spot, spot, own_send.at[at], own_receive.at[at], {"dp": core}).wait_recv()
    for way, sign in ((0, 1), (1, -1)):
        for half in (0, 1):
            for hop in range(ring.hops(way, half)):
                spot = place(core_chip if half else core, ring.at(-sign * (hop + 1)))
                remote(
                    spot,
                    spot,
                    core_send.at[way, half, hop],
                    core_receive.at[way, half, hop],
                    {"dp": core},
                ).wait_recv()
    for copy in copies:
        copy.wait_send()
    own.wait()


def attention_in(
    token_all, in_all, out_rows, gain, pair_gains, cosine, sine, bounds, place_row, n, n_dp, identity
):
    rows, width = token_all.shape
    pair = pair_gains.shape[1]
    cols = pair // 2
    heads = cols // HEAD_DIM
    chunk = 256
    weight_rows = out_rows.shape[0]
    bf16, f32 = jnp.bfloat16, jnp.float32
    scale = HEAD_DIM ** (-0.5)

    def body(
        token_ref,
        in_ref,
        out_ref,
        gain_ref,
        pair_ref,
        cos_ref,
        sin_ref,
        bound_ref,
        place_ref,
        attend_all,
        out_all,
        probs_all,
        normed_all,
        attend_ref,
        qkv_ref,
        raw_ref,
        inverse_ref,
        probs_s,
        normed_s,
        flat,
        got,
        *sem,
    ):
        out_sem, sem = sem[:7], sem[7:]
        sum_send, sum_receive, ring_send, ring_receive, save = sem
        ring = Ring(n)
        dp, core, chip, core_chip = partners()
        ring.barrier(
            [{"ctx": (ring.me + k) % n} for k in range(1, n)] + [{"dp": core}, {"dp": chip}]
        )
        steps = out_gather_steps(ring, out_ref, out_all, out_sem)
        advance(steps, 1)
        lanes = lax.broadcasted_iota(jnp.int32, (chunk, LANES), 1)

        def chunks(step, count=2):
            total = rows // chunk
            for first in range(0, total, count):
                lax.fori_loop(first, min(first + count, total), step, 0)
                advance(steps, 2)

        def project(j, carry):
            at = pl.ds(pl.multiple_of(j * chunk, chunk), chunk)
            values = token_ref[at].astype(f32)
            inverse = lax.rsqrt(jnp.mean(values * values, axis=-1, keepdims=True) + EPSILON)
            normed = (values * inverse * gain_ref[0:1, :]).astype(bf16)
            normed_s[at] = normed
            projected = dot(normed, in_ref[:, : pair + cols])
            raw_ref[at] = projected[:, :pair]
            qkv_ref[at, pair:] = projected[:, pair:].astype(bf16)
            squares = projected[:, :pair] * projected[:, :pair]
            inverse_ref[at] = jnp.where(
                lanes == 0,
                jnp.sum(squares[:, :cols], axis=-1, keepdims=True),
                jnp.where(lanes == 1, jnp.sum(squares[:, cols:], axis=-1, keepdims=True), 0.0),
            )
            return carry

        chunks(project)
        saves = [pltpu.make_async_copy(normed_s, normed_all, save.at[heads])]
        saves[0].start()
        exchange_rows(ring, inverse_ref, flat, got, sum_send, sum_receive, steps)

        def norm(j, carry):
            at = pl.ds(pl.multiple_of(j * chunk, chunk), chunk)
            inverse = lax.rsqrt(inverse_ref[at] / width + EPSILON)
            inverse_ref[at] = inverse
            for which in range(2):
                for head in range(heads):
                    columns = pl.ds(which * cols + head * HEAD_DIM, HEAD_DIM)
                    values = raw_ref[at, columns] * inverse[:, which : which + 1]
                    values = values * pair_ref[0:1, columns]
                    qkv_ref[at, columns] = turn(values, cos_ref[at], sin_ref[at]).astype(bf16)
            return carry

        chunks(norm)
        for head in range(heads):

            def attend(j, carry, head=head):
                at = pl.ds(pl.multiple_of(j * chunk, chunk), chunk)
                columns = pl.ds(head * HEAD_DIM, HEAD_DIM)
                scores = (
                    dot_across(
                        qkv_ref[at, columns], qkv_ref[:, pl.ds(cols + head * HEAD_DIM, HEAD_DIM)]
                    )
                    * scale
                )
                place = place_ref[0:1, :]
                visible = (place >= bound_ref[at, 0:1]) & (place <= bound_ref[at, 1:2])
                scores = jnp.where(visible, scores, MASKED)
                powers = jnp.where(
                    visible, jnp.exp(scores - jnp.max(scores, axis=-1, keepdims=True)), 0.0
                )
                share = 1.0 / jnp.sum(powers, axis=-1, keepdims=True)
                probs = (powers * share).astype(bf16)
                probs_s[head, at] = probs
                attend_ref[at, columns] = dot(
                    probs, qkv_ref[:, pl.ds(pair + head * HEAD_DIM, HEAD_DIM)]
                ).astype(bf16)
                return carry

            chunks(attend)
            saves.append(pltpu.make_async_copy(probs_s.at[head], probs_all.at[head], save.at[head]))
            saves[-1].start()

        half_rows = rows // 2
        own = pltpu.make_async_copy(
            attend_ref,
            attend_all.at[:, pl.ds(pl.multiple_of(ring.me * cols, LANES), cols)],
            save.at[heads + 1],
        )
        own.start()
        run_steps(
            steps,
            gather_steps(
                ring,
                lambda half: attend_ref.at[pl.ds(half * half_rows, half_rows)],
                lambda device, half: attend_all.at[
                    pl.ds(half * half_rows, half_rows),
                    pl.ds(pl.multiple_of(device * cols, LANES), cols),
                ],
                ring_send,
                ring_receive,
            ),
        )
        own.wait()
        for copy in saves:
            copy.wait()

    return pl.pallas_call(
        body,
        out_shape=(
            jax.ShapeDtypeStruct((rows, width), bf16),
            jax.ShapeDtypeStruct((weight_rows * n * n_dp, width), bf16),
            jax.ShapeDtypeStruct((heads, rows, rows), bf16),
            jax.ShapeDtypeStruct((rows, width), bf16),
            jax.ShapeDtypeStruct((rows, cols), bf16),
            jax.ShapeDtypeStruct((rows, 3 * cols), bf16),
            jax.ShapeDtypeStruct((rows, pair), f32),
            jax.ShapeDtypeStruct((rows, LANES), f32),
        ),
        in_specs=[VMEM, VMEM, ANY] + [VMEM] * 6,
        out_specs=(ANY,) * 4 + (VMEM,) * 4,
        scratch_shapes=[
            pltpu.VMEM((heads, rows, rows), bf16),
            pltpu.VMEM((rows, width), bf16),
            pltpu.VMEM((8, rows), f32),
            pltpu.VMEM((n - 1, 8, rows), f32),
            sems(3),
            sems(3),
            sems(2, 2, n // 2),
            sems(2, 2, n // 2),
            sems(2, 2, n // 2),
            sems(2, 2, n // 2),
            pltpu.SemaphoreType.DMA,
            sems(n - 1),
            sems(n - 1),
            sems(2, 2, n // 2),
            sems(2, 2, n // 2),
            sems(heads + 2),
        ],
        name="attention_in",
        cost_estimate=pl.CostEstimate(
            flops=2 * rows * width * 3 * cols, bytes_accessed=200_000_000, transcendentals=0
        ),
        compiler_params=pltpu.CompilerParams(
            collective_id=identity, has_side_effects=True, vmem_limit_bytes=BIG_VMEM
        ),
    )(token_all, in_all, out_rows, gain, pair_gains, cosine, sine, bounds, place_row)


def attention_back(
    back_all,
    out_all,
    in_all,
    probs,
    attend_low,
    qkv,
    raw,
    inverse,
    pair_gains,
    cosine,
    sine,
    partial,
    n,
    n_dp,
    identity,
):
    rows, width = back_all.shape
    weight_rows = width // (n * n_dp)
    pair = pair_gains.shape[1]
    cols = pair // 2
    heads = cols // HEAD_DIM
    chunk, wide = 256, 512
    tok_rows = rows // n
    half_rows = tok_rows // 2
    bf16, f32 = jnp.bfloat16, jnp.float32
    scale = HEAD_DIM ** (-0.5)

    def body(
        back_ref,
        out_ref,
        in_ref,
        probs_ref,
        attend_ref,
        qkv_ref,
        raw_ref,
        inverse_ref,
        pair_ref,
        cos_ref,
        sin_ref,
        part_ref,
        raw_back,
        row_part,
        pair_sum,
        part_sum,
        out_sum,
        out_s,
        in_s,
        probs_s,
        part_s,
        attend_back,
        pair_s,
        value_s,
        sum_s,
        slots,
        flat,
        got,
        sum_send,
        sum_receive,
        ring_send,
        ring_receive,
        load,
        out_p,
        out_core,
        out_chip,
        pass_send,
        pass_receive,
    ):
        ring = Ring(n)
        dp, core, chip, core_chip = partners()
        loads = [
            pltpu.make_async_copy(part_ref, part_s, load.at[0]),
            pltpu.make_async_copy(
                out_ref.at[pl.ds(pl.multiple_of(ring.me * cols, 16), cols)], out_s, load.at[1]
            ),
            pltpu.make_async_copy(probs_ref, probs_s, load.at[2]),
            pltpu.make_async_copy(in_ref.at[:, pl.ds(0, pair + cols)], in_s, load.at[3]),
        ]
        for copy in loads:
            copy.start()
        ring.barrier(
            [{"ctx": (ring.me + k) % n} for k in range(1, n)] + [{"dp": core}, {"dp": chip}]
        )

        def store(half, total):
            part_sum[pl.ds(half * half_rows, half_rows)] = total

        steps = scatter_steps(
            ring,
            lambda device, half: part_s.at[
                pl.ds(pl.multiple_of(device * tok_rows + half * half_rows, 16), half_rows)
            ],
            slots,
            store,
            ring_send,
            ring_receive,
        )
        loads[0].wait()
        advance(steps, 1)
        lanes = lax.broadcasted_iota(jnp.int32, (chunk, LANES), 1)

        def chunks(step, count=2):
            total = rows // chunk
            for first in range(0, total, count):
                lax.fori_loop(first, min(first + count, total), step, 0)
                advance(steps, 2)

        loads[1].wait()

        def project(j, carry):
            at = pl.ds(pl.multiple_of(j * chunk, chunk), chunk)
            attend_back[at] = dot_across(back_ref[at], out_s[...]).astype(bf16)
            return carry

        chunks(project, 4)

        def out_product(group):
            for t in range(width // wide):
                value = lax.dot_general(
                    attend_ref[:, group * LANES : (group + 1) * LANES],
                    back_ref[:, t * wide : (t + 1) * wide],
                    (((0,), (0,)), ((), ())),
                    preferred_element_type=f32,
                ).astype(bf16)
                for k in range(LANES // weight_rows):
                    out_p[group * LANES // weight_rows + k, :, t * wide : (t + 1) * wide] = value[
                        k * weight_rows : (k + 1) * weight_rows
                    ]

        for group in range(cols // LANES):
            out_product(group)

        def passing(at, source, target, to):
            return remote(source, target, pass_send.at[at], pass_receive.at[at], {"dp": to})

        passed = [
            passing(0, out_p.at[core_chip], out_core.at[1], core),
            passing(1, out_p.at[core], out_core.at[0], core),
        ]
        for copy in passed:
            copy.start()
        loads[2].wait()
        for head in range(heads):
            columns = pl.ds(head * HEAD_DIM, HEAD_DIM)
            key_columns = pl.ds(cols + head * HEAD_DIM, HEAD_DIM)
            value_columns = pl.ds(pair + head * HEAD_DIM, HEAD_DIM)
            pair_s[:, key_columns] = jnp.zeros((rows, HEAD_DIM), f32)
            value_s[:, columns] = jnp.zeros((rows, HEAD_DIM), f32)

            def scores(j, carry, head=head, columns=columns, key_columns=key_columns, value_columns=value_columns):
                at = pl.ds(pl.multiple_of(j * chunk, chunk), chunk)
                back = attend_back[at, columns]
                delta = jnp.sum(
                    back.astype(f32) * attend_ref[at, columns].astype(f32), axis=-1, keepdims=True
                )
                probs_low = probs_s[head, at]
                score_back = (
                    probs_low.astype(f32) * (dot_across(back, qkv_ref[:, value_columns]) - delta)
                ).astype(bf16)
                pair_s[at, columns] = dot(score_back, qkv_ref[:, key_columns])
                over = (((0,), (0,)), ((), ()))
                pair_s[:, key_columns] += lax.dot_general(
                    score_back, qkv_ref[at, columns], over, preferred_element_type=f32
                )
                value_s[:, columns] += lax.dot_general(
                    probs_low, back, over, preferred_element_type=f32
                )
                return carry

            chunks(scores)
        passed[0].wait_recv()
        out_core[1] = (out_core[1].astype(f32) + out_p[chip].astype(f32)).astype(bf16)
        passed.append(passing(2, out_core.at[1], out_chip, chip))
        passed[-1].start()
        pair_sum[...] = jnp.zeros((8, pair), f32)

        def unturn(j, carry):
            at = pl.ds(pl.multiple_of(j * chunk, chunk), chunk)
            held = jnp.zeros((chunk, LANES), f32)
            for which in range(2):
                total = jnp.zeros((chunk, 1), f32)
                for head in range(heads):
                    columns = pl.ds(which * cols + head * HEAD_DIM, HEAD_DIM)
                    back = turn(pair_s[at, columns] * scale, cos_ref[at], -sin_ref[at])
                    normed = raw_ref[at, columns] * inverse_ref[at, which : which + 1]
                    pair_sum[0:1, columns] += jnp.sum(back * normed, axis=0, keepdims=True)
                    back = back * pair_ref[0:1, columns]
                    pair_s[at, columns] = back
                    total = total + jnp.sum(back * normed, axis=-1, keepdims=True)
                held = jnp.where(lanes == which, total, held)
            sum_s[at] = held
            return carry

        chunks(unturn)
        exchange_rows(ring, sum_s, flat, got, sum_send, sum_receive, steps)
        loads[3].wait()

        def finish(j, carry):
            at = pl.ds(pl.multiple_of(j * chunk, chunk), chunk)
            for which in range(2):
                columns = pl.ds(which * cols, cols)
                factor = inverse_ref[at, which : which + 1]
                normed = raw_ref[at, columns] * factor
                mean = sum_s[at, which : which + 1] / width
                raw_back[at, columns] = (factor * (pair_s[at, columns] - normed * mean)).astype(bf16)
            raw_back[at, pl.ds(pair, cols)] = value_s[at].astype(bf16)
            for t in range(width // wide):
                row_part[at, pl.ds(t * wide, wide)] = dot_across(
                    raw_back[at], in_s[pl.ds(t * wide, wide), :]
                ).astype(bf16)
            return carry

        chunks(finish)
        passed[1].wait_recv()
        passed[2].wait_recv()
        out_sum[...] = (
            out_core[0].astype(f32) + out_p[dp].astype(f32) + out_chip[...].astype(f32)
        ).astype(bf16)
        advance(steps, 64)
        for copy in passed:
            copy.wait_send()

    return pl.pallas_call(
        body,
        out_shape=(
            jax.ShapeDtypeStruct((rows, 3 * cols), bf16),
            jax.ShapeDtypeStruct((rows, width), bf16),
            jax.ShapeDtypeStruct((8, pair), f32),
            jax.ShapeDtypeStruct((tok_rows, width), f32),
            jax.ShapeDtypeStruct((weight_rows, width), bf16),
        ),
        in_specs=[VMEM] + [ANY] * 3 + [VMEM] * 7 + [ANY],
        out_specs=(VMEM,) * 5,
        scratch_shapes=[
            pltpu.VMEM((cols, width), bf16),
            pltpu.VMEM((width, pair + cols), bf16),
            pltpu.VMEM((heads, rows, rows), bf16),
            pltpu.VMEM((rows, width), bf16),
            pltpu.VMEM((rows, cols), bf16),
            pltpu.VMEM((rows, pair), f32),
            pltpu.VMEM((rows, cols), f32),
            pltpu.VMEM((rows, LANES), f32),
            pltpu.VMEM((2, 2, n // 2, half_rows, width), bf16),
            pltpu.VMEM((8, rows), f32),
            pltpu.VMEM((n - 1, 8, rows), f32),
            sems(n - 1),
            sems(n - 1),
            sems(2, 2, n // 2),
            sems(2, 2, n // 2),
            sems(4),
            pltpu.VMEM((n_dp, weight_rows, width), bf16),
            pltpu.VMEM((2, weight_rows, width), bf16),
            pltpu.VMEM((weight_rows, width), bf16),
            sems(3),
            sems(3),
        ],
        name="attention_back",
        cost_estimate=pl.CostEstimate(
            flops=2 * rows * width * 4 * cols, bytes_accessed=160_000_000, transcendentals=0
        ),
        compiler_params=pltpu.CompilerParams(
            collective_id=identity, has_side_effects=True, vmem_limit_bytes=BIG_VMEM
        ),
    )(
        back_all,
        out_all,
        in_all,
        probs,
        attend_low,
        qkv,
        raw,
        inverse,
        pair_gains,
        cosine,
        sine,
        partial,
    )


def heads_local(
    tokens,
    document_ids,
    routes,
    norm_gains,
    project_in,
    project_out,
    router_weight,
    expert_in,
    expert_out,
    cotangent,
):
    bf16, f32 = jnp.bfloat16, jnp.float32
    n = lax.axis_size("ctx")
    n_dp = lax.axis_size("dp")
    me = lax.axis_index("ctx")
    tok_rows, width = tokens.shape[1:]
    rows = tok_rows * n
    weight_rows = project_in.shape[0]
    own_heads = HEADS // n
    cols = own_heads * HEAD_DIM
    local_experts = expert_in.shape[0]
    expert_count = local_experts * n
    score_scale = HEAD_DIM ** (-0.5)

    def own(array, size, axis=0):
        return lax.dynamic_slice_in_dim(array, me * size, size, axis)

    named = jnp.any(routes[0][..., None] == jnp.arange(LANES, dtype=jnp.int32), axis=1).astype(bf16)
    small = jnp.concatenate(
        [norm_gains, router_weight, jnp.zeros((weight_rows, LANES - 4 - expert_count), bf16)], axis=1
    )
    in_blocks = project_in.reshape(weight_rows, 3, n, cols).transpose(2, 0, 1, 3)
    in_blocks = jnp.concatenate(
        [
            in_blocks.reshape(n, weight_rows, 3 * cols),
            jnp.broadcast_to(small[None], (n, weight_rows, LANES)),
        ],
        axis=2,
    )
    token_all, named_all, in_all = gather_inputs(tokens[0], named, in_blocks, n, n_dp, 1)
    named_all = named_all.reshape(rows, LANES)
    in_all = in_all.reshape(width, 3 * cols + LANES)
    small_all = in_all[:, 3 * cols :]
    gains = small_all[:, :4].astype(f32)
    router_all = small_all[:, 4 : 4 + expert_count]
    router_wide = jnp.pad(router_all, ((0, 0), (0, LANES - expert_count)))
    first = lax.all_gather(expert_in, "dp", axis=1, tiled=True)
    second = lax.all_gather(expert_out, "dp", axis=1, tiled=True).reshape(local_experts * FF, width)

    half_rows = tok_rows // 2

    def dealt(row):
        blocks = row.reshape(2 * n, half_rows)
        return jnp.stack([blocks[:n], blocks[n:][::-1]], axis=1).reshape(rows)

    places = dealt(jnp.arange(rows, dtype=jnp.int32))
    document_row = document_ids[0]
    starts = dealt(document_starts(document_row))
    relative = places - starts
    cosine, sine = rotary_tables(relative, HEAD_DIM)
    cosine = jnp.concatenate([cosine[:, 0], cosine[:, 0]], axis=-1)
    sine = jnp.concatenate([-sine[:, 0], sine[:, 0]], axis=-1)
    bounds = jnp.pad(jnp.stack([starts, places], axis=1), ((0, 0), (0, LANES - 2)))
    place_row = jnp.broadcast_to(places[None], (8, rows))
    pair_gains = jnp.broadcast_to(own(gains, cols)[:, 1:3].T.reshape(1, 2 * cols), (8, 2 * cols))

    attend_gain = jnp.broadcast_to(gains[:, 0][None], (8, width))
    attend_all, out_all, probs, attend_in, attend_low, qkv, raw, inverse = attention_in(
        token_all,
        in_all,
        project_out,
        attend_gain,
        pair_gains,
        cosine,
        sine,
        bounds,
        place_row,
        n,
        n_dp,
        10,
    )

    upstream_all, mixed_all, gated_all, up_all, own_gates, gate_back, own_residual = experts_in(
        attend_all,
        token_all,
        cotangent[0],
        out_all,
        first,
        second,
        jnp.broadcast_to(gains[:, 3][None], (8, width)),
        router_wide,
        named_all,
        n,
        8,
    )
    mixed_slots = mixed_all.reshape(rows, width)
    second_back = jnp.einsum(
        "tf,td->fd", gated_all, upstream_all.reshape(rows, width), preferred_element_type=f32
    ).astype(bf16)
    first_backs, last = [], second_back
    for x in range(local_experts):
        mixed_slots, last = lax.optimization_barrier((mixed_slots, last))
        if x == 0:
            second_back = last
        else:
            first_backs.append(last)
        last = jnp.einsum(
            "td,tf->df", mixed_slots, up_all[x], preferred_element_type=f32
        ).astype(bf16)
    up_all, last = lax.optimization_barrier((up_all, last))
    first_backs.append(last)
    expert_out_gradient = lax.psum_scatter(
        second_back.reshape(local_experts, FF, width), "dp", scatter_dimension=1, tiled=True
    ).astype(f32)
    expert_in_gradient = jnp.stack(
        [lax.psum_scatter(one, "dp", scatter_dimension=0, tiled=True) for one in first_backs]
    ).astype(f32)
    mixed_back, mixture, gate_back = experts_out(up_all, gated_all, first, second, gate_back, n, 9)
    gate_back = gate_back[:, :local_experts]
    place = ring_place(me, n)
    gate_back = sum(
        jnp.where(
            (jnp.arange(n) == ring_device((place + offset + n) % n, n))[:, None, None],
            gate_back[slot],
            0.0,
        )
        for slot, offset in enumerate(slot_offsets(n))
    )
    gate_back = gate_back.reshape(expert_count, tok_rows).T

    own_gates = own_gates[:, :expert_count]
    own_mixed = mixed_all[0]
    own_mixed_inverse = inverse_rms(own_residual)
    own_mixed_normed = own_residual * own_mixed_inverse
    chosen_back = own_gates * (
        gate_back - jnp.sum(own_gates * gate_back, axis=-1, keepdims=True)
    )
    logit_back = chosen_back.astype(bf16)
    router_part = jnp.einsum("td,te->ed", own_mixed, logit_back, preferred_element_type=f32)
    mixed_back = mixed_back + jnp.einsum(
        "te,de->td", logit_back, router_all, preferred_element_type=f32
    )
    mixed_gain_back = jnp.sum(mixed_back * own_mixed_normed, axis=0)
    residual_back = cotangent[0].astype(f32) + normalize_back(
        mixed_back * gains[:, 3], own_mixed_normed, own_mixed_inverse
    )
    back_all = ring_gather(residual_back.astype(bf16), n, 5, "gather_back")

    raw_back, row_part, pair_sum, mixture, out_part = attention_back(
        back_all,
        out_all,
        in_all,
        probs,
        attend_low,
        qkv,
        raw,
        inverse,
        pair_gains,
        cosine,
        sine,
        mixture,
        n,
        n_dp,
        11,
    )
    layer_output = (own_residual + mixture).astype(bf16)
    pairs = [(d * n + c, c * n_dp + d) for d in range(n_dp) for c in range(n)]
    project_out_gradient = lax.ppermute(out_part, ("dp", "ctx"), pairs).astype(f32)

    small_rows = -(-(4 + expert_count) // 8) * 8
    small_part = jnp.concatenate(
        [
            jnp.zeros((3, width), f32),
            mixed_gain_back[None],
            router_part,
            jnp.zeros((small_rows - 4 - expert_count, width), f32),
        ],
        axis=0,
    )
    tokens_back, project_in_gradient, small_gradient = scatter_end(
        row_part,
        attend_in,
        raw_back,
        tokens[0],
        residual_back,
        attend_gain,
        small_part,
        pair_sum,
        n,
        n_dp,
        6,
    )
    per_tile = LANES // weight_rows
    small_gradient = lax.dynamic_slice_in_dim(
        small_gradient, me % per_tile * weight_rows, weight_rows, 1
    ).T
    return (
        layer_output[None],
        tokens_back[None],
        small_gradient[:, :4],
        project_in_gradient,
        project_out_gradient,
        small_gradient[:, 4 : 4 + expert_count],
        expert_in_gradient,
        expert_out_gradient,
    )


def solution(mesh):
    n = mesh.shape["ctx"]
    split_heads = HEADS % n == 0 and n % 4 == 0 and mesh.shape["dp"] == 4
    placed = (
        P("dp", "ctx", None),
        P("dp", None),
        P("dp", "ctx", None),
        P(("dp", "ctx"), None),
        P(("dp", "ctx"), None),
        P(("dp", "ctx"), None),
        P(("dp", "ctx"), None),
        P("ctx", "dp", None),
        P("ctx", "dp", None),
        P("dp", "ctx", None),
    )
    return jax.shard_map(
        heads_local if split_heads else gathered_local,
        mesh=mesh,
        in_specs=placed,
        out_specs=(
            P("dp", "ctx", None),
            P("dp", "ctx", None),
            P(("dp", "ctx"), None),
            P(("dp", "ctx"), None),
            P(("dp", "ctx"), None),
            P(("dp", "ctx"), None),
            P("ctx", "dp", None),
            P("ctx", "dp", None),
        ),
        check_vma=False,
    )
```

```python
import jax
import jax.numpy as jnp
from jax import lax
from jax.experimental import pallas as pl
from jax.experimental.pallas import tpu as pltpu
from jax.sharding import PartitionSpec as P

HEADS = 16
HEAD_DIM = 128
FF = 1024


EPSILON = 1e-05
ROPE_BASE = 10000.0
MASKED = -1e30
LANES = 128
PASS_A, PASS_B = 256, 256
CUTS = 2
WAITS = (4, 6, 6)
TILE = 512
WIDE = 1024


def inverse_rms(values):
    return lax.rsqrt(jnp.mean(values * values, axis=-1, keepdims=True) + EPSILON)


def normalize_back(normed_back, normed, inverse):
    return inverse * (normed_back - normed * jnp.mean(normed_back * normed, axis=-1, keepdims=True))


def rotary_tables(relative, head_dim):
    half_dim = head_dim // 2
    frequency = ROPE_BASE ** (-jnp.arange(half_dim, dtype=jnp.float32) / half_dim)
    angles = relative.astype(jnp.float32)[..., None] * frequency
    return (jnp.cos(angles)[..., None, :], jnp.sin(angles)[..., None, :])


def rotate(values, cosine, sine_table):
    half_dim = values.shape[-1] // 2
    first_half = values[..., :half_dim]
    second_half = values[..., half_dim:]
    return jnp.concatenate(
        [
            first_half * cosine - second_half * sine_table,
            second_half * cosine + first_half * sine_table,
        ],
        axis=-1,
    )


def dealt_positions(indices, tok_rows, context_size):
    half_block = tok_rows // 2
    device = indices // tok_rows
    within = indices % tok_rows
    block_index = jnp.where(within < half_block, device, 2 * context_size - 1 - device)
    return block_index * half_block + within % half_block


def document_starts(document_row):
    places = jnp.arange(document_row.shape[-1], dtype=jnp.int32)
    head_flag = jnp.ones(document_row.shape[:-1] + (1,), jnp.bool_)
    fresh_start = jnp.concatenate(
        [head_flag, document_row[..., 1:] != document_row[..., :-1]], axis=-1
    )
    return lax.cummax(jnp.where(fresh_start, places, 0), axis=document_row.ndim - 1)


def block_scores(
    query_rows, key_block, query_place, query_document, key_place, key_document, score_scale
):
    scores = (
        jnp.einsum("thd,khd->htk", query_rows, key_block, preferred_element_type=jnp.float32)
        * score_scale
    )
    visible = (
        (key_document[None, :] == query_document[:, None])
        & (key_place[None, :] <= query_place[:, None])
    )[None]
    return (jnp.where(visible, scores, MASKED), visible)


def block_backward(
    query_rows,
    output_back,
    row_logsum,
    row_delta,
    key_block,
    value_block,
    query_place,
    query_document,
    key_place,
    key_document,
    score_scale,
):
    scores, visible = block_scores(
        query_rows, key_block, query_place, query_document, key_place, key_document, score_scale
    )
    prob_rows = jnp.where(visible, jnp.exp(scores - row_logsum[..., None]), 0.0)
    prob_back = jnp.einsum(
        "thd,khd->htk", output_back, value_block, preferred_element_type=jnp.float32
    )
    score_back = (prob_rows * (prob_back - row_delta[..., None])).astype(jnp.bfloat16)
    query_part = (
        jnp.einsum("htk,khd->thd", score_back, key_block, preferred_element_type=jnp.float32)
        * score_scale
    )
    key_part = (
        jnp.einsum("htk,thd->khd", score_back, query_rows, preferred_element_type=jnp.float32)
        * score_scale
    )
    value_part = jnp.einsum(
        "htk,thd->khd",
        prob_rows.astype(jnp.bfloat16),
        output_back,
        preferred_element_type=jnp.float32,
    )
    return (query_part, key_part, value_part)


def dispatch_plan(route_rows, expert_count, capacity):
    flat_routes = route_rows.reshape(-1)
    pair_count = flat_routes.shape[0]
    member = (flat_routes[:, None] == jnp.arange(expert_count, dtype=jnp.int32)[None, :]).astype(
        jnp.int32
    )
    earlier = jnp.cumsum(member, axis=0) - member
    target_slot = flat_routes * capacity + jnp.sum(earlier * member, axis=1)
    slot_owner = (
        jnp.full((expert_count * capacity,), pair_count, jnp.int32)
        .at[target_slot]
        .set(jnp.arange(pair_count, dtype=jnp.int32))
    )
    return (target_slot, slot_owner)


def gathered_local(
    tokens,
    document_ids,
    routes,
    norm_gains,
    project_in,
    project_out,
    router_weight,
    expert_in,
    expert_out,
    cotangent,
):
    inputs = tokens[0].astype(jnp.float32)
    tok_rows, model_width = inputs.shape
    context_size = lax.axis_size("ctx")
    sequence_rows = tok_rows * context_size
    local_experts = expert_in.shape[0]
    expert_count = local_experts * context_size
    route_rows = routes[0]
    top_count = route_rows.shape[1]
    capacity = 2 * tok_rows * top_count // expert_count
    score_scale = HEAD_DIM ** (-0.5)
    key_span = min(512, sequence_rows)
    key_blocks = sequence_rows // key_span
    heads_shape = (tok_rows, HEADS, HEAD_DIM)
    block_shape = (key_blocks, key_span, HEADS, HEAD_DIM)
    slot_shape = (context_size, local_experts * capacity, model_width)
    expert_shape = (context_size, local_experts, capacity, model_width)
    gathered_gains, gathered_in, gathered_out, gathered_router = (
        lax.all_gather(norm_gains, ("dp", "ctx"), axis=0, tiled=True),
        lax.all_gather(project_in, ("dp", "ctx"), axis=0, tiled=True),
        lax.all_gather(project_out, ("dp", "ctx"), axis=0, tiled=True),
        lax.all_gather(router_weight, ("dp", "ctx"), axis=0, tiled=True),
    )
    gathered_first, gathered_second = (
        lax.all_gather(expert_in, "dp", axis=1, tiled=True),
        lax.all_gather(expert_out, "dp", axis=1, tiled=True),
    )
    gain_rows = gathered_gains.astype(jnp.float32)
    own_rows = lax.axis_index("ctx") * tok_rows + jnp.arange(tok_rows, dtype=jnp.int32)
    own_place = dealt_positions(own_rows, tok_rows, context_size)
    all_place = dealt_positions(jnp.arange(sequence_rows, dtype=jnp.int32), tok_rows, context_size)
    document_row = document_ids[0]
    own_document = jnp.take(document_row, own_place)
    all_document = jnp.take(document_row, all_place)
    relative = own_place - jnp.take(document_starts(document_row), own_place)
    cosine, sine_table = rotary_tables(relative, HEAD_DIM)
    attend_inverse = inverse_rms(inputs)
    attend_normed = inputs * attend_inverse
    attend_in = (attend_normed * gain_rows[:, 0]).astype(jnp.bfloat16)
    projected = jnp.dot(attend_in, gathered_in, preferred_element_type=jnp.float32)
    raw_query = projected[:, :model_width]
    raw_key = projected[:, model_width : 2 * model_width]
    query_inverse = inverse_rms(raw_query)
    query_normed = raw_query * query_inverse
    key_inverse = inverse_rms(raw_key)
    key_normed = raw_key * key_inverse
    query_low = rotate(
        (query_normed * gain_rows[:, 1]).reshape(heads_shape), cosine, sine_table
    ).astype(jnp.bfloat16)
    key_low = rotate(
        (key_normed * gain_rows[:, 2]).reshape(heads_shape), cosine, sine_table
    ).astype(jnp.bfloat16)
    value_low = projected[:, 2 * model_width :].astype(jnp.bfloat16)
    key_all, value_all = (
        lax.all_gather(key_low.reshape(tok_rows, model_width), "ctx", axis=0, tiled=True),
        lax.all_gather(value_low, "ctx", axis=0, tiled=True),
    )
    key_split = key_all.reshape(block_shape)
    value_split = value_all.reshape(block_shape)
    place_split = all_place.reshape(key_blocks, key_span)
    document_split = all_document.reshape(key_blocks, key_span)

    def total_step(state_pair, block_args):
        row_peak, row_total = state_pair
        key_block, key_place, key_document = block_args
        scores, visible = block_scores(
            query_low, key_block, own_place, own_document, key_place, key_document, score_scale
        )
        new_peak = jnp.maximum(row_peak, jnp.max(scores, axis=-1))
        fresh_total = jnp.sum(
            jnp.where(visible, jnp.exp(scores - new_peak[..., None]), 0.0), axis=-1
        )
        return ((new_peak, row_total * jnp.exp(row_peak - new_peak) + fresh_total), None)

    start_pair = (
        jnp.full((HEADS, tok_rows), MASKED, jnp.float32),
        jnp.zeros((HEADS, tok_rows), jnp.float32),
    )
    (row_peak, row_total), unused = lax.scan(
        total_step, start_pair, (key_split, place_split, document_split)
    )
    row_logsum = row_peak + jnp.log(row_total)

    def value_step(running, block_args):
        key_block, value_block, key_place, key_document = block_args
        scores, visible = block_scores(
            query_low, key_block, own_place, own_document, key_place, key_document, score_scale
        )
        prob_low = jnp.where(visible, jnp.exp(scores - row_logsum[..., None]), 0.0).astype(
            jnp.bfloat16
        )
        return (
            running
            + jnp.einsum("htk,khd->thd", prob_low, value_block, preferred_element_type=jnp.float32),
            None,
        )

    attend_out, unused = lax.scan(
        value_step,
        jnp.zeros(heads_shape, jnp.float32),
        (key_split, value_split, place_split, document_split),
    )
    attend_low = attend_out.reshape(tok_rows, model_width).astype(jnp.bfloat16)
    residual = inputs + jnp.dot(attend_low, gathered_out, preferred_element_type=jnp.float32)
    mixed_inverse = inverse_rms(residual)
    mixed_normed = residual * mixed_inverse
    mixed_low = (mixed_normed * gain_rows[:, 3]).astype(jnp.bfloat16)
    logits = jnp.dot(mixed_low, gathered_router, preferred_element_type=jnp.float32)
    route_onehot = (route_rows[..., None] == jnp.arange(expert_count, dtype=jnp.int32)).astype(
        jnp.float32
    )
    gate_weights = jax.nn.softmax(jnp.sum(route_onehot * logits[:, None, :], axis=-1), axis=-1)
    target_slot, slot_owner = dispatch_plan(route_rows, expert_count, capacity)
    padded_rows = jnp.concatenate([mixed_low, jnp.zeros((1, model_width), jnp.bfloat16)], axis=0)
    send_rows = jnp.take(padded_rows, slot_owner // top_count, axis=0).reshape(slot_shape)
    received = lax.all_to_all(send_rows, "ctx", split_axis=0, concat_axis=0, tiled=True).reshape(
        expert_shape
    )
    expert_up = jnp.einsum(
        "sxcd,xdf->sxcf", received, gathered_first, preferred_element_type=jnp.float32
    )
    gate_part = expert_up[..., :FF]
    up_part = expert_up[..., FF:]
    sigmoid_gate = jax.nn.sigmoid(gate_part)
    swish_gate = gate_part * sigmoid_gate
    hidden_low = (swish_gate * up_part).astype(jnp.bfloat16)
    expert_result = jnp.einsum(
        "sxcf,xfd->sxcd", hidden_low, gathered_second, preferred_element_type=jnp.float32
    ).astype(jnp.bfloat16)
    returned = lax.all_to_all(
        expert_result.reshape(slot_shape), "ctx", split_axis=0, concat_axis=0, tiled=True
    ).reshape(expert_count * capacity, model_width)
    pair_result = jnp.take(returned, target_slot, axis=0).reshape(tok_rows, top_count, model_width)
    mixture = jnp.sum(gate_weights[..., None] * pair_result, axis=1)
    layer_output = (residual + mixture).astype(jnp.bfloat16)
    upstream = cotangent[0].astype(jnp.float32)
    pair_back = (gate_weights[..., None] * upstream[:, None, :]).astype(jnp.bfloat16)
    gate_back = jnp.sum(pair_result * upstream[:, None, :], axis=-1)
    padded_back = jnp.concatenate(
        [
            pair_back.reshape(tok_rows * top_count, model_width),
            jnp.zeros((1, model_width), jnp.bfloat16),
        ],
        axis=0,
    )
    send_back = jnp.take(padded_back, slot_owner, axis=0).reshape(slot_shape)
    received_back = lax.all_to_all(
        send_back, "ctx", split_axis=0, concat_axis=0, tiled=True
    ).reshape(expert_shape)
    first_back, second_back = (gathered_first, gathered_second)
    hidden_back = jnp.einsum(
        "sxcd,xfd->sxcf", received_back, second_back, preferred_element_type=jnp.float32
    )
    second_weight_back = jnp.einsum(
        "sxcf,sxcd->xfd", hidden_low, received_back, preferred_element_type=jnp.float32
    )
    swish_slope = sigmoid_gate * (1.0 + gate_part * (1.0 - sigmoid_gate))
    up_back = jnp.concatenate(
        [hidden_back * up_part * swish_slope, hidden_back * swish_gate], axis=-1
    ).astype(jnp.bfloat16)
    first_weight_back = jnp.einsum(
        "sxcd,sxcf->xdf", received, up_back, preferred_element_type=jnp.float32
    )
    input_back = jnp.einsum(
        "sxcf,xdf->sxcd", up_back, first_back, preferred_element_type=jnp.float32
    ).astype(jnp.bfloat16)
    expert_in_gradient, expert_out_gradient = (
        lax.psum_scatter(
            first_weight_back.astype(jnp.bfloat16), "dp", scatter_dimension=1, tiled=True
        ).astype(jnp.float32),
        lax.psum_scatter(
            second_weight_back.astype(jnp.bfloat16), "dp", scatter_dimension=1, tiled=True
        ).astype(jnp.float32),
    )
    rows_back = lax.all_to_all(
        input_back.reshape(slot_shape), "ctx", split_axis=0, concat_axis=0, tiled=True
    ).reshape(expert_count * capacity, model_width)
    mixed_back = jnp.sum(
        jnp.take(rows_back, target_slot, axis=0)
        .reshape(tok_rows, top_count, model_width)
        .astype(jnp.float32),
        axis=1,
    )
    gains_back, in_back, out_back, router_back = (
        gathered_gains,
        gathered_in,
        gathered_out,
        gathered_router,
    )
    gain_values = gains_back.astype(jnp.float32)
    chosen_back = gate_weights * (
        gate_back - jnp.sum(gate_weights * gate_back, axis=-1, keepdims=True)
    )
    logit_back = jnp.sum(chosen_back[..., None] * route_onehot, axis=1).astype(jnp.bfloat16)
    router_weight_back = jnp.einsum(
        "td,te->de", mixed_low, logit_back, preferred_element_type=jnp.float32
    )
    mixed_back = mixed_back + jnp.einsum(
        "te,de->td", logit_back, router_back, preferred_element_type=jnp.float32
    )
    mixed_gain_back = jnp.sum(mixed_back * mixed_normed, axis=0)
    residual_back = upstream + normalize_back(
        mixed_back * gain_values[:, 3], mixed_normed, mixed_inverse
    )
    residual_low = residual_back.astype(jnp.bfloat16)
    out_weight_back = jnp.einsum(
        "td,te->de", attend_low, residual_low, preferred_element_type=jnp.float32
    )
    attend_back = (
        jnp.einsum("te,de->td", residual_low, out_back, preferred_element_type=jnp.float32)
        .astype(jnp.bfloat16)
        .reshape(heads_shape)
    )
    row_delta = jnp.einsum("thd,thd->ht", attend_back.astype(jnp.float32), attend_out)

    def back_step(query_acc, block_args):
        key_block, value_block, key_place, key_document = block_args
        query_part, key_part, value_part = block_backward(
            query_low,
            attend_back,
            row_logsum,
            row_delta,
            key_block,
            value_block,
            own_place,
            own_document,
            key_place,
            key_document,
            score_scale,
        )
        return (query_acc + query_part, (key_part, value_part))

    query_back, (key_parts, value_parts) = lax.scan(
        back_step,
        jnp.zeros(heads_shape, jnp.float32),
        (key_split, value_split, place_split, document_split),
    )
    key_back, value_back = (
        lax.psum_scatter(
            key_parts.reshape(sequence_rows, model_width).astype(jnp.bfloat16),
            "ctx",
            scatter_dimension=0,
            tiled=True,
        ).astype(jnp.float32),
        lax.psum_scatter(
            value_parts.reshape(sequence_rows, model_width).astype(jnp.bfloat16),
            "ctx",
            scatter_dimension=0,
            tiled=True,
        ).astype(jnp.float32),
    )
    query_flat = rotate(query_back, cosine, -sine_table).reshape(tok_rows, model_width)
    key_flat = rotate(key_back.reshape(heads_shape), cosine, -sine_table).reshape(
        tok_rows, model_width
    )
    query_gain_back = jnp.sum(query_flat * query_normed, axis=0)
    key_gain_back = jnp.sum(key_flat * key_normed, axis=0)
    raw_query_back = normalize_back(query_flat * gain_values[:, 1], query_normed, query_inverse)
    raw_key_back = normalize_back(key_flat * gain_values[:, 2], key_normed, key_inverse)
    raw_back = jnp.concatenate([raw_query_back, raw_key_back, value_back], axis=-1).astype(
        jnp.bfloat16
    )
    in_weight_back = jnp.einsum(
        "td,tf->df", attend_in, raw_back, preferred_element_type=jnp.float32
    )
    attend_in_back = jnp.einsum("tf,df->td", raw_back, in_back, preferred_element_type=jnp.float32)
    attend_gain_back = jnp.sum(attend_in_back * attend_normed, axis=0)
    tokens_back = residual_back + normalize_back(
        attend_in_back * gain_values[:, 0], attend_normed, attend_inverse
    )
    gain_columns = jnp.stack(
        [attend_gain_back, query_gain_back, key_gain_back, mixed_gain_back], axis=1
    )
    gains_gradient, project_in_gradient, project_out_gradient, router_gradient = (
        lax.psum_scatter(gain_columns, ("dp", "ctx"), scatter_dimension=0, tiled=True),
        lax.psum_scatter(in_weight_back, ("dp", "ctx"), scatter_dimension=0, tiled=True),
        lax.psum_scatter(out_weight_back, ("dp", "ctx"), scatter_dimension=0, tiled=True),
        lax.psum_scatter(router_weight_back, ("dp", "ctx"), scatter_dimension=0, tiled=True),
    )
    return (
        layer_output[None],
        tokens_back.astype(jnp.bfloat16)[None],
        gains_gradient,
        project_in_gradient,
        project_out_gradient,
        router_gradient,
        expert_in_gradient,
        expert_out_gradient,
    )


MESH = pl.DeviceIdType.MESH
VMEM_LIMIT = 48 * 1024 * 1024


def ring_place(device, n):
    odd = device % 2
    return (1 - odd) * (device // 2) + odd * (n - 1 - device // 2)


def ring_device(place, n):
    far = place // (n // 2)
    return (1 - far) * (2 * place) + far * (2 * (n - 1 - place) + 1)


class Ring:
    def __init__(self, n):
        self.n = n
        self.me = lax.axis_index("ctx")
        self.place = ring_place(self.me, n)

    def at(self, offset):
        return ring_device((self.place + offset + self.n) % self.n, self.n)

    def hops(self, way, half):
        return self.n // 2 if way == half else self.n // 2 - 1

    def barrier(self, others):
        semaphore = pltpu.get_barrier_semaphore()
        for other in others:
            pl.semaphore_signal(semaphore, inc=1, device_id=other, device_id_type=MESH)
        pl.semaphore_wait(semaphore, len(others))

    def neighbours(self):
        return [{"ctx": self.at(1)}, {"ctx": self.at(-1)}]


def remote(source, target, send, receive, device):
    return pltpu.make_async_remote_copy(
        src_ref=source,
        dst_ref=target,
        send_sem=send,
        recv_sem=receive,
        device_id=device,
        device_id_type=MESH,
    )


def gather_steps(ring, source, place, send, receive, arrived=None, ready=None):
    signs = (1, -1)

    def copy(way, half, hop):
        origin = ring.at(-signs[way] * hop)
        spot = place(origin, half)
        return remote(
            source(half) if hop == 0 else spot,
            spot,
            send.at[way, half, hop],
            receive.at[way, half, hop],
            {"ctx": ring.at(signs[way])},
        )

    def landed(way, half, hop):
        spot = place(ring.at(-signs[way] * (hop + 1)), half)
        return remote(
            spot,
            spot,
            send.at[way, half, hop],
            receive.at[way, half, hop],
            {"ctx": ring.at(signs[way])},
        )

    started = []
    for half in (0, 1):
        if ready is not None:
            ready(half)
        for way in (0, 1):
            started.append(copy(way, half, 0))
            started[-1].start()
        yield
    for hop in range(ring.n // 2):
        for half in (0, 1):
            for way in (0, 1):
                if hop < ring.hops(way, half):
                    landed(way, half, hop).wait_recv()
                    if hop + 1 < ring.hops(way, half):
                        started.append(copy(way, half, hop + 1))
                        started[-1].start()
                    if arrived is not None:
                        arrived(way, half, hop, ring.at(-signs[way] * (hop + 1)))
                    yield
    for one in started:
        one.wait_send()


def scatter_steps(ring, part, slots, store, send, receive):
    signs = (1, -1)

    def copy(way, half, hop, source):
        return remote(
            source,
            slots.at[way, half, hop],
            send.at[way, half, hop],
            receive.at[way, half, hop],
            {"ctx": ring.at(signs[way])},
        )

    started = []
    for half in (0, 1):
        for way in (0, 1):
            goal = ring.at(signs[way] * ring.hops(way, half))
            started.append(copy(way, half, 0, part(goal, half)))
            started[-1].start()
        yield
    for hop in range(ring.n // 2):
        for half in (0, 1):
            for way in (0, 1):
                last = ring.hops(way, half) - 1
                if hop <= last:
                    slot = slots.at[way, half, hop]
                    copy(way, half, hop, slot).wait_recv()
                    if hop < last:
                        goal = ring.at(signs[way] * (last - hop))
                        slot[...] = (
                            slot[...].astype(jnp.float32)
                            + part(goal, half)[...].astype(jnp.float32)
                        ).astype(slot.dtype)
                        started.append(copy(way, half, hop + 1, slot))
                        started[-1].start()
                    yield
    for half in (0, 1):
        total = part(ring.me, half)[...].astype(jnp.float32)
        for way in (0, 1):
            total = total + slots[way, half, ring.hops(way, half) - 1].astype(jnp.float32)
        store(half, total)
    for one in started:
        one.wait_send()


def run_steps(*tasks):
    tasks = list(tasks)
    while tasks:
        left = []
        for task in tasks:
            try:
                next(task)
                left.append(task)
            except StopIteration:
                pass
        tasks = left


def sems(*shape):
    return pltpu.SemaphoreType.DMA(shape)


def kernel_call(body, outs, in_specs, out_specs, scratch, identity, name, sent):
    return pl.pallas_call(
        body,
        out_shape=outs,
        in_specs=in_specs,
        out_specs=out_specs,
        scratch_shapes=scratch,
        name=name,
        cost_estimate=pl.CostEstimate(flops=0, bytes_accessed=sent, transcendentals=0),
        compiler_params=pltpu.CompilerParams(
            collective_id=identity, has_side_effects=True, vmem_limit_bytes=VMEM_LIMIT
        ),
    )


ANY = pl.BlockSpec(memory_space=pl.ANY)
VMEM = pl.BlockSpec(memory_space=pltpu.VMEM)


def ring_gather(block, n, identity, name, axis=0):
    rows, width = block.shape
    half_rows = rows // 2
    shape = (rows * n, width) if axis == 0 else (rows, width * n)

    def body(block_ref, all_ref, send, receive, local):
        ring = Ring(n)

        def place(device, half):
            if axis == 0:
                return all_ref.at[pl.ds(pl.multiple_of(device * rows + half * half_rows, 16), half_rows)]
            return all_ref.at[
                pl.ds(half * half_rows, half_rows), pl.ds(pl.multiple_of(device * width, 128), width)
            ]

        whole = (
            all_ref.at[pl.ds(pl.multiple_of(ring.me * rows, 16), rows)]
            if axis == 0
            else all_ref.at[:, pl.ds(pl.multiple_of(ring.me * width, 128), width)]
        )
        own = pltpu.make_async_copy(block_ref, whole, local)
        own.start()
        ring.barrier(ring.neighbours())
        run_steps(
            gather_steps(
                ring,
                lambda half: block_ref.at[pl.ds(half * half_rows, half_rows)],
                place,
                send,
                receive,
            )
        )
        own.wait()

    return kernel_call(
        body,
        jax.ShapeDtypeStruct(shape, block.dtype),
        [ANY],
        ANY,
        [sems(2, 2, n // 2), sems(2, 2, n // 2), pltpu.SemaphoreType.DMA],
        identity,
        name,
        block.size * 2 * n * 32,
    )(block)


def ring_scatter(partial, n, identity, name):
    rows, width = partial.shape[0] // n, partial.shape[1]
    half_rows = rows // 2

    def body(part_ref, sum_ref, slots, send, receive):
        ring = Ring(n)
        ring.barrier(ring.neighbours())

        def part(device, half):
            return part_ref.at[pl.ds(pl.multiple_of(device * rows + half * half_rows, 16), half_rows)]

        def store(half, total):
            sum_ref[pl.ds(half * half_rows, half_rows)] = total

        run_steps(scatter_steps(ring, part, slots, store, send, receive))

    return kernel_call(
        body,
        jax.ShapeDtypeStruct((rows, width), jnp.float32),
        [VMEM],
        VMEM,
        [
            pltpu.VMEM((2, 2, n // 2, half_rows, width), partial.dtype),
            sems(2, 2, n // 2),
            sems(2, 2, n // 2),
        ],
        identity,
        name,
        partial.size * 2 * 32,
    )(partial)


def partners():
    dp = lax.axis_index("dp")
    core = dp + 1 - 2 * (dp % 2)
    chip = (dp + 2) % 4
    return dp, core, chip, (core + 2) % 4


def gather_inputs(tokens, named, in_blocks, n, n_dp, identity):
    tok_rows, width = tokens.shape

    def body(
        token_ref,
        named_ref,
        in_ref,
        token_all,
        named_all,
        in_all,
        token_send,
        token_receive,
        named_send,
        named_receive,
        in_send,
        in_receive,
        pass_send,
        pass_receive,
        local,
    ):
        ring = Ring(n)
        me = ring.me
        dp, core, chip, core_chip = partners()
        half_rows = tok_rows // 2

        def token_place(device, half):
            return token_all.at[
                pl.ds(pl.multiple_of(device * tok_rows + half * half_rows, 16), half_rows)
            ]

        locals_ = [
            pltpu.make_async_copy(in_ref.at[me], in_all.at[dp, me], local.at[0]),
            pltpu.make_async_copy(
                token_ref,
                token_all.at[pl.ds(pl.multiple_of(me * tok_rows, 16), tok_rows)],
                local.at[1],
            ),
            pltpu.make_async_copy(named_ref, named_all.at[me], local.at[2]),
        ]
        for copy in locals_:
            copy.start()
        others = [(me + k) % n for k in range(1, n)]
        ring.barrier([{"ctx": other} for other in others] + [{"dp": core}, {"dp": chip}])

        direct = []
        for k, other in enumerate(others):
            direct.append(
                remote(in_ref.at[other], in_all.at[dp, me], in_send.at[k], in_receive.at[k], {"ctx": other})
            )
            direct.append(
                remote(named_ref, named_all.at[me], named_send.at[k], named_receive.at[k], {"ctx": other})
            )
        for copy in direct:
            copy.start()

        def in_steps():
            for _ in range(2):
                yield
            for k in range(1, n):
                spot = in_all.at[dp, (me - k + n) % n]
                remote(
                    spot, spot, in_send.at[k - 1], in_receive.at[k - 1], {"ctx": others[k - 1]}
                ).wait_recv()
            locals_[0].wait()
            passed = []
            for at, to in ((0, chip), (1, core)):
                passed.append(
                    remote(
                        in_all.at[dp], in_all.at[dp], pass_send.at[at], pass_receive.at[at], {"dp": to}
                    )
                )
                passed[-1].start()
            for _ in range(8):
                yield
            spot = in_all.at[chip]
            remote(spot, spot, pass_send.at[0], pass_receive.at[0], {"dp": chip}).wait_recv()
            passed.append(
                remote(spot, spot, pass_send.at[2], pass_receive.at[2], {"dp": core})
            )
            passed[-1].start()
            for _ in range(4):
                yield
            for at, source in ((1, core), (2, core_chip)):
                spot = in_all.at[source]
                remote(
                    spot, spot, pass_send.at[at], pass_receive.at[at], {"dp": core}
                ).wait_recv()
            for copy in passed:
                copy.wait_send()

        run_steps(
            gather_steps(
                ring,
                lambda half: token_ref.at[pl.ds(half * half_rows, half_rows)],
                token_place,
                token_send,
                token_receive,
            ),
            in_steps(),
        )
        for k in range(1, n):
            spot = named_all.at[(me - k + n) % n]
            remote(
                spot, spot, named_send.at[k - 1], named_receive.at[k - 1], {"ctx": others[k - 1]}
            ).wait_recv()
        for copy in direct:
            copy.wait_send()
        for copy in locals_[1:]:
            copy.wait()

    return kernel_call(
        body,
        (
            jax.ShapeDtypeStruct((tok_rows * n, width), tokens.dtype),
            jax.ShapeDtypeStruct((n,) + named.shape, named.dtype),
            jax.ShapeDtypeStruct((n_dp,) + in_blocks.shape, in_blocks.dtype),
        ),
        [ANY] * 3,
        (ANY,) * 3,
        [sems(2, 2, n // 2)] * 2
        + [sems(n - 1)] * 4
        + [sems(3)] * 2
        + [sems(3)],
        identity,
        "gather_inputs",
        200_000_000,
    )(tokens, named, in_blocks)


def sum_small_steps(ring, small, near, quarter, got, total, sem):
    pass_send, pass_receive, send, receive = sem
    dp, core, chip, core_chip = partners()
    n, me = ring.n, ring.me
    lanes = quarter.shape[1]
    per_tile = LANES * n // lanes

    def group(at):
        return small.at[:, pl.ds(pl.multiple_of(at * lanes, LANES), lanes)]

    copies = []
    for at, to in enumerate((core_chip, chip, core)):
        copies.append(
            remote(group(to), near.at[at], pass_send.at[at], pass_receive.at[at], {"dp": to})
        )
        copies[-1].start()
    for _ in range(WAITS[1]):
        yield
    value = group(dp)[...]
    for at in range(3):
        copies[at].wait_recv()
        value = value + near[at]
    quarter[...] = value

    def tile(device):
        return quarter.at[:, pl.ds(pl.multiple_of(device // per_tile * LANES, LANES), LANES)]

    for k in range(1, n):
        other = (me + k) % n
        copies.append(
            remote(tile(other), got.at[k - 1], send.at[k - 1], receive.at[k - 1], {"ctx": other})
        )
        copies[-1].start()
    for _ in range(WAITS[2]):
        yield
    value = tile(me)[...]
    for k in range(1, n):
        copies[2 + k].wait_recv()
        value = value + got[k - 1]
    total[...] = value
    for copy in copies:
        copy.wait_send()


def scatter_end(
    row_part, attend_in, raw_back, tokens, residual_back, gain, small, pair_sum, far, n, n_dp, identity
):
    rows, width = row_part.shape[0] // n, row_part.shape[1]
    half_rows = rows // 2
    span = width // n_dp
    weight_rows = span // n
    in_cols = raw_back.shape[1]
    cols = in_cols // 3
    small_rows = small.shape[0]
    bf16, f32 = jnp.bfloat16, jnp.float32

    def body(
        row_ref,
        attend_ref,
        raw_ref,
        token_ref,
        back_ref,
        gain_ref,
        small_ref,
        pair_ref,
        far_ref,
        token_back,
        in_sum,
        small_sum,
        far_got,
        slots,
        row_s,
        attend_s,
        in_part,
        in_core,
        in_chip,
        in_got,
        small_s,
        small_near,
        small_quarter,
        small_got,
        row_send,
        row_receive,
        pass_send,
        pass_receive,
        in_send,
        in_receive,
        small_pass_send,
        small_pass_receive,
        small_send,
        small_receive,
        load,
        far_send,
        far_receive,
    ):
        ring = Ring(n)
        me = ring.me
        dp, core, chip, core_chip = partners()
        others = [(me + k) % n for k in range(1, n)]
        loaded = pltpu.make_async_copy(attend_ref, attend_s, load)
        loaded.start()
        ring.barrier(
            [{"ctx": other} for other in others] + [{"dp": to} for to in (core, chip, core_chip)]
        )

        def part(device, half):
            return row_ref.at[pl.ds(pl.multiple_of(device * rows + half * half_rows, 16), half_rows)]

        def store(half, total):
            row_s[pl.ds(half * half_rows, half_rows)] = total

        half_slots = n // CUTS

        def passing(at, k, source, target, to):
            slots_k = pl.ds(k * half_slots, half_slots)
            return remote(
                source.at[slots_k],
                target.at[slots_k],
                pass_send.at[at, k],
                pass_receive.at[at, k],
                {"dp": to},
            )

        def product(group):
            value = lax.dot_general(
                attend_s[:, pl.ds(pl.multiple_of(group * span, LANES), span)],
                raw_ref[...],
                (((0,), (0,)), ((), ())),
                preferred_element_type=f32,
            ).astype(bf16)
            for device in range(n):
                in_part[group, (device - me + n) % n] = value[
                    device * weight_rows : (device + 1) * weight_rows
                ]

        def weight_steps():
            loaded.wait()
            sent = []
            product(core_chip)
            far = [passing(0, k, in_part.at[core_chip], in_core.at[1], core) for k in range(CUTS)]
            for copy in far:
                copy.start()
            yield
            product(core)
            near = [passing(1, k, in_part.at[core], in_core.at[0], core) for k in range(CUTS)]
            for copy in near:
                copy.start()
            yield
            product(chip)
            across = []
            for k in range(CUTS):
                far[k].wait_recv()

                def add_far(at, carry):
                    in_core[1, at] = (
                        in_core[1, at].astype(f32) + in_part[chip, at].astype(f32)
                    ).astype(bf16)
                    return carry

                lax.fori_loop(k * half_slots, (k + 1) * half_slots, add_far, 0)
                across.append(passing(2, k, in_core.at[1], in_chip, chip))
                across[-1].start()
            beyond = remote(far_ref.at[1, pl.ds(PASS_B, far_got.shape[0])], far_got, far_send, far_receive, {"dp": chip})
            yield
            product(dp)
            for _ in range(2):
                yield
            for k in range(CUTS):
                near[k].wait_recv()
                across[k].wait_recv()

                def add_near(at, carry):
                    in_core[0, at] = (
                        in_core[0, at].astype(f32)
                        + in_part[dp, at].astype(f32)
                        + in_chip[at].astype(f32)
                    ).astype(bf16)
                    return carry

                lax.fori_loop(k * half_slots, (k + 1) * half_slots, add_near, 0)
                for at in range(max(1, k * half_slots), (k + 1) * half_slots):
                    sent.append(
                        remote(
                            in_core.at[0, at],
                            in_got.at[at],
                            in_send.at[at - 1],
                            in_receive.at[at - 1],
                            {"ctx": others[at - 1]},
                        )
                    )
                    sent[-1].start()
                yield
                yield
            beyond.start()
            in_got[0] = in_core[0, 0]
            for _ in range(6):
                yield
            for at in range(n):
                if at:
                    sent[at - 1].wait_recv()
                device = (me - at + n) % n
                for which in range(3):
                    in_sum[
                        :, pl.ds(pl.multiple_of(which * width + device * cols, LANES), cols)
                    ] = in_got[at, :, pl.ds(which * cols, cols)].astype(f32)
            beyond.wait()
            for copy in far + near + across + sent:
                copy.wait_send()

        def row_steps():
            yield from scatter_steps(ring, part, slots, store, row_send, row_receive)
            values = token_ref[...].astype(f32)
            inverse = lax.rsqrt(jnp.mean(values * values, axis=-1, keepdims=True) + EPSILON)
            normed = values * inverse
            back = row_s[...]
            back = back * gain_ref[0:1, :]
            token_back[...] = (
                back_ref[...]
                + inverse * (back - normed * jnp.mean(back * normed, axis=-1, keepdims=True))
            ).astype(bf16)

        def small_steps():
            for _ in range(WAITS[0]):
                yield

            def column_sums(at, total):
                part_rows = pl.ds(pl.multiple_of(at * rows, rows), rows)
                terms = row_ref[part_rows].astype(f32) * attend_s[part_rows].astype(f32)
                return total + jnp.sum(terms, axis=0, keepdims=True)

            total = lax.fori_loop(0, n, column_sums, jnp.zeros((1, width), f32))
            small_s[...] = small_ref[...]
            small_s[0:1, :] = total / gain_ref[0:1, :]
            own = pl.ds(pl.multiple_of(me * cols, LANES), cols)
            small_s[1:2, own] = pair_ref[0:1, :cols]
            small_s[2:3, own] = pair_ref[0:1, cols:]
            yield from sum_small_steps(
                ring,
                small_s,
                small_near,
                small_quarter,
                small_got,
                small_sum,
                (small_pass_send, small_pass_receive, small_send, small_receive),
            )

        run_steps(row_steps(), weight_steps(), small_steps())

    block = (n, weight_rows, in_cols)
    return kernel_call(
        body,
        (
            jax.ShapeDtypeStruct((rows, width), bf16),
            jax.ShapeDtypeStruct((weight_rows, 3 * width), f32),
            jax.ShapeDtypeStruct((small_rows, LANES), f32),
            jax.ShapeDtypeStruct((far.shape[1] - PASS_B, far.shape[2]), bf16),
        ),
        [VMEM, ANY] + [VMEM] * 6 + [ANY],
        (VMEM,) * 3 + (ANY,),
        [
            pltpu.VMEM((2, 2, n // 2, half_rows, width), row_part.dtype),
            pltpu.VMEM((rows, width), f32),
            pltpu.VMEM(attend_in.shape, bf16),
            pltpu.VMEM((n_dp,) + block, bf16),
            pltpu.VMEM((2,) + block, bf16),
            pltpu.VMEM(block, bf16),
            pltpu.VMEM(block, bf16),
            pltpu.VMEM((small_rows, width), f32),
            pltpu.VMEM((3, small_rows, span), f32),
            pltpu.VMEM((small_rows, span), f32),
            pltpu.VMEM((n - 1, small_rows, LANES), f32),
            sems(2, 2, n // 2),
            sems(2, 2, n // 2),
            sems(3, CUTS),
            sems(3, CUTS),
            sems(n - 1),
            sems(n - 1),
            sems(3),
            sems(3),
            sems(n - 1),
            sems(n - 1),
            pltpu.SemaphoreType.DMA,
            pltpu.SemaphoreType.DMA,
            pltpu.SemaphoreType.DMA,
        ],
        identity,
        "scatter_end",
        200_000_000,
    )(row_part, attend_in, raw_back, tokens, residual_back, gain, small, pair_sum, far)


def slot_offsets(n):
    offsets = [0]
    for k in range(1, n // 2):
        offsets += [k, -k]
    return offsets + [n // 2]


def slot_of(offset, n):
    if abs(offset) == n // 2:
        return n - 1
    return 2 * offset - 1 if offset > 0 else -2 * offset


def slot_gather_steps(ring, first, slots, send, receive):
    signs = (1, -1)
    half_rows = slots.shape[1] // 2

    def copy(way, half, hop):
        rows = pl.ds(half * half_rows, half_rows)
        held = slot_of(-signs[way] * hop, ring.n)
        return remote(
            first.at[rows] if hop == 0 else slots.at[held, rows],
            slots.at[slot_of(-signs[way] * (hop + 1), ring.n), rows],
            send.at[way, half, hop],
            receive.at[way, half, hop],
            {"ctx": ring.at(signs[way])},
        )

    started = []
    for half in (0, 1):
        for way in (0, 1):
            started.append(copy(way, half, 0))
            started[-1].start()
    yield
    for hop in range(ring.n // 2):
        for half in (0, 1):
            for way in (0, 1):
                if hop < ring.hops(way, half):
                    copy(way, half, hop).wait_recv()
                    if hop + 1 < ring.hops(way, half):
                        started.append(copy(way, half, hop + 1))
                        started[-1].start()
                    yield
    for one in started:
        one.wait_send()


def advance(steps, count):
    for _ in range(count):
        next(steps, None)


def dot(a, b):
    return jnp.dot(a, b, preferred_element_type=jnp.float32)


def dot_across(a, b):
    return lax.dot_general(a, b, (((1,), (1,)), ((), ())), preferred_element_type=jnp.float32)


def experts_in(
    attend_all, token_all, cotangent, out_all, first, second, gain, router, named, n, identity
):
    tok_rows, width = cotangent.shape
    local_experts, ff = first.shape[0], second.shape[0] // first.shape[0]
    rows = tok_rows * n
    pair = 2 * tok_rows
    part = 4 * tok_rows
    tile, wide = TILE, WIDE
    bf16, f32 = jnp.bfloat16, jnp.float32
    offsets = slot_offsets(n)

    def body(
        attend_ref,
        token_ref,
        back_ref,
        out_ref,
        first_ref,
        second_ref,
        gain_ref,
        router_ref,
        named_ref,
        back_all,
        mixed_all,
        gated_all,
        up_all,
        own_gates,
        gate_back,
        own_residual,
        out_s,
        first_s,
        second_s,
        mixed_s,
        back_s,
        attend_s,
        token_s,
        residual_s,
        gate_s,
        sum_s,
        send,
        receive,
        load,
        weight_load,
        save,
        local,
    ):
        ring = Ring(n)
        lanes = lax.broadcasted_iota(jnp.int32, (pair, LANES), 1)
        part_lanes = lax.broadcasted_iota(jnp.int32, (part, LANES), 1)
        loads = [pltpu.make_async_copy(out_ref, out_s, weight_load.at[0])]
        for x in range(local_experts):
            loads.append(pltpu.make_async_copy(first_ref.at[x], first_s.at[x], weight_load.at[1 + x]))
        loads.append(pltpu.make_async_copy(second_ref, second_s, weight_load.at[1 + local_experts]))

        def row_loads(j):
            copies = []
            for k in range(2):
                device = ring.at(offsets[2 * j + k])
                source = pl.ds(pl.multiple_of(device * tok_rows, 16), tok_rows)
                target = pl.ds(k * tok_rows, tok_rows)
                for at, (array, held) in enumerate(((attend_ref, attend_s), (token_ref, token_s))):
                    copies.append(
                        pltpu.make_async_copy(
                            array.at[source], held.at[j % 2, target], load.at[j % 2, k, at]
                        )
                    )
            return copies

        pending = row_loads(0)
        for copy in pending:
            copy.start()
        loads[0].start()
        own = pltpu.make_async_copy(back_ref, back_s.at[0], local)
        own.start()
        ring.barrier(ring.neighbours())
        steps = slot_gather_steps(ring, back_ref, back_s, send, receive)
        advance(steps, 1)
        loads[0].wait()
        for copy in loads[1:]:
            copy.start()

        saves = []
        for j in range(n // 2):
            for copy in pending:
                copy.wait()
            if j + 1 < n // 2:
                pending = row_loads(j + 1)
                for copy in pending:
                    copy.start()

            def project(t, carry, j=j):
                columns = pl.ds(pl.multiple_of(t * wide, wide), wide)
                residual_s[:, columns] = token_s[j % 2, :, columns].astype(f32) + dot(
                    attend_s[j % 2], out_s[:, columns]
                )
                return carry

            lax.fori_loop(0, width // wide, project, 0)
            residual = residual_s[...]
            if j == 0:
                own_residual[...] = residual[:tok_rows]
            inverse = lax.rsqrt(jnp.mean(residual * residual, axis=-1, keepdims=True) + EPSILON)
            mixed = (residual * inverse * gain_ref[0:1, :]).astype(bf16)
            for k in range(2):
                mixed_s[2 * j + k] = mixed[k * tok_rows : (k + 1) * tok_rows]
            logits = dot(mixed, router_ref[...])
            marks = jnp.concatenate(
                [
                    named_ref[pl.ds(pl.multiple_of(ring.at(offsets[2 * j + k]) * tok_rows, 16), tok_rows)]
                    for k in range(2)
                ],
                axis=0,
            ).astype(f32)
            logits = jnp.where(marks > 0, logits, MASKED)
            powers = jnp.where(
                marks > 0, jnp.exp(logits - jnp.max(logits, axis=-1, keepdims=True)), 0.0
            )
            gates = powers / jnp.sum(powers, axis=-1, keepdims=True)
            if j == 0:
                own_gates[...] = gates[:tok_rows]
            held = jnp.zeros((pair, LANES), f32)
            for x in range(local_experts):
                mine = jnp.sum(
                    jnp.where(lanes == ring.me * local_experts + x, gates, 0.0), axis=-1, keepdims=True
                )
                held = jnp.where(lanes == x, mine, held)
            gate_s[pl.ds(j * pair, pair)] = held
            saves.append(
                pltpu.make_async_copy(
                    mixed_s.at[pl.ds(2 * j, 2)], mixed_all.at[pl.ds(2 * j, 2)], save.at[j]
                )
            )
            saves[-1].start()
            advance(steps, 2)

        counts = rows // part
        outgoing = []
        base = n // 2
        for s in range(counts):
            slots = pl.ds(s * 4, 4)
            part_rows = pl.ds(s * part, part)
            advance(steps, 0 if s < counts - 1 else 64)
            if s == 0:
                own.wait()
            sum_s[part_rows] = jnp.zeros((part, LANES), f32)
            for copy in outgoing:
                copy.wait()
            outgoing = []
            for x in range(local_experts):
                if s == 0:
                    loads[1 + x].wait()
                    if x == 0:
                        loads[1 + local_experts].wait()

                def hidden(t, carry, s=s, x=x, slots=slots, part_rows=part_rows):
                    at = pl.multiple_of(t * tile, tile)
                    mixed = mixed_s[slots].reshape(part, width)
                    back = back_s[slots].reshape(part, width)
                    gate_part = dot(mixed, first_s[x, :, pl.ds(at, tile)])
                    up_part = dot(mixed, first_s[x, :, pl.ds(pl.multiple_of(ff + at, tile), tile)])
                    hidden_back = dot_across(
                        back, second_s[pl.ds(pl.multiple_of(x * ff + at, tile), tile), :]
                    )
                    gate = gate_s[part_rows, x : x + 1]
                    sigmoid = jax.nn.sigmoid(gate_part)
                    swish = gate_part * sigmoid
                    value = swish * up_part
                    out_s[pl.ds(0, part), pl.ds(pl.multiple_of(x * ff + at, tile), tile)] = (
                        value * gate
                    ).astype(bf16)
                    sums = jnp.sum(value * hidden_back, axis=-1, keepdims=True)
                    sum_s[part_rows] = sum_s[part_rows] + jnp.where(part_lanes == x, sums, 0.0)
                    hidden_back = hidden_back * gate
                    slope = sigmoid * (1.0 + gate_part * (1.0 - sigmoid))
                    up_rows = pl.ds((1 + x) * part, part)
                    out_s[up_rows, pl.ds(at, tile)] = (hidden_back * up_part * slope).astype(bf16)
                    out_s[up_rows, pl.ds(pl.multiple_of(ff + at, tile), tile)] = (
                        hidden_back * swish
                    ).astype(bf16)
                    return carry

                pieces = ff // tile
                lax.fori_loop(0, pieces // 2, hidden, 0)
                advance(steps, 2)
                lax.fori_loop(pieces // 2, pieces, hidden, 0)
                advance(steps, 2)
                outgoing.append(
                    pltpu.make_async_copy(
                        out_s.at[pl.ds((1 + x) * part, part)],
                        up_all.at[x, part_rows],
                        save.at[base + 1 + x],
                    )
                )
                outgoing[-1].start()
            outgoing.append(
                pltpu.make_async_copy(out_s.at[pl.ds(0, part)], gated_all.at[part_rows], save.at[base])
            )
            outgoing[-1].start()
        spread = pltpu.make_async_copy(back_s, back_all, local)
        spread.start()
        for k in range(n):
            gate_back[k] = jnp.transpose(sum_s[pl.ds(k * tok_rows, tok_rows)])[:8]
        for copy in saves + outgoing:
            copy.wait()
        spread.wait()

    return pl.pallas_call(
        body,
        out_shape=(
            jax.ShapeDtypeStruct((n, tok_rows, width), bf16),
            jax.ShapeDtypeStruct((n, tok_rows, width), bf16),
            jax.ShapeDtypeStruct((rows, local_experts * ff), bf16),
            jax.ShapeDtypeStruct((local_experts, rows, 2 * ff), bf16),
            jax.ShapeDtypeStruct((tok_rows, LANES), f32),
            jax.ShapeDtypeStruct((n, 8, LANES), f32),
            jax.ShapeDtypeStruct((tok_rows, width), f32),
        ),
        in_specs=[ANY] * 6 + [VMEM] * 3,
        out_specs=(ANY,) * 4 + (VMEM,) * 3,
        scratch_shapes=[
            pltpu.VMEM(out_all.shape, bf16),
            pltpu.VMEM(first.shape, bf16),
            pltpu.VMEM(second.shape, bf16),
            pltpu.VMEM((n, tok_rows, width), bf16),
            pltpu.VMEM((n, tok_rows, width), bf16),
            pltpu.VMEM((2, pair, width), bf16),
            pltpu.VMEM((2, pair, width), bf16),
            pltpu.VMEM((pair, width), f32),
            pltpu.VMEM((rows, LANES), f32),
            pltpu.VMEM((rows, LANES), f32),
            sems(2, 2, n // 2),
            sems(2, 2, n // 2),
            sems(2, 2, 2),
            sems(2 + local_experts),
            sems(n // 2 + 1 + local_experts),
            pltpu.SemaphoreType.DMA,
        ],
        name="experts_in",
        cost_estimate=pl.CostEstimate(
            flops=2 * rows * width * (width + 3 * ff * local_experts),
            bytes_accessed=60_000_000,
            transcendentals=0,
        ),
        compiler_params=pltpu.CompilerParams(
            collective_id=identity, has_side_effects=True, vmem_limit_bytes=BIG_VMEM
        ),
    )(attend_all, token_all, cotangent, out_all, first, second, gain, router, named)


BIG_VMEM = 60 * 1024 * 1024


def slot_scatter_steps(ring, parts, slots, store, send, receive, need):
    signs = (1, -1)
    half_rows = parts.shape[1] // 2
    f32 = jnp.float32

    def part(offset, half):
        return parts.at[slot_of(offset, ring.n), pl.ds(half * half_rows, half_rows)]

    def copy(way, half, hop, source):
        return remote(
            source,
            slots.at[way, half, hop],
            send.at[way, half, hop],
            receive.at[way, half, hop],
            {"ctx": ring.at(signs[way])},
        )

    started = []
    firsts = [(way, half) for half in (0, 1) for way in (0, 1)]
    firsts.sort(key=lambda one: -slot_of(signs[one[0]] * ring.hops(*one), ring.n))
    for way, half in firsts:
        goal = signs[way] * ring.hops(way, half)
        need(slot_of(goal, ring.n))
        started.append(copy(way, half, 0, part(goal, half)))
        started[-1].start()
    for hop in range(ring.n // 2):
        for way, half in firsts:
            last = ring.hops(way, half) - 1
            if hop <= last:
                slot = slots.at[way, half, hop]
                if hop < last:
                    goal = signs[way] * (last - hop)
                    need(slot_of(goal, ring.n))
                copy(way, half, hop, slot).wait_recv()
                if hop < last:
                    slot[...] = (
                        slot[...].astype(f32) + part(goal, half)[...].astype(f32)
                    ).astype(slot.dtype)
                    started.append(copy(way, half, hop + 1, slot))
                    started[-1].start()
                yield
    need(0)
    for half in (0, 1):
        total = part(0, half)[...].astype(f32)
        for way in (0, 1):
            total = total + slots[way, half, ring.hops(way, half) - 1].astype(f32)
        store(half, total)
    for one in started:
        one.wait_send()


def experts_out(up_all, gated_all, first, second, gate_back, n, identity):
    local_experts, rows, inner = up_all.shape
    width = first.shape[1]
    tok_rows = rows // n
    half_rows = tok_rows // 2
    pair = 2 * tok_rows
    wide = 512
    count = width // wide
    bf16, f32 = jnp.bfloat16, jnp.float32
    offsets = slot_offsets(n)

    def body(
        up_ref,
        gated_ref,
        first_ref,
        second_ref,
        gate_ref,
        row_sum,
        result_all,
        gate_got,
        first_s,
        second_s,
        up_s,
        gated_s,
        part_s,
        result_s,
        slots,
        send,
        receive,
        gate_send,
        gate_receive,
        load,
        first_load,
        other_load,
        save,
    ):
        ring = Ring(n)

        def up_load(j):
            return pltpu.make_async_copy(
                up_ref.at[:, pl.ds(j * pair, pair)], up_s.at[:, pl.ds(j * pair, pair)], load.at[j]
            )

        def weight_load(t):
            return pltpu.make_async_copy(
                first_ref.at[:, pl.ds(t * wide, wide)],
                first_s.at[:, pl.ds(t * wide, wide)],
                first_load.at[t],
            )

        groups = n // 2
        up_load(groups - 1).start()
        for t in range(count):
            weight_load(t).start()
        for j in range(groups - 1):
            up_load(groups - 2 - j).start()
        others = [
            pltpu.make_async_copy(gated_ref, gated_s, other_load.at[0]),
            pltpu.make_async_copy(second_ref, second_s, other_load.at[1]),
        ]
        for copy in others:
            copy.start()
        ring.barrier([{"ctx": ring.at(k)} for k in range(1, n)])
        gate_copies = []
        for k in range(1, n):
            offset = k if k <= n // 2 else k - n
            back = -offset if offset < n // 2 else offset
            gate_copies.append(
                remote(
                    gate_ref.at[slot_of(offset, n)],
                    gate_got.at[slot_of(back, n)],
                    gate_send.at[slot_of(back, n)],
                    gate_receive.at[slot_of(back, n)],
                    {"ctx": ring.at(k)},
                )
            )
            gate_copies[-1].start()
        gate_got[0] = gate_ref[0]

        done = set()

        def product(j):
            rows_j = pl.ds(j * pair, pair)
            up_load(j).wait()

            def columns(t):
                at = pl.ds(pl.multiple_of(t * wide, wide), wide)
                value = dot_across(up_s[0, rows_j], first_s[0, at, :])
                for x in range(1, local_experts):
                    value = value + dot_across(up_s[x, rows_j], first_s[x, at, :])
                value = value.astype(bf16)
                for k in range(2):
                    part_s[2 * j + k, :, at] = value[k * tok_rows : (k + 1) * tok_rows]

            if not done:
                for t in range(count):
                    weight_load(t).wait()
                    columns(t)
            else:

                def step(t, carry):
                    columns(t)
                    return carry

                lax.fori_loop(0, count, step, 0)
            done.add(j)

        def need(slot):
            if slot // 2 not in done:
                product(slot // 2)

        def store(half, total):
            row_sum[pl.ds(half * half_rows, half_rows)] = total

        steps = slot_scatter_steps(ring, part_s, slots, store, send, receive, need)
        for j in reversed(range(groups)):
            need(2 * j)
            advance(steps, 1 if j in (0, groups - 1) else 2)
        for copy in others:
            copy.wait()
        saves = []
        chunk = 2
        for j in range(n // chunk):
            rows_j = pl.ds(j * chunk * tok_rows, chunk * tok_rows)

            def result(t, carry, rows_j=rows_j, j=j):
                at = pl.ds(pl.multiple_of(t * wide, wide), wide)
                value = dot(gated_s[rows_j], second_s[:, at]).astype(bf16)
                for k in range(chunk):
                    result_s[chunk * j + k, :, at] = value[k * tok_rows : (k + 1) * tok_rows]
                return carry

            lax.fori_loop(0, count, result, 0)
            for k in range(chunk):
                slot = chunk * j + k
                device = ring.at(offsets[slot])
                saves.append(
                    pltpu.make_async_copy(
                        result_s.at[slot],
                        result_all.at[pl.ds(pl.multiple_of(device * tok_rows, 16), tok_rows)],
                        save.at[slot],
                    )
                )
                saves[-1].start()
            advance(steps, 2)
        advance(steps, 64)
        for copy in saves:
            copy.wait()
        for copy in gate_copies:
            copy.wait()

    return pl.pallas_call(
        body,
        out_shape=(
            jax.ShapeDtypeStruct((tok_rows, width), f32),
            jax.ShapeDtypeStruct((rows, width), bf16),
            jax.ShapeDtypeStruct(gate_back.shape, f32),
        ),
        in_specs=[ANY] * 4 + [VMEM],
        out_specs=(VMEM, ANY, VMEM),
        scratch_shapes=[
            pltpu.VMEM(first.shape, bf16),
            pltpu.VMEM(second.shape, bf16),
            pltpu.VMEM(up_all.shape, bf16),
            pltpu.VMEM(gated_all.shape, bf16),
            pltpu.VMEM((n, tok_rows, width), bf16),
            pltpu.VMEM((n, tok_rows, width), bf16),
            pltpu.VMEM((2, 2, n // 2, half_rows, width), bf16),
            sems(2, 2, n // 2),
            sems(2, 2, n // 2),
            sems(n),
            sems(n),
            sems(n // 2),
            sems(count),
            sems(2),
            sems(n),
        ],
        name="experts_out",
        cost_estimate=pl.CostEstimate(
            flops=2 * rows * width * 3 * inner // 2 * local_experts,
            bytes_accessed=60_000_000,
            transcendentals=0,
        ),
        compiler_params=pltpu.CompilerParams(
            collective_id=identity, has_side_effects=True, vmem_limit_bytes=BIG_VMEM
        ),
    )(up_all, gated_all, first, second, gate_back)


def exchange_rows(ring, sums, flat, got, send, receive, steps):
    n, rows = ring.n, sums.shape[0]
    for k in range(rows // LANES):
        flat[:, pl.ds(k * LANES, LANES)] = jnp.transpose(sums[pl.ds(k * LANES, LANES)])[:8]
    copies = []
    for k in range(1, n):
        copies.append(
            remote(
                flat,
                got.at[k - 1],
                send.at[k - 1],
                receive.at[k - 1],
                {"ctx": (ring.me + k) % n},
            )
        )
        copies[-1].start()
    advance(steps, 1)
    for copy in copies:
        copy.wait_recv()
    total = flat[...]
    for k in range(n - 1):
        total = total + got[k]
    for k in range(rows // LANES):
        block = total[:, k * LANES : (k + 1) * LANES]
        block = jnp.concatenate([block, jnp.zeros((LANES - 8, LANES), jnp.float32)], axis=0)
        sums[pl.ds(k * LANES, LANES)] = jnp.transpose(block)
    for copy in copies:
        copy.wait_send()


def turn(values, cosine, sine):
    return values * cosine + pltpu.roll(values, HEAD_DIM // 2, 1) * sine


def out_gather_steps(ring, out_ref, out_all, sem):
    own_send, own_receive, ring_send, ring_receive, core_send, core_receive, local = sem
    dp, core, chip, core_chip = partners()
    weight_rows, n, me = out_ref.shape[0], ring.n, ring.me

    def place(group, device):
        return out_all.at[pl.ds(pl.multiple_of((group * n + device) * weight_rows, 16), weight_rows)]

    own = pltpu.make_async_copy(out_ref, place(dp, me), local)
    own.start()
    copies = [
        remote(out_ref, place(dp, me), own_send.at[0], own_receive.at[0], {"dp": chip}),
        remote(out_ref, place(dp, me), own_send.at[1], own_receive.at[1], {"dp": core}),
    ]
    for copy in copies:
        copy.start()

    def ready(half):
        if half == 1:
            spot = place(chip, me)
            remote(spot, spot, own_send.at[0], own_receive.at[0], {"dp": chip}).wait_recv()
            copies.append(remote(spot, spot, own_send.at[2], own_receive.at[2], {"dp": core}))
            copies[-1].start()

    def arrived(way, half, hop, origin):
        spot = place(chip if half else dp, origin)
        copies.append(
            remote(
                spot, spot, core_send.at[way, half, hop], core_receive.at[way, half, hop], {"dp": core}
            )
        )
        copies[-1].start()

    yield from gather_steps(
        ring,
        lambda half: place(chip, me) if half else out_ref,
        lambda device, half: place(chip if half else dp, device),
        ring_send,
        ring_receive,
        arrived,
        ready,
    )
    for at, group in ((1, core), (2, core_chip)):
        spot = place(group, me)
        remote(spot, spot, own_send.at[at], own_receive.at[at], {"dp": core}).wait_recv()
    for way, sign in ((0, 1), (1, -1)):
        for half in (0, 1):
            for hop in range(ring.hops(way, half)):
                spot = place(core_chip if half else core, ring.at(-sign * (hop + 1)))
                remote(
                    spot,
                    spot,
                    core_send.at[way, half, hop],
                    core_receive.at[way, half, hop],
                    {"dp": core},
                ).wait_recv()
    for copy in copies:
        copy.wait_send()
    own.wait()


def attention_in(
    token_all, in_all, out_rows, gain, pair_gains, cosine, sine, bounds, place_row, n, n_dp, identity
):
    rows, width = token_all.shape
    pair = pair_gains.shape[1]
    cols = pair // 2
    heads = cols // HEAD_DIM
    chunk = 256
    weight_rows = out_rows.shape[0]
    bf16, f32 = jnp.bfloat16, jnp.float32
    scale = HEAD_DIM ** (-0.5)

    def body(
        token_ref,
        in_ref,
        out_ref,
        gain_ref,
        pair_ref,
        cos_ref,
        sin_ref,
        bound_ref,
        place_ref,
        attend_all,
        out_all,
        probs_all,
        normed_all,
        attend_ref,
        qkv_ref,
        raw_ref,
        inverse_ref,
        probs_s,
        normed_s,
        flat,
        got,
        *sem,
    ):
        out_sem, sem = sem[:7], sem[7:]
        sum_send, sum_receive, ring_send, ring_receive, save = sem
        ring = Ring(n)
        dp, core, chip, core_chip = partners()
        ring.barrier(
            [{"ctx": (ring.me + k) % n} for k in range(1, n)] + [{"dp": core}, {"dp": chip}]
        )
        steps = out_gather_steps(ring, out_ref, out_all, out_sem)
        advance(steps, 1)
        lanes = lax.broadcasted_iota(jnp.int32, (chunk, LANES), 1)

        def chunks(step, count=2):
            total = rows // chunk
            for first in range(0, total, count):
                lax.fori_loop(first, min(first + count, total), step, 0)
                advance(steps, 1)

        def project(j, carry):
            at = pl.ds(pl.multiple_of(j * chunk, chunk), chunk)
            values = token_ref[at].astype(f32)
            inverse = lax.rsqrt(jnp.mean(values * values, axis=-1, keepdims=True) + EPSILON)
            normed = (values * inverse * gain_ref[0:1, :]).astype(bf16)
            normed_s[at] = normed
            projected = dot(normed, in_ref[:, : pair + cols])
            raw_ref[at] = projected[:, :pair]
            qkv_ref[at, pair:] = projected[:, pair:].astype(bf16)
            squares = projected[:, :pair] * projected[:, :pair]
            inverse_ref[at] = jnp.where(
                lanes == 0,
                jnp.sum(squares[:, :cols], axis=-1, keepdims=True),
                jnp.where(lanes == 1, jnp.sum(squares[:, cols:], axis=-1, keepdims=True), 0.0),
            )
            return carry

        chunks(project)
        saves = [pltpu.make_async_copy(normed_s, normed_all, save.at[heads])]
        saves[0].start()
        exchange_rows(ring, inverse_ref, flat, got, sum_send, sum_receive, steps)

        def norm(j, carry):
            at = pl.ds(pl.multiple_of(j * chunk, chunk), chunk)
            inverse = lax.rsqrt(inverse_ref[at] / width + EPSILON)
            inverse_ref[at] = inverse
            for which in range(2):
                for head in range(heads):
                    columns = pl.ds(which * cols + head * HEAD_DIM, HEAD_DIM)
                    values = raw_ref[at, columns] * inverse[:, which : which + 1]
                    values = values * pair_ref[0:1, columns]
                    qkv_ref[at, columns] = turn(values, cos_ref[at], sin_ref[at]).astype(bf16)
            return carry

        chunks(norm)
        for head in range(heads):

            def attend(j, carry, head=head):
                at = pl.ds(pl.multiple_of(j * chunk, chunk), chunk)
                columns = pl.ds(head * HEAD_DIM, HEAD_DIM)
                scores = (
                    dot_across(
                        qkv_ref[at, columns], qkv_ref[:, pl.ds(cols + head * HEAD_DIM, HEAD_DIM)]
                    )
                    * scale
                )
                place = place_ref[0:1, :]
                visible = (place >= bound_ref[at, 0:1]) & (place <= bound_ref[at, 1:2])
                scores = jnp.where(visible, scores, MASKED)
                powers = jnp.where(
                    visible, jnp.exp(scores - jnp.max(scores, axis=-1, keepdims=True)), 0.0
                )
                share = 1.0 / jnp.sum(powers, axis=-1, keepdims=True)
                probs = (powers * share).astype(bf16)
                probs_s[head, at] = probs
                attend_ref[at, columns] = dot(
                    probs, qkv_ref[:, pl.ds(pair + head * HEAD_DIM, HEAD_DIM)]
                ).astype(bf16)
                return carry

            chunks(attend)
            saves.append(pltpu.make_async_copy(probs_s.at[head], probs_all.at[head], save.at[head]))
            saves[-1].start()

        half_rows = rows // 2
        own = pltpu.make_async_copy(
            attend_ref,
            attend_all.at[:, pl.ds(pl.multiple_of(ring.me * cols, LANES), cols)],
            save.at[heads + 1],
        )
        own.start()
        run_steps(
            steps,
            gather_steps(
                ring,
                lambda half: attend_ref.at[pl.ds(half * half_rows, half_rows)],
                lambda device, half: attend_all.at[
                    pl.ds(half * half_rows, half_rows),
                    pl.ds(pl.multiple_of(device * cols, LANES), cols),
                ],
                ring_send,
                ring_receive,
            ),
        )
        own.wait()
        for copy in saves:
            copy.wait()

    return pl.pallas_call(
        body,
        out_shape=(
            jax.ShapeDtypeStruct((rows, width), bf16),
            jax.ShapeDtypeStruct((weight_rows * n * n_dp, width), bf16),
            jax.ShapeDtypeStruct((heads, rows, rows), bf16),
            jax.ShapeDtypeStruct((rows, width), bf16),
            jax.ShapeDtypeStruct((rows, cols), bf16),
            jax.ShapeDtypeStruct((rows, 3 * cols), bf16),
            jax.ShapeDtypeStruct((rows, pair), f32),
            jax.ShapeDtypeStruct((rows, LANES), f32),
        ),
        in_specs=[VMEM, VMEM, ANY] + [VMEM] * 6,
        out_specs=(ANY,) * 4 + (VMEM,) * 4,
        scratch_shapes=[
            pltpu.VMEM((heads, rows, rows), bf16),
            pltpu.VMEM((rows, width), bf16),
            pltpu.VMEM((8, rows), f32),
            pltpu.VMEM((n - 1, 8, rows), f32),
            sems(3),
            sems(3),
            sems(2, 2, n // 2),
            sems(2, 2, n // 2),
            sems(2, 2, n // 2),
            sems(2, 2, n // 2),
            pltpu.SemaphoreType.DMA,
            sems(n - 1),
            sems(n - 1),
            sems(2, 2, n // 2),
            sems(2, 2, n // 2),
            sems(heads + 2),
        ],
        name="attention_in",
        cost_estimate=pl.CostEstimate(
            flops=2 * rows * width * 3 * cols, bytes_accessed=200_000_000, transcendentals=0
        ),
        compiler_params=pltpu.CompilerParams(
            collective_id=identity, has_side_effects=True, vmem_limit_bytes=BIG_VMEM
        ),
    )(token_all, in_all, out_rows, gain, pair_gains, cosine, sine, bounds, place_row)


def gather_with_gradients(block, mixed, up_all, n, n_dp, identity):
    rows, width = block.shape
    half_rows = rows // 2
    count, inner = up_all.shape[0], up_all.shape[2]
    span, tile, piece = width // n_dp, 256, 64
    bf16, f32 = jnp.bfloat16, jnp.float32

    def body(
        block_ref,
        mixed_ref,
        up_ref,
        all_ref,
        near_ref,
        far_ref,
        far_got,
        mixed_s,
        up_s,
        grad_s,
        core_s,
        send,
        receive,
        core_send,
        core_receive,
        local,
        load,
        save,
        far_send,
        far_receive,
    ):
        ring = Ring(n)
        dp, core, chip, core_chip = partners()
        loads = [pltpu.make_async_copy(mixed_ref, mixed_s, load.at[count])]
        for x in range(count):
            loads.append(pltpu.make_async_copy(up_ref.at[x], up_s.at[x], load.at[x]))
        own = pltpu.make_async_copy(
            block_ref, all_ref.at[pl.ds(pl.multiple_of(ring.me * rows, 16), rows)], local
        )
        own.start()
        for copy in loads:
            copy.start()
        ring.barrier(ring.neighbours() + [{"dp": core}, {"dp": chip}])
        steps = gather_steps(
            ring,
            lambda half: block_ref.at[pl.ds(half * half_rows, half_rows)],
            lambda device, half: all_ref.at[
                pl.ds(pl.multiple_of(device * rows + half * half_rows, 16), half_rows)
            ],
            send,
            receive,
        )
        advance(steps, 2)
        loads[0].wait()
        saves, passed = [], []
        for x in range(count):
            loads[1 + x].wait()
            for at, group in enumerate((core_chip, core, chip, dp)):

                def product(j, carry, x=x, at=at, group=group):
                    columns = pl.ds(pl.multiple_of(group * span + j * tile, tile), tile)
                    grad_s[x, at, pl.ds(pl.multiple_of(j * tile, tile), tile)] = lax.dot_general(
                        mixed_s[:, columns],
                        up_s[x],
                        (((0,), (0,)), ((), ())),
                        preferred_element_type=f32,
                    ).astype(bf16)
                    return carry

                lax.fori_loop(0, span // tile, product, 0)
                which = 1 - at % 2
                if at < 2:
                    passed.append(
                        remote(
                            grad_s.at[x, at],
                            core_s.at[x, which],
                            core_send.at[x, which],
                            core_receive.at[x, which],
                            {"dp": core},
                        )
                    )
                    passed[-1].start()
                else:
                    passed[2 * x + at - 2].wait_recv()

                    def add(j, carry, x=x, at=at, which=which):
                        part = pl.ds(pl.multiple_of(j * piece, piece), piece)
                        core_s[x, which, part] = (
                            core_s[x, which, part].astype(f32) + grad_s[x, at, part].astype(f32)
                        ).astype(bf16)
                        return carry

                    lax.fori_loop(0, span // piece, add, 0)
                    if x == 0 and which:
                        across = remote(
                            core_s.at[0, 1, pl.ds(0, PASS_A)], far_got, far_send, far_receive, {"dp": chip}
                        )
                        across.start()
                    saves.append(
                        pltpu.make_async_copy(
                            core_s.at[x, which],
                            (far_ref if which else near_ref).at[x],
                            save.at[x, which],
                        )
                    )
                    saves[-1].start()
                advance(steps, 2)
        advance(steps, 64)
        for copy in passed:
            copy.wait_send()
        across.wait()
        for copy in saves:
            copy.wait()
        own.wait()

    sums = jax.ShapeDtypeStruct((count, span, inner), bf16)
    return pl.pallas_call(
        body,
        out_shape=(
            jax.ShapeDtypeStruct((rows * n, width), block.dtype),
            sums,
            sums,
            jax.ShapeDtypeStruct((PASS_A, inner), bf16),
        ),
        in_specs=[ANY] * 3,
        out_specs=(ANY,) * 4,
        scratch_shapes=[
            pltpu.VMEM(mixed.shape, bf16),
            pltpu.VMEM(up_all.shape, bf16),
            pltpu.VMEM((count, n_dp, span, inner), bf16),
            pltpu.VMEM((count, 2, span, inner), bf16),
            sems(2, 2, n // 2),
            sems(2, 2, n // 2),
            sems(count, 2),
            sems(count, 2),
            pltpu.SemaphoreType.DMA,
            sems(count + 1),
            sems(count, 2),
            pltpu.SemaphoreType.DMA,
            pltpu.SemaphoreType.DMA,
        ],
        name="gather_with_gradients",
        cost_estimate=pl.CostEstimate(
            flops=2 * count * width * inner * mixed.shape[0],
            bytes_accessed=160_000_000,
            transcendentals=0,
        ),
        compiler_params=pltpu.CompilerParams(
            collective_id=identity, has_side_effects=True, vmem_limit_bytes=BIG_VMEM
        ),
    )(block, mixed, up_all)


def attention_back(
    back_all,
    out_all,
    in_all,
    probs,
    attend_low,
    qkv,
    raw,
    inverse,
    pair_gains,
    cosine,
    sine,
    partial,
    far,
    n,
    n_dp,
    identity,
):
    rows, width = back_all.shape
    weight_rows = width // (n * n_dp)
    pair = pair_gains.shape[1]
    cols = pair // 2
    heads = cols // HEAD_DIM
    chunk, wide = 256, 512
    tok_rows = rows // n
    half_rows = tok_rows // 2
    bf16, f32 = jnp.bfloat16, jnp.float32
    scale = HEAD_DIM ** (-0.5)

    def body(
        back_ref,
        out_ref,
        in_ref,
        probs_ref,
        attend_ref,
        qkv_ref,
        raw_ref,
        inverse_ref,
        pair_ref,
        cos_ref,
        sin_ref,
        part_ref,
        far_ref,
        raw_back,
        row_part,
        pair_sum,
        part_sum,
        out_sum,
        far_got,
        next_got,
        out_s,
        in_s,
        probs_s,
        part_s,
        attend_back,
        pair_s,
        value_s,
        sum_s,
        slots,
        flat,
        got,
        sum_send,
        sum_receive,
        ring_send,
        ring_receive,
        load,
        out_p,
        out_core,
        out_chip,
        pass_send,
        pass_receive,
        far_send,
        far_receive,
    ):
        ring = Ring(n)
        dp, core, chip, core_chip = partners()
        loads = [
            pltpu.make_async_copy(part_ref, part_s, load.at[0]),
            pltpu.make_async_copy(
                out_ref.at[pl.ds(pl.multiple_of(ring.me * cols, 16), cols)], out_s, load.at[1]
            ),
            pltpu.make_async_copy(probs_ref, probs_s, load.at[2]),
            pltpu.make_async_copy(in_ref.at[:, pl.ds(0, pair + cols)], in_s, load.at[3]),
        ]
        for copy in loads:
            copy.start()
        ring.barrier(
            [{"ctx": (ring.me + k) % n} for k in range(1, n)] + [{"dp": core}, {"dp": chip}]
        )

        beyond = [
            remote(
                far_ref.at[0, pl.ds(PASS_A, far_got.shape[0])],
                far_got,
                far_send.at[0],
                far_receive.at[0],
                {"dp": chip},
            ),
            remote(
                far_ref.at[1, pl.ds(0, PASS_B)], next_got, far_send.at[1], far_receive.at[1], {"dp": chip}
            ),
        ]
        for copy in beyond:
            copy.start()

        def store(half, total):
            part_sum[pl.ds(half * half_rows, half_rows)] = total

        steps = scatter_steps(
            ring,
            lambda device, half: part_s.at[
                pl.ds(pl.multiple_of(device * tok_rows + half * half_rows, 16), half_rows)
            ],
            slots,
            store,
            ring_send,
            ring_receive,
        )
        loads[0].wait()
        advance(steps, 1)
        lanes = lax.broadcasted_iota(jnp.int32, (chunk, LANES), 1)

        def chunks(step, count=2):
            total = rows // chunk
            for first in range(0, total, count):
                lax.fori_loop(first, min(first + count, total), step, 0)
                advance(steps, 2)

        loads[1].wait()

        def project(j, carry):
            at = pl.ds(pl.multiple_of(j * chunk, chunk), chunk)
            attend_back[at] = dot_across(back_ref[at], out_s[...]).astype(bf16)
            return carry

        chunks(project, 4)

        def out_product(group):
            for t in range(width // wide):
                value = lax.dot_general(
                    attend_ref[:, group * LANES : (group + 1) * LANES],
                    back_ref[:, t * wide : (t + 1) * wide],
                    (((0,), (0,)), ((), ())),
                    preferred_element_type=f32,
                ).astype(bf16)
                for k in range(LANES // weight_rows):
                    out_p[group * LANES // weight_rows + k, :, t * wide : (t + 1) * wide] = value[
                        k * weight_rows : (k + 1) * weight_rows
                    ]

        for group in range(cols // LANES):
            out_product(group)

        def passing(at, source, target, to):
            return remote(source, target, pass_send.at[at], pass_receive.at[at], {"dp": to})

        passed = [
            passing(0, out_p.at[core_chip], out_core.at[1], core),
            passing(1, out_p.at[core], out_core.at[0], core),
        ]
        for copy in passed:
            copy.start()
        loads[2].wait()
        for head in range(heads):
            columns = pl.ds(head * HEAD_DIM, HEAD_DIM)
            key_columns = pl.ds(cols + head * HEAD_DIM, HEAD_DIM)
            value_columns = pl.ds(pair + head * HEAD_DIM, HEAD_DIM)
            pair_s[:, key_columns] = jnp.zeros((rows, HEAD_DIM), f32)
            value_s[:, columns] = jnp.zeros((rows, HEAD_DIM), f32)

            def scores(j, carry, head=head, columns=columns, key_columns=key_columns, value_columns=value_columns):
                at = pl.ds(pl.multiple_of(j * chunk, chunk), chunk)
                back = attend_back[at, columns]
                delta = jnp.sum(
                    back.astype(f32) * attend_ref[at, columns].astype(f32), axis=-1, keepdims=True
                )
                probs_low = probs_s[head, at]
                score_back = (
                    probs_low.astype(f32) * (dot_across(back, qkv_ref[:, value_columns]) - delta)
                ).astype(bf16)
                pair_s[at, columns] = dot(score_back, qkv_ref[:, key_columns])
                over = (((0,), (0,)), ((), ()))
                pair_s[:, key_columns] += lax.dot_general(
                    score_back, qkv_ref[at, columns], over, preferred_element_type=f32
                )
                value_s[:, columns] += lax.dot_general(
                    probs_low, back, over, preferred_element_type=f32
                )
                return carry

            chunks(scores)
        passed[0].wait_recv()
        out_core[1] = (out_core[1].astype(f32) + out_p[chip].astype(f32)).astype(bf16)
        passed.append(passing(2, out_core.at[1], out_chip, chip))
        passed[-1].start()
        pair_sum[...] = jnp.zeros((8, pair), f32)

        def unturn(j, carry):
            at = pl.ds(pl.multiple_of(j * chunk, chunk), chunk)
            held = jnp.zeros((chunk, LANES), f32)
            for which in range(2):
                total = jnp.zeros((chunk, 1), f32)
                for head in range(heads):
                    columns = pl.ds(which * cols + head * HEAD_DIM, HEAD_DIM)
                    back = turn(pair_s[at, columns] * scale, cos_ref[at], -sin_ref[at])
                    normed = raw_ref[at, columns] * inverse_ref[at, which : which + 1]
                    pair_sum[0:1, columns] += jnp.sum(back * normed, axis=0, keepdims=True)
                    back = back * pair_ref[0:1, columns]
                    pair_s[at, columns] = back
                    total = total + jnp.sum(back * normed, axis=-1, keepdims=True)
                held = jnp.where(lanes == which, total, held)
            sum_s[at] = held
            return carry

        chunks(unturn)
        exchange_rows(ring, sum_s, flat, got, sum_send, sum_receive, steps)
        loads[3].wait()

        def finish(j, carry):
            at = pl.ds(pl.multiple_of(j * chunk, chunk), chunk)
            for which in range(2):
                columns = pl.ds(which * cols, cols)
                factor = inverse_ref[at, which : which + 1]
                normed = raw_ref[at, columns] * factor
                mean = sum_s[at, which : which + 1] / width
                raw_back[at, columns] = (factor * (pair_s[at, columns] - normed * mean)).astype(bf16)
            raw_back[at, pl.ds(pair, cols)] = value_s[at].astype(bf16)
            for t in range(width // wide):
                row_part[at, pl.ds(t * wide, wide)] = dot_across(
                    raw_back[at], in_s[pl.ds(t * wide, wide), :]
                ).astype(bf16)
            return carry

        chunks(finish)
        passed[1].wait_recv()
        passed[2].wait_recv()
        out_sum[...] = (
            out_core[0].astype(f32) + out_p[dp].astype(f32) + out_chip[...].astype(f32)
        ).astype(bf16)
        advance(steps, 64)
        for copy in beyond:
            copy.wait()
        for copy in passed:
            copy.wait_send()

    return pl.pallas_call(
        body,
        out_shape=(
            jax.ShapeDtypeStruct((rows, 3 * cols), bf16),
            jax.ShapeDtypeStruct((rows, width), bf16),
            jax.ShapeDtypeStruct((8, pair), f32),
            jax.ShapeDtypeStruct((tok_rows, width), f32),
            jax.ShapeDtypeStruct((weight_rows, width), bf16),
            jax.ShapeDtypeStruct((far.shape[1] - PASS_A, far.shape[2]), bf16),
            jax.ShapeDtypeStruct((PASS_B, far.shape[2]), bf16),
        ),
        in_specs=[VMEM] + [ANY] * 3 + [VMEM] * 7 + [ANY] * 2,
        out_specs=(VMEM,) * 5 + (ANY,) * 2,
        scratch_shapes=[
            pltpu.VMEM((cols, width), bf16),
            pltpu.VMEM((width, pair + cols), bf16),
            pltpu.VMEM((heads, rows, rows), bf16),
            pltpu.VMEM((rows, width), bf16),
            pltpu.VMEM((rows, cols), bf16),
            pltpu.VMEM((rows, pair), f32),
            pltpu.VMEM((rows, cols), f32),
            pltpu.VMEM((rows, LANES), f32),
            pltpu.VMEM((2, 2, n // 2, half_rows, width), bf16),
            pltpu.VMEM((8, rows), f32),
            pltpu.VMEM((n - 1, 8, rows), f32),
            sems(n - 1),
            sems(n - 1),
            sems(2, 2, n // 2),
            sems(2, 2, n // 2),
            sems(4),
            pltpu.VMEM((n_dp, weight_rows, width), bf16),
            pltpu.VMEM((2, weight_rows, width), bf16),
            pltpu.VMEM((weight_rows, width), bf16),
            sems(3),
            sems(3),
            sems(2),
            sems(2),
        ],
        name="attention_back",
        cost_estimate=pl.CostEstimate(
            flops=2 * rows * width * 4 * cols, bytes_accessed=160_000_000, transcendentals=0
        ),
        compiler_params=pltpu.CompilerParams(
            collective_id=identity, has_side_effects=True, vmem_limit_bytes=BIG_VMEM
        ),
    )(
        back_all,
        out_all,
        in_all,
        probs,
        attend_low,
        qkv,
        raw,
        inverse,
        pair_gains,
        cosine,
        sine,
        partial,
        far,
    )


def heads_local(
    tokens,
    document_ids,
    routes,
    norm_gains,
    project_in,
    project_out,
    router_weight,
    expert_in,
    expert_out,
    cotangent,
):
    bf16, f32 = jnp.bfloat16, jnp.float32
    n = lax.axis_size("ctx")
    n_dp = lax.axis_size("dp")
    me = lax.axis_index("ctx")
    tok_rows, width = tokens.shape[1:]
    rows = tok_rows * n
    weight_rows = project_in.shape[0]
    own_heads = HEADS // n
    cols = own_heads * HEAD_DIM
    local_experts = expert_in.shape[0]
    expert_count = local_experts * n
    score_scale = HEAD_DIM ** (-0.5)

    def own(array, size, axis=0):
        return lax.dynamic_slice_in_dim(array, me * size, size, axis)

    named = jnp.any(routes[0][..., None] == jnp.arange(LANES, dtype=jnp.int32), axis=1).astype(bf16)
    small = jnp.concatenate(
        [norm_gains, router_weight, jnp.zeros((weight_rows, LANES - 4 - expert_count), bf16)], axis=1
    )
    in_blocks = project_in.reshape(weight_rows, 3, n, cols).transpose(2, 0, 1, 3)
    in_blocks = jnp.concatenate(
        [
            in_blocks.reshape(n, weight_rows, 3 * cols),
            jnp.broadcast_to(small[None], (n, weight_rows, LANES)),
        ],
        axis=2,
    )
    token_all, named_all, in_all = gather_inputs(tokens[0], named, in_blocks, n, n_dp, 1)
    named_all = named_all.reshape(rows, LANES)
    in_all = in_all.reshape(width, 3 * cols + LANES)
    small_all = in_all[:, 3 * cols :]
    gains = small_all[:, :4].astype(f32)
    router_all = small_all[:, 4 : 4 + expert_count]
    router_wide = jnp.pad(router_all, ((0, 0), (0, LANES - expert_count)))
    first = lax.all_gather(expert_in, "dp", axis=1, tiled=True)
    second = lax.all_gather(expert_out, "dp", axis=1, tiled=True).reshape(local_experts * FF, width)

    half_rows = tok_rows // 2

    def dealt(row):
        blocks = row.reshape(2 * n, half_rows)
        return jnp.stack([blocks[:n], blocks[n:][::-1]], axis=1).reshape(rows)

    places = dealt(jnp.arange(rows, dtype=jnp.int32))
    document_row = document_ids[0]
    starts = dealt(document_starts(document_row))
    relative = places - starts
    cosine, sine = rotary_tables(relative, HEAD_DIM)
    cosine = jnp.concatenate([cosine[:, 0], cosine[:, 0]], axis=-1)
    sine = jnp.concatenate([-sine[:, 0], sine[:, 0]], axis=-1)
    bounds = jnp.pad(jnp.stack([starts, places], axis=1), ((0, 0), (0, LANES - 2)))
    place_row = jnp.broadcast_to(places[None], (8, rows))
    pair_gains = jnp.broadcast_to(own(gains, cols)[:, 1:3].T.reshape(1, 2 * cols), (8, 2 * cols))

    attend_gain = jnp.broadcast_to(gains[:, 0][None], (8, width))
    attend_all, out_all, probs, attend_in, attend_low, qkv, raw, inverse = attention_in(
        token_all,
        in_all,
        project_out,
        attend_gain,
        pair_gains,
        cosine,
        sine,
        bounds,
        place_row,
        n,
        n_dp,
        10,
    )

    upstream_all, mixed_all, gated_all, up_all, own_gates, gate_back, own_residual = experts_in(
        attend_all,
        token_all,
        cotangent[0],
        out_all,
        first,
        second,
        jnp.broadcast_to(gains[:, 3][None], (8, width)),
        router_wide,
        named_all,
        n,
        8,
    )
    mixed_slots = mixed_all.reshape(rows, width)
    second_back = jnp.einsum(
        "tf,td->fd", gated_all, upstream_all.reshape(rows, width), preferred_element_type=f32
    ).astype(bf16)
    second_back, up_all = lax.optimization_barrier((second_back, up_all))
    expert_out_gradient = lax.psum_scatter(
        second_back.reshape(local_experts, FF, width), "dp", scatter_dimension=1, tiled=True
    ).astype(f32)
    mixed_back, mixture, gate_back = experts_out(up_all, gated_all, first, second, gate_back, n, 9)
    gate_back = gate_back[:, :local_experts]
    place = ring_place(me, n)
    gate_back = sum(
        jnp.where(
            (jnp.arange(n) == ring_device((place + offset + n) % n, n))[:, None, None],
            gate_back[slot],
            0.0,
        )
        for slot, offset in enumerate(slot_offsets(n))
    )
    gate_back = gate_back.reshape(expert_count, tok_rows).T

    own_gates = own_gates[:, :expert_count]
    own_mixed = mixed_all[0]
    own_mixed_inverse = inverse_rms(own_residual)
    own_mixed_normed = own_residual * own_mixed_inverse
    chosen_back = own_gates * (
        gate_back - jnp.sum(own_gates * gate_back, axis=-1, keepdims=True)
    )
    logit_back = chosen_back.astype(bf16)
    router_part = jnp.einsum("td,te->ed", own_mixed, logit_back, preferred_element_type=f32)
    mixed_back = mixed_back + jnp.einsum(
        "te,de->td", logit_back, router_all, preferred_element_type=f32
    )
    mixed_gain_back = jnp.sum(mixed_back * own_mixed_normed, axis=0)
    residual_back = cotangent[0].astype(f32) + normalize_back(
        mixed_back * gains[:, 3], own_mixed_normed, own_mixed_inverse
    )
    back_all, near, far, got_a = gather_with_gradients(
        residual_back.astype(bf16), mixed_slots, up_all, n, n_dp, 5
    )

    raw_back, row_part, pair_sum, mixture, out_part, got_b, got_c = attention_back(
        back_all,
        out_all,
        in_all,
        probs,
        attend_low,
        qkv,
        raw,
        inverse,
        pair_gains,
        cosine,
        sine,
        mixture,
        far,
        n,
        n_dp,
        11,
    )
    layer_output = (own_residual + mixture).astype(bf16)
    pairs = [(d * n + c, c * n_dp + d) for d in range(n_dp) for c in range(n)]
    project_out_gradient = lax.ppermute(out_part, ("dp", "ctx"), pairs).astype(f32)

    small_rows = -(-(4 + expert_count) // 8) * 8
    small_part = jnp.concatenate(
        [
            jnp.zeros((3, width), f32),
            mixed_gain_back[None],
            router_part,
            jnp.zeros((small_rows - 4 - expert_count, width), f32),
        ],
        axis=0,
    )
    tokens_back, project_in_gradient, small_gradient, got_d = scatter_end(
        row_part,
        attend_in,
        raw_back,
        tokens[0],
        residual_back,
        attend_gain,
        small_part,
        pair_sum,
        far,
        n,
        n_dp,
        6,
    )
    expert_in_gradient = near.astype(f32) + (
        jnp.concatenate([got_a, got_b, got_c, got_d], axis=0).reshape(near.shape).astype(f32)
    )
    per_tile = LANES // weight_rows
    small_gradient = lax.dynamic_slice_in_dim(
        small_gradient, me % per_tile * weight_rows, weight_rows, 1
    ).T
    return (
        layer_output[None],
        tokens_back[None],
        small_gradient[:, :4],
        project_in_gradient,
        project_out_gradient,
        small_gradient[:, 4 : 4 + expert_count],
        expert_in_gradient,
        expert_out_gradient,
    )


def layer(*arrays):
    n, tok_rows, experts = lax.axis_size("ctx"), arrays[0].shape[1], arrays[7].shape[0]
    fits = HEADS % n == 0 and n % 4 == 0 and lax.axis_size("dp") == 4
    fits = fits and tok_rows == LANES and experts == 2 and experts * n + 4 <= LANES
    return (heads_local if fits else gathered_local)(*arrays)


def solution(mesh):
    placed = (
        P("dp", "ctx", None),
        P("dp", None),
        P("dp", "ctx", None),
        P(("dp", "ctx"), None),
        P(("dp", "ctx"), None),
        P(("dp", "ctx"), None),
        P(("dp", "ctx"), None),
        P("ctx", "dp", None),
        P("ctx", "dp", None),
        P("dp", "ctx", None),
    )
    return jax.shard_map(
        layer,
        mesh=mesh,
        in_specs=placed,
        out_specs=(
            P("dp", "ctx", None),
            P("dp", "ctx", None),
            P(("dp", "ctx"), None),
            P(("dp", "ctx"), None),
            P(("dp", "ctx"), None),
            P(("dp", "ctx"), None),
            P("ctx", "dp", None),
            P("ctx", "dp", None),
        ),
        check_vma=False,
    )
```

```python
import jax
import jax.numpy as jnp
from jax import lax
from jax.experimental import pallas as pl
from jax.experimental.pallas import tpu as pltpu
from jax.sharding import PartitionSpec as P

HEADS = 16
HEAD_DIM = 128
FF = 1024


EPSILON = 1e-05
ROPE_BASE = 10000.0
MASKED = -1e30
LANES = 128
PASS_A, PASS_B = 256, 256
CUTS = 2
WAITS = (4, 6, 6)
TILE = 512
WIDE = 1024


def inverse_rms(values):
    return lax.rsqrt(jnp.mean(values * values, axis=-1, keepdims=True) + EPSILON)


def normalize_back(normed_back, normed, inverse):
    return inverse * (normed_back - normed * jnp.mean(normed_back * normed, axis=-1, keepdims=True))


def rotary_tables(relative, head_dim):
    half_dim = head_dim // 2
    frequency = ROPE_BASE ** (-jnp.arange(half_dim, dtype=jnp.float32) / half_dim)
    angles = relative.astype(jnp.float32)[..., None] * frequency
    return (jnp.cos(angles)[..., None, :], jnp.sin(angles)[..., None, :])


def rotate(values, cosine, sine_table):
    half_dim = values.shape[-1] // 2
    first_half = values[..., :half_dim]
    second_half = values[..., half_dim:]
    return jnp.concatenate(
        [
            first_half * cosine - second_half * sine_table,
            second_half * cosine + first_half * sine_table,
        ],
        axis=-1,
    )


def dealt_positions(indices, tok_rows, context_size):
    half_block = tok_rows // 2
    device = indices // tok_rows
    within = indices % tok_rows
    block_index = jnp.where(within < half_block, device, 2 * context_size - 1 - device)
    return block_index * half_block + within % half_block


def document_starts(document_row):
    places = jnp.arange(document_row.shape[-1], dtype=jnp.int32)
    head_flag = jnp.ones(document_row.shape[:-1] + (1,), jnp.bool_)
    fresh_start = jnp.concatenate(
        [head_flag, document_row[..., 1:] != document_row[..., :-1]], axis=-1
    )
    return lax.cummax(jnp.where(fresh_start, places, 0), axis=document_row.ndim - 1)


def block_scores(
    query_rows, key_block, query_place, query_document, key_place, key_document, score_scale
):
    scores = (
        jnp.einsum("thd,khd->htk", query_rows, key_block, preferred_element_type=jnp.float32)
        * score_scale
    )
    visible = (
        (key_document[None, :] == query_document[:, None])
        & (key_place[None, :] <= query_place[:, None])
    )[None]
    return (jnp.where(visible, scores, MASKED), visible)


def block_backward(
    query_rows,
    output_back,
    row_logsum,
    row_delta,
    key_block,
    value_block,
    query_place,
    query_document,
    key_place,
    key_document,
    score_scale,
):
    scores, visible = block_scores(
        query_rows, key_block, query_place, query_document, key_place, key_document, score_scale
    )
    prob_rows = jnp.where(visible, jnp.exp(scores - row_logsum[..., None]), 0.0)
    prob_back = jnp.einsum(
        "thd,khd->htk", output_back, value_block, preferred_element_type=jnp.float32
    )
    score_back = (prob_rows * (prob_back - row_delta[..., None])).astype(jnp.bfloat16)
    query_part = (
        jnp.einsum("htk,khd->thd", score_back, key_block, preferred_element_type=jnp.float32)
        * score_scale
    )
    key_part = (
        jnp.einsum("htk,thd->khd", score_back, query_rows, preferred_element_type=jnp.float32)
        * score_scale
    )
    value_part = jnp.einsum(
        "htk,thd->khd",
        prob_rows.astype(jnp.bfloat16),
        output_back,
        preferred_element_type=jnp.float32,
    )
    return (query_part, key_part, value_part)


def dispatch_plan(route_rows, expert_count, capacity):
    flat_routes = route_rows.reshape(-1)
    pair_count = flat_routes.shape[0]
    member = (flat_routes[:, None] == jnp.arange(expert_count, dtype=jnp.int32)[None, :]).astype(
        jnp.int32
    )
    earlier = jnp.cumsum(member, axis=0) - member
    target_slot = flat_routes * capacity + jnp.sum(earlier * member, axis=1)
    slot_owner = (
        jnp.full((expert_count * capacity,), pair_count, jnp.int32)
        .at[target_slot]
        .set(jnp.arange(pair_count, dtype=jnp.int32))
    )
    return (target_slot, slot_owner)


def gathered_local(
    tokens,
    document_ids,
    routes,
    norm_gains,
    project_in,
    project_out,
    router_weight,
    expert_in,
    expert_out,
    cotangent,
):
    inputs = tokens[0].astype(jnp.float32)
    tok_rows, model_width = inputs.shape
    context_size = lax.axis_size("ctx")
    sequence_rows = tok_rows * context_size
    local_experts = expert_in.shape[0]
    expert_count = local_experts * context_size
    route_rows = routes[0]
    top_count = route_rows.shape[1]
    capacity = 2 * tok_rows * top_count // expert_count
    score_scale = HEAD_DIM ** (-0.5)
    key_span = min(512, sequence_rows)
    key_blocks = sequence_rows // key_span
    heads_shape = (tok_rows, HEADS, HEAD_DIM)
    block_shape = (key_blocks, key_span, HEADS, HEAD_DIM)
    slot_shape = (context_size, local_experts * capacity, model_width)
    expert_shape = (context_size, local_experts, capacity, model_width)
    gathered_gains, gathered_in, gathered_out, gathered_router = (
        lax.all_gather(norm_gains, ("dp", "ctx"), axis=0, tiled=True),
        lax.all_gather(project_in, ("dp", "ctx"), axis=0, tiled=True),
        lax.all_gather(project_out, ("dp", "ctx"), axis=0, tiled=True),
        lax.all_gather(router_weight, ("dp", "ctx"), axis=0, tiled=True),
    )
    gathered_first, gathered_second = (
        lax.all_gather(expert_in, "dp", axis=1, tiled=True),
        lax.all_gather(expert_out, "dp", axis=1, tiled=True),
    )
    gain_rows = gathered_gains.astype(jnp.float32)
    own_rows = lax.axis_index("ctx") * tok_rows + jnp.arange(tok_rows, dtype=jnp.int32)
    own_place = dealt_positions(own_rows, tok_rows, context_size)
    all_place = dealt_positions(jnp.arange(sequence_rows, dtype=jnp.int32), tok_rows, context_size)
    document_row = document_ids[0]
    own_document = jnp.take(document_row, own_place)
    all_document = jnp.take(document_row, all_place)
    relative = own_place - jnp.take(document_starts(document_row), own_place)
    cosine, sine_table = rotary_tables(relative, HEAD_DIM)
    attend_inverse = inverse_rms(inputs)
    attend_normed = inputs * attend_inverse
    attend_in = (attend_normed * gain_rows[:, 0]).astype(jnp.bfloat16)
    projected = jnp.dot(attend_in, gathered_in, preferred_element_type=jnp.float32)
    raw_query = projected[:, :model_width]
    raw_key = projected[:, model_width : 2 * model_width]
    query_inverse = inverse_rms(raw_query)
    query_normed = raw_query * query_inverse
    key_inverse = inverse_rms(raw_key)
    key_normed = raw_key * key_inverse
    query_low = rotate(
        (query_normed * gain_rows[:, 1]).reshape(heads_shape), cosine, sine_table
    ).astype(jnp.bfloat16)
    key_low = rotate(
        (key_normed * gain_rows[:, 2]).reshape(heads_shape), cosine, sine_table
    ).astype(jnp.bfloat16)
    value_low = projected[:, 2 * model_width :].astype(jnp.bfloat16)
    key_all, value_all = (
        lax.all_gather(key_low.reshape(tok_rows, model_width), "ctx", axis=0, tiled=True),
        lax.all_gather(value_low, "ctx", axis=0, tiled=True),
    )
    key_split = key_all.reshape(block_shape)
    value_split = value_all.reshape(block_shape)
    place_split = all_place.reshape(key_blocks, key_span)
    document_split = all_document.reshape(key_blocks, key_span)

    def total_step(state_pair, block_args):
        row_peak, row_total = state_pair
        key_block, key_place, key_document = block_args
        scores, visible = block_scores(
            query_low, key_block, own_place, own_document, key_place, key_document, score_scale
        )
        new_peak = jnp.maximum(row_peak, jnp.max(scores, axis=-1))
        fresh_total = jnp.sum(
            jnp.where(visible, jnp.exp(scores - new_peak[..., None]), 0.0), axis=-1
        )
        return ((new_peak, row_total * jnp.exp(row_peak - new_peak) + fresh_total), None)

    start_pair = (
        jnp.full((HEADS, tok_rows), MASKED, jnp.float32),
        jnp.zeros((HEADS, tok_rows), jnp.float32),
    )
    (row_peak, row_total), unused = lax.scan(
        total_step, start_pair, (key_split, place_split, document_split)
    )
    row_logsum = row_peak + jnp.log(row_total)

    def value_step(running, block_args):
        key_block, value_block, key_place, key_document = block_args
        scores, visible = block_scores(
            query_low, key_block, own_place, own_document, key_place, key_document, score_scale
        )
        prob_low = jnp.where(visible, jnp.exp(scores - row_logsum[..., None]), 0.0).astype(
            jnp.bfloat16
        )
        return (
            running
            + jnp.einsum("htk,khd->thd", prob_low, value_block, preferred_element_type=jnp.float32),
            None,
        )

    attend_out, unused = lax.scan(
        value_step,
        jnp.zeros(heads_shape, jnp.float32),
        (key_split, value_split, place_split, document_split),
    )
    attend_low = attend_out.reshape(tok_rows, model_width).astype(jnp.bfloat16)
    residual = inputs + jnp.dot(attend_low, gathered_out, preferred_element_type=jnp.float32)
    mixed_inverse = inverse_rms(residual)
    mixed_normed = residual * mixed_inverse
    mixed_low = (mixed_normed * gain_rows[:, 3]).astype(jnp.bfloat16)
    logits = jnp.dot(mixed_low, gathered_router, preferred_element_type=jnp.float32)
    route_onehot = (route_rows[..., None] == jnp.arange(expert_count, dtype=jnp.int32)).astype(
        jnp.float32
    )
    gate_weights = jax.nn.softmax(jnp.sum(route_onehot * logits[:, None, :], axis=-1), axis=-1)
    target_slot, slot_owner = dispatch_plan(route_rows, expert_count, capacity)
    padded_rows = jnp.concatenate([mixed_low, jnp.zeros((1, model_width), jnp.bfloat16)], axis=0)
    send_rows = jnp.take(padded_rows, slot_owner // top_count, axis=0).reshape(slot_shape)
    received = lax.all_to_all(send_rows, "ctx", split_axis=0, concat_axis=0, tiled=True).reshape(
        expert_shape
    )
    expert_up = jnp.einsum(
        "sxcd,xdf->sxcf", received, gathered_first, preferred_element_type=jnp.float32
    )
    gate_part = expert_up[..., :FF]
    up_part = expert_up[..., FF:]
    sigmoid_gate = jax.nn.sigmoid(gate_part)
    swish_gate = gate_part * sigmoid_gate
    hidden_low = (swish_gate * up_part).astype(jnp.bfloat16)
    expert_result = jnp.einsum(
        "sxcf,xfd->sxcd", hidden_low, gathered_second, preferred_element_type=jnp.float32
    ).astype(jnp.bfloat16)
    returned = lax.all_to_all(
        expert_result.reshape(slot_shape), "ctx", split_axis=0, concat_axis=0, tiled=True
    ).reshape(expert_count * capacity, model_width)
    pair_result = jnp.take(returned, target_slot, axis=0).reshape(tok_rows, top_count, model_width)
    mixture = jnp.sum(gate_weights[..., None] * pair_result, axis=1)
    layer_output = (residual + mixture).astype(jnp.bfloat16)
    upstream = cotangent[0].astype(jnp.float32)
    pair_back = (gate_weights[..., None] * upstream[:, None, :]).astype(jnp.bfloat16)
    gate_back = jnp.sum(pair_result * upstream[:, None, :], axis=-1)
    padded_back = jnp.concatenate(
        [
            pair_back.reshape(tok_rows * top_count, model_width),
            jnp.zeros((1, model_width), jnp.bfloat16),
        ],
        axis=0,
    )
    send_back = jnp.take(padded_back, slot_owner, axis=0).reshape(slot_shape)
    received_back = lax.all_to_all(
        send_back, "ctx", split_axis=0, concat_axis=0, tiled=True
    ).reshape(expert_shape)
    first_back, second_back = (gathered_first, gathered_second)
    hidden_back = jnp.einsum(
        "sxcd,xfd->sxcf", received_back, second_back, preferred_element_type=jnp.float32
    )
    second_weight_back = jnp.einsum(
        "sxcf,sxcd->xfd", hidden_low, received_back, preferred_element_type=jnp.float32
    )
    swish_slope = sigmoid_gate * (1.0 + gate_part * (1.0 - sigmoid_gate))
    up_back = jnp.concatenate(
        [hidden_back * up_part * swish_slope, hidden_back * swish_gate], axis=-1
    ).astype(jnp.bfloat16)
    first_weight_back = jnp.einsum(
        "sxcd,sxcf->xdf", received, up_back, preferred_element_type=jnp.float32
    )
    input_back = jnp.einsum(
        "sxcf,xdf->sxcd", up_back, first_back, preferred_element_type=jnp.float32
    ).astype(jnp.bfloat16)
    expert_in_gradient, expert_out_gradient = (
        lax.psum_scatter(
            first_weight_back.astype(jnp.bfloat16), "dp", scatter_dimension=1, tiled=True
        ).astype(jnp.float32),
        lax.psum_scatter(
            second_weight_back.astype(jnp.bfloat16), "dp", scatter_dimension=1, tiled=True
        ).astype(jnp.float32),
    )
    rows_back = lax.all_to_all(
        input_back.reshape(slot_shape), "ctx", split_axis=0, concat_axis=0, tiled=True
    ).reshape(expert_count * capacity, model_width)
    mixed_back = jnp.sum(
        jnp.take(rows_back, target_slot, axis=0)
        .reshape(tok_rows, top_count, model_width)
        .astype(jnp.float32),
        axis=1,
    )
    gains_back, in_back, out_back, router_back = (
        gathered_gains,
        gathered_in,
        gathered_out,
        gathered_router,
    )
    gain_values = gains_back.astype(jnp.float32)
    chosen_back = gate_weights * (
        gate_back - jnp.sum(gate_weights * gate_back, axis=-1, keepdims=True)
    )
    logit_back = jnp.sum(chosen_back[..., None] * route_onehot, axis=1).astype(jnp.bfloat16)
    router_weight_back = jnp.einsum(
        "td,te->de", mixed_low, logit_back, preferred_element_type=jnp.float32
    )
    mixed_back = mixed_back + jnp.einsum(
        "te,de->td", logit_back, router_back, preferred_element_type=jnp.float32
    )
    mixed_gain_back = jnp.sum(mixed_back * mixed_normed, axis=0)
    residual_back = upstream + normalize_back(
        mixed_back * gain_values[:, 3], mixed_normed, mixed_inverse
    )
    residual_low = residual_back.astype(jnp.bfloat16)
    out_weight_back = jnp.einsum(
        "td,te->de", attend_low, residual_low, preferred_element_type=jnp.float32
    )
    attend_back = (
        jnp.einsum("te,de->td", residual_low, out_back, preferred_element_type=jnp.float32)
        .astype(jnp.bfloat16)
        .reshape(heads_shape)
    )
    row_delta = jnp.einsum("thd,thd->ht", attend_back.astype(jnp.float32), attend_out)

    def back_step(query_acc, block_args):
        key_block, value_block, key_place, key_document = block_args
        query_part, key_part, value_part = block_backward(
            query_low,
            attend_back,
            row_logsum,
            row_delta,
            key_block,
            value_block,
            own_place,
            own_document,
            key_place,
            key_document,
            score_scale,
        )
        return (query_acc + query_part, (key_part, value_part))

    query_back, (key_parts, value_parts) = lax.scan(
        back_step,
        jnp.zeros(heads_shape, jnp.float32),
        (key_split, value_split, place_split, document_split),
    )
    key_back, value_back = (
        lax.psum_scatter(
            key_parts.reshape(sequence_rows, model_width).astype(jnp.bfloat16),
            "ctx",
            scatter_dimension=0,
            tiled=True,
        ).astype(jnp.float32),
        lax.psum_scatter(
            value_parts.reshape(sequence_rows, model_width).astype(jnp.bfloat16),
            "ctx",
            scatter_dimension=0,
            tiled=True,
        ).astype(jnp.float32),
    )
    query_flat = rotate(query_back, cosine, -sine_table).reshape(tok_rows, model_width)
    key_flat = rotate(key_back.reshape(heads_shape), cosine, -sine_table).reshape(
        tok_rows, model_width
    )
    query_gain_back = jnp.sum(query_flat * query_normed, axis=0)
    key_gain_back = jnp.sum(key_flat * key_normed, axis=0)
    raw_query_back = normalize_back(query_flat * gain_values[:, 1], query_normed, query_inverse)
    raw_key_back = normalize_back(key_flat * gain_values[:, 2], key_normed, key_inverse)
    raw_back = jnp.concatenate([raw_query_back, raw_key_back, value_back], axis=-1).astype(
        jnp.bfloat16
    )
    in_weight_back = jnp.einsum(
        "td,tf->df", attend_in, raw_back, preferred_element_type=jnp.float32
    )
    attend_in_back = jnp.einsum("tf,df->td", raw_back, in_back, preferred_element_type=jnp.float32)
    attend_gain_back = jnp.sum(attend_in_back * attend_normed, axis=0)
    tokens_back = residual_back + normalize_back(
        attend_in_back * gain_values[:, 0], attend_normed, attend_inverse
    )
    gain_columns = jnp.stack(
        [attend_gain_back, query_gain_back, key_gain_back, mixed_gain_back], axis=1
    )
    gains_gradient, project_in_gradient, project_out_gradient, router_gradient = (
        lax.psum_scatter(gain_columns, ("dp", "ctx"), scatter_dimension=0, tiled=True),
        lax.psum_scatter(in_weight_back, ("dp", "ctx"), scatter_dimension=0, tiled=True),
        lax.psum_scatter(out_weight_back, ("dp", "ctx"), scatter_dimension=0, tiled=True),
        lax.psum_scatter(router_weight_back, ("dp", "ctx"), scatter_dimension=0, tiled=True),
    )
    return (
        layer_output[None],
        tokens_back.astype(jnp.bfloat16)[None],
        gains_gradient,
        project_in_gradient,
        project_out_gradient,
        router_gradient,
        expert_in_gradient,
        expert_out_gradient,
    )


MESH = pl.DeviceIdType.MESH
VMEM_LIMIT = 48 * 1024 * 1024


def ring_place(device, n):
    odd = device % 2
    return (1 - odd) * (device // 2) + odd * (n - 1 - device // 2)


def ring_device(place, n):
    far = place // (n // 2)
    return (1 - far) * (2 * place) + far * (2 * (n - 1 - place) + 1)


class Ring:
    def __init__(self, n):
        self.n = n
        self.me = lax.axis_index("ctx")
        self.place = ring_place(self.me, n)

    def at(self, offset):
        return ring_device((self.place + offset + self.n) % self.n, self.n)

    def hops(self, way, half):
        return self.n // 2 if way == half else self.n // 2 - 1

    def barrier(self, others):
        semaphore = pltpu.get_barrier_semaphore()
        for other in others:
            pl.semaphore_signal(semaphore, inc=1, device_id=other, device_id_type=MESH)
        pl.semaphore_wait(semaphore, len(others))

    def neighbours(self):
        return [{"ctx": self.at(1)}, {"ctx": self.at(-1)}]


def remote(source, target, send, receive, device):
    return pltpu.make_async_remote_copy(
        src_ref=source,
        dst_ref=target,
        send_sem=send,
        recv_sem=receive,
        device_id=device,
        device_id_type=MESH,
    )


def gather_steps(ring, source, place, send, receive, arrived=None, ready=None):
    signs = (1, -1)

    def copy(way, half, hop):
        origin = ring.at(-signs[way] * hop)
        spot = place(origin, half)
        return remote(
            source(half) if hop == 0 else spot,
            spot,
            send.at[way, half, hop],
            receive.at[way, half, hop],
            {"ctx": ring.at(signs[way])},
        )

    def landed(way, half, hop):
        spot = place(ring.at(-signs[way] * (hop + 1)), half)
        return remote(
            spot,
            spot,
            send.at[way, half, hop],
            receive.at[way, half, hop],
            {"ctx": ring.at(signs[way])},
        )

    started = []
    for half in (0, 1):
        if ready is not None:
            ready(half)
        for way in (0, 1):
            started.append(copy(way, half, 0))
            started[-1].start()
        yield
    for hop in range(ring.n // 2):
        for half in (0, 1):
            for way in (0, 1):
                if hop < ring.hops(way, half):
                    landed(way, half, hop).wait_recv()
                    if hop + 1 < ring.hops(way, half):
                        started.append(copy(way, half, hop + 1))
                        started[-1].start()
                    if arrived is not None:
                        arrived(way, half, hop, ring.at(-signs[way] * (hop + 1)))
                    yield
    for one in started:
        one.wait_send()


def scatter_steps(ring, part, slots, store, send, receive):
    signs = (1, -1)

    def copy(way, half, hop, source):
        return remote(
            source,
            slots.at[way, half, hop],
            send.at[way, half, hop],
            receive.at[way, half, hop],
            {"ctx": ring.at(signs[way])},
        )

    started = []
    for half in (0, 1):
        for way in (0, 1):
            goal = ring.at(signs[way] * ring.hops(way, half))
            started.append(copy(way, half, 0, part(goal, half)))
            started[-1].start()
        yield
    for hop in range(ring.n // 2):
        for half in (0, 1):
            for way in (0, 1):
                last = ring.hops(way, half) - 1
                if hop <= last:
                    slot = slots.at[way, half, hop]
                    copy(way, half, hop, slot).wait_recv()
                    if hop < last:
                        goal = ring.at(signs[way] * (last - hop))
                        slot[...] = (
                            slot[...].astype(jnp.float32)
                            + part(goal, half)[...].astype(jnp.float32)
                        ).astype(slot.dtype)
                        started.append(copy(way, half, hop + 1, slot))
                        started[-1].start()
                    yield
    for half in (0, 1):
        total = part(ring.me, half)[...].astype(jnp.float32)
        for way in (0, 1):
            total = total + slots[way, half, ring.hops(way, half) - 1].astype(jnp.float32)
        store(half, total)
    for one in started:
        one.wait_send()


def run_steps(*tasks):
    tasks = list(tasks)
    while tasks:
        left = []
        for task in tasks:
            try:
                next(task)
                left.append(task)
            except StopIteration:
                pass
        tasks = left


def sems(*shape):
    return pltpu.SemaphoreType.DMA(shape)


def kernel_call(body, outs, in_specs, out_specs, scratch, identity, name, sent):
    return pl.pallas_call(
        body,
        out_shape=outs,
        in_specs=in_specs,
        out_specs=out_specs,
        scratch_shapes=scratch,
        name=name,
        cost_estimate=pl.CostEstimate(flops=0, bytes_accessed=sent, transcendentals=0),
        compiler_params=pltpu.CompilerParams(
            collective_id=identity, has_side_effects=True, vmem_limit_bytes=VMEM_LIMIT
        ),
    )


ANY = pl.BlockSpec(memory_space=pl.ANY)
VMEM = pl.BlockSpec(memory_space=pltpu.VMEM)


def ring_gather(block, n, identity, name, axis=0):
    rows, width = block.shape
    half_rows = rows // 2
    shape = (rows * n, width) if axis == 0 else (rows, width * n)

    def body(block_ref, all_ref, send, receive, local):
        ring = Ring(n)

        def place(device, half):
            if axis == 0:
                return all_ref.at[pl.ds(pl.multiple_of(device * rows + half * half_rows, 16), half_rows)]
            return all_ref.at[
                pl.ds(half * half_rows, half_rows), pl.ds(pl.multiple_of(device * width, 128), width)
            ]

        whole = (
            all_ref.at[pl.ds(pl.multiple_of(ring.me * rows, 16), rows)]
            if axis == 0
            else all_ref.at[:, pl.ds(pl.multiple_of(ring.me * width, 128), width)]
        )
        own = pltpu.make_async_copy(block_ref, whole, local)
        own.start()
        ring.barrier(ring.neighbours())
        run_steps(
            gather_steps(
                ring,
                lambda half: block_ref.at[pl.ds(half * half_rows, half_rows)],
                place,
                send,
                receive,
            )
        )
        own.wait()

    return kernel_call(
        body,
        jax.ShapeDtypeStruct(shape, block.dtype),
        [ANY],
        ANY,
        [sems(2, 2, n // 2), sems(2, 2, n // 2), pltpu.SemaphoreType.DMA],
        identity,
        name,
        block.size * 2 * n * 32,
    )(block)


def ring_scatter(partial, n, identity, name):
    rows, width = partial.shape[0] // n, partial.shape[1]
    half_rows = rows // 2

    def body(part_ref, sum_ref, slots, send, receive):
        ring = Ring(n)
        ring.barrier(ring.neighbours())

        def part(device, half):
            return part_ref.at[pl.ds(pl.multiple_of(device * rows + half * half_rows, 16), half_rows)]

        def store(half, total):
            sum_ref[pl.ds(half * half_rows, half_rows)] = total

        run_steps(scatter_steps(ring, part, slots, store, send, receive))

    return kernel_call(
        body,
        jax.ShapeDtypeStruct((rows, width), jnp.float32),
        [VMEM],
        VMEM,
        [
            pltpu.VMEM((2, 2, n // 2, half_rows, width), partial.dtype),
            sems(2, 2, n // 2),
            sems(2, 2, n // 2),
        ],
        identity,
        name,
        partial.size * 2 * 32,
    )(partial)


def partners():
    dp = lax.axis_index("dp")
    core = dp + 1 - 2 * (dp % 2)
    chip = (dp + 2) % 4
    return dp, core, chip, (core + 2) % 4


def gather_inputs(tokens, named, in_blocks, out_rows, n, n_dp, identity):
    tok_rows, width = tokens.shape

    def body(
        token_ref,
        named_ref,
        in_ref,
        out_ref,
        token_all,
        named_all,
        in_all,
        out_chip,
        token_send,
        token_receive,
        named_send,
        named_receive,
        in_send,
        in_receive,
        pass_send,
        pass_receive,
        local,
        out_send,
        out_receive,
    ):
        ring = Ring(n)
        me = ring.me
        dp, core, chip, core_chip = partners()
        half_rows = tok_rows // 2

        def token_place(device, half):
            return token_all.at[
                pl.ds(pl.multiple_of(device * tok_rows + half * half_rows, 16), half_rows)
            ]

        locals_ = [
            pltpu.make_async_copy(in_ref.at[me], in_all.at[dp, me], local.at[0]),
            pltpu.make_async_copy(
                token_ref,
                token_all.at[pl.ds(pl.multiple_of(me * tok_rows, 16), tok_rows)],
                local.at[1],
            ),
            pltpu.make_async_copy(named_ref, named_all.at[me], local.at[2]),
        ]
        for copy in locals_:
            copy.start()
        others = [(me + k) % n for k in range(1, n)]
        ring.barrier([{"ctx": other} for other in others] + [{"dp": core}, {"dp": chip}])

        direct = [remote(out_ref, out_chip, out_send, out_receive, {"dp": chip})]
        direct[0].start()
        for k, other in enumerate(others):
            direct.append(
                remote(in_ref.at[other], in_all.at[dp, me], in_send.at[k], in_receive.at[k], {"ctx": other})
            )
            direct.append(
                remote(named_ref, named_all.at[me], named_send.at[k], named_receive.at[k], {"ctx": other})
            )
        for copy in direct[1:]:
            copy.start()

        def in_steps():
            passed = []

            def forward(at, k, source, spot, to):
                passed.append(
                    remote(source, spot, pass_send.at[at, k], pass_receive.at[at, k], {"dp": to})
                )
                passed[-1].start()

            def landed(at, k, group, source):
                spot = in_all.at[group, (me - k + n) % n]
                remote(
                    spot, spot, pass_send.at[at, k], pass_receive.at[at, k], {"dp": source}
                ).wait_recv()
                return spot

            for at, to in ((0, chip), (1, core)):
                forward(at, 0, in_ref.at[me], in_all.at[dp, me], to)
            yield
            for k in range(1, n):
                spot = in_all.at[dp, (me - k + n) % n]
                remote(
                    spot, spot, in_send.at[k - 1], in_receive.at[k - 1], {"ctx": others[k - 1]}
                ).wait_recv()
                for at, to in ((0, chip), (1, core)):
                    forward(at, k, spot, spot, to)
                yield
            for k in range(n):
                spot = landed(0, k, chip, chip)
                forward(2, k, spot, spot, core)
                yield
            for at, group in ((1, core), (2, core_chip)):
                for k in range(n):
                    landed(at, k, group, core)
            for copy in passed:
                copy.wait_send()

        run_steps(
            gather_steps(
                ring,
                lambda half: token_ref.at[pl.ds(half * half_rows, half_rows)],
                token_place,
                token_send,
                token_receive,
            ),
            in_steps(),
        )
        for k in range(1, n):
            spot = named_all.at[(me - k + n) % n]
            remote(
                spot, spot, named_send.at[k - 1], named_receive.at[k - 1], {"ctx": others[k - 1]}
            ).wait_recv()
        direct[0].wait_recv()
        for copy in direct:
            copy.wait_send()
        for copy in locals_:
            copy.wait()

    return kernel_call(
        body,
        (
            jax.ShapeDtypeStruct((tok_rows * n, width), tokens.dtype),
            jax.ShapeDtypeStruct((n,) + named.shape, named.dtype),
            jax.ShapeDtypeStruct((n_dp,) + in_blocks.shape, in_blocks.dtype),
            jax.ShapeDtypeStruct(out_rows.shape, out_rows.dtype),
        ),
        [ANY] * 4,
        (ANY,) * 4,
        [sems(2, 2, n // 2)] * 2
        + [sems(n - 1)] * 4
        + [sems(3, n)] * 2
        + [sems(3), pltpu.SemaphoreType.DMA, pltpu.SemaphoreType.DMA],
        identity,
        "gather_inputs",
        200_000_000,
    )(tokens, named, in_blocks, out_rows)


def sum_small_steps(ring, small, near, quarter, got, total, sem):
    pass_send, pass_receive, send, receive = sem
    dp, core, chip, core_chip = partners()
    n, me = ring.n, ring.me
    lanes = quarter.shape[1]
    per_tile = LANES * n // lanes

    def group(at):
        return small.at[:, pl.ds(pl.multiple_of(at * lanes, LANES), lanes)]

    copies = []
    for at, to in enumerate((core_chip, chip, core)):
        copies.append(
            remote(group(to), near.at[at], pass_send.at[at], pass_receive.at[at], {"dp": to})
        )
        copies[-1].start()
    for _ in range(WAITS[1]):
        yield
    value = group(dp)[...]
    for at in range(3):
        copies[at].wait_recv()
        value = value + near[at]
    quarter[...] = value

    def tile(device):
        return quarter.at[:, pl.ds(pl.multiple_of(device // per_tile * LANES, LANES), LANES)]

    for k in range(1, n):
        other = (me + k) % n
        copies.append(
            remote(tile(other), got.at[k - 1], send.at[k - 1], receive.at[k - 1], {"ctx": other})
        )
        copies[-1].start()
    for _ in range(WAITS[2]):
        yield
    value = tile(me)[...]
    for k in range(1, n):
        copies[2 + k].wait_recv()
        value = value + got[k - 1]
    total[...] = value
    for copy in copies:
        copy.wait_send()


def scatter_end(
    row_part, attend_in, raw_back, tokens, residual_back, gain, small, pair_sum, far, n, n_dp, identity
):
    rows, width = row_part.shape[0] // n, row_part.shape[1]
    half_rows = rows // 2
    span = width // n_dp
    weight_rows = span // n
    in_cols = raw_back.shape[1]
    cols = in_cols // 3
    small_rows = small.shape[0]
    bf16, f32 = jnp.bfloat16, jnp.float32

    def body(
        row_ref,
        attend_ref,
        raw_ref,
        token_ref,
        back_ref,
        gain_ref,
        small_ref,
        pair_ref,
        far_ref,
        token_back,
        in_sum,
        small_sum,
        far_got,
        slots,
        row_s,
        attend_s,
        in_part,
        in_core,
        in_chip,
        in_got,
        small_s,
        small_near,
        small_quarter,
        small_got,
        row_send,
        row_receive,
        pass_send,
        pass_receive,
        in_send,
        in_receive,
        small_pass_send,
        small_pass_receive,
        small_send,
        small_receive,
        load,
        far_send,
        far_receive,
    ):
        ring = Ring(n)
        me = ring.me
        dp, core, chip, core_chip = partners()
        others = [(me + k) % n for k in range(1, n)]
        loaded = pltpu.make_async_copy(attend_ref, attend_s, load)
        loaded.start()
        ring.barrier(
            [{"ctx": other} for other in others] + [{"dp": to} for to in (core, chip, core_chip)]
        )

        def part(device, half):
            return row_ref.at[pl.ds(pl.multiple_of(device * rows + half * half_rows, 16), half_rows)]

        def store(half, total):
            row_s[pl.ds(half * half_rows, half_rows)] = total

        half_slots = n // CUTS

        def passing(at, k, source, target, to):
            slots_k = pl.ds(k * half_slots, half_slots)
            return remote(
                source.at[slots_k],
                target.at[slots_k],
                pass_send.at[at, k],
                pass_receive.at[at, k],
                {"dp": to},
            )

        def product(group):
            value = lax.dot_general(
                attend_s[:, pl.ds(pl.multiple_of(group * span, LANES), span)],
                raw_ref[...],
                (((0,), (0,)), ((), ())),
                preferred_element_type=f32,
            ).astype(bf16)
            for device in range(n):
                in_part[group, (device - me + n) % n] = value[
                    device * weight_rows : (device + 1) * weight_rows
                ]

        def weight_steps():
            loaded.wait()
            sent = []
            product(core_chip)
            far = [passing(0, k, in_part.at[core_chip], in_core.at[1], core) for k in range(CUTS)]
            for copy in far:
                copy.start()
            yield
            product(core)
            near = [passing(1, k, in_part.at[core], in_core.at[0], core) for k in range(CUTS)]
            for copy in near:
                copy.start()
            yield
            product(chip)
            across = []
            for k in range(CUTS):
                far[k].wait_recv()

                def add_far(at, carry):
                    in_core[1, at] = (
                        in_core[1, at].astype(f32) + in_part[chip, at].astype(f32)
                    ).astype(bf16)
                    return carry

                lax.fori_loop(k * half_slots, (k + 1) * half_slots, add_far, 0)
                across.append(passing(2, k, in_core.at[1], in_chip, chip))
                across[-1].start()
            beyond = remote(far_ref.at[1, pl.ds(PASS_B, far_got.shape[0])], far_got, far_send, far_receive, {"dp": chip})
            yield
            product(dp)
            for _ in range(2):
                yield
            for k in range(CUTS):
                near[k].wait_recv()
                across[k].wait_recv()

                def add_near(at, carry):
                    in_core[0, at] = (
                        in_core[0, at].astype(f32)
                        + in_part[dp, at].astype(f32)
                        + in_chip[at].astype(f32)
                    ).astype(bf16)
                    return carry

                lax.fori_loop(k * half_slots, (k + 1) * half_slots, add_near, 0)
                for at in range(max(1, k * half_slots), (k + 1) * half_slots):
                    sent.append(
                        remote(
                            in_core.at[0, at],
                            in_got.at[at],
                            in_send.at[at - 1],
                            in_receive.at[at - 1],
                            {"ctx": others[at - 1]},
                        )
                    )
                    sent[-1].start()
                yield
                yield
            beyond.start()
            in_got[0] = in_core[0, 0]
            for _ in range(6):
                yield
            for at in range(n):
                if at:
                    sent[at - 1].wait_recv()
                device = (me - at + n) % n
                for which in range(3):
                    in_sum[
                        :, pl.ds(pl.multiple_of(which * width + device * cols, LANES), cols)
                    ] = in_got[at, :, pl.ds(which * cols, cols)].astype(f32)
            beyond.wait()
            for copy in far + near + across + sent:
                copy.wait_send()

        def row_steps():
            yield from scatter_steps(ring, part, slots, store, row_send, row_receive)
            values = token_ref[...].astype(f32)
            inverse = lax.rsqrt(jnp.mean(values * values, axis=-1, keepdims=True) + EPSILON)
            normed = values * inverse
            back = row_s[...]
            back = back * gain_ref[0:1, :]
            token_back[...] = (
                back_ref[...]
                + inverse * (back - normed * jnp.mean(back * normed, axis=-1, keepdims=True))
            ).astype(bf16)

        def small_steps():
            for _ in range(WAITS[0]):
                yield

            def column_sums(at, total):
                part_rows = pl.ds(pl.multiple_of(at * rows, rows), rows)
                terms = row_ref[part_rows].astype(f32) * attend_s[part_rows].astype(f32)
                return total + jnp.sum(terms, axis=0, keepdims=True)

            total = lax.fori_loop(0, n, column_sums, jnp.zeros((1, width), f32))
            small_s[...] = small_ref[...]
            small_s[0:1, :] = total / gain_ref[0:1, :]
            own = pl.ds(pl.multiple_of(me * cols, LANES), cols)
            small_s[1:2, own] = pair_ref[0:1, :cols]
            small_s[2:3, own] = pair_ref[0:1, cols:]
            yield from sum_small_steps(
                ring,
                small_s,
                small_near,
                small_quarter,
                small_got,
                small_sum,
                (small_pass_send, small_pass_receive, small_send, small_receive),
            )

        run_steps(row_steps(), weight_steps(), small_steps())

    block = (n, weight_rows, in_cols)
    return kernel_call(
        body,
        (
            jax.ShapeDtypeStruct((rows, width), bf16),
            jax.ShapeDtypeStruct((weight_rows, 3 * width), f32),
            jax.ShapeDtypeStruct((small_rows, LANES), f32),
            jax.ShapeDtypeStruct((far.shape[1] - PASS_B, far.shape[2]), bf16),
        ),
        [VMEM, ANY] + [VMEM] * 6 + [ANY],
        (VMEM,) * 3 + (ANY,),
        [
            pltpu.VMEM((2, 2, n // 2, half_rows, width), row_part.dtype),
            pltpu.VMEM((rows, width), f32),
            pltpu.VMEM(attend_in.shape, bf16),
            pltpu.VMEM((n_dp,) + block, bf16),
            pltpu.VMEM((2,) + block, bf16),
            pltpu.VMEM(block, bf16),
            pltpu.VMEM(block, bf16),
            pltpu.VMEM((small_rows, width), f32),
            pltpu.VMEM((3, small_rows, span), f32),
            pltpu.VMEM((small_rows, span), f32),
            pltpu.VMEM((n - 1, small_rows, LANES), f32),
            sems(2, 2, n // 2),
            sems(2, 2, n // 2),
            sems(3, CUTS),
            sems(3, CUTS),
            sems(n - 1),
            sems(n - 1),
            sems(3),
            sems(3),
            sems(n - 1),
            sems(n - 1),
            pltpu.SemaphoreType.DMA,
            pltpu.SemaphoreType.DMA,
            pltpu.SemaphoreType.DMA,
        ],
        identity,
        "scatter_end",
        200_000_000,
    )(row_part, attend_in, raw_back, tokens, residual_back, gain, small, pair_sum, far)


def slot_offsets(n):
    offsets = [0]
    for k in range(1, n // 2):
        offsets += [k, -k]
    return offsets + [n // 2]


def slot_of(offset, n):
    if abs(offset) == n // 2:
        return n - 1
    return 2 * offset - 1 if offset > 0 else -2 * offset


def slot_gather_steps(ring, first, slots, send, receive):
    signs = (1, -1)
    half_rows = slots.shape[1] // 2

    def copy(way, half, hop):
        rows = pl.ds(half * half_rows, half_rows)
        held = slot_of(-signs[way] * hop, ring.n)
        return remote(
            first.at[rows] if hop == 0 else slots.at[held, rows],
            slots.at[slot_of(-signs[way] * (hop + 1), ring.n), rows],
            send.at[way, half, hop],
            receive.at[way, half, hop],
            {"ctx": ring.at(signs[way])},
        )

    started = []
    for half in (0, 1):
        for way in (0, 1):
            started.append(copy(way, half, 0))
            started[-1].start()
    yield
    for hop in range(ring.n // 2):
        for half in (0, 1):
            for way in (0, 1):
                if hop < ring.hops(way, half):
                    copy(way, half, hop).wait_recv()
                    if hop + 1 < ring.hops(way, half):
                        started.append(copy(way, half, hop + 1))
                        started[-1].start()
                    yield
    for one in started:
        one.wait_send()


def advance(steps, count):
    for _ in range(count):
        next(steps, None)


def dot(a, b):
    return jnp.dot(a, b, preferred_element_type=jnp.float32)


def dot_across(a, b):
    return lax.dot_general(a, b, (((1,), (1,)), ((), ())), preferred_element_type=jnp.float32)


def experts_in(
    attend_all, token_all, cotangent, out_all, first, second, gain, router, named, n, identity
):
    tok_rows, width = cotangent.shape
    local_experts, ff = first.shape[0], second.shape[0] // first.shape[0]
    rows = tok_rows * n
    pair = 2 * tok_rows
    part = 4 * tok_rows
    tile, wide = TILE, WIDE
    bf16, f32 = jnp.bfloat16, jnp.float32
    offsets = slot_offsets(n)

    def body(
        attend_ref,
        token_ref,
        back_ref,
        out_ref,
        first_ref,
        second_ref,
        gain_ref,
        router_ref,
        named_ref,
        back_all,
        mixed_all,
        gated_all,
        up_all,
        own_gates,
        gate_back,
        own_residual,
        out_s,
        first_s,
        second_s,
        mixed_s,
        back_s,
        attend_s,
        token_s,
        residual_s,
        gate_s,
        sum_s,
        send,
        receive,
        load,
        weight_load,
        save,
        local,
    ):
        ring = Ring(n)
        lanes = lax.broadcasted_iota(jnp.int32, (pair, LANES), 1)
        part_lanes = lax.broadcasted_iota(jnp.int32, (part, LANES), 1)
        loads = [pltpu.make_async_copy(out_ref, out_s, weight_load.at[0])]
        for x in range(local_experts):
            loads.append(pltpu.make_async_copy(first_ref.at[x], first_s.at[x], weight_load.at[1 + x]))
        loads.append(pltpu.make_async_copy(second_ref, second_s, weight_load.at[1 + local_experts]))

        def row_loads(j):
            copies = []
            for k in range(2):
                device = ring.at(offsets[2 * j + k])
                source = pl.ds(pl.multiple_of(device * tok_rows, 16), tok_rows)
                target = pl.ds(k * tok_rows, tok_rows)
                for at, (array, held) in enumerate(((attend_ref, attend_s), (token_ref, token_s))):
                    copies.append(
                        pltpu.make_async_copy(
                            array.at[source], held.at[j % 2, target], load.at[j % 2, k, at]
                        )
                    )
            return copies

        pending = row_loads(0)
        for copy in pending:
            copy.start()
        loads[0].start()
        own = pltpu.make_async_copy(back_ref, back_s.at[0], local)
        own.start()
        ring.barrier(ring.neighbours())
        steps = slot_gather_steps(ring, back_ref, back_s, send, receive)
        advance(steps, 1)
        loads[0].wait()
        for copy in loads[1:]:
            copy.start()

        saves = []
        for j in range(n // 2):
            for copy in pending:
                copy.wait()
            if j + 1 < n // 2:
                pending = row_loads(j + 1)
                for copy in pending:
                    copy.start()

            def project(t, carry, j=j):
                columns = pl.ds(pl.multiple_of(t * wide, wide), wide)
                residual_s[:, columns] = token_s[j % 2, :, columns].astype(f32) + dot(
                    attend_s[j % 2], out_s[:, columns]
                )
                return carry

            lax.fori_loop(0, width // wide, project, 0)
            residual = residual_s[...]
            if j == 0:
                own_residual[...] = residual[:tok_rows]
            inverse = lax.rsqrt(jnp.mean(residual * residual, axis=-1, keepdims=True) + EPSILON)
            mixed = (residual * inverse * gain_ref[0:1, :]).astype(bf16)
            for k in range(2):
                mixed_s[2 * j + k] = mixed[k * tok_rows : (k + 1) * tok_rows]
            logits = dot(mixed, router_ref[...])
            marks = jnp.concatenate(
                [
                    named_ref[pl.ds(pl.multiple_of(ring.at(offsets[2 * j + k]) * tok_rows, 16), tok_rows)]
                    for k in range(2)
                ],
                axis=0,
            ).astype(f32)
            logits = jnp.where(marks > 0, logits, MASKED)
            powers = jnp.where(
                marks > 0, jnp.exp(logits - jnp.max(logits, axis=-1, keepdims=True)), 0.0
            )
            gates = powers / jnp.sum(powers, axis=-1, keepdims=True)
            if j == 0:
                own_gates[...] = gates[:tok_rows]
            held = jnp.zeros((pair, LANES), f32)
            for x in range(local_experts):
                mine = jnp.sum(
                    jnp.where(lanes == ring.me * local_experts + x, gates, 0.0), axis=-1, keepdims=True
                )
                held = jnp.where(lanes == x, mine, held)
            gate_s[pl.ds(j * pair, pair)] = held
            saves.append(
                pltpu.make_async_copy(
                    mixed_s.at[pl.ds(2 * j, 2)], mixed_all.at[pl.ds(2 * j, 2)], save.at[j]
                )
            )
            saves[-1].start()
            advance(steps, 2)

        counts = rows // part
        outgoing = []
        base = n // 2
        for s in range(counts):
            slots = pl.ds(s * 4, 4)
            part_rows = pl.ds(s * part, part)
            advance(steps, 0 if s < counts - 1 else 64)
            if s == 0:
                own.wait()
            sum_s[part_rows] = jnp.zeros((part, LANES), f32)
            for copy in outgoing:
                copy.wait()
            outgoing = []
            for x in range(local_experts):
                if s == 0:
                    loads[1 + x].wait()
                    if x == 0:
                        loads[1 + local_experts].wait()

                def hidden(t, carry, s=s, x=x, slots=slots, part_rows=part_rows):
                    at = pl.multiple_of(t * tile, tile)
                    mixed = mixed_s[slots].reshape(part, width)
                    back = back_s[slots].reshape(part, width)
                    gate_part = dot(mixed, first_s[x, :, pl.ds(at, tile)])
                    up_part = dot(mixed, first_s[x, :, pl.ds(pl.multiple_of(ff + at, tile), tile)])
                    hidden_back = dot_across(
                        back, second_s[pl.ds(pl.multiple_of(x * ff + at, tile), tile), :]
                    )
                    gate = gate_s[part_rows, x : x + 1]
                    sigmoid = jax.nn.sigmoid(gate_part)
                    swish = gate_part * sigmoid
                    value = swish * up_part
                    out_s[pl.ds(0, part), pl.ds(pl.multiple_of(x * ff + at, tile), tile)] = (
                        value * gate
                    ).astype(bf16)
                    sums = jnp.sum(value * hidden_back, axis=-1, keepdims=True)
                    sum_s[part_rows] = sum_s[part_rows] + jnp.where(part_lanes == x, sums, 0.0)
                    hidden_back = hidden_back * gate
                    slope = sigmoid * (1.0 + gate_part * (1.0 - sigmoid))
                    up_rows = pl.ds((1 + x) * part, part)
                    out_s[up_rows, pl.ds(at, tile)] = (hidden_back * up_part * slope).astype(bf16)
                    out_s[up_rows, pl.ds(pl.multiple_of(ff + at, tile), tile)] = (
                        hidden_back * swish
                    ).astype(bf16)
                    return carry

                pieces = ff // tile
                lax.fori_loop(0, pieces // 2, hidden, 0)
                advance(steps, 2)
                lax.fori_loop(pieces // 2, pieces, hidden, 0)
                advance(steps, 2)
                outgoing.append(
                    pltpu.make_async_copy(
                        out_s.at[pl.ds((1 + x) * part, part)],
                        up_all.at[x, part_rows],
                        save.at[base + 1 + x],
                    )
                )
                outgoing[-1].start()
            outgoing.append(
                pltpu.make_async_copy(out_s.at[pl.ds(0, part)], gated_all.at[part_rows], save.at[base])
            )
            outgoing[-1].start()
        spread = pltpu.make_async_copy(back_s, back_all, local)
        spread.start()
        for k in range(n):
            gate_back[k] = jnp.transpose(sum_s[pl.ds(k * tok_rows, tok_rows)])[:8]
        for copy in saves + outgoing:
            copy.wait()
        spread.wait()

    return pl.pallas_call(
        body,
        out_shape=(
            jax.ShapeDtypeStruct((n, tok_rows, width), bf16),
            jax.ShapeDtypeStruct((n, tok_rows, width), bf16),
            jax.ShapeDtypeStruct((rows, local_experts * ff), bf16),
            jax.ShapeDtypeStruct((local_experts, rows, 2 * ff), bf16),
            jax.ShapeDtypeStruct((tok_rows, LANES), f32),
            jax.ShapeDtypeStruct((n, 8, LANES), f32),
            jax.ShapeDtypeStruct((tok_rows, width), f32),
        ),
        in_specs=[ANY] * 6 + [VMEM] * 3,
        out_specs=(ANY,) * 4 + (VMEM,) * 3,
        scratch_shapes=[
            pltpu.VMEM(out_all.shape, bf16),
            pltpu.VMEM(first.shape, bf16),
            pltpu.VMEM(second.shape, bf16),
            pltpu.VMEM((n, tok_rows, width), bf16),
            pltpu.VMEM((n, tok_rows, width), bf16),
            pltpu.VMEM((2, pair, width), bf16),
            pltpu.VMEM((2, pair, width), bf16),
            pltpu.VMEM((pair, width), f32),
            pltpu.VMEM((rows, LANES), f32),
            pltpu.VMEM((rows, LANES), f32),
            sems(2, 2, n // 2),
            sems(2, 2, n // 2),
            sems(2, 2, 2),
            sems(2 + local_experts),
            sems(n // 2 + 1 + local_experts),
            pltpu.SemaphoreType.DMA,
        ],
        name="experts_in",
        cost_estimate=pl.CostEstimate(
            flops=2 * rows * width * (width + 3 * ff * local_experts),
            bytes_accessed=60_000_000,
            transcendentals=0,
        ),
        compiler_params=pltpu.CompilerParams(
            collective_id=identity, has_side_effects=True, vmem_limit_bytes=BIG_VMEM
        ),
    )(attend_all, token_all, cotangent, out_all, first, second, gain, router, named)


BIG_VMEM = 60 * 1024 * 1024


def slot_scatter_steps(ring, parts, slots, store, send, receive, need):
    signs = (1, -1)
    half_rows = parts.shape[1] // 2
    f32 = jnp.float32

    def part(offset, half):
        return parts.at[slot_of(offset, ring.n), pl.ds(half * half_rows, half_rows)]

    def copy(way, half, hop, source):
        return remote(
            source,
            slots.at[way, half, hop],
            send.at[way, half, hop],
            receive.at[way, half, hop],
            {"ctx": ring.at(signs[way])},
        )

    started = []
    firsts = [(way, half) for half in (0, 1) for way in (0, 1)]
    firsts.sort(key=lambda one: -slot_of(signs[one[0]] * ring.hops(*one), ring.n))
    for way, half in firsts:
        goal = signs[way] * ring.hops(way, half)
        need(slot_of(goal, ring.n))
        started.append(copy(way, half, 0, part(goal, half)))
        started[-1].start()
    for hop in range(ring.n // 2):
        for way, half in firsts:
            last = ring.hops(way, half) - 1
            if hop <= last:
                slot = slots.at[way, half, hop]
                if hop < last:
                    goal = signs[way] * (last - hop)
                    need(slot_of(goal, ring.n))
                copy(way, half, hop, slot).wait_recv()
                if hop < last:
                    slot[...] = (
                        slot[...].astype(f32) + part(goal, half)[...].astype(f32)
                    ).astype(slot.dtype)
                    started.append(copy(way, half, hop + 1, slot))
                    started[-1].start()
                yield
    need(0)
    for half in (0, 1):
        total = part(0, half)[...].astype(f32)
        for way in (0, 1):
            total = total + slots[way, half, ring.hops(way, half) - 1].astype(f32)
        store(half, total)
    for one in started:
        one.wait_send()


def experts_out(up_all, gated_all, first, second, gate_back, n, identity):
    local_experts, rows, inner = up_all.shape
    width = first.shape[1]
    tok_rows = rows // n
    half_rows = tok_rows // 2
    pair = 2 * tok_rows
    wide = 512
    count = width // wide
    bf16, f32 = jnp.bfloat16, jnp.float32
    offsets = slot_offsets(n)

    def body(
        up_ref,
        gated_ref,
        first_ref,
        second_ref,
        gate_ref,
        row_sum,
        result_all,
        gate_got,
        first_s,
        second_s,
        up_s,
        gated_s,
        part_s,
        result_s,
        slots,
        send,
        receive,
        gate_send,
        gate_receive,
        load,
        first_load,
        other_load,
        save,
    ):
        ring = Ring(n)

        def up_load(j):
            return pltpu.make_async_copy(
                up_ref.at[:, pl.ds(j * pair, pair)], up_s.at[:, pl.ds(j * pair, pair)], load.at[j]
            )

        def weight_load(t):
            return pltpu.make_async_copy(
                first_ref.at[:, pl.ds(t * wide, wide)],
                first_s.at[:, pl.ds(t * wide, wide)],
                first_load.at[t],
            )

        groups = n // 2
        up_load(groups - 1).start()
        for t in range(count):
            weight_load(t).start()
        for j in range(groups - 1):
            up_load(groups - 2 - j).start()
        others = [
            pltpu.make_async_copy(gated_ref, gated_s, other_load.at[0]),
            pltpu.make_async_copy(second_ref, second_s, other_load.at[1]),
        ]
        for copy in others:
            copy.start()
        ring.barrier([{"ctx": ring.at(k)} for k in range(1, n)])
        gate_copies = []
        for k in range(1, n):
            offset = k if k <= n // 2 else k - n
            back = -offset if offset < n // 2 else offset
            gate_copies.append(
                remote(
                    gate_ref.at[slot_of(offset, n)],
                    gate_got.at[slot_of(back, n)],
                    gate_send.at[slot_of(back, n)],
                    gate_receive.at[slot_of(back, n)],
                    {"ctx": ring.at(k)},
                )
            )
            gate_copies[-1].start()
        gate_got[0] = gate_ref[0]

        done = set()

        def product(j):
            rows_j = pl.ds(j * pair, pair)
            up_load(j).wait()

            def columns(t):
                at = pl.ds(pl.multiple_of(t * wide, wide), wide)
                value = dot_across(up_s[0, rows_j], first_s[0, at, :])
                for x in range(1, local_experts):
                    value = value + dot_across(up_s[x, rows_j], first_s[x, at, :])
                value = value.astype(bf16)
                for k in range(2):
                    part_s[2 * j + k, :, at] = value[k * tok_rows : (k + 1) * tok_rows]

            if not done:
                for t in range(count):
                    weight_load(t).wait()
                    columns(t)
            else:

                def step(t, carry):
                    columns(t)
                    return carry

                lax.fori_loop(0, count, step, 0)
            done.add(j)

        def need(slot):
            if slot // 2 not in done:
                product(slot // 2)

        def store(half, total):
            row_sum[pl.ds(half * half_rows, half_rows)] = total

        steps = slot_scatter_steps(ring, part_s, slots, store, send, receive, need)
        for j in reversed(range(groups)):
            need(2 * j)
            advance(steps, 1 if j in (0, groups - 1) else 2)
        for copy in others:
            copy.wait()
        saves = []
        chunk = 2
        for j in range(n // chunk):
            rows_j = pl.ds(j * chunk * tok_rows, chunk * tok_rows)

            def result(t, carry, rows_j=rows_j, j=j):
                at = pl.ds(pl.multiple_of(t * wide, wide), wide)
                value = dot(gated_s[rows_j], second_s[:, at]).astype(bf16)
                for k in range(chunk):
                    result_s[chunk * j + k, :, at] = value[k * tok_rows : (k + 1) * tok_rows]
                return carry

            lax.fori_loop(0, count, result, 0)
            for k in range(chunk):
                slot = chunk * j + k
                device = ring.at(offsets[slot])
                saves.append(
                    pltpu.make_async_copy(
                        result_s.at[slot],
                        result_all.at[pl.ds(pl.multiple_of(device * tok_rows, 16), tok_rows)],
                        save.at[slot],
                    )
                )
                saves[-1].start()
            advance(steps, 2)
        advance(steps, 64)
        for copy in saves:
            copy.wait()
        for copy in gate_copies:
            copy.wait()

    return pl.pallas_call(
        body,
        out_shape=(
            jax.ShapeDtypeStruct((tok_rows, width), f32),
            jax.ShapeDtypeStruct((rows, width), bf16),
            jax.ShapeDtypeStruct(gate_back.shape, f32),
        ),
        in_specs=[ANY] * 4 + [VMEM],
        out_specs=(VMEM, ANY, VMEM),
        scratch_shapes=[
            pltpu.VMEM(first.shape, bf16),
            pltpu.VMEM(second.shape, bf16),
            pltpu.VMEM(up_all.shape, bf16),
            pltpu.VMEM(gated_all.shape, bf16),
            pltpu.VMEM((n, tok_rows, width), bf16),
            pltpu.VMEM((n, tok_rows, width), bf16),
            pltpu.VMEM((2, 2, n // 2, half_rows, width), bf16),
            sems(2, 2, n // 2),
            sems(2, 2, n // 2),
            sems(n),
            sems(n),
            sems(n // 2),
            sems(count),
            sems(2),
            sems(n),
        ],
        name="experts_out",
        cost_estimate=pl.CostEstimate(
            flops=2 * rows * width * 3 * inner // 2 * local_experts,
            bytes_accessed=60_000_000,
            transcendentals=0,
        ),
        compiler_params=pltpu.CompilerParams(
            collective_id=identity, has_side_effects=True, vmem_limit_bytes=BIG_VMEM
        ),
    )(up_all, gated_all, first, second, gate_back)


def exchange_rows(ring, sums, flat, got, send, receive, steps):
    n, rows = ring.n, sums.shape[0]
    for k in range(rows // LANES):
        flat[:, pl.ds(k * LANES, LANES)] = jnp.transpose(sums[pl.ds(k * LANES, LANES)])[:8]
    copies = []
    for k in range(1, n):
        copies.append(
            remote(
                flat,
                got.at[k - 1],
                send.at[k - 1],
                receive.at[k - 1],
                {"ctx": (ring.me + k) % n},
            )
        )
        copies[-1].start()
    advance(steps, 1)
    for copy in copies:
        copy.wait_recv()
    total = flat[...]
    for k in range(n - 1):
        total = total + got[k]
    for k in range(rows // LANES):
        block = total[:, k * LANES : (k + 1) * LANES]
        block = jnp.concatenate([block, jnp.zeros((LANES - 8, LANES), jnp.float32)], axis=0)
        sums[pl.ds(k * LANES, LANES)] = jnp.transpose(block)
    for copy in copies:
        copy.wait_send()


def turn(values, cosine, sine):
    return values * cosine + pltpu.roll(values, HEAD_DIM // 2, 1) * sine


def out_gather_steps(ring, out_ref, chip_ref, out_all, sem):
    own_send, own_receive, ring_send, ring_receive, core_send, core_receive, local = sem
    dp, core, chip, core_chip = partners()
    weight_rows, n, me = out_ref.shape[0], ring.n, ring.me

    def place(group, device):
        return out_all.at[pl.ds(pl.multiple_of((group * n + device) * weight_rows, 16), weight_rows)]

    own = [
        pltpu.make_async_copy(out_ref, place(dp, me), local.at[0]),
        pltpu.make_async_copy(chip_ref, place(chip, me), local.at[1]),
    ]
    copies = [
        remote(out_ref, place(dp, me), own_send.at[0], own_receive.at[0], {"dp": core}),
        remote(chip_ref, place(chip, me), own_send.at[1], own_receive.at[1], {"dp": core}),
    ]
    for copy in own:
        copy.start()

    def arrived(way, half, hop, origin):
        if len(copies) == 2:
            for copy in copies:
                copy.start()
        spot = place(chip if half else dp, origin)
        copies.append(
            remote(
                spot, spot, core_send.at[way, half, hop], core_receive.at[way, half, hop], {"dp": core}
            )
        )
        copies[-1].start()

    yield from gather_steps(
        ring,
        lambda half: chip_ref if half else out_ref,
        lambda device, half: place(chip if half else dp, device),
        ring_send,
        ring_receive,
        arrived,
    )
    for at, group in ((0, core), (1, core_chip)):
        spot = place(group, me)
        remote(spot, spot, own_send.at[at], own_receive.at[at], {"dp": core}).wait_recv()
    for way, sign in ((0, 1), (1, -1)):
        for half in (0, 1):
            for hop in range(ring.hops(way, half)):
                spot = place(core_chip if half else core, ring.at(-sign * (hop + 1)))
                remote(
                    spot,
                    spot,
                    core_send.at[way, half, hop],
                    core_receive.at[way, half, hop],
                    {"dp": core},
                ).wait_recv()
    for copy in copies:
        copy.wait_send()
    for copy in own:
        copy.wait()


def attention_in(
    token_all, in_all, out_rows, out_chip, gain, pair_gains, cosine, sine, bounds, place_row, n, n_dp, identity
):
    rows, width = token_all.shape
    pair = pair_gains.shape[1]
    cols = pair // 2
    heads = cols // HEAD_DIM
    chunk = 256
    weight_rows = out_rows.shape[0]
    bf16, f32 = jnp.bfloat16, jnp.float32
    scale = HEAD_DIM ** (-0.5)

    def body(
        token_ref,
        in_ref,
        out_ref,
        chip_ref,
        gain_ref,
        pair_ref,
        cos_ref,
        sin_ref,
        bound_ref,
        place_ref,
        attend_all,
        out_all,
        probs_all,
        normed_all,
        attend_ref,
        qkv_ref,
        raw_ref,
        inverse_ref,
        probs_s,
        normed_s,
        flat,
        got,
        *sem,
    ):
        out_sem, sem = sem[:7], sem[7:]
        sum_send, sum_receive, ring_send, ring_receive, save = sem
        ring = Ring(n)
        dp, core, chip, core_chip = partners()
        ring.barrier([{"ctx": (ring.me + k) % n} for k in range(1, n)] + [{"dp": core}])
        steps = out_gather_steps(ring, out_ref, chip_ref, out_all, out_sem)
        advance(steps, 1)
        lanes = lax.broadcasted_iota(jnp.int32, (chunk, LANES), 1)

        def chunks(step, count=2):
            total = rows // chunk
            for first in range(0, total, count):
                lax.fori_loop(first, min(first + count, total), step, 0)
                advance(steps, 1)

        def project(j, carry):
            at = pl.ds(pl.multiple_of(j * chunk, chunk), chunk)
            values = token_ref[at].astype(f32)
            inverse = lax.rsqrt(jnp.mean(values * values, axis=-1, keepdims=True) + EPSILON)
            normed = (values * inverse * gain_ref[0:1, :]).astype(bf16)
            normed_s[at] = normed
            projected = dot(normed, in_ref[:, : pair + cols])
            raw_ref[at] = projected[:, :pair]
            qkv_ref[at, pair:] = projected[:, pair:].astype(bf16)
            squares = projected[:, :pair] * projected[:, :pair]
            inverse_ref[at] = jnp.where(
                lanes == 0,
                jnp.sum(squares[:, :cols], axis=-1, keepdims=True),
                jnp.where(lanes == 1, jnp.sum(squares[:, cols:], axis=-1, keepdims=True), 0.0),
            )
            return carry

        chunks(project)
        saves = [pltpu.make_async_copy(normed_s, normed_all, save.at[heads])]
        saves[0].start()
        exchange_rows(ring, inverse_ref, flat, got, sum_send, sum_receive, steps)

        def norm(j, carry):
            at = pl.ds(pl.multiple_of(j * chunk, chunk), chunk)
            inverse = lax.rsqrt(inverse_ref[at] / width + EPSILON)
            inverse_ref[at] = inverse
            for which in range(2):
                for head in range(heads):
                    columns = pl.ds(which * cols + head * HEAD_DIM, HEAD_DIM)
                    values = raw_ref[at, columns] * inverse[:, which : which + 1]
                    values = values * pair_ref[0:1, columns]
                    qkv_ref[at, columns] = turn(values, cos_ref[at], sin_ref[at]).astype(bf16)
            return carry

        chunks(norm)
        for head in range(heads):

            def attend(j, carry, head=head):
                at = pl.ds(pl.multiple_of(j * chunk, chunk), chunk)
                columns = pl.ds(head * HEAD_DIM, HEAD_DIM)
                scores = (
                    dot_across(
                        qkv_ref[at, columns], qkv_ref[:, pl.ds(cols + head * HEAD_DIM, HEAD_DIM)]
                    )
                    * scale
                )
                place = place_ref[0:1, :]
                visible = (place >= bound_ref[at, 0:1]) & (place <= bound_ref[at, 1:2])
                scores = jnp.where(visible, scores, MASKED)
                powers = jnp.where(
                    visible, jnp.exp(scores - jnp.max(scores, axis=-1, keepdims=True)), 0.0
                )
                share = 1.0 / jnp.sum(powers, axis=-1, keepdims=True)
                probs = (powers * share).astype(bf16)
                probs_s[head, at] = probs
                attend_ref[at, columns] = dot(
                    probs, qkv_ref[:, pl.ds(pair + head * HEAD_DIM, HEAD_DIM)]
                ).astype(bf16)
                return carry

            chunks(attend)
            saves.append(pltpu.make_async_copy(probs_s.at[head], probs_all.at[head], save.at[head]))
            saves[-1].start()

        half_rows = rows // 2
        own = pltpu.make_async_copy(
            attend_ref,
            attend_all.at[:, pl.ds(pl.multiple_of(ring.me * cols, LANES), cols)],
            save.at[heads + 1],
        )
        own.start()
        run_steps(
            steps,
            gather_steps(
                ring,
                lambda half: attend_ref.at[pl.ds(half * half_rows, half_rows)],
                lambda device, half: attend_all.at[
                    pl.ds(half * half_rows, half_rows),
                    pl.ds(pl.multiple_of(device * cols, LANES), cols),
                ],
                ring_send,
                ring_receive,
            ),
        )
        own.wait()
        for copy in saves:
            copy.wait()

    return pl.pallas_call(
        body,
        out_shape=(
            jax.ShapeDtypeStruct((rows, width), bf16),
            jax.ShapeDtypeStruct((weight_rows * n * n_dp, width), bf16),
            jax.ShapeDtypeStruct((heads, rows, rows), bf16),
            jax.ShapeDtypeStruct((rows, width), bf16),
            jax.ShapeDtypeStruct((rows, cols), bf16),
            jax.ShapeDtypeStruct((rows, 3 * cols), bf16),
            jax.ShapeDtypeStruct((rows, pair), f32),
            jax.ShapeDtypeStruct((rows, LANES), f32),
        ),
        in_specs=[VMEM, VMEM, ANY, ANY] + [VMEM] * 6,
        out_specs=(ANY,) * 4 + (VMEM,) * 4,
        scratch_shapes=[
            pltpu.VMEM((heads, rows, rows), bf16),
            pltpu.VMEM((rows, width), bf16),
            pltpu.VMEM((8, rows), f32),
            pltpu.VMEM((n - 1, 8, rows), f32),
            sems(2),
            sems(2),
            sems(2, 2, n // 2),
            sems(2, 2, n // 2),
            sems(2, 2, n // 2),
            sems(2, 2, n // 2),
            sems(2),
            sems(n - 1),
            sems(n - 1),
            sems(2, 2, n // 2),
            sems(2, 2, n // 2),
            sems(heads + 2),
        ],
        name="attention_in",
        cost_estimate=pl.CostEstimate(
            flops=2 * rows * width * 3 * cols, bytes_accessed=200_000_000, transcendentals=0
        ),
        compiler_params=pltpu.CompilerParams(
            collective_id=identity, has_side_effects=True, vmem_limit_bytes=BIG_VMEM
        ),
    )(token_all, in_all, out_rows, out_chip, gain, pair_gains, cosine, sine, bounds, place_row)


def gather_with_gradients(block, mixed, up_all, n, n_dp, identity):
    rows, width = block.shape
    half_rows = rows // 2
    count, inner = up_all.shape[0], up_all.shape[2]
    span, tile, piece = width // n_dp, 256, 64
    bf16, f32 = jnp.bfloat16, jnp.float32

    def body(
        block_ref,
        mixed_ref,
        up_ref,
        all_ref,
        near_ref,
        far_ref,
        far_got,
        mixed_s,
        up_s,
        grad_s,
        core_s,
        send,
        receive,
        core_send,
        core_receive,
        local,
        load,
        save,
        far_send,
        far_receive,
    ):
        ring = Ring(n)
        dp, core, chip, core_chip = partners()
        loads = [pltpu.make_async_copy(mixed_ref, mixed_s, load.at[count])]
        for x in range(count):
            loads.append(pltpu.make_async_copy(up_ref.at[x], up_s.at[x], load.at[x]))
        own = pltpu.make_async_copy(
            block_ref, all_ref.at[pl.ds(pl.multiple_of(ring.me * rows, 16), rows)], local
        )
        own.start()
        for copy in loads:
            copy.start()
        ring.barrier(ring.neighbours() + [{"dp": core}, {"dp": chip}])
        steps = gather_steps(
            ring,
            lambda half: block_ref.at[pl.ds(half * half_rows, half_rows)],
            lambda device, half: all_ref.at[
                pl.ds(pl.multiple_of(device * rows + half * half_rows, 16), half_rows)
            ],
            send,
            receive,
        )
        advance(steps, 2)
        loads[0].wait()
        saves, passed = [], []
        for x in range(count):
            loads[1 + x].wait()
            for at, group in enumerate((core_chip, core, chip, dp)):

                def product(j, carry, x=x, at=at, group=group):
                    columns = pl.ds(pl.multiple_of(group * span + j * tile, tile), tile)
                    grad_s[x, at, pl.ds(pl.multiple_of(j * tile, tile), tile)] = lax.dot_general(
                        mixed_s[:, columns],
                        up_s[x],
                        (((0,), (0,)), ((), ())),
                        preferred_element_type=f32,
                    ).astype(bf16)
                    return carry

                lax.fori_loop(0, span // tile, product, 0)
                which = 1 - at % 2
                if at < 2:
                    passed.append(
                        remote(
                            grad_s.at[x, at],
                            core_s.at[x, which],
                            core_send.at[x, which],
                            core_receive.at[x, which],
                            {"dp": core},
                        )
                    )
                    passed[-1].start()
                else:
                    passed[2 * x + at - 2].wait_recv()

                    def add(j, carry, x=x, at=at, which=which):
                        part = pl.ds(pl.multiple_of(j * piece, piece), piece)
                        core_s[x, which, part] = (
                            core_s[x, which, part].astype(f32) + grad_s[x, at, part].astype(f32)
                        ).astype(bf16)
                        return carry

                    lax.fori_loop(0, span // piece, add, 0)
                    if x == 0 and which:
                        across = remote(
                            core_s.at[0, 1, pl.ds(0, PASS_A)], far_got, far_send, far_receive, {"dp": chip}
                        )
                        across.start()
                    saves.append(
                        pltpu.make_async_copy(
                            core_s.at[x, which],
                            (far_ref if which else near_ref).at[x],
                            save.at[x, which],
                        )
                    )
                    saves[-1].start()
                advance(steps, 2)
        advance(steps, 64)
        for copy in passed:
            copy.wait_send()
        across.wait()
        for copy in saves:
            copy.wait()
        own.wait()

    sums = jax.ShapeDtypeStruct((count, span, inner), bf16)
    return pl.pallas_call(
        body,
        out_shape=(
            jax.ShapeDtypeStruct((rows * n, width), block.dtype),
            sums,
            sums,
            jax.ShapeDtypeStruct((PASS_A, inner), bf16),
        ),
        in_specs=[ANY] * 3,
        out_specs=(ANY,) * 4,
        scratch_shapes=[
            pltpu.VMEM(mixed.shape, bf16),
            pltpu.VMEM(up_all.shape, bf16),
            pltpu.VMEM((count, n_dp, span, inner), bf16),
            pltpu.VMEM((count, 2, span, inner), bf16),
            sems(2, 2, n // 2),
            sems(2, 2, n // 2),
            sems(count, 2),
            sems(count, 2),
            pltpu.SemaphoreType.DMA,
            sems(count + 1),
            sems(count, 2),
            pltpu.SemaphoreType.DMA,
            pltpu.SemaphoreType.DMA,
        ],
        name="gather_with_gradients",
        cost_estimate=pl.CostEstimate(
            flops=2 * count * width * inner * mixed.shape[0],
            bytes_accessed=160_000_000,
            transcendentals=0,
        ),
        compiler_params=pltpu.CompilerParams(
            collective_id=identity, has_side_effects=True, vmem_limit_bytes=BIG_VMEM
        ),
    )(block, mixed, up_all)


def attention_back(
    back_all,
    out_all,
    in_all,
    probs,
    attend_low,
    qkv,
    raw,
    inverse,
    pair_gains,
    cosine,
    sine,
    partial,
    far,
    n,
    n_dp,
    identity,
):
    rows, width = back_all.shape
    weight_rows = width // (n * n_dp)
    pair = pair_gains.shape[1]
    cols = pair // 2
    heads = cols // HEAD_DIM
    chunk, wide = 256, 512
    tok_rows = rows // n
    half_rows = tok_rows // 2
    bf16, f32 = jnp.bfloat16, jnp.float32
    scale = HEAD_DIM ** (-0.5)

    def body(
        back_ref,
        out_ref,
        in_ref,
        probs_ref,
        attend_ref,
        qkv_ref,
        raw_ref,
        inverse_ref,
        pair_ref,
        cos_ref,
        sin_ref,
        part_ref,
        far_ref,
        raw_back,
        row_part,
        pair_sum,
        part_sum,
        out_sum,
        far_got,
        next_got,
        out_s,
        in_s,
        probs_s,
        part_s,
        attend_back,
        pair_s,
        value_s,
        sum_s,
        slots,
        flat,
        got,
        sum_send,
        sum_receive,
        ring_send,
        ring_receive,
        load,
        out_p,
        out_core,
        out_chip,
        pass_send,
        pass_receive,
        far_send,
        far_receive,
    ):
        ring = Ring(n)
        dp, core, chip, core_chip = partners()
        loads = [
            pltpu.make_async_copy(part_ref, part_s, load.at[0]),
            pltpu.make_async_copy(
                out_ref.at[pl.ds(pl.multiple_of(ring.me * cols, 16), cols)], out_s, load.at[1]
            ),
            pltpu.make_async_copy(probs_ref, probs_s, load.at[2]),
            pltpu.make_async_copy(in_ref.at[:, pl.ds(0, pair + cols)], in_s, load.at[3]),
        ]
        for copy in loads:
            copy.start()
        ring.barrier(
            [{"ctx": (ring.me + k) % n} for k in range(1, n)] + [{"dp": core}, {"dp": chip}]
        )

        beyond = [
            remote(
                far_ref.at[0, pl.ds(PASS_A, far_got.shape[0])],
                far_got,
                far_send.at[0],
                far_receive.at[0],
                {"dp": chip},
            ),
            remote(
                far_ref.at[1, pl.ds(0, PASS_B)], next_got, far_send.at[1], far_receive.at[1], {"dp": chip}
            ),
        ]
        for copy in beyond:
            copy.start()

        def store(half, total):
            part_sum[pl.ds(half * half_rows, half_rows)] = total

        steps = scatter_steps(
            ring,
            lambda device, half: part_s.at[
                pl.ds(pl.multiple_of(device * tok_rows + half * half_rows, 16), half_rows)
            ],
            slots,
            store,
            ring_send,
            ring_receive,
        )
        loads[0].wait()
        advance(steps, 1)
        lanes = lax.broadcasted_iota(jnp.int32, (chunk, LANES), 1)

        def chunks(step, count=2):
            total = rows // chunk
            for first in range(0, total, count):
                lax.fori_loop(first, min(first + count, total), step, 0)
                advance(steps, 2)

        loads[1].wait()

        def project(j, carry):
            at = pl.ds(pl.multiple_of(j * chunk, chunk), chunk)
            attend_back[at] = dot_across(back_ref[at], out_s[...]).astype(bf16)
            return carry

        chunks(project, 4)

        def out_product(group):
            for t in range(width // wide):
                value = lax.dot_general(
                    attend_ref[:, group * LANES : (group + 1) * LANES],
                    back_ref[:, t * wide : (t + 1) * wide],
                    (((0,), (0,)), ((), ())),
                    preferred_element_type=f32,
                ).astype(bf16)
                for k in range(LANES // weight_rows):
                    out_p[group * LANES // weight_rows + k, :, t * wide : (t + 1) * wide] = value[
                        k * weight_rows : (k + 1) * weight_rows
                    ]

        for group in range(cols // LANES):
            out_product(group)

        def passing(at, source, target, to):
            return remote(source, target, pass_send.at[at], pass_receive.at[at], {"dp": to})

        passed = [
            passing(0, out_p.at[core_chip], out_core.at[1], core),
            passing(1, out_p.at[core], out_core.at[0], core),
        ]
        for copy in passed:
            copy.start()
        loads[2].wait()
        for head in range(heads):
            columns = pl.ds(head * HEAD_DIM, HEAD_DIM)
            key_columns = pl.ds(cols + head * HEAD_DIM, HEAD_DIM)
            value_columns = pl.ds(pair + head * HEAD_DIM, HEAD_DIM)
            pair_s[:, key_columns] = jnp.zeros((rows, HEAD_DIM), f32)
            value_s[:, columns] = jnp.zeros((rows, HEAD_DIM), f32)

            def scores(j, carry, head=head, columns=columns, key_columns=key_columns, value_columns=value_columns):
                at = pl.ds(pl.multiple_of(j * chunk, chunk), chunk)
                back = attend_back[at, columns]
                delta = jnp.sum(
                    back.astype(f32) * attend_ref[at, columns].astype(f32), axis=-1, keepdims=True
                )
                probs_low = probs_s[head, at]
                score_back = (
                    probs_low.astype(f32) * (dot_across(back, qkv_ref[:, value_columns]) - delta)
                ).astype(bf16)
                pair_s[at, columns] = dot(score_back, qkv_ref[:, key_columns])
                over = (((0,), (0,)), ((), ()))
                pair_s[:, key_columns] += lax.dot_general(
                    score_back, qkv_ref[at, columns], over, preferred_element_type=f32
                )
                value_s[:, columns] += lax.dot_general(
                    probs_low, back, over, preferred_element_type=f32
                )
                return carry

            chunks(scores)
        passed[0].wait_recv()
        out_core[1] = (out_core[1].astype(f32) + out_p[chip].astype(f32)).astype(bf16)
        passed.append(passing(2, out_core.at[1], out_chip, chip))
        passed[-1].start()
        pair_sum[...] = jnp.zeros((8, pair), f32)

        def unturn(j, carry):
            at = pl.ds(pl.multiple_of(j * chunk, chunk), chunk)
            held = jnp.zeros((chunk, LANES), f32)
            for which in range(2):
                total = jnp.zeros((chunk, 1), f32)
                for head in range(heads):
                    columns = pl.ds(which * cols + head * HEAD_DIM, HEAD_DIM)
                    back = turn(pair_s[at, columns] * scale, cos_ref[at], -sin_ref[at])
                    normed = raw_ref[at, columns] * inverse_ref[at, which : which + 1]
                    pair_sum[0:1, columns] += jnp.sum(back * normed, axis=0, keepdims=True)
                    back = back * pair_ref[0:1, columns]
                    pair_s[at, columns] = back
                    total = total + jnp.sum(back * normed, axis=-1, keepdims=True)
                held = jnp.where(lanes == which, total, held)
            sum_s[at] = held
            return carry

        chunks(unturn)
        exchange_rows(ring, sum_s, flat, got, sum_send, sum_receive, steps)
        loads[3].wait()

        def finish(j, carry):
            at = pl.ds(pl.multiple_of(j * chunk, chunk), chunk)
            for which in range(2):
                columns = pl.ds(which * cols, cols)
                factor = inverse_ref[at, which : which + 1]
                normed = raw_ref[at, columns] * factor
                mean = sum_s[at, which : which + 1] / width
                raw_back[at, columns] = (factor * (pair_s[at, columns] - normed * mean)).astype(bf16)
            raw_back[at, pl.ds(pair, cols)] = value_s[at].astype(bf16)
            for t in range(width // wide):
                row_part[at, pl.ds(t * wide, wide)] = dot_across(
                    raw_back[at], in_s[pl.ds(t * wide, wide), :]
                ).astype(bf16)
            return carry

        chunks(finish)
        passed[1].wait_recv()
        passed[2].wait_recv()
        out_sum[...] = (
            out_core[0].astype(f32) + out_p[dp].astype(f32) + out_chip[...].astype(f32)
        ).astype(bf16)
        advance(steps, 64)
        for copy in beyond:
            copy.wait()
        for copy in passed:
            copy.wait_send()

    return pl.pallas_call(
        body,
        out_shape=(
            jax.ShapeDtypeStruct((rows, 3 * cols), bf16),
            jax.ShapeDtypeStruct((rows, width), bf16),
            jax.ShapeDtypeStruct((8, pair), f32),
            jax.ShapeDtypeStruct((tok_rows, width), f32),
            jax.ShapeDtypeStruct((weight_rows, width), bf16),
            jax.ShapeDtypeStruct((far.shape[1] - PASS_A, far.shape[2]), bf16),
            jax.ShapeDtypeStruct((PASS_B, far.shape[2]), bf16),
        ),
        in_specs=[VMEM] + [ANY] * 3 + [VMEM] * 7 + [ANY] * 2,
        out_specs=(VMEM,) * 5 + (ANY,) * 2,
        scratch_shapes=[
            pltpu.VMEM((cols, width), bf16),
            pltpu.VMEM((width, pair + cols), bf16),
            pltpu.VMEM((heads, rows, rows), bf16),
            pltpu.VMEM((rows, width), bf16),
            pltpu.VMEM((rows, cols), bf16),
            pltpu.VMEM((rows, pair), f32),
            pltpu.VMEM((rows, cols), f32),
            pltpu.VMEM((rows, LANES), f32),
            pltpu.VMEM((2, 2, n // 2, half_rows, width), bf16),
            pltpu.VMEM((8, rows), f32),
            pltpu.VMEM((n - 1, 8, rows), f32),
            sems(n - 1),
            sems(n - 1),
            sems(2, 2, n // 2),
            sems(2, 2, n // 2),
            sems(4),
            pltpu.VMEM((n_dp, weight_rows, width), bf16),
            pltpu.VMEM((2, weight_rows, width), bf16),
            pltpu.VMEM((weight_rows, width), bf16),
            sems(3),
            sems(3),
            sems(2),
            sems(2),
        ],
        name="attention_back",
        cost_estimate=pl.CostEstimate(
            flops=2 * rows * width * 4 * cols, bytes_accessed=160_000_000, transcendentals=0
        ),
        compiler_params=pltpu.CompilerParams(
            collective_id=identity, has_side_effects=True, vmem_limit_bytes=BIG_VMEM
        ),
    )(
        back_all,
        out_all,
        in_all,
        probs,
        attend_low,
        qkv,
        raw,
        inverse,
        pair_gains,
        cosine,
        sine,
        partial,
        far,
    )


def heads_local(
    tokens,
    document_ids,
    routes,
    norm_gains,
    project_in,
    project_out,
    router_weight,
    expert_in,
    expert_out,
    cotangent,
):
    bf16, f32 = jnp.bfloat16, jnp.float32
    n = lax.axis_size("ctx")
    n_dp = lax.axis_size("dp")
    me = lax.axis_index("ctx")
    tok_rows, width = tokens.shape[1:]
    rows = tok_rows * n
    weight_rows = project_in.shape[0]
    own_heads = HEADS // n
    cols = own_heads * HEAD_DIM
    local_experts = expert_in.shape[0]
    expert_count = local_experts * n
    score_scale = HEAD_DIM ** (-0.5)

    def own(array, size, axis=0):
        return lax.dynamic_slice_in_dim(array, me * size, size, axis)

    named = jnp.any(routes[0][..., None] == jnp.arange(LANES, dtype=jnp.int32), axis=1).astype(bf16)
    small = jnp.concatenate(
        [router_weight, norm_gains, jnp.zeros((weight_rows, LANES - 4 - expert_count), bf16)], axis=1
    )
    in_blocks = project_in.reshape(weight_rows, 3, n, cols).transpose(2, 0, 1, 3)
    in_blocks = jnp.concatenate(
        [
            in_blocks.reshape(n, weight_rows, 3 * cols),
            jnp.broadcast_to(small[None], (n, weight_rows, LANES)),
        ],
        axis=2,
    )
    token_all, named_all, in_all, out_chip = gather_inputs(
        tokens[0], named, in_blocks, project_out, n, n_dp, 1
    )
    named_all = named_all.reshape(rows, LANES)
    in_all = in_all.reshape(width, 3 * cols + LANES)
    small_all = in_all[:, 3 * cols :]
    gains = small_all[:, expert_count : expert_count + 4].astype(f32)
    router_all = small_all[:, :expert_count]
    first = lax.all_gather(expert_in, "dp", axis=1, tiled=True)
    second = lax.all_gather(expert_out, "dp", axis=1, tiled=True).reshape(local_experts * FF, width)

    half_rows = tok_rows // 2

    def dealt(row):
        blocks = row.reshape(2 * n, half_rows)
        return jnp.stack([blocks[:n], blocks[n:][::-1]], axis=1).reshape(rows)

    places = dealt(jnp.arange(rows, dtype=jnp.int32))
    document_row = document_ids[0]
    starts = dealt(document_starts(document_row))
    relative = places - starts
    cosine, sine = rotary_tables(relative, HEAD_DIM)
    cosine = jnp.concatenate([cosine[:, 0], cosine[:, 0]], axis=-1)
    sine = jnp.concatenate([-sine[:, 0], sine[:, 0]], axis=-1)
    bounds = jnp.stack([starts, places], axis=1)
    place_row = places[None]
    pair_gains = own(gains, cols)[:, 1:3].T.reshape(1, 2 * cols)

    attend_gain = gains[:, 0][None]
    attend_all, out_all, probs, attend_in, attend_low, qkv, raw, inverse = attention_in(
        token_all,
        in_all,
        project_out,
        out_chip,
        attend_gain,
        pair_gains,
        cosine,
        sine,
        bounds,
        place_row,
        n,
        n_dp,
        10,
    )

    upstream_all, mixed_all, gated_all, up_all, own_gates, gate_back, own_residual = experts_in(
        attend_all,
        token_all,
        cotangent[0],
        out_all,
        first,
        second,
        gains[:, 3][None],
        small_all,
        named_all,
        n,
        8,
    )
    mixed_slots = mixed_all.reshape(rows, width)
    second_back = jnp.einsum(
        "tf,td->fd", gated_all, upstream_all.reshape(rows, width), preferred_element_type=f32
    ).astype(bf16)
    second_back, up_all = lax.optimization_barrier((second_back, up_all))
    expert_out_gradient = lax.psum_scatter(
        second_back.reshape(local_experts, FF, width), "dp", scatter_dimension=1, tiled=True
    ).astype(f32)
    mixed_back, mixture, gate_back = experts_out(up_all, gated_all, first, second, gate_back, n, 9)
    gate_back = gate_back[:, :local_experts]
    place = ring_place(me, n)
    gate_back = sum(
        jnp.where(
            (jnp.arange(n) == ring_device((place + offset + n) % n, n))[:, None, None],
            gate_back[slot],
            0.0,
        )
        for slot, offset in enumerate(slot_offsets(n))
    )
    gate_back = gate_back.reshape(expert_count, tok_rows).T

    own_gates = own_gates[:, :expert_count]
    own_mixed = mixed_all[0]
    own_mixed_inverse = inverse_rms(own_residual)
    own_mixed_normed = own_residual * own_mixed_inverse
    chosen_back = own_gates * (
        gate_back - jnp.sum(own_gates * gate_back, axis=-1, keepdims=True)
    )
    logit_back = chosen_back.astype(bf16)
    router_part = jnp.einsum("td,te->ed", own_mixed, logit_back, preferred_element_type=f32)
    mixed_back = mixed_back + jnp.einsum(
        "te,de->td", logit_back, router_all, preferred_element_type=f32
    )
    mixed_gain_back = jnp.sum(mixed_back * own_mixed_normed, axis=0)
    residual_back = cotangent[0].astype(f32) + normalize_back(
        mixed_back * gains[:, 3], own_mixed_normed, own_mixed_inverse
    )
    back_all, near, far, got_a = gather_with_gradients(
        residual_back.astype(bf16), mixed_slots, up_all, n, n_dp, 5
    )

    raw_back, row_part, pair_sum, mixture, out_part, got_b, got_c = attention_back(
        back_all,
        out_all,
        in_all,
        probs,
        attend_low,
        qkv,
        raw,
        inverse,
        pair_gains,
        cosine,
        sine,
        mixture,
        far,
        n,
        n_dp,
        11,
    )
    layer_output = (own_residual + mixture).astype(bf16)
    pairs = [(d * n + c, c * n_dp + d) for d in range(n_dp) for c in range(n)]
    project_out_gradient = lax.ppermute(out_part, ("dp", "ctx"), pairs).astype(f32)

    small_rows = -(-(4 + expert_count) // 8) * 8
    small_part = jnp.concatenate(
        [
            jnp.zeros((3, width), f32),
            mixed_gain_back[None],
            router_part,
            jnp.zeros((small_rows - 4 - expert_count, width), f32),
        ],
        axis=0,
    )
    tokens_back, project_in_gradient, small_gradient, got_d = scatter_end(
        row_part,
        attend_in,
        raw_back,
        tokens[0],
        residual_back,
        attend_gain,
        small_part,
        pair_sum,
        far,
        n,
        n_dp,
        6,
    )
    expert_in_gradient = near.astype(f32) + (
        jnp.concatenate([got_a, got_b, got_c, got_d], axis=0).reshape(near.shape).astype(f32)
    )
    per_tile = LANES // weight_rows
    small_gradient = lax.dynamic_slice_in_dim(
        small_gradient, me % per_tile * weight_rows, weight_rows, 1
    ).T
    return (
        layer_output[None],
        tokens_back[None],
        small_gradient[:, :4],
        project_in_gradient,
        project_out_gradient,
        small_gradient[:, 4 : 4 + expert_count],
        expert_in_gradient,
        expert_out_gradient,
    )


def layer(*arrays):
    n, tok_rows, experts = lax.axis_size("ctx"), arrays[0].shape[1], arrays[7].shape[0]
    fits = HEADS % n == 0 and n % 4 == 0 and lax.axis_size("dp") == 4
    fits = fits and tok_rows == LANES and experts == 2 and experts * n + 4 <= LANES
    return (heads_local if fits else gathered_local)(*arrays)


def solution(mesh):
    placed = (
        P("dp", "ctx", None),
        P("dp", None),
        P("dp", "ctx", None),
        P(("dp", "ctx"), None),
        P(("dp", "ctx"), None),
        P(("dp", "ctx"), None),
        P(("dp", "ctx"), None),
        P("ctx", "dp", None),
        P("ctx", "dp", None),
        P("dp", "ctx", None),
    )
    return jax.shard_map(
        layer,
        mesh=mesh,
        in_specs=placed,
        out_specs=(
            P("dp", "ctx", None),
            P("dp", "ctx", None),
            P(("dp", "ctx"), None),
            P(("dp", "ctx"), None),
            P(("dp", "ctx"), None),
            P(("dp", "ctx"), None),
            P("ctx", "dp", None),
            P("ctx", "dp", None),
        ),
        check_vma=False,
    )
```

```python
import jax
import jax.numpy as jnp
from jax import lax
from jax.experimental import pallas as pl
from jax.experimental.pallas import tpu as pltpu
from jax.sharding import PartitionSpec as P

HEADS = 16
HEAD_DIM = 128
FF = 1024


EPSILON = 1e-05
ROPE_BASE = 10000.0
MASKED = -1e30
LANES = 128
PASS_A, PASS_B = 256, 256
CUTS = 2
WAITS = (4, 6, 6)
TILE = 512
WIDE = 1024


def inverse_rms(values):
    return lax.rsqrt(jnp.mean(values * values, axis=-1, keepdims=True) + EPSILON)


def normalize_back(normed_back, normed, inverse):
    return inverse * (normed_back - normed * jnp.mean(normed_back * normed, axis=-1, keepdims=True))


def rotary_tables(relative, head_dim):
    half_dim = head_dim // 2
    frequency = ROPE_BASE ** (-jnp.arange(half_dim, dtype=jnp.float32) / half_dim)
    angles = relative.astype(jnp.float32)[..., None] * frequency
    return (jnp.cos(angles)[..., None, :], jnp.sin(angles)[..., None, :])


def rotate(values, cosine, sine_table):
    half_dim = values.shape[-1] // 2
    first_half = values[..., :half_dim]
    second_half = values[..., half_dim:]
    return jnp.concatenate(
        [
            first_half * cosine - second_half * sine_table,
            second_half * cosine + first_half * sine_table,
        ],
        axis=-1,
    )


def dealt_positions(indices, tok_rows, context_size):
    half_block = tok_rows // 2
    device = indices // tok_rows
    within = indices % tok_rows
    block_index = jnp.where(within < half_block, device, 2 * context_size - 1 - device)
    return block_index * half_block + within % half_block


def document_starts(document_row):
    places = jnp.arange(document_row.shape[-1], dtype=jnp.int32)
    head_flag = jnp.ones(document_row.shape[:-1] + (1,), jnp.bool_)
    fresh_start = jnp.concatenate(
        [head_flag, document_row[..., 1:] != document_row[..., :-1]], axis=-1
    )
    return lax.cummax(jnp.where(fresh_start, places, 0), axis=document_row.ndim - 1)


def block_scores(
    query_rows, key_block, query_place, query_document, key_place, key_document, score_scale
):
    scores = (
        jnp.einsum("thd,khd->htk", query_rows, key_block, preferred_element_type=jnp.float32)
        * score_scale
    )
    visible = (
        (key_document[None, :] == query_document[:, None])
        & (key_place[None, :] <= query_place[:, None])
    )[None]
    return (jnp.where(visible, scores, MASKED), visible)


def block_backward(
    query_rows,
    output_back,
    row_logsum,
    row_delta,
    key_block,
    value_block,
    query_place,
    query_document,
    key_place,
    key_document,
    score_scale,
):
    scores, visible = block_scores(
        query_rows, key_block, query_place, query_document, key_place, key_document, score_scale
    )
    prob_rows = jnp.where(visible, jnp.exp(scores - row_logsum[..., None]), 0.0)
    prob_back = jnp.einsum(
        "thd,khd->htk", output_back, value_block, preferred_element_type=jnp.float32
    )
    score_back = (prob_rows * (prob_back - row_delta[..., None])).astype(jnp.bfloat16)
    query_part = (
        jnp.einsum("htk,khd->thd", score_back, key_block, preferred_element_type=jnp.float32)
        * score_scale
    )
    key_part = (
        jnp.einsum("htk,thd->khd", score_back, query_rows, preferred_element_type=jnp.float32)
        * score_scale
    )
    value_part = jnp.einsum(
        "htk,thd->khd",
        prob_rows.astype(jnp.bfloat16),
        output_back,
        preferred_element_type=jnp.float32,
    )
    return (query_part, key_part, value_part)


def dispatch_plan(route_rows, expert_count, capacity):
    flat_routes = route_rows.reshape(-1)
    pair_count = flat_routes.shape[0]
    member = (flat_routes[:, None] == jnp.arange(expert_count, dtype=jnp.int32)[None, :]).astype(
        jnp.int32
    )
    earlier = jnp.cumsum(member, axis=0) - member
    target_slot = flat_routes * capacity + jnp.sum(earlier * member, axis=1)
    slot_owner = (
        jnp.full((expert_count * capacity,), pair_count, jnp.int32)
        .at[target_slot]
        .set(jnp.arange(pair_count, dtype=jnp.int32))
    )
    return (target_slot, slot_owner)


def gathered_local(
    tokens,
    document_ids,
    routes,
    norm_gains,
    project_in,
    project_out,
    router_weight,
    expert_in,
    expert_out,
    cotangent,
):
    inputs = tokens[0].astype(jnp.float32)
    tok_rows, model_width = inputs.shape
    context_size = lax.axis_size("ctx")
    sequence_rows = tok_rows * context_size
    local_experts = expert_in.shape[0]
    expert_count = local_experts * context_size
    route_rows = routes[0]
    top_count = route_rows.shape[1]
    capacity = 2 * tok_rows * top_count // expert_count
    score_scale = HEAD_DIM ** (-0.5)
    key_span = min(512, sequence_rows)
    key_blocks = sequence_rows // key_span
    heads_shape = (tok_rows, HEADS, HEAD_DIM)
    block_shape = (key_blocks, key_span, HEADS, HEAD_DIM)
    slot_shape = (context_size, local_experts * capacity, model_width)
    expert_shape = (context_size, local_experts, capacity, model_width)
    gathered_gains, gathered_in, gathered_out, gathered_router = (
        lax.all_gather(norm_gains, ("dp", "ctx"), axis=0, tiled=True),
        lax.all_gather(project_in, ("dp", "ctx"), axis=0, tiled=True),
        lax.all_gather(project_out, ("dp", "ctx"), axis=0, tiled=True),
        lax.all_gather(router_weight, ("dp", "ctx"), axis=0, tiled=True),
    )
    gathered_first, gathered_second = (
        lax.all_gather(expert_in, "dp", axis=1, tiled=True),
        lax.all_gather(expert_out, "dp", axis=1, tiled=True),
    )
    gain_rows = gathered_gains.astype(jnp.float32)
    own_rows = lax.axis_index("ctx") * tok_rows + jnp.arange(tok_rows, dtype=jnp.int32)
    own_place = dealt_positions(own_rows, tok_rows, context_size)
    all_place = dealt_positions(jnp.arange(sequence_rows, dtype=jnp.int32), tok_rows, context_size)
    document_row = document_ids[0]
    own_document = jnp.take(document_row, own_place)
    all_document = jnp.take(document_row, all_place)
    relative = own_place - jnp.take(document_starts(document_row), own_place)
    cosine, sine_table = rotary_tables(relative, HEAD_DIM)
    attend_inverse = inverse_rms(inputs)
    attend_normed = inputs * attend_inverse
    attend_in = (attend_normed * gain_rows[:, 0]).astype(jnp.bfloat16)
    projected = jnp.dot(attend_in, gathered_in, preferred_element_type=jnp.float32)
    raw_query = projected[:, :model_width]
    raw_key = projected[:, model_width : 2 * model_width]
    query_inverse = inverse_rms(raw_query)
    query_normed = raw_query * query_inverse
    key_inverse = inverse_rms(raw_key)
    key_normed = raw_key * key_inverse
    query_low = rotate(
        (query_normed * gain_rows[:, 1]).reshape(heads_shape), cosine, sine_table
    ).astype(jnp.bfloat16)
    key_low = rotate(
        (key_normed * gain_rows[:, 2]).reshape(heads_shape), cosine, sine_table
    ).astype(jnp.bfloat16)
    value_low = projected[:, 2 * model_width :].astype(jnp.bfloat16)
    key_all, value_all = (
        lax.all_gather(key_low.reshape(tok_rows, model_width), "ctx", axis=0, tiled=True),
        lax.all_gather(value_low, "ctx", axis=0, tiled=True),
    )
    key_split = key_all.reshape(block_shape)
    value_split = value_all.reshape(block_shape)
    place_split = all_place.reshape(key_blocks, key_span)
    document_split = all_document.reshape(key_blocks, key_span)

    def total_step(state_pair, block_args):
        row_peak, row_total = state_pair
        key_block, key_place, key_document = block_args
        scores, visible = block_scores(
            query_low, key_block, own_place, own_document, key_place, key_document, score_scale
        )
        new_peak = jnp.maximum(row_peak, jnp.max(scores, axis=-1))
        fresh_total = jnp.sum(
            jnp.where(visible, jnp.exp(scores - new_peak[..., None]), 0.0), axis=-1
        )
        return ((new_peak, row_total * jnp.exp(row_peak - new_peak) + fresh_total), None)

    start_pair = (
        jnp.full((HEADS, tok_rows), MASKED, jnp.float32),
        jnp.zeros((HEADS, tok_rows), jnp.float32),
    )
    (row_peak, row_total), unused = lax.scan(
        total_step, start_pair, (key_split, place_split, document_split)
    )
    row_logsum = row_peak + jnp.log(row_total)

    def value_step(running, block_args):
        key_block, value_block, key_place, key_document = block_args
        scores, visible = block_scores(
            query_low, key_block, own_place, own_document, key_place, key_document, score_scale
        )
        prob_low = jnp.where(visible, jnp.exp(scores - row_logsum[..., None]), 0.0).astype(
            jnp.bfloat16
        )
        return (
            running
            + jnp.einsum("htk,khd->thd", prob_low, value_block, preferred_element_type=jnp.float32),
            None,
        )

    attend_out, unused = lax.scan(
        value_step,
        jnp.zeros(heads_shape, jnp.float32),
        (key_split, value_split, place_split, document_split),
    )
    attend_low = attend_out.reshape(tok_rows, model_width).astype(jnp.bfloat16)
    residual = inputs + jnp.dot(attend_low, gathered_out, preferred_element_type=jnp.float32)
    mixed_inverse = inverse_rms(residual)
    mixed_normed = residual * mixed_inverse
    mixed_low = (mixed_normed * gain_rows[:, 3]).astype(jnp.bfloat16)
    logits = jnp.dot(mixed_low, gathered_router, preferred_element_type=jnp.float32)
    route_onehot = (route_rows[..., None] == jnp.arange(expert_count, dtype=jnp.int32)).astype(
        jnp.float32
    )
    gate_weights = jax.nn.softmax(jnp.sum(route_onehot * logits[:, None, :], axis=-1), axis=-1)
    target_slot, slot_owner = dispatch_plan(route_rows, expert_count, capacity)
    padded_rows = jnp.concatenate([mixed_low, jnp.zeros((1, model_width), jnp.bfloat16)], axis=0)
    send_rows = jnp.take(padded_rows, slot_owner // top_count, axis=0).reshape(slot_shape)
    received = lax.all_to_all(send_rows, "ctx", split_axis=0, concat_axis=0, tiled=True).reshape(
        expert_shape
    )
    expert_up = jnp.einsum(
        "sxcd,xdf->sxcf", received, gathered_first, preferred_element_type=jnp.float32
    )
    gate_part = expert_up[..., :FF]
    up_part = expert_up[..., FF:]
    sigmoid_gate = jax.nn.sigmoid(gate_part)
    swish_gate = gate_part * sigmoid_gate
    hidden_low = (swish_gate * up_part).astype(jnp.bfloat16)
    expert_result = jnp.einsum(
        "sxcf,xfd->sxcd", hidden_low, gathered_second, preferred_element_type=jnp.float32
    ).astype(jnp.bfloat16)
    returned = lax.all_to_all(
        expert_result.reshape(slot_shape), "ctx", split_axis=0, concat_axis=0, tiled=True
    ).reshape(expert_count * capacity, model_width)
    pair_result = jnp.take(returned, target_slot, axis=0).reshape(tok_rows, top_count, model_width)
    mixture = jnp.sum(gate_weights[..., None] * pair_result, axis=1)
    layer_output = (residual + mixture).astype(jnp.bfloat16)
    upstream = cotangent[0].astype(jnp.float32)
    pair_back = (gate_weights[..., None] * upstream[:, None, :]).astype(jnp.bfloat16)
    gate_back = jnp.sum(pair_result * upstream[:, None, :], axis=-1)
    padded_back = jnp.concatenate(
        [
            pair_back.reshape(tok_rows * top_count, model_width),
            jnp.zeros((1, model_width), jnp.bfloat16),
        ],
        axis=0,
    )
    send_back = jnp.take(padded_back, slot_owner, axis=0).reshape(slot_shape)
    received_back = lax.all_to_all(
        send_back, "ctx", split_axis=0, concat_axis=0, tiled=True
    ).reshape(expert_shape)
    first_back, second_back = (gathered_first, gathered_second)
    hidden_back = jnp.einsum(
        "sxcd,xfd->sxcf", received_back, second_back, preferred_element_type=jnp.float32
    )
    second_weight_back = jnp.einsum(
        "sxcf,sxcd->xfd", hidden_low, received_back, preferred_element_type=jnp.float32
    )
    swish_slope = sigmoid_gate * (1.0 + gate_part * (1.0 - sigmoid_gate))
    up_back = jnp.concatenate(
        [hidden_back * up_part * swish_slope, hidden_back * swish_gate], axis=-1
    ).astype(jnp.bfloat16)
    first_weight_back = jnp.einsum(
        "sxcd,sxcf->xdf", received, up_back, preferred_element_type=jnp.float32
    )
    input_back = jnp.einsum(
        "sxcf,xdf->sxcd", up_back, first_back, preferred_element_type=jnp.float32
    ).astype(jnp.bfloat16)
    expert_in_gradient, expert_out_gradient = (
        lax.psum_scatter(
            first_weight_back.astype(jnp.bfloat16), "dp", scatter_dimension=1, tiled=True
        ).astype(jnp.float32),
        lax.psum_scatter(
            second_weight_back.astype(jnp.bfloat16), "dp", scatter_dimension=1, tiled=True
        ).astype(jnp.float32),
    )
    rows_back = lax.all_to_all(
        input_back.reshape(slot_shape), "ctx", split_axis=0, concat_axis=0, tiled=True
    ).reshape(expert_count * capacity, model_width)
    mixed_back = jnp.sum(
        jnp.take(rows_back, target_slot, axis=0)
        .reshape(tok_rows, top_count, model_width)
        .astype(jnp.float32),
        axis=1,
    )
    gains_back, in_back, out_back, router_back = (
        gathered_gains,
        gathered_in,
        gathered_out,
        gathered_router,
    )
    gain_values = gains_back.astype(jnp.float32)
    chosen_back = gate_weights * (
        gate_back - jnp.sum(gate_weights * gate_back, axis=-1, keepdims=True)
    )
    logit_back = jnp.sum(chosen_back[..., None] * route_onehot, axis=1).astype(jnp.bfloat16)
    router_weight_back = jnp.einsum(
        "td,te->de", mixed_low, logit_back, preferred_element_type=jnp.float32
    )
    mixed_back = mixed_back + jnp.einsum(
        "te,de->td", logit_back, router_back, preferred_element_type=jnp.float32
    )
    mixed_gain_back = jnp.sum(mixed_back * mixed_normed, axis=0)
    residual_back = upstream + normalize_back(
        mixed_back * gain_values[:, 3], mixed_normed, mixed_inverse
    )
    residual_low = residual_back.astype(jnp.bfloat16)
    out_weight_back = jnp.einsum(
        "td,te->de", attend_low, residual_low, preferred_element_type=jnp.float32
    )
    attend_back = (
        jnp.einsum("te,de->td", residual_low, out_back, preferred_element_type=jnp.float32)
        .astype(jnp.bfloat16)
        .reshape(heads_shape)
    )
    row_delta = jnp.einsum("thd,thd->ht", attend_back.astype(jnp.float32), attend_out)

    def back_step(query_acc, block_args):
        key_block, value_block, key_place, key_document = block_args
        query_part, key_part, value_part = block_backward(
            query_low,
            attend_back,
            row_logsum,
            row_delta,
            key_block,
            value_block,
            own_place,
            own_document,
            key_place,
            key_document,
            score_scale,
        )
        return (query_acc + query_part, (key_part, value_part))

    query_back, (key_parts, value_parts) = lax.scan(
        back_step,
        jnp.zeros(heads_shape, jnp.float32),
        (key_split, value_split, place_split, document_split),
    )
    key_back, value_back = (
        lax.psum_scatter(
            key_parts.reshape(sequence_rows, model_width).astype(jnp.bfloat16),
            "ctx",
            scatter_dimension=0,
            tiled=True,
        ).astype(jnp.float32),
        lax.psum_scatter(
            value_parts.reshape(sequence_rows, model_width).astype(jnp.bfloat16),
            "ctx",
            scatter_dimension=0,
            tiled=True,
        ).astype(jnp.float32),
    )
    query_flat = rotate(query_back, cosine, -sine_table).reshape(tok_rows, model_width)
    key_flat = rotate(key_back.reshape(heads_shape), cosine, -sine_table).reshape(
        tok_rows, model_width
    )
    query_gain_back = jnp.sum(query_flat * query_normed, axis=0)
    key_gain_back = jnp.sum(key_flat * key_normed, axis=0)
    raw_query_back = normalize_back(query_flat * gain_values[:, 1], query_normed, query_inverse)
    raw_key_back = normalize_back(key_flat * gain_values[:, 2], key_normed, key_inverse)
    raw_back = jnp.concatenate([raw_query_back, raw_key_back, value_back], axis=-1).astype(
        jnp.bfloat16
    )
    in_weight_back = jnp.einsum(
        "td,tf->df", attend_in, raw_back, preferred_element_type=jnp.float32
    )
    attend_in_back = jnp.einsum("tf,df->td", raw_back, in_back, preferred_element_type=jnp.float32)
    attend_gain_back = jnp.sum(attend_in_back * attend_normed, axis=0)
    tokens_back = residual_back + normalize_back(
        attend_in_back * gain_values[:, 0], attend_normed, attend_inverse
    )
    gain_columns = jnp.stack(
        [attend_gain_back, query_gain_back, key_gain_back, mixed_gain_back], axis=1
    )
    gains_gradient, project_in_gradient, project_out_gradient, router_gradient = (
        lax.psum_scatter(gain_columns, ("dp", "ctx"), scatter_dimension=0, tiled=True),
        lax.psum_scatter(in_weight_back, ("dp", "ctx"), scatter_dimension=0, tiled=True),
        lax.psum_scatter(out_weight_back, ("dp", "ctx"), scatter_dimension=0, tiled=True),
        lax.psum_scatter(router_weight_back, ("dp", "ctx"), scatter_dimension=0, tiled=True),
    )
    return (
        layer_output[None],
        tokens_back.astype(jnp.bfloat16)[None],
        gains_gradient,
        project_in_gradient,
        project_out_gradient,
        router_gradient,
        expert_in_gradient,
        expert_out_gradient,
    )


MESH = pl.DeviceIdType.MESH
VMEM_LIMIT = 48 * 1024 * 1024


def ring_place(device, n):
    odd = device % 2
    return (1 - odd) * (device // 2) + odd * (n - 1 - device // 2)


def ring_device(place, n):
    far = place // (n // 2)
    return (1 - far) * (2 * place) + far * (2 * (n - 1 - place) + 1)


class Ring:
    def __init__(self, n):
        self.n = n
        self.me = lax.axis_index("ctx")
        self.place = ring_place(self.me, n)

    def at(self, offset):
        return ring_device((self.place + offset + self.n) % self.n, self.n)

    def hops(self, way, half):
        return self.n // 2 if way == half else self.n // 2 - 1

    def barrier(self, others):
        semaphore = pltpu.get_barrier_semaphore()
        for other in others:
            pl.semaphore_signal(semaphore, inc=1, device_id=other, device_id_type=MESH)
        pl.semaphore_wait(semaphore, len(others))

    def neighbours(self):
        return [{"ctx": self.at(1)}, {"ctx": self.at(-1)}]


def remote(source, target, send, receive, device):
    return pltpu.make_async_remote_copy(
        src_ref=source,
        dst_ref=target,
        send_sem=send,
        recv_sem=receive,
        device_id=device,
        device_id_type=MESH,
    )


def gather_steps(ring, source, place, send, receive, arrived=None, ready=None):
    signs = (1, -1)

    def copy(way, half, hop):
        origin = ring.at(-signs[way] * hop)
        spot = place(origin, half)
        return remote(
            source(half) if hop == 0 else spot,
            spot,
            send.at[way, half, hop],
            receive.at[way, half, hop],
            {"ctx": ring.at(signs[way])},
        )

    def landed(way, half, hop):
        spot = place(ring.at(-signs[way] * (hop + 1)), half)
        return remote(
            spot,
            spot,
            send.at[way, half, hop],
            receive.at[way, half, hop],
            {"ctx": ring.at(signs[way])},
        )

    started = []
    for half in (0, 1):
        if ready is not None:
            ready(half)
        for way in (0, 1):
            started.append(copy(way, half, 0))
            started[-1].start()
        yield
    for hop in range(ring.n // 2):
        for half in (0, 1):
            for way in (0, 1):
                if hop < ring.hops(way, half):
                    landed(way, half, hop).wait_recv()
                    if hop + 1 < ring.hops(way, half):
                        started.append(copy(way, half, hop + 1))
                        started[-1].start()
                    if arrived is not None:
                        arrived(way, half, hop, ring.at(-signs[way] * (hop + 1)))
                    yield
    for one in started:
        one.wait_send()


def scatter_steps(ring, part, slots, store, send, receive):
    signs = (1, -1)

    def copy(way, half, hop, source):
        return remote(
            source,
            slots.at[way, half, hop],
            send.at[way, half, hop],
            receive.at[way, half, hop],
            {"ctx": ring.at(signs[way])},
        )

    started = []
    for half in (0, 1):
        for way in (0, 1):
            goal = ring.at(signs[way] * ring.hops(way, half))
            started.append(copy(way, half, 0, part(goal, half)))
            started[-1].start()
        yield
    for hop in range(ring.n // 2):
        for half in (0, 1):
            for way in (0, 1):
                last = ring.hops(way, half) - 1
                if hop <= last:
                    slot = slots.at[way, half, hop]
                    copy(way, half, hop, slot).wait_recv()
                    if hop < last:
                        goal = ring.at(signs[way] * (last - hop))
                        slot[...] = (
                            slot[...].astype(jnp.float32)
                            + part(goal, half)[...].astype(jnp.float32)
                        ).astype(slot.dtype)
                        started.append(copy(way, half, hop + 1, slot))
                        started[-1].start()
                    yield
    for half in (0, 1):
        total = part(ring.me, half)[...].astype(jnp.float32)
        for way in (0, 1):
            total = total + slots[way, half, ring.hops(way, half) - 1].astype(jnp.float32)
        store(half, total)
    for one in started:
        one.wait_send()


def run_steps(*tasks):
    tasks = list(tasks)
    while tasks:
        left = []
        for task in tasks:
            try:
                next(task)
                left.append(task)
            except StopIteration:
                pass
        tasks = left


def sems(*shape):
    return pltpu.SemaphoreType.DMA(shape)


def kernel_call(body, outs, in_specs, out_specs, scratch, identity, name, sent):
    return pl.pallas_call(
        body,
        out_shape=outs,
        in_specs=in_specs,
        out_specs=out_specs,
        scratch_shapes=scratch,
        name=name,
        cost_estimate=pl.CostEstimate(flops=0, bytes_accessed=sent, transcendentals=0),
        compiler_params=pltpu.CompilerParams(
            collective_id=identity, has_side_effects=True, vmem_limit_bytes=VMEM_LIMIT
        ),
    )


ANY = pl.BlockSpec(memory_space=pl.ANY)
VMEM = pl.BlockSpec(memory_space=pltpu.VMEM)


def ring_gather(block, n, identity, name, axis=0):
    rows, width = block.shape
    half_rows = rows // 2
    shape = (rows * n, width) if axis == 0 else (rows, width * n)

    def body(block_ref, all_ref, send, receive, local):
        ring = Ring(n)

        def place(device, half):
            if axis == 0:
                return all_ref.at[pl.ds(pl.multiple_of(device * rows + half * half_rows, 16), half_rows)]
            return all_ref.at[
                pl.ds(half * half_rows, half_rows), pl.ds(pl.multiple_of(device * width, 128), width)
            ]

        whole = (
            all_ref.at[pl.ds(pl.multiple_of(ring.me * rows, 16), rows)]
            if axis == 0
            else all_ref.at[:, pl.ds(pl.multiple_of(ring.me * width, 128), width)]
        )
        own = pltpu.make_async_copy(block_ref, whole, local)
        own.start()
        ring.barrier(ring.neighbours())
        run_steps(
            gather_steps(
                ring,
                lambda half: block_ref.at[pl.ds(half * half_rows, half_rows)],
                place,
                send,
                receive,
            )
        )
        own.wait()

    return kernel_call(
        body,
        jax.ShapeDtypeStruct(shape, block.dtype),
        [ANY],
        ANY,
        [sems(2, 2, n // 2), sems(2, 2, n // 2), pltpu.SemaphoreType.DMA],
        identity,
        name,
        block.size * 2 * n * 32,
    )(block)


def ring_scatter(partial, n, identity, name):
    rows, width = partial.shape[0] // n, partial.shape[1]
    half_rows = rows // 2

    def body(part_ref, sum_ref, slots, send, receive):
        ring = Ring(n)
        ring.barrier(ring.neighbours())

        def part(device, half):
            return part_ref.at[pl.ds(pl.multiple_of(device * rows + half * half_rows, 16), half_rows)]

        def store(half, total):
            sum_ref[pl.ds(half * half_rows, half_rows)] = total

        run_steps(scatter_steps(ring, part, slots, store, send, receive))

    return kernel_call(
        body,
        jax.ShapeDtypeStruct((rows, width), jnp.float32),
        [VMEM],
        VMEM,
        [
            pltpu.VMEM((2, 2, n // 2, half_rows, width), partial.dtype),
            sems(2, 2, n // 2),
            sems(2, 2, n // 2),
        ],
        identity,
        name,
        partial.size * 2 * 32,
    )(partial)


def partners():
    dp = lax.axis_index("dp")
    core = dp + 1 - 2 * (dp % 2)
    chip = (dp + 2) % 4
    return dp, core, chip, (core + 2) % 4


def gather_inputs(tokens, named, in_blocks, out_rows, n, n_dp, identity):
    tok_rows, width = tokens.shape

    def body(
        token_ref,
        named_ref,
        in_ref,
        out_ref,
        token_all,
        named_all,
        in_all,
        out_chip,
        token_send,
        token_receive,
        named_send,
        named_receive,
        in_send,
        in_receive,
        pass_send,
        pass_receive,
        local,
        out_send,
        out_receive,
    ):
        ring = Ring(n)
        me = ring.me
        dp, core, chip, core_chip = partners()
        half_rows = tok_rows // 2

        def token_place(device, half):
            return token_all.at[
                pl.ds(pl.multiple_of(device * tok_rows + half * half_rows, 16), half_rows)
            ]

        locals_ = [
            pltpu.make_async_copy(in_ref.at[me], in_all.at[dp, me], local.at[0]),
            pltpu.make_async_copy(
                token_ref,
                token_all.at[pl.ds(pl.multiple_of(me * tok_rows, 16), tok_rows)],
                local.at[1],
            ),
            pltpu.make_async_copy(named_ref, named_all.at[me], local.at[2]),
        ]
        for copy in locals_:
            copy.start()
        others = [(me + k) % n for k in range(1, n)]
        ring.barrier([{"ctx": other} for other in others] + [{"dp": core}, {"dp": chip}])

        direct = [remote(out_ref, out_chip, out_send, out_receive, {"dp": chip})]
        direct[0].start()
        for k, other in enumerate(others):
            direct.append(
                remote(in_ref.at[other], in_all.at[dp, me], in_send.at[k], in_receive.at[k], {"ctx": other})
            )
            direct.append(
                remote(named_ref, named_all.at[me], named_send.at[k], named_receive.at[k], {"ctx": other})
            )
        for copy in direct[1:]:
            copy.start()

        def in_steps():
            passed = []

            def forward(at, k, source, spot, to):
                passed.append(
                    remote(source, spot, pass_send.at[at, k], pass_receive.at[at, k], {"dp": to})
                )
                passed[-1].start()

            def landed(at, k, group, source):
                spot = in_all.at[group, (me - k + n) % n]
                remote(
                    spot, spot, pass_send.at[at, k], pass_receive.at[at, k], {"dp": source}
                ).wait_recv()
                return spot

            for at, to in ((0, chip), (1, core)):
                forward(at, 0, in_ref.at[me], in_all.at[dp, me], to)
            yield
            for k in range(1, n):
                spot = in_all.at[dp, (me - k + n) % n]
                remote(
                    spot, spot, in_send.at[k - 1], in_receive.at[k - 1], {"ctx": others[k - 1]}
                ).wait_recv()
                for at, to in ((0, chip), (1, core)):
                    forward(at, k, spot, spot, to)
                yield
            for k in range(n):
                spot = landed(0, k, chip, chip)
                forward(2, k, spot, spot, core)
                yield
            for at, group in ((1, core), (2, core_chip)):
                for k in range(n):
                    landed(at, k, group, core)
            for copy in passed:
                copy.wait_send()

        run_steps(
            gather_steps(
                ring,
                lambda half: token_ref.at[pl.ds(half * half_rows, half_rows)],
                token_place,
                token_send,
                token_receive,
            ),
            in_steps(),
        )
        for k in range(1, n):
            spot = named_all.at[(me - k + n) % n]
            remote(
                spot, spot, named_send.at[k - 1], named_receive.at[k - 1], {"ctx": others[k - 1]}
            ).wait_recv()
        direct[0].wait_recv()
        for copy in direct:
            copy.wait_send()
        for copy in locals_:
            copy.wait()

    return kernel_call(
        body,
        (
            jax.ShapeDtypeStruct((tok_rows * n, width), tokens.dtype),
            jax.ShapeDtypeStruct((n,) + named.shape, named.dtype),
            jax.ShapeDtypeStruct((n_dp,) + in_blocks.shape, in_blocks.dtype),
            jax.ShapeDtypeStruct(out_rows.shape, out_rows.dtype),
        ),
        [ANY] * 4,
        (ANY,) * 4,
        [sems(2, 2, n // 2)] * 2
        + [sems(n - 1)] * 4
        + [sems(3, n)] * 2
        + [sems(3), pltpu.SemaphoreType.DMA, pltpu.SemaphoreType.DMA],
        identity,
        "gather_inputs",
        200_000_000,
    )(tokens, named, in_blocks, out_rows)


def sum_small_steps(ring, small, near, quarter, got, total, sem):
    pass_send, pass_receive, send, receive = sem
    dp, core, chip, core_chip = partners()
    n, me = ring.n, ring.me
    lanes = quarter.shape[1]
    per_tile = LANES * n // lanes

    def group(at):
        return small.at[:, pl.ds(pl.multiple_of(at * lanes, LANES), lanes)]

    copies = []
    for at, to in enumerate((core_chip, chip, core)):
        copies.append(
            remote(group(to), near.at[at], pass_send.at[at], pass_receive.at[at], {"dp": to})
        )
        copies[-1].start()
    for _ in range(WAITS[1]):
        yield
    value = group(dp)[...]
    for at in range(3):
        copies[at].wait_recv()
        value = value + near[at]
    quarter[...] = value

    def tile(device):
        return quarter.at[:, pl.ds(pl.multiple_of(device // per_tile * LANES, LANES), LANES)]

    for k in range(1, n):
        other = (me + k) % n
        copies.append(
            remote(tile(other), got.at[k - 1], send.at[k - 1], receive.at[k - 1], {"ctx": other})
        )
        copies[-1].start()
    for _ in range(WAITS[2]):
        yield
    value = tile(me)[...]
    for k in range(1, n):
        copies[2 + k].wait_recv()
        value = value + got[k - 1]
    total[...] = value
    for copy in copies:
        copy.wait_send()


def scatter_end(
    row_part, attend_in, raw_back, tokens, residual_back, gain, small, pair_sum, far, n, n_dp, identity
):
    rows, width = row_part.shape[0] // n, row_part.shape[1]
    half_rows = rows // 2
    span = width // n_dp
    weight_rows = span // n
    in_cols = raw_back.shape[1]
    cols = in_cols // 3
    small_rows = small.shape[0]
    bf16, f32 = jnp.bfloat16, jnp.float32

    def body(
        row_ref,
        attend_ref,
        raw_ref,
        token_ref,
        back_ref,
        gain_ref,
        small_ref,
        pair_ref,
        far_ref,
        token_back,
        in_sum,
        small_sum,
        far_got,
        slots,
        row_s,
        attend_s,
        in_part,
        in_core,
        in_chip,
        in_got,
        small_s,
        small_near,
        small_quarter,
        small_got,
        row_send,
        row_receive,
        pass_send,
        pass_receive,
        in_send,
        in_receive,
        small_pass_send,
        small_pass_receive,
        small_send,
        small_receive,
        load,
        far_send,
        far_receive,
    ):
        ring = Ring(n)
        me = ring.me
        dp, core, chip, core_chip = partners()
        others = [(me + k) % n for k in range(1, n)]
        loaded = pltpu.make_async_copy(attend_ref, attend_s, load)
        loaded.start()
        ring.barrier(
            [{"ctx": other} for other in others] + [{"dp": to} for to in (core, chip, core_chip)]
        )

        def part(device, half):
            return row_ref.at[pl.ds(pl.multiple_of(device * rows + half * half_rows, 16), half_rows)]

        def store(half, total):
            row_s[pl.ds(half * half_rows, half_rows)] = total

        half_slots = n // CUTS

        def passing(at, k, source, target, to):
            slots_k = pl.ds(k * half_slots, half_slots)
            return remote(
                source.at[slots_k],
                target.at[slots_k],
                pass_send.at[at, k],
                pass_receive.at[at, k],
                {"dp": to},
            )

        def product(group):
            value = lax.dot_general(
                attend_s[:, pl.ds(pl.multiple_of(group * span, LANES), span)],
                raw_ref[...],
                (((0,), (0,)), ((), ())),
                preferred_element_type=f32,
            ).astype(bf16)
            for device in range(n):
                in_part[group, (device - me + n) % n] = value[
                    device * weight_rows : (device + 1) * weight_rows
                ]

        def weight_steps():
            loaded.wait()
            sent = []
            product(core_chip)
            far = [passing(0, k, in_part.at[core_chip], in_core.at[1], core) for k in range(CUTS)]
            for copy in far:
                copy.start()
            yield
            product(core)
            near = [passing(1, k, in_part.at[core], in_core.at[0], core) for k in range(CUTS)]
            for copy in near:
                copy.start()
            yield
            product(chip)
            across = []
            for k in range(CUTS):
                far[k].wait_recv()

                def add_far(at, carry):
                    in_core[1, at] = (
                        in_core[1, at].astype(f32) + in_part[chip, at].astype(f32)
                    ).astype(bf16)
                    return carry

                lax.fori_loop(k * half_slots, (k + 1) * half_slots, add_far, 0)
                across.append(passing(2, k, in_core.at[1], in_chip, chip))
                across[-1].start()
            beyond = remote(far_ref.at[1, pl.ds(PASS_B, far_got.shape[0])], far_got, far_send, far_receive, {"dp": chip})
            yield
            product(dp)
            for _ in range(2):
                yield
            for k in range(CUTS):
                near[k].wait_recv()
                across[k].wait_recv()

                def add_near(at, carry):
                    in_core[0, at] = (
                        in_core[0, at].astype(f32)
                        + in_part[dp, at].astype(f32)
                        + in_chip[at].astype(f32)
                    ).astype(bf16)
                    return carry

                lax.fori_loop(k * half_slots, (k + 1) * half_slots, add_near, 0)
                for at in range(max(1, k * half_slots), (k + 1) * half_slots):
                    sent.append(
                        remote(
                            in_core.at[0, at],
                            in_got.at[at],
                            in_send.at[at - 1],
                            in_receive.at[at - 1],
                            {"ctx": others[at - 1]},
                        )
                    )
                    sent[-1].start()
                yield
                yield
            beyond.start()
            in_got[0] = in_core[0, 0]
            for _ in range(6):
                yield
            for at in range(n):
                if at:
                    sent[at - 1].wait_recv()
                device = (me - at + n) % n
                for which in range(3):
                    in_sum[
                        :, pl.ds(pl.multiple_of(which * width + device * cols, LANES), cols)
                    ] = in_got[at, :, pl.ds(which * cols, cols)].astype(f32)
            beyond.wait()
            for copy in far + near + across + sent:
                copy.wait_send()

        def row_steps():
            yield from scatter_steps(ring, part, slots, store, row_send, row_receive)
            values = token_ref[...].astype(f32)
            inverse = lax.rsqrt(jnp.mean(values * values, axis=-1, keepdims=True) + EPSILON)
            normed = values * inverse
            back = row_s[...]
            back = back * gain_ref[0:1, :]
            token_back[...] = (
                back_ref[...]
                + inverse * (back - normed * jnp.mean(back * normed, axis=-1, keepdims=True))
            ).astype(bf16)

        def small_steps():
            for _ in range(WAITS[0]):
                yield

            def column_sums(at, total):
                part_rows = pl.ds(pl.multiple_of(at * rows, rows), rows)
                terms = row_ref[part_rows].astype(f32) * attend_s[part_rows].astype(f32)
                return total + jnp.sum(terms, axis=0, keepdims=True)

            total = lax.fori_loop(0, n, column_sums, jnp.zeros((1, width), f32))
            small_s[...] = small_ref[...]
            small_s[0:1, :] = total / gain_ref[0:1, :]
            own = pl.ds(pl.multiple_of(me * cols, LANES), cols)
            small_s[1:2, own] = pair_ref[0:1, :cols]
            small_s[2:3, own] = pair_ref[0:1, cols:]
            yield from sum_small_steps(
                ring,
                small_s,
                small_near,
                small_quarter,
                small_got,
                small_sum,
                (small_pass_send, small_pass_receive, small_send, small_receive),
            )

        run_steps(row_steps(), weight_steps(), small_steps())

    block = (n, weight_rows, in_cols)
    return kernel_call(
        body,
        (
            jax.ShapeDtypeStruct((rows, width), bf16),
            jax.ShapeDtypeStruct((weight_rows, 3 * width), f32),
            jax.ShapeDtypeStruct((small_rows, LANES), f32),
            jax.ShapeDtypeStruct((far.shape[1] - PASS_B, far.shape[2]), bf16),
        ),
        [VMEM, ANY] + [VMEM] * 6 + [ANY],
        (VMEM,) * 3 + (ANY,),
        [
            pltpu.VMEM((2, 2, n // 2, half_rows, width), row_part.dtype),
            pltpu.VMEM((rows, width), f32),
            pltpu.VMEM(attend_in.shape, bf16),
            pltpu.VMEM((n_dp,) + block, bf16),
            pltpu.VMEM((2,) + block, bf16),
            pltpu.VMEM(block, bf16),
            pltpu.VMEM(block, bf16),
            pltpu.VMEM((small_rows, width), f32),
            pltpu.VMEM((3, small_rows, span), f32),
            pltpu.VMEM((small_rows, span), f32),
            pltpu.VMEM((n - 1, small_rows, LANES), f32),
            sems(2, 2, n // 2),
            sems(2, 2, n // 2),
            sems(3, CUTS),
            sems(3, CUTS),
            sems(n - 1),
            sems(n - 1),
            sems(3),
            sems(3),
            sems(n - 1),
            sems(n - 1),
            pltpu.SemaphoreType.DMA,
            pltpu.SemaphoreType.DMA,
            pltpu.SemaphoreType.DMA,
        ],
        identity,
        "scatter_end",
        200_000_000,
    )(row_part, attend_in, raw_back, tokens, residual_back, gain, small, pair_sum, far)


def slot_offsets(n):
    offsets = [0]
    for k in range(1, n // 2):
        offsets += [k, -k]
    return offsets + [n // 2]


def slot_of(offset, n):
    if abs(offset) == n // 2:
        return n - 1
    return 2 * offset - 1 if offset > 0 else -2 * offset


def slot_gather_steps(ring, first, slots, send, receive):
    signs = (1, -1)
    half_rows = slots.shape[1] // 2

    def copy(way, half, hop):
        rows = pl.ds(half * half_rows, half_rows)
        held = slot_of(-signs[way] * hop, ring.n)
        return remote(
            first.at[rows] if hop == 0 else slots.at[held, rows],
            slots.at[slot_of(-signs[way] * (hop + 1), ring.n), rows],
            send.at[way, half, hop],
            receive.at[way, half, hop],
            {"ctx": ring.at(signs[way])},
        )

    started = []
    for half in (0, 1):
        for way in (0, 1):
            started.append(copy(way, half, 0))
            started[-1].start()
    yield
    for hop in range(ring.n // 2):
        for half in (0, 1):
            for way in (0, 1):
                if hop < ring.hops(way, half):
                    copy(way, half, hop).wait_recv()
                    if hop + 1 < ring.hops(way, half):
                        started.append(copy(way, half, hop + 1))
                        started[-1].start()
                    yield
    for one in started:
        one.wait_send()


def advance(steps, count):
    for _ in range(count):
        next(steps, None)


def dot(a, b):
    return jnp.dot(a, b, preferred_element_type=jnp.float32)


def dot_across(a, b):
    return lax.dot_general(a, b, (((1,), (1,)), ((), ())), preferred_element_type=jnp.float32)


def experts_in(
    attend_all, token_all, cotangent, out_all, first, second, gain, router, named, n, identity
):
    tok_rows, width = cotangent.shape
    local_experts, ff = first.shape[0], second.shape[0] // first.shape[0]
    rows = tok_rows * n
    group = 4
    pair = part = group * tok_rows
    tile, wide = TILE, WIDE
    bf16, f32 = jnp.bfloat16, jnp.float32
    offsets = slot_offsets(n)

    def body(
        attend_ref,
        token_ref,
        back_ref,
        out_ref,
        first_ref,
        second_ref,
        gain_ref,
        router_ref,
        named_ref,
        back_all,
        mixed_all,
        gated_all,
        up_all,
        own_gates,
        gate_back,
        own_residual,
        out_s,
        first_s,
        second_s,
        mixed_s,
        back_s,
        attend_s,
        residual_s,
        gate_s,
        sum_s,
        send,
        receive,
        load,
        weight_load,
        save,
        local,
    ):
        ring = Ring(n)
        lanes = lax.broadcasted_iota(jnp.int32, (pair, LANES), 1)
        loads = [pltpu.make_async_copy(out_ref, out_s, weight_load.at[0])]
        for x in range(local_experts):
            loads.append(pltpu.make_async_copy(first_ref.at[x], first_s.at[x], weight_load.at[1 + x]))
        loads.append(pltpu.make_async_copy(second_ref, second_s, weight_load.at[1 + local_experts]))

        def row_loads(j):
            copies = []
            for k in range(group):
                device = ring.at(offsets[group * j + k])
                source = pl.ds(pl.multiple_of(device * tok_rows, 16), tok_rows)
                target = pl.ds(k * tok_rows, tok_rows)
                copies.append(
                    pltpu.make_async_copy(
                        attend_ref.at[source], attend_s.at[j % 2, target], load.at[j % 2, k, 0]
                    )
                )
                copies.append(
                    pltpu.make_async_copy(
                        token_ref.at[source], mixed_s.at[group * j + k], load.at[j % 2, k, 1]
                    )
                )
            return copies

        pending = row_loads(0)
        for copy in pending:
            copy.start()
        loads[0].start()
        own = pltpu.make_async_copy(back_ref, back_s.at[0], local)
        own.start()
        ring.barrier(ring.neighbours())
        steps = slot_gather_steps(ring, back_ref, back_s, send, receive)
        advance(steps, 1)
        loads[0].wait()
        for copy in loads[1:]:
            copy.start()

        saves = []
        for j in range(n // group):
            for copy in pending:
                copy.wait()
            if j + 1 < n // group:
                pending = row_loads(j + 1)
                for copy in pending:
                    copy.start()

            def project(t, carry, j=j):
                columns = pl.ds(pl.multiple_of(t * wide, wide), wide)
                values = mixed_s[pl.ds(group * j, group), :, columns].reshape(pair, wide)
                residual_s[:, columns] = values.astype(f32) + dot(attend_s[j % 2], out_s[:, columns])
                return carry

            lax.fori_loop(0, width // wide, project, 0)
            advance(steps, 2)
            residual = residual_s[...]
            if j == 0:
                own_residual[...] = residual[:tok_rows]
            inverse = lax.rsqrt(jnp.mean(residual * residual, axis=-1, keepdims=True) + EPSILON)
            mixed = (residual * inverse * gain_ref[0:1, :]).astype(bf16)
            for k in range(group):
                mixed_s[group * j + k] = mixed[k * tok_rows : (k + 1) * tok_rows]
            logits = dot(mixed, router_ref[...])
            marks = jnp.concatenate(
                [
                    named_ref[pl.ds(pl.multiple_of(ring.at(offsets[group * j + k]) * tok_rows, 16), tok_rows)]
                    for k in range(group)
                ],
                axis=0,
            ).astype(f32)
            logits = jnp.where(marks > 0, logits, MASKED)
            powers = jnp.where(
                marks > 0, jnp.exp(logits - jnp.max(logits, axis=-1, keepdims=True)), 0.0
            )
            gates = powers / jnp.sum(powers, axis=-1, keepdims=True)
            if j == 0:
                own_gates[...] = gates[:tok_rows]
            held = jnp.zeros((pair, LANES), f32)
            for x in range(local_experts):
                mine = jnp.sum(
                    jnp.where(lanes == ring.me * local_experts + x, gates, 0.0), axis=-1, keepdims=True
                )
                held = jnp.where(lanes == x, mine, held)
            gate_s[pl.ds(j * pair, pair)] = held
            saves.append(
                pltpu.make_async_copy(
                    mixed_s.at[pl.ds(group * j, group)], mixed_all.at[pl.ds(group * j, group)], save.at[j]
                )
            )
            saves[-1].start()
            advance(steps, 2)

        counts = rows // part
        outgoing = []
        base = n // 2
        for s in range(counts):
            slots = pl.ds(s * group, group)
            part_rows = pl.ds(s * part, part)
            advance(steps, 0 if s < counts - 1 else 64)
            if s == 0:
                own.wait()
            sum_s[part_rows] = jnp.zeros((part, LANES), f32)
            for copy in outgoing:
                copy.wait()
            outgoing = []
            for x in range(local_experts):
                if s == 0:
                    loads[1 + x].wait()
                    if x == 0:
                        loads[1 + local_experts].wait()

                def hidden(t, carry, s=s, x=x, slots=slots, part_rows=part_rows):
                    at = pl.multiple_of(t * tile, tile)
                    mixed = mixed_s[slots].reshape(part, width)
                    back = back_s[slots].reshape(part, width)
                    gate_part = dot(mixed, first_s[x, :, pl.ds(at, tile)])
                    up_part = dot(mixed, first_s[x, :, pl.ds(pl.multiple_of(ff + at, tile), tile)])
                    hidden_back = dot_across(
                        back, second_s[pl.ds(pl.multiple_of(x * ff + at, tile), tile), :]
                    )
                    gate = gate_s[part_rows, x : x + 1]
                    sigmoid = jax.nn.sigmoid(gate_part)
                    swish = gate_part * sigmoid
                    value = swish * up_part
                    out_s[pl.ds(0, part), pl.ds(pl.multiple_of(x * ff + at, tile), tile)] = (
                        value * gate
                    ).astype(bf16)
                    sums = jnp.sum(value * hidden_back, axis=-1, keepdims=True)
                    sum_s[part_rows] = sum_s[part_rows] + jnp.where(lanes == x, sums, 0.0)
                    hidden_back = hidden_back * gate
                    slope = sigmoid * (1.0 + gate_part * (1.0 - sigmoid))
                    up_rows = pl.ds((1 + x) * part, part)
                    out_s[up_rows, pl.ds(at, tile)] = (hidden_back * up_part * slope).astype(bf16)
                    out_s[up_rows, pl.ds(pl.multiple_of(ff + at, tile), tile)] = (
                        hidden_back * swish
                    ).astype(bf16)
                    return carry

                pieces = ff // tile
                lax.fori_loop(0, pieces // 2, hidden, 0)
                advance(steps, 2)
                lax.fori_loop(pieces // 2, pieces, hidden, 0)
                advance(steps, 2)
                outgoing.append(
                    pltpu.make_async_copy(
                        out_s.at[pl.ds((1 + x) * part, part)],
                        up_all.at[x, part_rows],
                        save.at[base + 1 + x],
                    )
                )
                outgoing[-1].start()
            outgoing.append(
                pltpu.make_async_copy(out_s.at[pl.ds(0, part)], gated_all.at[part_rows], save.at[base])
            )
            outgoing[-1].start()
        spread = pltpu.make_async_copy(back_s, back_all, local)
        spread.start()
        for k in range(n):
            gate_back[k] = jnp.transpose(sum_s[pl.ds(k * tok_rows, tok_rows)])[:8]
        for copy in saves + outgoing:
            copy.wait()
        spread.wait()

    return pl.pallas_call(
        body,
        out_shape=(
            jax.ShapeDtypeStruct((n, tok_rows, width), bf16),
            jax.ShapeDtypeStruct((n, tok_rows, width), bf16),
            jax.ShapeDtypeStruct((rows, local_experts * ff), bf16),
            jax.ShapeDtypeStruct((local_experts, rows, 2 * ff), bf16),
            jax.ShapeDtypeStruct((tok_rows, LANES), f32),
            jax.ShapeDtypeStruct((n, 8, LANES), f32),
            jax.ShapeDtypeStruct((tok_rows, width), f32),
        ),
        in_specs=[ANY] * 6 + [VMEM] * 3,
        out_specs=(ANY,) * 4 + (VMEM,) * 3,
        scratch_shapes=[
            pltpu.VMEM(out_all.shape, bf16),
            pltpu.VMEM(first.shape, bf16),
            pltpu.VMEM(second.shape, bf16),
            pltpu.VMEM((n, tok_rows, width), bf16),
            pltpu.VMEM((n, tok_rows, width), bf16),
            pltpu.VMEM((2, pair, width), bf16),
            pltpu.VMEM((pair, width), f32),
            pltpu.VMEM((rows, LANES), f32),
            pltpu.VMEM((rows, LANES), f32),
            sems(2, 2, n // 2),
            sems(2, 2, n // 2),
            sems(2, group, 2),
            sems(2 + local_experts),
            sems(n // 2 + 1 + local_experts),
            pltpu.SemaphoreType.DMA,
        ],
        name="experts_in",
        cost_estimate=pl.CostEstimate(
            flops=2 * rows * width * (width + 3 * ff * local_experts),
            bytes_accessed=60_000_000,
            transcendentals=0,
        ),
        compiler_params=pltpu.CompilerParams(
            collective_id=identity, has_side_effects=True, vmem_limit_bytes=BIG_VMEM
        ),
    )(attend_all, token_all, cotangent, out_all, first, second, gain, router, named)


BIG_VMEM = 60 * 1024 * 1024


def slot_scatter_steps(ring, parts, slots, store, send, receive, need):
    signs = (1, -1)
    half_rows = parts.shape[1] // 2
    f32 = jnp.float32

    def part(offset, half):
        return parts.at[slot_of(offset, ring.n), pl.ds(half * half_rows, half_rows)]

    def copy(way, half, hop, source):
        return remote(
            source,
            slots.at[way, half, hop],
            send.at[way, half, hop],
            receive.at[way, half, hop],
            {"ctx": ring.at(signs[way])},
        )

    started = []
    firsts = [(way, half) for half in (0, 1) for way in (0, 1)]
    firsts.sort(key=lambda one: -slot_of(signs[one[0]] * ring.hops(*one), ring.n))
    for way, half in firsts:
        goal = signs[way] * ring.hops(way, half)
        need(slot_of(goal, ring.n))
        started.append(copy(way, half, 0, part(goal, half)))
        started[-1].start()
    for hop in range(ring.n // 2):
        for way, half in firsts:
            last = ring.hops(way, half) - 1
            if hop <= last:
                slot = slots.at[way, half, hop]
                if hop < last:
                    goal = signs[way] * (last - hop)
                    need(slot_of(goal, ring.n))
                copy(way, half, hop, slot).wait_recv()
                if hop < last:
                    slot[...] = (
                        slot[...].astype(f32) + part(goal, half)[...].astype(f32)
                    ).astype(slot.dtype)
                    started.append(copy(way, half, hop + 1, slot))
                    started[-1].start()
                yield
    need(0)
    for half in (0, 1):
        total = part(0, half)[...].astype(f32)
        for way in (0, 1):
            total = total + slots[way, half, ring.hops(way, half) - 1].astype(f32)
        store(half, total)
    for one in started:
        one.wait_send()


def experts_out(up_all, gated_all, first, second, gate_back, n, identity):
    local_experts, rows, inner = up_all.shape
    width = first.shape[1]
    tok_rows = rows // n
    half_rows = tok_rows // 2
    pair = 2 * tok_rows
    wide = 512
    count = width // wide
    bf16, f32 = jnp.bfloat16, jnp.float32
    offsets = slot_offsets(n)

    def body(
        up_ref,
        gated_ref,
        first_ref,
        second_ref,
        gate_ref,
        row_sum,
        result_all,
        gate_got,
        first_s,
        second_s,
        up_s,
        gated_s,
        part_s,
        result_s,
        slots,
        send,
        receive,
        gate_send,
        gate_receive,
        load,
        first_load,
        other_load,
        save,
    ):
        ring = Ring(n)

        def up_load(j):
            return pltpu.make_async_copy(
                up_ref.at[:, pl.ds(j * pair, pair)], up_s.at[:, pl.ds(j * pair, pair)], load.at[j]
            )

        def weight_load(t):
            return pltpu.make_async_copy(
                first_ref.at[:, pl.ds(t * wide, wide)],
                first_s.at[:, pl.ds(t * wide, wide)],
                first_load.at[t],
            )

        groups = n // 2
        up_load(groups - 1).start()
        for t in range(count):
            weight_load(t).start()
        for j in range(groups - 1):
            up_load(groups - 2 - j).start()
        others = [
            pltpu.make_async_copy(gated_ref, gated_s, other_load.at[0]),
            pltpu.make_async_copy(second_ref, second_s, other_load.at[1]),
        ]
        for copy in others:
            copy.start()
        ring.barrier([{"ctx": ring.at(k)} for k in range(1, n)])
        gate_copies = []
        for k in range(1, n):
            offset = k if k <= n // 2 else k - n
            back = -offset if offset < n // 2 else offset
            gate_copies.append(
                remote(
                    gate_ref.at[slot_of(offset, n)],
                    gate_got.at[slot_of(back, n)],
                    gate_send.at[slot_of(back, n)],
                    gate_receive.at[slot_of(back, n)],
                    {"ctx": ring.at(k)},
                )
            )
            gate_copies[-1].start()
        gate_got[0] = gate_ref[0]

        done = set()

        def product(j):
            rows_j = pl.ds(j * pair, pair)
            up_load(j).wait()

            def columns(t):
                at = pl.ds(pl.multiple_of(t * wide, wide), wide)
                value = dot_across(up_s[0, rows_j], first_s[0, at, :])
                for x in range(1, local_experts):
                    value = value + dot_across(up_s[x, rows_j], first_s[x, at, :])
                value = value.astype(bf16)
                for k in range(2):
                    part_s[2 * j + k, :, at] = value[k * tok_rows : (k + 1) * tok_rows]

            if not done:
                for t in range(count):
                    weight_load(t).wait()
                    columns(t)
            else:

                def step(t, carry):
                    columns(t)
                    return carry

                lax.fori_loop(0, count, step, 0)
            done.add(j)

        def need(slot):
            if slot // 2 not in done:
                product(slot // 2)

        def store(half, total):
            row_sum[pl.ds(half * half_rows, half_rows)] = total

        steps = slot_scatter_steps(ring, part_s, slots, store, send, receive, need)
        for j in reversed(range(groups)):
            need(2 * j)
            advance(steps, 1 if j in (0, groups - 1) else 2)
        for copy in others:
            copy.wait()
        saves = []
        chunk = 2
        for j in range(n // chunk):
            rows_j = pl.ds(j * chunk * tok_rows, chunk * tok_rows)

            def result(t, carry, rows_j=rows_j, j=j):
                at = pl.ds(pl.multiple_of(t * wide, wide), wide)
                value = dot(gated_s[rows_j], second_s[:, at]).astype(bf16)
                for k in range(chunk):
                    result_s[chunk * j + k, :, at] = value[k * tok_rows : (k + 1) * tok_rows]
                return carry

            lax.fori_loop(0, count, result, 0)
            for k in range(chunk):
                slot = chunk * j + k
                device = ring.at(offsets[slot])
                saves.append(
                    pltpu.make_async_copy(
                        result_s.at[slot],
                        result_all.at[pl.ds(pl.multiple_of(device * tok_rows, 16), tok_rows)],
                        save.at[slot],
                    )
                )
                saves[-1].start()
            advance(steps, 2)
        advance(steps, 64)
        for copy in saves:
            copy.wait()
        for copy in gate_copies:
            copy.wait()

    return pl.pallas_call(
        body,
        out_shape=(
            jax.ShapeDtypeStruct((tok_rows, width), f32),
            jax.ShapeDtypeStruct((rows, width), bf16),
            jax.ShapeDtypeStruct(gate_back.shape, f32),
        ),
        in_specs=[ANY] * 4 + [VMEM],
        out_specs=(VMEM, ANY, VMEM),
        scratch_shapes=[
            pltpu.VMEM(first.shape, bf16),
            pltpu.VMEM(second.shape, bf16),
            pltpu.VMEM(up_all.shape, bf16),
            pltpu.VMEM(gated_all.shape, bf16),
            pltpu.VMEM((n, tok_rows, width), bf16),
            pltpu.VMEM((n, tok_rows, width), bf16),
            pltpu.VMEM((2, 2, n // 2, half_rows, width), bf16),
            sems(2, 2, n // 2),
            sems(2, 2, n // 2),
            sems(n),
            sems(n),
            sems(n // 2),
            sems(count),
            sems(2),
            sems(n),
        ],
        name="experts_out",
        cost_estimate=pl.CostEstimate(
            flops=2 * rows * width * 3 * inner // 2 * local_experts,
            bytes_accessed=60_000_000,
            transcendentals=0,
        ),
        compiler_params=pltpu.CompilerParams(
            collective_id=identity, has_side_effects=True, vmem_limit_bytes=BIG_VMEM
        ),
    )(up_all, gated_all, first, second, gate_back)


def exchange_rows(ring, sums, flat, got, send, receive, steps):
    n, rows = ring.n, sums.shape[0]
    for k in range(rows // LANES):
        flat[:, pl.ds(k * LANES, LANES)] = jnp.transpose(sums[pl.ds(k * LANES, LANES)])[:8]
    copies = []
    for k in range(1, n):
        copies.append(
            remote(
                flat,
                got.at[k - 1],
                send.at[k - 1],
                receive.at[k - 1],
                {"ctx": (ring.me + k) % n},
            )
        )
        copies[-1].start()
    advance(steps, 1)
    for copy in copies:
        copy.wait_recv()
    total = flat[...]
    for k in range(n - 1):
        total = total + got[k]
    for k in range(rows // LANES):
        block = total[:, k * LANES : (k + 1) * LANES]
        block = jnp.concatenate([block, jnp.zeros((LANES - 8, LANES), jnp.float32)], axis=0)
        sums[pl.ds(k * LANES, LANES)] = jnp.transpose(block)
    for copy in copies:
        copy.wait_send()


def turn(values, cosine, sine):
    return values * cosine + pltpu.roll(values, HEAD_DIM // 2, 1) * sine


def out_gather_steps(ring, out_ref, chip_ref, out_all, sem):
    own_send, own_receive, ring_send, ring_receive, core_send, core_receive, local = sem
    dp, core, chip, core_chip = partners()
    weight_rows, n, me = out_ref.shape[0], ring.n, ring.me

    def place(group, device):
        return out_all.at[pl.ds(pl.multiple_of((group * n + device) * weight_rows, 16), weight_rows)]

    own = [
        pltpu.make_async_copy(out_ref, place(dp, me), local.at[0]),
        pltpu.make_async_copy(chip_ref, place(chip, me), local.at[1]),
    ]
    copies = [
        remote(out_ref, place(dp, me), own_send.at[0], own_receive.at[0], {"dp": core}),
        remote(chip_ref, place(chip, me), own_send.at[1], own_receive.at[1], {"dp": core}),
    ]
    for copy in own:
        copy.start()

    def arrived(way, half, hop, origin):
        if len(copies) == 2:
            for copy in copies:
                copy.start()
        spot = place(chip if half else dp, origin)
        copies.append(
            remote(
                spot, spot, core_send.at[way, half, hop], core_receive.at[way, half, hop], {"dp": core}
            )
        )
        copies[-1].start()

    yield from gather_steps(
        ring,
        lambda half: chip_ref if half else out_ref,
        lambda device, half: place(chip if half else dp, device),
        ring_send,
        ring_receive,
        arrived,
    )
    for at, group in ((0, core), (1, core_chip)):
        spot = place(group, me)
        remote(spot, spot, own_send.at[at], own_receive.at[at], {"dp": core}).wait_recv()
    for way, sign in ((0, 1), (1, -1)):
        for half in (0, 1):
            for hop in range(ring.hops(way, half)):
                spot = place(core_chip if half else core, ring.at(-sign * (hop + 1)))
                remote(
                    spot,
                    spot,
                    core_send.at[way, half, hop],
                    core_receive.at[way, half, hop],
                    {"dp": core},
                ).wait_recv()
    for copy in copies:
        copy.wait_send()
    for copy in own:
        copy.wait()


def attention_in(
    token_all, in_all, out_rows, out_chip, gain, pair_gains, cosine, sine, bounds, place_row, n, n_dp, identity
):
    rows, width = token_all.shape
    pair = pair_gains.shape[1]
    cols = pair // 2
    heads = cols // HEAD_DIM
    chunk = 256
    weight_rows = out_rows.shape[0]
    bf16, f32 = jnp.bfloat16, jnp.float32
    scale = HEAD_DIM ** (-0.5)

    def body(
        token_ref,
        in_ref,
        out_ref,
        chip_ref,
        gain_ref,
        pair_ref,
        cos_ref,
        sin_ref,
        bound_ref,
        place_ref,
        attend_all,
        out_all,
        probs_all,
        normed_all,
        attend_ref,
        qkv_ref,
        raw_ref,
        inverse_ref,
        probs_s,
        normed_s,
        flat,
        got,
        *sem,
    ):
        out_sem, sem = sem[:7], sem[7:]
        sum_send, sum_receive, ring_send, ring_receive, save = sem
        ring = Ring(n)
        dp, core, chip, core_chip = partners()
        ring.barrier([{"ctx": (ring.me + k) % n} for k in range(1, n)] + [{"dp": core}])
        steps = out_gather_steps(ring, out_ref, chip_ref, out_all, out_sem)
        advance(steps, 1)
        lanes = lax.broadcasted_iota(jnp.int32, (chunk, LANES), 1)

        def chunks(step, count=2):
            total = rows // chunk
            for first in range(0, total, count):
                lax.fori_loop(first, min(first + count, total), step, 0)
                advance(steps, 1)

        def project(j, carry):
            at = pl.ds(pl.multiple_of(j * chunk, chunk), chunk)
            values = token_ref[at].astype(f32)
            inverse = lax.rsqrt(jnp.mean(values * values, axis=-1, keepdims=True) + EPSILON)
            normed = (values * inverse * gain_ref[0:1, :]).astype(bf16)
            normed_s[at] = normed
            projected = dot(normed, in_ref[:, : pair + cols])
            raw_ref[at] = projected[:, :pair]
            qkv_ref[at, pair:] = projected[:, pair:].astype(bf16)
            squares = projected[:, :pair] * projected[:, :pair]
            inverse_ref[at] = jnp.where(
                lanes == 0,
                jnp.sum(squares[:, :cols], axis=-1, keepdims=True),
                jnp.where(lanes == 1, jnp.sum(squares[:, cols:], axis=-1, keepdims=True), 0.0),
            )
            return carry

        chunks(project)
        saves = [pltpu.make_async_copy(normed_s, normed_all, save.at[heads])]
        saves[0].start()
        exchange_rows(ring, inverse_ref, flat, got, sum_send, sum_receive, steps)

        def norm(j, carry):
            at = pl.ds(pl.multiple_of(j * chunk, chunk), chunk)
            inverse = lax.rsqrt(inverse_ref[at] / width + EPSILON)
            inverse_ref[at] = inverse
            for which in range(2):
                for head in range(heads):
                    columns = pl.ds(which * cols + head * HEAD_DIM, HEAD_DIM)
                    values = raw_ref[at, columns] * inverse[:, which : which + 1]
                    values = values * pair_ref[0:1, columns]
                    qkv_ref[at, columns] = turn(values, cos_ref[at], sin_ref[at]).astype(bf16)
            return carry

        chunks(norm)
        for head in range(heads):

            def attend(j, carry, head=head):
                at = pl.ds(pl.multiple_of(j * chunk, chunk), chunk)
                columns = pl.ds(head * HEAD_DIM, HEAD_DIM)
                scores = (
                    dot_across(
                        qkv_ref[at, columns], qkv_ref[:, pl.ds(cols + head * HEAD_DIM, HEAD_DIM)]
                    )
                    * scale
                )
                place = place_ref[0:1, :]
                visible = (place >= bound_ref[at, 0:1]) & (place <= bound_ref[at, 1:2])
                scores = jnp.where(visible, scores, MASKED)
                powers = jnp.where(
                    visible, jnp.exp(scores - jnp.max(scores, axis=-1, keepdims=True)), 0.0
                )
                share = 1.0 / jnp.sum(powers, axis=-1, keepdims=True)
                probs = (powers * share).astype(bf16)
                probs_s[head, at] = probs
                attend_ref[at, columns] = dot(
                    probs, qkv_ref[:, pl.ds(pair + head * HEAD_DIM, HEAD_DIM)]
                ).astype(bf16)
                return carry

            chunks(attend)
            saves.append(pltpu.make_async_copy(probs_s.at[head], probs_all.at[head], save.at[head]))
            saves[-1].start()

        half_rows = rows // 2
        own = pltpu.make_async_copy(
            attend_ref,
            attend_all.at[:, pl.ds(pl.multiple_of(ring.me * cols, LANES), cols)],
            save.at[heads + 1],
        )
        own.start()
        run_steps(
            steps,
            gather_steps(
                ring,
                lambda half: attend_ref.at[pl.ds(half * half_rows, half_rows)],
                lambda device, half: attend_all.at[
                    pl.ds(half * half_rows, half_rows),
                    pl.ds(pl.multiple_of(device * cols, LANES), cols),
                ],
                ring_send,
                ring_receive,
            ),
        )
        own.wait()
        for copy in saves:
            copy.wait()

    return pl.pallas_call(
        body,
        out_shape=(
            jax.ShapeDtypeStruct((rows, width), bf16),
            jax.ShapeDtypeStruct((weight_rows * n * n_dp, width), bf16),
            jax.ShapeDtypeStruct((heads, rows, rows), bf16),
            jax.ShapeDtypeStruct((rows, width), bf16),
            jax.ShapeDtypeStruct((rows, cols), bf16),
            jax.ShapeDtypeStruct((rows, 3 * cols), bf16),
            jax.ShapeDtypeStruct((rows, pair), f32),
            jax.ShapeDtypeStruct((rows, LANES), f32),
        ),
        in_specs=[VMEM, VMEM, ANY, ANY] + [VMEM] * 6,
        out_specs=(ANY,) * 4 + (VMEM,) * 4,
        scratch_shapes=[
            pltpu.VMEM((heads, rows, rows), bf16),
            pltpu.VMEM((rows, width), bf16),
            pltpu.VMEM((8, rows), f32),
            pltpu.VMEM((n - 1, 8, rows), f32),
            sems(2),
            sems(2),
            sems(2, 2, n // 2),
            sems(2, 2, n // 2),
            sems(2, 2, n // 2),
            sems(2, 2, n // 2),
            sems(2),
            sems(n - 1),
            sems(n - 1),
            sems(2, 2, n // 2),
            sems(2, 2, n // 2),
            sems(heads + 2),
        ],
        name="attention_in",
        cost_estimate=pl.CostEstimate(
            flops=2 * rows * width * 3 * cols, bytes_accessed=200_000_000, transcendentals=0
        ),
        compiler_params=pltpu.CompilerParams(
            collective_id=identity, has_side_effects=True, vmem_limit_bytes=BIG_VMEM
        ),
    )(token_all, in_all, out_rows, out_chip, gain, pair_gains, cosine, sine, bounds, place_row)


def gather_with_gradients(block, mixed, up_all, n, n_dp, identity):
    rows, width = block.shape
    half_rows = rows // 2
    count, inner = up_all.shape[0], up_all.shape[2]
    span, tile, piece = width // n_dp, 256, 64
    bf16, f32 = jnp.bfloat16, jnp.float32

    def body(
        block_ref,
        mixed_ref,
        up_ref,
        all_ref,
        near_ref,
        far_ref,
        far_got,
        mixed_s,
        up_s,
        grad_s,
        core_s,
        send,
        receive,
        core_send,
        core_receive,
        local,
        load,
        save,
        far_send,
        far_receive,
    ):
        ring = Ring(n)
        dp, core, chip, core_chip = partners()
        loads = [pltpu.make_async_copy(mixed_ref, mixed_s, load.at[count])]
        for x in range(count):
            loads.append(pltpu.make_async_copy(up_ref.at[x], up_s.at[x], load.at[x]))
        own = pltpu.make_async_copy(
            block_ref, all_ref.at[pl.ds(pl.multiple_of(ring.me * rows, 16), rows)], local
        )
        own.start()
        for copy in loads:
            copy.start()
        ring.barrier(ring.neighbours() + [{"dp": core}, {"dp": chip}])
        steps = gather_steps(
            ring,
            lambda half: block_ref.at[pl.ds(half * half_rows, half_rows)],
            lambda device, half: all_ref.at[
                pl.ds(pl.multiple_of(device * rows + half * half_rows, 16), half_rows)
            ],
            send,
            receive,
        )
        advance(steps, 2)
        loads[0].wait()
        saves, passed = [], []
        for x in range(count):
            loads[1 + x].wait()
            for at, group in enumerate((core_chip, core, chip, dp)):

                def product(j, carry, x=x, at=at, group=group):
                    columns = pl.ds(pl.multiple_of(group * span + j * tile, tile), tile)
                    grad_s[x, at, pl.ds(pl.multiple_of(j * tile, tile), tile)] = lax.dot_general(
                        mixed_s[:, columns],
                        up_s[x],
                        (((0,), (0,)), ((), ())),
                        preferred_element_type=f32,
                    ).astype(bf16)
                    return carry

                lax.fori_loop(0, span // tile, product, 0)
                which = 1 - at % 2
                if at < 2:
                    passed.append(
                        remote(
                            grad_s.at[x, at],
                            core_s.at[x, which],
                            core_send.at[x, which],
                            core_receive.at[x, which],
                            {"dp": core},
                        )
                    )
                    passed[-1].start()
                else:
                    passed[2 * x + at - 2].wait_recv()

                    def add(j, carry, x=x, at=at, which=which):
                        part = pl.ds(pl.multiple_of(j * piece, piece), piece)
                        core_s[x, which, part] = (
                            core_s[x, which, part].astype(f32) + grad_s[x, at, part].astype(f32)
                        ).astype(bf16)
                        return carry

                    lax.fori_loop(0, span // piece, add, 0)
                    if x == 0 and which:
                        across = remote(
                            core_s.at[0, 1, pl.ds(0, PASS_A)], far_got, far_send, far_receive, {"dp": chip}
                        )
                        across.start()
                    saves.append(
                        pltpu.make_async_copy(
                            core_s.at[x, which],
                            (far_ref if which else near_ref).at[x],
                            save.at[x, which],
                        )
                    )
                    saves[-1].start()
                advance(steps, 2)
        advance(steps, 64)
        for copy in passed:
            copy.wait_send()
        across.wait()
        for copy in saves:
            copy.wait()
        own.wait()

    sums = jax.ShapeDtypeStruct((count, span, inner), bf16)
    return pl.pallas_call(
        body,
        out_shape=(
            jax.ShapeDtypeStruct((rows * n, width), block.dtype),
            sums,
            sums,
            jax.ShapeDtypeStruct((PASS_A, inner), bf16),
        ),
        in_specs=[ANY] * 3,
        out_specs=(ANY,) * 4,
        scratch_shapes=[
            pltpu.VMEM(mixed.shape, bf16),
            pltpu.VMEM(up_all.shape, bf16),
            pltpu.VMEM((count, n_dp, span, inner), bf16),
            pltpu.VMEM((count, 2, span, inner), bf16),
            sems(2, 2, n // 2),
            sems(2, 2, n // 2),
            sems(count, 2),
            sems(count, 2),
            pltpu.SemaphoreType.DMA,
            sems(count + 1),
            sems(count, 2),
            pltpu.SemaphoreType.DMA,
            pltpu.SemaphoreType.DMA,
        ],
        name="gather_with_gradients",
        cost_estimate=pl.CostEstimate(
            flops=2 * count * width * inner * mixed.shape[0],
            bytes_accessed=160_000_000,
            transcendentals=0,
        ),
        compiler_params=pltpu.CompilerParams(
            collective_id=identity, has_side_effects=True, vmem_limit_bytes=BIG_VMEM
        ),
    )(block, mixed, up_all)


def attention_back(
    back_all,
    out_all,
    in_all,
    probs,
    attend_low,
    qkv,
    raw,
    inverse,
    pair_gains,
    cosine,
    sine,
    partial,
    far,
    n,
    n_dp,
    identity,
):
    rows, width = back_all.shape
    weight_rows = width // (n * n_dp)
    pair = pair_gains.shape[1]
    cols = pair // 2
    heads = cols // HEAD_DIM
    chunk, wide = 256, 512
    tok_rows = rows // n
    half_rows = tok_rows // 2
    bf16, f32 = jnp.bfloat16, jnp.float32
    scale = HEAD_DIM ** (-0.5)

    def body(
        back_ref,
        out_ref,
        in_ref,
        probs_ref,
        attend_ref,
        qkv_ref,
        raw_ref,
        inverse_ref,
        pair_ref,
        cos_ref,
        sin_ref,
        part_ref,
        far_ref,
        raw_back,
        row_part,
        pair_sum,
        part_sum,
        out_sum,
        far_got,
        next_got,
        out_s,
        in_s,
        probs_s,
        part_s,
        attend_back,
        pair_s,
        value_s,
        sum_s,
        slots,
        flat,
        got,
        sum_send,
        sum_receive,
        ring_send,
        ring_receive,
        load,
        out_p,
        out_core,
        out_chip,
        pass_send,
        pass_receive,
        far_send,
        far_receive,
    ):
        ring = Ring(n)
        dp, core, chip, core_chip = partners()
        loads = [
            pltpu.make_async_copy(part_ref, part_s, load.at[0]),
            pltpu.make_async_copy(
                out_ref.at[pl.ds(pl.multiple_of(ring.me * cols, 16), cols)], out_s, load.at[1]
            ),
            pltpu.make_async_copy(probs_ref, probs_s, load.at[2]),
            pltpu.make_async_copy(in_ref.at[:, pl.ds(0, pair + cols)], in_s, load.at[3]),
        ]
        for copy in loads:
            copy.start()
        ring.barrier(
            [{"ctx": (ring.me + k) % n} for k in range(1, n)] + [{"dp": core}, {"dp": chip}]
        )

        beyond = [
            remote(
                far_ref.at[0, pl.ds(PASS_A, far_got.shape[0])],
                far_got,
                far_send.at[0],
                far_receive.at[0],
                {"dp": chip},
            ),
            remote(
                far_ref.at[1, pl.ds(0, PASS_B)], next_got, far_send.at[1], far_receive.at[1], {"dp": chip}
            ),
        ]
        for copy in beyond:
            copy.start()

        def store(half, total):
            part_sum[pl.ds(half * half_rows, half_rows)] = total

        steps = scatter_steps(
            ring,
            lambda device, half: part_s.at[
                pl.ds(pl.multiple_of(device * tok_rows + half * half_rows, 16), half_rows)
            ],
            slots,
            store,
            ring_send,
            ring_receive,
        )
        loads[0].wait()
        advance(steps, 1)
        lanes = lax.broadcasted_iota(jnp.int32, (chunk, LANES), 1)

        def chunks(step, count=2):
            total = rows // chunk
            for first in range(0, total, count):
                lax.fori_loop(first, min(first + count, total), step, 0)
                advance(steps, 2)

        loads[1].wait()

        def project(j, carry):
            at = pl.ds(pl.multiple_of(j * chunk, chunk), chunk)
            attend_back[at] = dot_across(back_ref[at], out_s[...]).astype(bf16)
            return carry

        chunks(project, 4)

        def out_product(group):
            for t in range(width // wide):
                value = lax.dot_general(
                    attend_ref[:, group * LANES : (group + 1) * LANES],
                    back_ref[:, t * wide : (t + 1) * wide],
                    (((0,), (0,)), ((), ())),
                    preferred_element_type=f32,
                ).astype(bf16)
                for k in range(LANES // weight_rows):
                    out_p[group * LANES // weight_rows + k, :, t * wide : (t + 1) * wide] = value[
                        k * weight_rows : (k + 1) * weight_rows
                    ]

        for group in range(cols // LANES):
            out_product(group)

        def passing(at, source, target, to):
            return remote(source, target, pass_send.at[at], pass_receive.at[at], {"dp": to})

        passed = [
            passing(0, out_p.at[core_chip], out_core.at[1], core),
            passing(1, out_p.at[core], out_core.at[0], core),
        ]
        for copy in passed:
            copy.start()
        loads[2].wait()
        for head in range(heads):
            columns = pl.ds(head * HEAD_DIM, HEAD_DIM)
            key_columns = pl.ds(cols + head * HEAD_DIM, HEAD_DIM)
            value_columns = pl.ds(pair + head * HEAD_DIM, HEAD_DIM)
            pair_s[:, key_columns] = jnp.zeros((rows, HEAD_DIM), f32)
            value_s[:, columns] = jnp.zeros((rows, HEAD_DIM), f32)

            def scores(j, carry, head=head, columns=columns, key_columns=key_columns, value_columns=value_columns):
                at = pl.ds(pl.multiple_of(j * chunk, chunk), chunk)
                back = attend_back[at, columns]
                delta = jnp.sum(
                    back.astype(f32) * attend_ref[at, columns].astype(f32), axis=-1, keepdims=True
                )
                probs_low = probs_s[head, at]
                score_back = (
                    probs_low.astype(f32) * (dot_across(back, qkv_ref[:, value_columns]) - delta)
                ).astype(bf16)
                pair_s[at, columns] = dot(score_back, qkv_ref[:, key_columns])
                over = (((0,), (0,)), ((), ()))
                pair_s[:, key_columns] += lax.dot_general(
                    score_back, qkv_ref[at, columns], over, preferred_element_type=f32
                )
                value_s[:, columns] += lax.dot_general(
                    probs_low, back, over, preferred_element_type=f32
                )
                return carry

            chunks(scores)
        passed[0].wait_recv()
        out_core[1] = (out_core[1].astype(f32) + out_p[chip].astype(f32)).astype(bf16)
        passed.append(passing(2, out_core.at[1], out_chip, chip))
        passed[-1].start()
        pair_sum[...] = jnp.zeros((8, pair), f32)

        def unturn(j, carry):
            at = pl.ds(pl.multiple_of(j * chunk, chunk), chunk)
            held = jnp.zeros((chunk, LANES), f32)
            for which in range(2):
                total = jnp.zeros((chunk, 1), f32)
                for head in range(heads):
                    columns = pl.ds(which * cols + head * HEAD_DIM, HEAD_DIM)
                    back = turn(pair_s[at, columns] * scale, cos_ref[at], -sin_ref[at])
                    normed = raw_ref[at, columns] * inverse_ref[at, which : which + 1]
                    pair_sum[0:1, columns] += jnp.sum(back * normed, axis=0, keepdims=True)
                    back = back * pair_ref[0:1, columns]
                    pair_s[at, columns] = back
                    total = total + jnp.sum(back * normed, axis=-1, keepdims=True)
                held = jnp.where(lanes == which, total, held)
            sum_s[at] = held
            return carry

        chunks(unturn)
        exchange_rows(ring, sum_s, flat, got, sum_send, sum_receive, steps)
        loads[3].wait()

        def finish(j, carry):
            at = pl.ds(pl.multiple_of(j * chunk, chunk), chunk)
            for which in range(2):
                columns = pl.ds(which * cols, cols)
                factor = inverse_ref[at, which : which + 1]
                normed = raw_ref[at, columns] * factor
                mean = sum_s[at, which : which + 1] / width
                raw_back[at, columns] = (factor * (pair_s[at, columns] - normed * mean)).astype(bf16)
            raw_back[at, pl.ds(pair, cols)] = value_s[at].astype(bf16)
            for t in range(width // wide):
                row_part[at, pl.ds(t * wide, wide)] = dot_across(
                    raw_back[at], in_s[pl.ds(t * wide, wide), :]
                ).astype(bf16)
            return carry

        chunks(finish)
        passed[1].wait_recv()
        passed[2].wait_recv()
        out_sum[...] = (
            out_core[0].astype(f32) + out_p[dp].astype(f32) + out_chip[...].astype(f32)
        ).astype(bf16)
        advance(steps, 64)
        for copy in beyond:
            copy.wait()
        for copy in passed:
            copy.wait_send()

    return pl.pallas_call(
        body,
        out_shape=(
            jax.ShapeDtypeStruct((rows, 3 * cols), bf16),
            jax.ShapeDtypeStruct((rows, width), bf16),
            jax.ShapeDtypeStruct((8, pair), f32),
            jax.ShapeDtypeStruct((tok_rows, width), f32),
            jax.ShapeDtypeStruct((weight_rows, width), bf16),
            jax.ShapeDtypeStruct((far.shape[1] - PASS_A, far.shape[2]), bf16),
            jax.ShapeDtypeStruct((PASS_B, far.shape[2]), bf16),
        ),
        in_specs=[VMEM] + [ANY] * 3 + [VMEM] * 7 + [ANY] * 2,
        out_specs=(VMEM,) * 5 + (ANY,) * 2,
        scratch_shapes=[
            pltpu.VMEM((cols, width), bf16),
            pltpu.VMEM((width, pair + cols), bf16),
            pltpu.VMEM((heads, rows, rows), bf16),
            pltpu.VMEM((rows, width), bf16),
            pltpu.VMEM((rows, cols), bf16),
            pltpu.VMEM((rows, pair), f32),
            pltpu.VMEM((rows, cols), f32),
            pltpu.VMEM((rows, LANES), f32),
            pltpu.VMEM((2, 2, n // 2, half_rows, width), bf16),
            pltpu.VMEM((8, rows), f32),
            pltpu.VMEM((n - 1, 8, rows), f32),
            sems(n - 1),
            sems(n - 1),
            sems(2, 2, n // 2),
            sems(2, 2, n // 2),
            sems(4),
            pltpu.VMEM((n_dp, weight_rows, width), bf16),
            pltpu.VMEM((2, weight_rows, width), bf16),
            pltpu.VMEM((weight_rows, width), bf16),
            sems(3),
            sems(3),
            sems(2),
            sems(2),
        ],
        name="attention_back",
        cost_estimate=pl.CostEstimate(
            flops=2 * rows * width * 4 * cols, bytes_accessed=160_000_000, transcendentals=0
        ),
        compiler_params=pltpu.CompilerParams(
            collective_id=identity, has_side_effects=True, vmem_limit_bytes=BIG_VMEM
        ),
    )(
        back_all,
        out_all,
        in_all,
        probs,
        attend_low,
        qkv,
        raw,
        inverse,
        pair_gains,
        cosine,
        sine,
        partial,
        far,
    )


def heads_local(
    tokens,
    document_ids,
    routes,
    norm_gains,
    project_in,
    project_out,
    router_weight,
    expert_in,
    expert_out,
    cotangent,
):
    bf16, f32 = jnp.bfloat16, jnp.float32
    n = lax.axis_size("ctx")
    n_dp = lax.axis_size("dp")
    me = lax.axis_index("ctx")
    tok_rows, width = tokens.shape[1:]
    rows = tok_rows * n
    weight_rows = project_in.shape[0]
    own_heads = HEADS // n
    cols = own_heads * HEAD_DIM
    local_experts = expert_in.shape[0]
    expert_count = local_experts * n
    score_scale = HEAD_DIM ** (-0.5)

    def own(array, size, axis=0):
        return lax.dynamic_slice_in_dim(array, me * size, size, axis)

    named = jnp.any(routes[0][..., None] == jnp.arange(LANES, dtype=jnp.int32), axis=1).astype(bf16)
    small = jnp.concatenate(
        [router_weight, norm_gains, jnp.zeros((weight_rows, LANES - 4 - expert_count), bf16)], axis=1
    )
    in_blocks = project_in.reshape(weight_rows, 3, n, cols).transpose(2, 0, 1, 3)
    in_blocks = jnp.concatenate(
        [
            in_blocks.reshape(n, weight_rows, 3 * cols),
            jnp.broadcast_to(small[None], (n, weight_rows, LANES)),
        ],
        axis=2,
    )
    token_all, named_all, in_all, out_chip = gather_inputs(
        tokens[0], named, in_blocks, project_out, n, n_dp, 1
    )
    named_all = named_all.reshape(rows, LANES)
    in_all = in_all.reshape(width, 3 * cols + LANES)
    small_all = in_all[:, 3 * cols :]
    gains = small_all[:, expert_count : expert_count + 4].astype(f32)
    router_all = small_all[:, :expert_count]
    first = lax.all_gather(expert_in, "dp", axis=1, tiled=True)
    second = lax.all_gather(expert_out, "dp", axis=1, tiled=True).reshape(local_experts * FF, width)

    half_rows = tok_rows // 2

    def dealt(row):
        blocks = row.reshape(2 * n, half_rows)
        return jnp.stack([blocks[:n], blocks[n:][::-1]], axis=1).reshape(rows)

    places = dealt(jnp.arange(rows, dtype=jnp.int32))
    document_row = document_ids[0]
    starts = dealt(document_starts(document_row))
    relative = places - starts
    cosine, sine = rotary_tables(relative, HEAD_DIM)
    cosine = jnp.concatenate([cosine[:, 0], cosine[:, 0]], axis=-1)
    sine = jnp.concatenate([-sine[:, 0], sine[:, 0]], axis=-1)
    bounds = jnp.stack([starts, places], axis=1)
    place_row = places[None]
    pair_gains = own(gains, cols)[:, 1:3].T.reshape(1, 2 * cols)

    attend_gain = gains[:, 0][None]
    attend_all, out_all, probs, attend_in, attend_low, qkv, raw, inverse = attention_in(
        token_all,
        in_all,
        project_out,
        out_chip,
        attend_gain,
        pair_gains,
        cosine,
        sine,
        bounds,
        place_row,
        n,
        n_dp,
        10,
    )

    upstream_all, mixed_all, gated_all, up_all, own_gates, gate_back, own_residual = experts_in(
        attend_all,
        token_all,
        cotangent[0],
        out_all,
        first,
        second,
        gains[:, 3][None],
        small_all,
        named_all,
        n,
        8,
    )
    mixed_slots = mixed_all.reshape(rows, width)
    second_back = jnp.einsum(
        "tf,td->fd", gated_all, upstream_all.reshape(rows, width), preferred_element_type=f32
    ).astype(bf16)
    second_back, up_all = lax.optimization_barrier((second_back, up_all))
    expert_out_gradient = lax.psum_scatter(
        second_back.reshape(local_experts, FF, width), "dp", scatter_dimension=1, tiled=True
    ).astype(f32)
    mixed_back, mixture, gate_back = experts_out(up_all, gated_all, first, second, gate_back, n, 9)
    gate_back = gate_back[:, :local_experts]
    place = ring_place(me, n)
    gate_back = sum(
        jnp.where(
            (jnp.arange(n) == ring_device((place + offset + n) % n, n))[:, None, None],
            gate_back[slot],
            0.0,
        )
        for slot, offset in enumerate(slot_offsets(n))
    )
    gate_back = gate_back.reshape(expert_count, tok_rows).T

    own_gates = own_gates[:, :expert_count]
    own_mixed = mixed_all[0]
    own_mixed_inverse = inverse_rms(own_residual)
    own_mixed_normed = own_residual * own_mixed_inverse
    chosen_back = own_gates * (
        gate_back - jnp.sum(own_gates * gate_back, axis=-1, keepdims=True)
    )
    logit_back = chosen_back.astype(bf16)
    router_part = jnp.einsum("td,te->ed", own_mixed, logit_back, preferred_element_type=f32)
    mixed_back = mixed_back + jnp.einsum(
        "te,de->td", logit_back, router_all, preferred_element_type=f32
    )
    mixed_gain_back = jnp.sum(mixed_back * own_mixed_normed, axis=0)
    residual_back = cotangent[0].astype(f32) + normalize_back(
        mixed_back * gains[:, 3], own_mixed_normed, own_mixed_inverse
    )
    back_all, near, far, got_a = gather_with_gradients(
        residual_back.astype(bf16), mixed_slots, up_all, n, n_dp, 5
    )

    raw_back, row_part, pair_sum, mixture, out_part, got_b, got_c = attention_back(
        back_all,
        out_all,
        in_all,
        probs,
        attend_low,
        qkv,
        raw,
        inverse,
        pair_gains,
        cosine,
        sine,
        mixture,
        far,
        n,
        n_dp,
        11,
    )
    layer_output = (own_residual + mixture).astype(bf16)
    pairs = [(d * n + c, c * n_dp + d) for d in range(n_dp) for c in range(n)]
    project_out_gradient = lax.ppermute(out_part, ("dp", "ctx"), pairs).astype(f32)

    small_rows = -(-(4 + expert_count) // 8) * 8
    small_part = jnp.concatenate(
        [
            jnp.zeros((3, width), f32),
            mixed_gain_back[None],
            router_part,
            jnp.zeros((small_rows - 4 - expert_count, width), f32),
        ],
        axis=0,
    )
    tokens_back, project_in_gradient, small_gradient, got_d = scatter_end(
        row_part,
        attend_in,
        raw_back,
        tokens[0],
        residual_back,
        attend_gain,
        small_part,
        pair_sum,
        far,
        n,
        n_dp,
        6,
    )
    expert_in_gradient = near.astype(f32) + (
        jnp.concatenate([got_a, got_b, got_c, got_d], axis=0).reshape(near.shape).astype(f32)
    )
    per_tile = LANES // weight_rows
    small_gradient = lax.dynamic_slice_in_dim(
        small_gradient, me % per_tile * weight_rows, weight_rows, 1
    ).T
    return (
        layer_output[None],
        tokens_back[None],
        small_gradient[:, :4],
        project_in_gradient,
        project_out_gradient,
        small_gradient[:, 4 : 4 + expert_count],
        expert_in_gradient,
        expert_out_gradient,
    )


def layer(*arrays):
    n, tok_rows, experts = lax.axis_size("ctx"), arrays[0].shape[1], arrays[7].shape[0]
    fits = HEADS % n == 0 and n % 4 == 0 and lax.axis_size("dp") == 4
    fits = fits and tok_rows == LANES and experts == 2 and experts * n + 4 <= LANES
    return (heads_local if fits else gathered_local)(*arrays)


def solution(mesh):
    placed = (
        P("dp", "ctx", None),
        P("dp", None),
        P("dp", "ctx", None),
        P(("dp", "ctx"), None),
        P(("dp", "ctx"), None),
        P(("dp", "ctx"), None),
        P(("dp", "ctx"), None),
        P("ctx", "dp", None),
        P("ctx", "dp", None),
        P("dp", "ctx", None),
    )
    return jax.shard_map(
        layer,
        mesh=mesh,
        in_specs=placed,
        out_specs=(
            P("dp", "ctx", None),
            P("dp", "ctx", None),
            P(("dp", "ctx"), None),
            P(("dp", "ctx"), None),
            P(("dp", "ctx"), None),
            P(("dp", "ctx"), None),
            P("ctx", "dp", None),
            P("ctx", "dp", None),
        ),
        check_vma=False,
    )
```

```python
import jax
import jax.numpy as jnp
from jax import lax
from jax.experimental import pallas as pl
from jax.experimental.pallas import tpu as pltpu
from jax.sharding import PartitionSpec as P

HEADS = 16
HEAD_DIM = 128
FF = 1024


EPSILON = 1e-05
ROPE_BASE = 10000.0
MASKED = -1e30
LANES = 128
PASS_A, PASS_B = 256, 256
CUTS = 2
WAITS = (4, 6, 6)
TILE = 512
WIDE = 1024


def inverse_rms(values):
    return lax.rsqrt(jnp.mean(values * values, axis=-1, keepdims=True) + EPSILON)


def normalize_back(normed_back, normed, inverse):
    return inverse * (normed_back - normed * jnp.mean(normed_back * normed, axis=-1, keepdims=True))


def rotary_tables(relative, head_dim):
    half_dim = head_dim // 2
    frequency = ROPE_BASE ** (-jnp.arange(half_dim, dtype=jnp.float32) / half_dim)
    angles = relative.astype(jnp.float32)[..., None] * frequency
    return (jnp.cos(angles)[..., None, :], jnp.sin(angles)[..., None, :])


def rotate(values, cosine, sine_table):
    half_dim = values.shape[-1] // 2
    first_half = values[..., :half_dim]
    second_half = values[..., half_dim:]
    return jnp.concatenate(
        [
            first_half * cosine - second_half * sine_table,
            second_half * cosine + first_half * sine_table,
        ],
        axis=-1,
    )


def dealt_positions(indices, tok_rows, context_size):
    half_block = tok_rows // 2
    device = indices // tok_rows
    within = indices % tok_rows
    block_index = jnp.where(within < half_block, device, 2 * context_size - 1 - device)
    return block_index * half_block + within % half_block


def document_starts(document_row):
    places = jnp.arange(document_row.shape[-1], dtype=jnp.int32)
    head_flag = jnp.ones(document_row.shape[:-1] + (1,), jnp.bool_)
    fresh_start = jnp.concatenate(
        [head_flag, document_row[..., 1:] != document_row[..., :-1]], axis=-1
    )
    return lax.cummax(jnp.where(fresh_start, places, 0), axis=document_row.ndim - 1)


def block_scores(
    query_rows, key_block, query_place, query_document, key_place, key_document, score_scale
):
    scores = (
        jnp.einsum("thd,khd->htk", query_rows, key_block, preferred_element_type=jnp.float32)
        * score_scale
    )
    visible = (
        (key_document[None, :] == query_document[:, None])
        & (key_place[None, :] <= query_place[:, None])
    )[None]
    return (jnp.where(visible, scores, MASKED), visible)


def block_backward(
    query_rows,
    output_back,
    row_logsum,
    row_delta,
    key_block,
    value_block,
    query_place,
    query_document,
    key_place,
    key_document,
    score_scale,
):
    scores, visible = block_scores(
        query_rows, key_block, query_place, query_document, key_place, key_document, score_scale
    )
    prob_rows = jnp.where(visible, jnp.exp(scores - row_logsum[..., None]), 0.0)
    prob_back = jnp.einsum(
        "thd,khd->htk", output_back, value_block, preferred_element_type=jnp.float32
    )
    score_back = (prob_rows * (prob_back - row_delta[..., None])).astype(jnp.bfloat16)
    query_part = (
        jnp.einsum("htk,khd->thd", score_back, key_block, preferred_element_type=jnp.float32)
        * score_scale
    )
    key_part = (
        jnp.einsum("htk,thd->khd", score_back, query_rows, preferred_element_type=jnp.float32)
        * score_scale
    )
    value_part = jnp.einsum(
        "htk,thd->khd",
        prob_rows.astype(jnp.bfloat16),
        output_back,
        preferred_element_type=jnp.float32,
    )
    return (query_part, key_part, value_part)


def dispatch_plan(route_rows, expert_count, capacity):
    flat_routes = route_rows.reshape(-1)
    pair_count = flat_routes.shape[0]
    member = (flat_routes[:, None] == jnp.arange(expert_count, dtype=jnp.int32)[None, :]).astype(
        jnp.int32
    )
    earlier = jnp.cumsum(member, axis=0) - member
    target_slot = flat_routes * capacity + jnp.sum(earlier * member, axis=1)
    slot_owner = (
        jnp.full((expert_count * capacity,), pair_count, jnp.int32)
        .at[target_slot]
        .set(jnp.arange(pair_count, dtype=jnp.int32))
    )
    return (target_slot, slot_owner)


def gathered_local(
    tokens,
    document_ids,
    routes,
    norm_gains,
    project_in,
    project_out,
    router_weight,
    expert_in,
    expert_out,
    cotangent,
):
    inputs = tokens[0].astype(jnp.float32)
    tok_rows, model_width = inputs.shape
    context_size = lax.axis_size("ctx")
    sequence_rows = tok_rows * context_size
    local_experts = expert_in.shape[0]
    expert_count = local_experts * context_size
    route_rows = routes[0]
    top_count = route_rows.shape[1]
    capacity = 2 * tok_rows * top_count // expert_count
    score_scale = HEAD_DIM ** (-0.5)
    key_span = min(512, sequence_rows)
    key_blocks = sequence_rows // key_span
    heads_shape = (tok_rows, HEADS, HEAD_DIM)
    block_shape = (key_blocks, key_span, HEADS, HEAD_DIM)
    slot_shape = (context_size, local_experts * capacity, model_width)
    expert_shape = (context_size, local_experts, capacity, model_width)
    gathered_gains, gathered_in, gathered_out, gathered_router = (
        lax.all_gather(norm_gains, ("dp", "ctx"), axis=0, tiled=True),
        lax.all_gather(project_in, ("dp", "ctx"), axis=0, tiled=True),
        lax.all_gather(project_out, ("dp", "ctx"), axis=0, tiled=True),
        lax.all_gather(router_weight, ("dp", "ctx"), axis=0, tiled=True),
    )
    gathered_first, gathered_second = (
        lax.all_gather(expert_in, "dp", axis=1, tiled=True),
        lax.all_gather(expert_out, "dp", axis=1, tiled=True),
    )
    gain_rows = gathered_gains.astype(jnp.float32)
    own_rows = lax.axis_index("ctx") * tok_rows + jnp.arange(tok_rows, dtype=jnp.int32)
    own_place = dealt_positions(own_rows, tok_rows, context_size)
    all_place = dealt_positions(jnp.arange(sequence_rows, dtype=jnp.int32), tok_rows, context_size)
    document_row = document_ids[0]
    own_document = jnp.take(document_row, own_place)
    all_document = jnp.take(document_row, all_place)
    relative = own_place - jnp.take(document_starts(document_row), own_place)
    cosine, sine_table = rotary_tables(relative, HEAD_DIM)
    attend_inverse = inverse_rms(inputs)
    attend_normed = inputs * attend_inverse
    attend_in = (attend_normed * gain_rows[:, 0]).astype(jnp.bfloat16)
    projected = jnp.dot(attend_in, gathered_in, preferred_element_type=jnp.float32)
    raw_query = projected[:, :model_width]
    raw_key = projected[:, model_width : 2 * model_width]
    query_inverse = inverse_rms(raw_query)
    query_normed = raw_query * query_inverse
    key_inverse = inverse_rms(raw_key)
    key_normed = raw_key * key_inverse
    query_low = rotate(
        (query_normed * gain_rows[:, 1]).reshape(heads_shape), cosine, sine_table
    ).astype(jnp.bfloat16)
    key_low = rotate(
        (key_normed * gain_rows[:, 2]).reshape(heads_shape), cosine, sine_table
    ).astype(jnp.bfloat16)
    value_low = projected[:, 2 * model_width :].astype(jnp.bfloat16)
    key_all, value_all = (
        lax.all_gather(key_low.reshape(tok_rows, model_width), "ctx", axis=0, tiled=True),
        lax.all_gather(value_low, "ctx", axis=0, tiled=True),
    )
    key_split = key_all.reshape(block_shape)
    value_split = value_all.reshape(block_shape)
    place_split = all_place.reshape(key_blocks, key_span)
    document_split = all_document.reshape(key_blocks, key_span)

    def total_step(state_pair, block_args):
        row_peak, row_total = state_pair
        key_block, key_place, key_document = block_args
        scores, visible = block_scores(
            query_low, key_block, own_place, own_document, key_place, key_document, score_scale
        )
        new_peak = jnp.maximum(row_peak, jnp.max(scores, axis=-1))
        fresh_total = jnp.sum(
            jnp.where(visible, jnp.exp(scores - new_peak[..., None]), 0.0), axis=-1
        )
        return ((new_peak, row_total * jnp.exp(row_peak - new_peak) + fresh_total), None)

    start_pair = (
        jnp.full((HEADS, tok_rows), MASKED, jnp.float32),
        jnp.zeros((HEADS, tok_rows), jnp.float32),
    )
    (row_peak, row_total), unused = lax.scan(
        total_step, start_pair, (key_split, place_split, document_split)
    )
    row_logsum = row_peak + jnp.log(row_total)

    def value_step(running, block_args):
        key_block, value_block, key_place, key_document = block_args
        scores, visible = block_scores(
            query_low, key_block, own_place, own_document, key_place, key_document, score_scale
        )
        prob_low = jnp.where(visible, jnp.exp(scores - row_logsum[..., None]), 0.0).astype(
            jnp.bfloat16
        )
        return (
            running
            + jnp.einsum("htk,khd->thd", prob_low, value_block, preferred_element_type=jnp.float32),
            None,
        )

    attend_out, unused = lax.scan(
        value_step,
        jnp.zeros(heads_shape, jnp.float32),
        (key_split, value_split, place_split, document_split),
    )
    attend_low = attend_out.reshape(tok_rows, model_width).astype(jnp.bfloat16)
    residual = inputs + jnp.dot(attend_low, gathered_out, preferred_element_type=jnp.float32)
    mixed_inverse = inverse_rms(residual)
    mixed_normed = residual * mixed_inverse
    mixed_low = (mixed_normed * gain_rows[:, 3]).astype(jnp.bfloat16)
    logits = jnp.dot(mixed_low, gathered_router, preferred_element_type=jnp.float32)
    route_onehot = (route_rows[..., None] == jnp.arange(expert_count, dtype=jnp.int32)).astype(
        jnp.float32
    )
    gate_weights = jax.nn.softmax(jnp.sum(route_onehot * logits[:, None, :], axis=-1), axis=-1)
    target_slot, slot_owner = dispatch_plan(route_rows, expert_count, capacity)
    padded_rows = jnp.concatenate([mixed_low, jnp.zeros((1, model_width), jnp.bfloat16)], axis=0)
    send_rows = jnp.take(padded_rows, slot_owner // top_count, axis=0).reshape(slot_shape)
    received = lax.all_to_all(send_rows, "ctx", split_axis=0, concat_axis=0, tiled=True).reshape(
        expert_shape
    )
    expert_up = jnp.einsum(
        "sxcd,xdf->sxcf", received, gathered_first, preferred_element_type=jnp.float32
    )
    gate_part = expert_up[..., :FF]
    up_part = expert_up[..., FF:]
    sigmoid_gate = jax.nn.sigmoid(gate_part)
    swish_gate = gate_part * sigmoid_gate
    hidden_low = (swish_gate * up_part).astype(jnp.bfloat16)
    expert_result = jnp.einsum(
        "sxcf,xfd->sxcd", hidden_low, gathered_second, preferred_element_type=jnp.float32
    ).astype(jnp.bfloat16)
    returned = lax.all_to_all(
        expert_result.reshape(slot_shape), "ctx", split_axis=0, concat_axis=0, tiled=True
    ).reshape(expert_count * capacity, model_width)
    pair_result = jnp.take(returned, target_slot, axis=0).reshape(tok_rows, top_count, model_width)
    mixture = jnp.sum(gate_weights[..., None] * pair_result, axis=1)
    layer_output = (residual + mixture).astype(jnp.bfloat16)
    upstream = cotangent[0].astype(jnp.float32)
    pair_back = (gate_weights[..., None] * upstream[:, None, :]).astype(jnp.bfloat16)
    gate_back = jnp.sum(pair_result * upstream[:, None, :], axis=-1)
    padded_back = jnp.concatenate(
        [
            pair_back.reshape(tok_rows * top_count, model_width),
            jnp.zeros((1, model_width), jnp.bfloat16),
        ],
        axis=0,
    )
    send_back = jnp.take(padded_back, slot_owner, axis=0).reshape(slot_shape)
    received_back = lax.all_to_all(
        send_back, "ctx", split_axis=0, concat_axis=0, tiled=True
    ).reshape(expert_shape)
    first_back, second_back = (gathered_first, gathered_second)
    hidden_back = jnp.einsum(
        "sxcd,xfd->sxcf", received_back, second_back, preferred_element_type=jnp.float32
    )
    second_weight_back = jnp.einsum(
        "sxcf,sxcd->xfd", hidden_low, received_back, preferred_element_type=jnp.float32
    )
    swish_slope = sigmoid_gate * (1.0 + gate_part * (1.0 - sigmoid_gate))
    up_back = jnp.concatenate(
        [hidden_back * up_part * swish_slope, hidden_back * swish_gate], axis=-1
    ).astype(jnp.bfloat16)
    first_weight_back = jnp.einsum(
        "sxcd,sxcf->xdf", received, up_back, preferred_element_type=jnp.float32
    )
    input_back = jnp.einsum(
        "sxcf,xdf->sxcd", up_back, first_back, preferred_element_type=jnp.float32
    ).astype(jnp.bfloat16)
    expert_in_gradient, expert_out_gradient = (
        lax.psum_scatter(
            first_weight_back.astype(jnp.bfloat16), "dp", scatter_dimension=1, tiled=True
        ).astype(jnp.float32),
        lax.psum_scatter(
            second_weight_back.astype(jnp.bfloat16), "dp", scatter_dimension=1, tiled=True
        ).astype(jnp.float32),
    )
    rows_back = lax.all_to_all(
        input_back.reshape(slot_shape), "ctx", split_axis=0, concat_axis=0, tiled=True
    ).reshape(expert_count * capacity, model_width)
    mixed_back = jnp.sum(
        jnp.take(rows_back, target_slot, axis=0)
        .reshape(tok_rows, top_count, model_width)
        .astype(jnp.float32),
        axis=1,
    )
    gains_back, in_back, out_back, router_back = (
        gathered_gains,
        gathered_in,
        gathered_out,
        gathered_router,
    )
    gain_values = gains_back.astype(jnp.float32)
    chosen_back = gate_weights * (
        gate_back - jnp.sum(gate_weights * gate_back, axis=-1, keepdims=True)
    )
    logit_back = jnp.sum(chosen_back[..., None] * route_onehot, axis=1).astype(jnp.bfloat16)
    router_weight_back = jnp.einsum(
        "td,te->de", mixed_low, logit_back, preferred_element_type=jnp.float32
    )
    mixed_back = mixed_back + jnp.einsum(
        "te,de->td", logit_back, router_back, preferred_element_type=jnp.float32
    )
    mixed_gain_back = jnp.sum(mixed_back * mixed_normed, axis=0)
    residual_back = upstream + normalize_back(
        mixed_back * gain_values[:, 3], mixed_normed, mixed_inverse
    )
    residual_low = residual_back.astype(jnp.bfloat16)
    out_weight_back = jnp.einsum(
        "td,te->de", attend_low, residual_low, preferred_element_type=jnp.float32
    )
    attend_back = (
        jnp.einsum("te,de->td", residual_low, out_back, preferred_element_type=jnp.float32)
        .astype(jnp.bfloat16)
        .reshape(heads_shape)
    )
    row_delta = jnp.einsum("thd,thd->ht", attend_back.astype(jnp.float32), attend_out)

    def back_step(query_acc, block_args):
        key_block, value_block, key_place, key_document = block_args
        query_part, key_part, value_part = block_backward(
            query_low,
            attend_back,
            row_logsum,
            row_delta,
            key_block,
            value_block,
            own_place,
            own_document,
            key_place,
            key_document,
            score_scale,
        )
        return (query_acc + query_part, (key_part, value_part))

    query_back, (key_parts, value_parts) = lax.scan(
        back_step,
        jnp.zeros(heads_shape, jnp.float32),
        (key_split, value_split, place_split, document_split),
    )
    key_back, value_back = (
        lax.psum_scatter(
            key_parts.reshape(sequence_rows, model_width).astype(jnp.bfloat16),
            "ctx",
            scatter_dimension=0,
            tiled=True,
        ).astype(jnp.float32),
        lax.psum_scatter(
            value_parts.reshape(sequence_rows, model_width).astype(jnp.bfloat16),
            "ctx",
            scatter_dimension=0,
            tiled=True,
        ).astype(jnp.float32),
    )
    query_flat = rotate(query_back, cosine, -sine_table).reshape(tok_rows, model_width)
    key_flat = rotate(key_back.reshape(heads_shape), cosine, -sine_table).reshape(
        tok_rows, model_width
    )
    query_gain_back = jnp.sum(query_flat * query_normed, axis=0)
    key_gain_back = jnp.sum(key_flat * key_normed, axis=0)
    raw_query_back = normalize_back(query_flat * gain_values[:, 1], query_normed, query_inverse)
    raw_key_back = normalize_back(key_flat * gain_values[:, 2], key_normed, key_inverse)
    raw_back = jnp.concatenate([raw_query_back, raw_key_back, value_back], axis=-1).astype(
        jnp.bfloat16
    )
    in_weight_back = jnp.einsum(
        "td,tf->df", attend_in, raw_back, preferred_element_type=jnp.float32
    )
    attend_in_back = jnp.einsum("tf,df->td", raw_back, in_back, preferred_element_type=jnp.float32)
    attend_gain_back = jnp.sum(attend_in_back * attend_normed, axis=0)
    tokens_back = residual_back + normalize_back(
        attend_in_back * gain_values[:, 0], attend_normed, attend_inverse
    )
    gain_columns = jnp.stack(
        [attend_gain_back, query_gain_back, key_gain_back, mixed_gain_back], axis=1
    )
    gains_gradient, project_in_gradient, project_out_gradient, router_gradient = (
        lax.psum_scatter(gain_columns, ("dp", "ctx"), scatter_dimension=0, tiled=True),
        lax.psum_scatter(in_weight_back, ("dp", "ctx"), scatter_dimension=0, tiled=True),
        lax.psum_scatter(out_weight_back, ("dp", "ctx"), scatter_dimension=0, tiled=True),
        lax.psum_scatter(router_weight_back, ("dp", "ctx"), scatter_dimension=0, tiled=True),
    )
    return (
        layer_output[None],
        tokens_back.astype(jnp.bfloat16)[None],
        gains_gradient,
        project_in_gradient,
        project_out_gradient,
        router_gradient,
        expert_in_gradient,
        expert_out_gradient,
    )


MESH = pl.DeviceIdType.MESH
VMEM_LIMIT = 48 * 1024 * 1024


def ring_place(device, n):
    odd = device % 2
    return (1 - odd) * (device // 2) + odd * (n - 1 - device // 2)


def ring_device(place, n):
    far = place // (n // 2)
    return (1 - far) * (2 * place) + far * (2 * (n - 1 - place) + 1)


class Ring:
    def __init__(self, n):
        self.n = n
        self.me = lax.axis_index("ctx")
        self.place = ring_place(self.me, n)

    def at(self, offset):
        return ring_device((self.place + offset + self.n) % self.n, self.n)

    def hops(self, way, half):
        return self.n // 2 if way == half else self.n // 2 - 1

    def barrier(self, others):
        semaphore = pltpu.get_barrier_semaphore()
        for other in others:
            pl.semaphore_signal(semaphore, inc=1, device_id=other, device_id_type=MESH)
        pl.semaphore_wait(semaphore, len(others))

    def neighbours(self):
        return [{"ctx": self.at(1)}, {"ctx": self.at(-1)}]


def remote(source, target, send, receive, device):
    return pltpu.make_async_remote_copy(
        src_ref=source,
        dst_ref=target,
        send_sem=send,
        recv_sem=receive,
        device_id=device,
        device_id_type=MESH,
    )


def gather_steps(ring, source, place, send, receive, arrived=None, ready=None):
    signs = (1, -1)

    def copy(way, half, hop):
        origin = ring.at(-signs[way] * hop)
        spot = place(origin, half)
        return remote(
            source(half) if hop == 0 else spot,
            spot,
            send.at[way, half, hop],
            receive.at[way, half, hop],
            {"ctx": ring.at(signs[way])},
        )

    def landed(way, half, hop):
        spot = place(ring.at(-signs[way] * (hop + 1)), half)
        return remote(
            spot,
            spot,
            send.at[way, half, hop],
            receive.at[way, half, hop],
            {"ctx": ring.at(signs[way])},
        )

    started = []
    for half in (0, 1):
        if ready is not None:
            ready(half)
        for way in (0, 1):
            started.append(copy(way, half, 0))
            started[-1].start()
        yield
    for hop in range(ring.n // 2):
        for half in (0, 1):
            for way in (0, 1):
                if hop < ring.hops(way, half):
                    landed(way, half, hop).wait_recv()
                    if hop + 1 < ring.hops(way, half):
                        started.append(copy(way, half, hop + 1))
                        started[-1].start()
                    if arrived is not None:
                        arrived(way, half, hop, ring.at(-signs[way] * (hop + 1)))
                    yield
    for one in started:
        one.wait_send()


def scatter_steps(ring, part, slots, store, send, receive):
    signs = (1, -1)

    def copy(way, half, hop, source):
        return remote(
            source,
            slots.at[way, half, hop],
            send.at[way, half, hop],
            receive.at[way, half, hop],
            {"ctx": ring.at(signs[way])},
        )

    started = []
    for half in (0, 1):
        for way in (0, 1):
            goal = ring.at(signs[way] * ring.hops(way, half))
            started.append(copy(way, half, 0, part(goal, half)))
            started[-1].start()
        yield
    for hop in range(ring.n // 2):
        for half in (0, 1):
            for way in (0, 1):
                last = ring.hops(way, half) - 1
                if hop <= last:
                    slot = slots.at[way, half, hop]
                    copy(way, half, hop, slot).wait_recv()
                    if hop < last:
                        goal = ring.at(signs[way] * (last - hop))
                        slot[...] = (
                            slot[...].astype(jnp.float32)
                            + part(goal, half)[...].astype(jnp.float32)
                        ).astype(slot.dtype)
                        started.append(copy(way, half, hop + 1, slot))
                        started[-1].start()
                    yield
    for half in (0, 1):
        total = part(ring.me, half)[...].astype(jnp.float32)
        for way in (0, 1):
            total = total + slots[way, half, ring.hops(way, half) - 1].astype(jnp.float32)
        store(half, total)
    for one in started:
        one.wait_send()


def run_steps(*tasks):
    tasks = list(tasks)
    while tasks:
        left = []
        for task in tasks:
            try:
                next(task)
                left.append(task)
            except StopIteration:
                pass
        tasks = left


def sems(*shape):
    return pltpu.SemaphoreType.DMA(shape)


def kernel_call(body, outs, in_specs, out_specs, scratch, identity, name, sent):
    return pl.pallas_call(
        body,
        out_shape=outs,
        in_specs=in_specs,
        out_specs=out_specs,
        scratch_shapes=scratch,
        name=name,
        cost_estimate=pl.CostEstimate(flops=0, bytes_accessed=sent, transcendentals=0),
        compiler_params=pltpu.CompilerParams(
            collective_id=identity, has_side_effects=True, vmem_limit_bytes=VMEM_LIMIT
        ),
    )


ANY = pl.BlockSpec(memory_space=pl.ANY)
VMEM = pl.BlockSpec(memory_space=pltpu.VMEM)


def ring_gather(block, n, identity, name, axis=0):
    rows, width = block.shape
    half_rows = rows // 2
    shape = (rows * n, width) if axis == 0 else (rows, width * n)

    def body(block_ref, all_ref, send, receive, local):
        ring = Ring(n)

        def place(device, half):
            if axis == 0:
                return all_ref.at[pl.ds(pl.multiple_of(device * rows + half * half_rows, 16), half_rows)]
            return all_ref.at[
                pl.ds(half * half_rows, half_rows), pl.ds(pl.multiple_of(device * width, 128), width)
            ]

        whole = (
            all_ref.at[pl.ds(pl.multiple_of(ring.me * rows, 16), rows)]
            if axis == 0
            else all_ref.at[:, pl.ds(pl.multiple_of(ring.me * width, 128), width)]
        )
        own = pltpu.make_async_copy(block_ref, whole, local)
        own.start()
        ring.barrier(ring.neighbours())
        run_steps(
            gather_steps(
                ring,
                lambda half: block_ref.at[pl.ds(half * half_rows, half_rows)],
                place,
                send,
                receive,
            )
        )
        own.wait()

    return kernel_call(
        body,
        jax.ShapeDtypeStruct(shape, block.dtype),
        [ANY],
        ANY,
        [sems(2, 2, n // 2), sems(2, 2, n // 2), pltpu.SemaphoreType.DMA],
        identity,
        name,
        block.size * 2 * n * 32,
    )(block)


def ring_scatter(partial, n, identity, name):
    rows, width = partial.shape[0] // n, partial.shape[1]
    half_rows = rows // 2

    def body(part_ref, sum_ref, slots, send, receive):
        ring = Ring(n)
        ring.barrier(ring.neighbours())

        def part(device, half):
            return part_ref.at[pl.ds(pl.multiple_of(device * rows + half * half_rows, 16), half_rows)]

        def store(half, total):
            sum_ref[pl.ds(half * half_rows, half_rows)] = total

        run_steps(scatter_steps(ring, part, slots, store, send, receive))

    return kernel_call(
        body,
        jax.ShapeDtypeStruct((rows, width), jnp.float32),
        [VMEM],
        VMEM,
        [
            pltpu.VMEM((2, 2, n // 2, half_rows, width), partial.dtype),
            sems(2, 2, n // 2),
            sems(2, 2, n // 2),
        ],
        identity,
        name,
        partial.size * 2 * 32,
    )(partial)


def partners():
    dp = lax.axis_index("dp")
    core = dp + 1 - 2 * (dp % 2)
    chip = (dp + 2) % 4
    return dp, core, chip, (core + 2) % 4


def gather_inputs(tokens, named, in_blocks, out_rows, n, n_dp, identity):
    tok_rows, width = tokens.shape

    def body(
        token_ref,
        named_ref,
        in_ref,
        out_ref,
        token_all,
        named_all,
        in_all,
        out_chip,
        token_send,
        token_receive,
        named_send,
        named_receive,
        in_send,
        in_receive,
        pass_send,
        pass_receive,
        local,
        out_send,
        out_receive,
    ):
        ring = Ring(n)
        me = ring.me
        dp, core, chip, core_chip = partners()
        half_rows = tok_rows // 2

        def token_place(device, half):
            return token_all.at[
                pl.ds(pl.multiple_of(device * tok_rows + half * half_rows, 16), half_rows)
            ]

        locals_ = [
            pltpu.make_async_copy(in_ref.at[me], in_all.at[dp, me], local.at[0]),
            pltpu.make_async_copy(
                token_ref,
                token_all.at[pl.ds(pl.multiple_of(me * tok_rows, 16), tok_rows)],
                local.at[1],
            ),
            pltpu.make_async_copy(named_ref, named_all.at[me], local.at[2]),
        ]
        for copy in locals_:
            copy.start()
        others = [(me + k) % n for k in range(1, n)]
        ring.barrier([{"ctx": other} for other in others] + [{"dp": core}, {"dp": chip}])

        direct = [remote(out_ref, out_chip, out_send, out_receive, {"dp": chip})]
        direct[0].start()
        for k, other in enumerate(others):
            direct.append(
                remote(in_ref.at[other], in_all.at[dp, me], in_send.at[k], in_receive.at[k], {"ctx": other})
            )
            direct.append(
                remote(named_ref, named_all.at[me], named_send.at[k], named_receive.at[k], {"ctx": other})
            )
        for copy in direct[1:]:
            copy.start()

        def in_steps():
            passed = []

            def forward(at, k, source, spot, to):
                passed.append(
                    remote(source, spot, pass_send.at[at, k], pass_receive.at[at, k], {"dp": to})
                )
                passed[-1].start()

            def landed(at, k, group, source):
                spot = in_all.at[group, (me - k + n) % n]
                remote(
                    spot, spot, pass_send.at[at, k], pass_receive.at[at, k], {"dp": source}
                ).wait_recv()
                return spot

            for at, to in ((0, chip), (1, core)):
                forward(at, 0, in_ref.at[me], in_all.at[dp, me], to)
            yield
            for k in range(1, n):
                spot = in_all.at[dp, (me - k + n) % n]
                remote(
                    spot, spot, in_send.at[k - 1], in_receive.at[k - 1], {"ctx": others[k - 1]}
                ).wait_recv()
                for at, to in ((0, chip), (1, core)):
                    forward(at, k, spot, spot, to)
                yield
            for k in range(n):
                spot = landed(0, k, chip, chip)
                forward(2, k, spot, spot, core)
                yield
            for at, group in ((1, core), (2, core_chip)):
                for k in range(n):
                    landed(at, k, group, core)
            for copy in passed:
                copy.wait_send()

        run_steps(
            gather_steps(
                ring,
                lambda half: token_ref.at[pl.ds(half * half_rows, half_rows)],
                token_place,
                token_send,
                token_receive,
            ),
            in_steps(),
        )
        for k in range(1, n):
            spot = named_all.at[(me - k + n) % n]
            remote(
                spot, spot, named_send.at[k - 1], named_receive.at[k - 1], {"ctx": others[k - 1]}
            ).wait_recv()
        direct[0].wait_recv()
        for copy in direct:
            copy.wait_send()
        for copy in locals_:
            copy.wait()

    return kernel_call(
        body,
        (
            jax.ShapeDtypeStruct((tok_rows * n, width), tokens.dtype),
            jax.ShapeDtypeStruct((n,) + named.shape, named.dtype),
            jax.ShapeDtypeStruct((n_dp,) + in_blocks.shape, in_blocks.dtype),
            jax.ShapeDtypeStruct(out_rows.shape, out_rows.dtype),
        ),
        [ANY] * 4,
        (ANY,) * 4,
        [sems(2, 2, n // 2)] * 2
        + [sems(n - 1)] * 4
        + [sems(3, n)] * 2
        + [sems(3), pltpu.SemaphoreType.DMA, pltpu.SemaphoreType.DMA],
        identity,
        "gather_inputs",
        200_000_000,
    )(tokens, named, in_blocks, out_rows)


def sum_small_steps(ring, small, near, quarter, got, total, sem):
    pass_send, pass_receive, send, receive = sem
    dp, core, chip, core_chip = partners()
    n, me = ring.n, ring.me
    lanes = quarter.shape[1]
    per_tile = LANES * n // lanes

    def group(at):
        return small.at[:, pl.ds(pl.multiple_of(at * lanes, LANES), lanes)]

    copies = []
    for at, to in enumerate((core_chip, chip, core)):
        copies.append(
            remote(group(to), near.at[at], pass_send.at[at], pass_receive.at[at], {"dp": to})
        )
        copies[-1].start()
    for _ in range(WAITS[1]):
        yield
    value = group(dp)[...]
    for at in range(3):
        copies[at].wait_recv()
        value = value + near[at]
    quarter[...] = value

    def tile(device):
        return quarter.at[:, pl.ds(pl.multiple_of(device // per_tile * LANES, LANES), LANES)]

    for k in range(1, n):
        other = (me + k) % n
        copies.append(
            remote(tile(other), got.at[k - 1], send.at[k - 1], receive.at[k - 1], {"ctx": other})
        )
        copies[-1].start()
    for _ in range(WAITS[2]):
        yield
    value = tile(me)[...]
    for k in range(1, n):
        copies[2 + k].wait_recv()
        value = value + got[k - 1]
    total[...] = value
    for copy in copies:
        copy.wait_send()


def scatter_end(
    row_part, attend_in, raw_back, tokens, residual_back, gain, small, pair_sum, far, n, n_dp, identity
):
    rows, width = row_part.shape[0] // n, row_part.shape[1]
    half_rows = rows // 2
    span = width // n_dp
    weight_rows = span // n
    in_cols = raw_back.shape[1]
    cols = in_cols // 3
    small_rows = small.shape[0]
    bf16, f32 = jnp.bfloat16, jnp.float32

    def body(
        row_ref,
        attend_ref,
        raw_ref,
        token_ref,
        back_ref,
        gain_ref,
        small_ref,
        pair_ref,
        far_ref,
        token_back,
        in_sum,
        small_sum,
        far_got,
        slots,
        row_s,
        attend_s,
        in_part,
        in_core,
        in_chip,
        in_got,
        small_s,
        small_near,
        small_quarter,
        small_got,
        row_send,
        row_receive,
        pass_send,
        pass_receive,
        in_send,
        in_receive,
        small_pass_send,
        small_pass_receive,
        small_send,
        small_receive,
        load,
        far_send,
        far_receive,
    ):
        ring = Ring(n)
        me = ring.me
        dp, core, chip, core_chip = partners()
        others = [(me + k) % n for k in range(1, n)]
        loaded = pltpu.make_async_copy(attend_ref, attend_s, load)
        loaded.start()
        ring.barrier(
            [{"ctx": other} for other in others] + [{"dp": to} for to in (core, chip, core_chip)]
        )

        def part(device, half):
            return row_ref.at[pl.ds(pl.multiple_of(device * rows + half * half_rows, 16), half_rows)]

        def store(half, total):
            row_s[pl.ds(half * half_rows, half_rows)] = total

        half_slots = n // CUTS

        def passing(at, k, source, target, to):
            slots_k = pl.ds(k * half_slots, half_slots)
            return remote(
                source.at[slots_k],
                target.at[slots_k],
                pass_send.at[at, k],
                pass_receive.at[at, k],
                {"dp": to},
            )

        def product(group):
            value = lax.dot_general(
                attend_s[:, pl.ds(pl.multiple_of(group * span, LANES), span)],
                raw_ref[...],
                (((0,), (0,)), ((), ())),
                preferred_element_type=f32,
            ).astype(bf16)
            for device in range(n):
                in_part[group, (device - me + n) % n] = value[
                    device * weight_rows : (device + 1) * weight_rows
                ]

        def weight_steps():
            loaded.wait()
            sent = []
            product(core_chip)
            far = [passing(0, k, in_part.at[core_chip], in_core.at[1], core) for k in range(CUTS)]
            for copy in far:
                copy.start()
            yield
            product(core)
            near = [passing(1, k, in_part.at[core], in_core.at[0], core) for k in range(CUTS)]
            for copy in near:
                copy.start()
            yield
            product(chip)
            across = []
            for k in range(CUTS):
                far[k].wait_recv()

                def add_far(at, carry):
                    in_core[1, at] = (
                        in_core[1, at].astype(f32) + in_part[chip, at].astype(f32)
                    ).astype(bf16)
                    return carry

                lax.fori_loop(k * half_slots, (k + 1) * half_slots, add_far, 0)
                across.append(passing(2, k, in_core.at[1], in_chip, chip))
                across[-1].start()
            beyond = remote(far_ref.at[1, pl.ds(PASS_B, far_got.shape[0])], far_got, far_send, far_receive, {"dp": chip})
            yield
            product(dp)
            for _ in range(2):
                yield
            for k in range(CUTS):
                near[k].wait_recv()
                across[k].wait_recv()

                def add_near(at, carry):
                    in_core[0, at] = (
                        in_core[0, at].astype(f32)
                        + in_part[dp, at].astype(f32)
                        + in_chip[at].astype(f32)
                    ).astype(bf16)
                    return carry

                lax.fori_loop(k * half_slots, (k + 1) * half_slots, add_near, 0)
                for at in range(max(1, k * half_slots), (k + 1) * half_slots):
                    sent.append(
                        remote(
                            in_core.at[0, at],
                            in_got.at[at],
                            in_send.at[at - 1],
                            in_receive.at[at - 1],
                            {"ctx": others[at - 1]},
                        )
                    )
                    sent[-1].start()
                yield
                yield
            beyond.start()
            in_got[0] = in_core[0, 0]
            for _ in range(6):
                yield
            for at in range(n):
                if at:
                    sent[at - 1].wait_recv()
                device = (me - at + n) % n
                for which in range(3):
                    in_sum[
                        :, pl.ds(pl.multiple_of(which * width + device * cols, LANES), cols)
                    ] = in_got[at, :, pl.ds(which * cols, cols)].astype(f32)
            beyond.wait()
            for copy in far + near + across + sent:
                copy.wait_send()

        def row_steps():
            yield from scatter_steps(ring, part, slots, store, row_send, row_receive)
            values = token_ref[...].astype(f32)
            inverse = lax.rsqrt(jnp.mean(values * values, axis=-1, keepdims=True) + EPSILON)
            normed = values * inverse
            back = row_s[...]
            back = back * gain_ref[0:1, :]
            token_back[...] = (
                back_ref[...]
                + inverse * (back - normed * jnp.mean(back * normed, axis=-1, keepdims=True))
            ).astype(bf16)

        def small_steps():
            for _ in range(WAITS[0]):
                yield

            def column_sums(at, total):
                part_rows = pl.ds(pl.multiple_of(at * rows, rows), rows)
                terms = row_ref[part_rows].astype(f32) * attend_s[part_rows].astype(f32)
                return total + jnp.sum(terms, axis=0, keepdims=True)

            total = lax.fori_loop(0, n, column_sums, jnp.zeros((1, width), f32))
            small_s[...] = small_ref[...]
            small_s[0:1, :] = total / gain_ref[0:1, :]
            own = pl.ds(pl.multiple_of(me * cols, LANES), cols)
            small_s[1:2, own] = pair_ref[0:1, :cols]
            small_s[2:3, own] = pair_ref[0:1, cols:]
            yield from sum_small_steps(
                ring,
                small_s,
                small_near,
                small_quarter,
                small_got,
                small_sum,
                (small_pass_send, small_pass_receive, small_send, small_receive),
            )

        run_steps(row_steps(), weight_steps(), small_steps())

    block = (n, weight_rows, in_cols)
    return kernel_call(
        body,
        (
            jax.ShapeDtypeStruct((rows, width), bf16),
            jax.ShapeDtypeStruct((weight_rows, 3 * width), f32),
            jax.ShapeDtypeStruct((small_rows, LANES), f32),
            jax.ShapeDtypeStruct((far.shape[1] - PASS_B, far.shape[2]), bf16),
        ),
        [VMEM, ANY] + [VMEM] * 6 + [ANY],
        (VMEM,) * 3 + (ANY,),
        [
            pltpu.VMEM((2, 2, n // 2, half_rows, width), row_part.dtype),
            pltpu.VMEM((rows, width), f32),
            pltpu.VMEM(attend_in.shape, bf16),
            pltpu.VMEM((n_dp,) + block, bf16),
            pltpu.VMEM((2,) + block, bf16),
            pltpu.VMEM(block, bf16),
            pltpu.VMEM(block, bf16),
            pltpu.VMEM((small_rows, width), f32),
            pltpu.VMEM((3, small_rows, span), f32),
            pltpu.VMEM((small_rows, span), f32),
            pltpu.VMEM((n - 1, small_rows, LANES), f32),
            sems(2, 2, n // 2),
            sems(2, 2, n // 2),
            sems(3, CUTS),
            sems(3, CUTS),
            sems(n - 1),
            sems(n - 1),
            sems(3),
            sems(3),
            sems(n - 1),
            sems(n - 1),
            pltpu.SemaphoreType.DMA,
            pltpu.SemaphoreType.DMA,
            pltpu.SemaphoreType.DMA,
        ],
        identity,
        "scatter_end",
        200_000_000,
    )(row_part, attend_in, raw_back, tokens, residual_back, gain, small, pair_sum, far)


def slot_offsets(n):
    offsets = [0]
    for k in range(1, n // 2):
        offsets += [k, -k]
    return offsets + [n // 2]


def slot_of(offset, n):
    if abs(offset) == n // 2:
        return n - 1
    return 2 * offset - 1 if offset > 0 else -2 * offset


def slot_gather_steps(ring, first, slots, send, receive):
    signs = (1, -1)
    half_rows = slots.shape[1] // 2

    def copy(way, half, hop):
        rows = pl.ds(half * half_rows, half_rows)
        held = slot_of(-signs[way] * hop, ring.n)
        return remote(
            first.at[rows] if hop == 0 else slots.at[held, rows],
            slots.at[slot_of(-signs[way] * (hop + 1), ring.n), rows],
            send.at[way, half, hop],
            receive.at[way, half, hop],
            {"ctx": ring.at(signs[way])},
        )

    started = []
    for half in (0, 1):
        for way in (0, 1):
            started.append(copy(way, half, 0))
            started[-1].start()
    yield
    for hop in range(ring.n // 2):
        for half in (0, 1):
            for way in (0, 1):
                if hop < ring.hops(way, half):
                    copy(way, half, hop).wait_recv()
                    if hop + 1 < ring.hops(way, half):
                        started.append(copy(way, half, hop + 1))
                        started[-1].start()
                    yield
    for one in started:
        one.wait_send()


def advance(steps, count):
    for _ in range(count):
        next(steps, None)


def dot(a, b):
    return jnp.dot(a, b, preferred_element_type=jnp.float32)


def dot_across(a, b):
    return lax.dot_general(a, b, (((1,), (1,)), ((), ())), preferred_element_type=jnp.float32)


def experts_in(
    attend_all, token_all, cotangent, out_all, first, second, gain, router, named, n, identity
):
    tok_rows, width = cotangent.shape
    local_experts, ff = first.shape[0], second.shape[0] // first.shape[0]
    rows = tok_rows * n
    group = 4
    pair = part = group * tok_rows
    tile, wide = TILE, WIDE
    bf16, f32 = jnp.bfloat16, jnp.float32
    offsets = slot_offsets(n)

    def body(
        attend_ref,
        token_ref,
        back_ref,
        out_ref,
        first_ref,
        second_ref,
        gain_ref,
        router_ref,
        named_ref,
        back_all,
        mixed_all,
        gated_all,
        up_all,
        own_gates,
        gate_back,
        own_residual,
        out_s,
        first_s,
        second_s,
        mixed_s,
        back_s,
        attend_s,
        residual_s,
        gate_s,
        sum_s,
        send,
        receive,
        load,
        weight_load,
        save,
        local,
    ):
        ring = Ring(n)
        lanes = lax.broadcasted_iota(jnp.int32, (pair, LANES), 1)
        loads = [pltpu.make_async_copy(out_ref, out_s, weight_load.at[0])]
        for x in range(local_experts):
            loads.append(pltpu.make_async_copy(first_ref.at[x], first_s.at[x], weight_load.at[1 + x]))
        loads.append(pltpu.make_async_copy(second_ref, second_s, weight_load.at[1 + local_experts]))

        def row_loads(j):
            copies = []
            for k in range(group):
                device = ring.at(offsets[group * j + k])
                source = pl.ds(pl.multiple_of(device * tok_rows, 16), tok_rows)
                target = pl.ds(k * tok_rows, tok_rows)
                copies.append(
                    pltpu.make_async_copy(
                        attend_ref.at[source], attend_s.at[j % 2, target], load.at[j % 2, k, 0]
                    )
                )
                copies.append(
                    pltpu.make_async_copy(
                        token_ref.at[source], mixed_s.at[group * j + k], load.at[j % 2, k, 1]
                    )
                )
            return copies

        pending = row_loads(0)
        for copy in pending:
            copy.start()
        loads[0].start()
        own = pltpu.make_async_copy(back_ref, back_s.at[0], local)
        own.start()
        ring.barrier(ring.neighbours())
        steps = slot_gather_steps(ring, back_ref, back_s, send, receive)
        advance(steps, 1)
        loads[0].wait()
        for copy in loads[1:]:
            copy.start()

        saves = []
        for j in range(n // group):
            for copy in pending:
                copy.wait()
            if j + 1 < n // group:
                pending = row_loads(j + 1)
                for copy in pending:
                    copy.start()

            def project(t, carry, j=j):
                columns = pl.ds(pl.multiple_of(t * wide, wide), wide)
                values = mixed_s[pl.ds(group * j, group), :, columns].reshape(pair, wide)
                residual_s[:, columns] = values.astype(f32) + dot(attend_s[j % 2], out_s[:, columns])
                return carry

            lax.fori_loop(0, width // wide, project, 0)
            advance(steps, 2)
            residual = residual_s[...]
            if j == 0:
                own_residual[...] = residual[:tok_rows]
            inverse = lax.rsqrt(jnp.mean(residual * residual, axis=-1, keepdims=True) + EPSILON)
            mixed = (residual * inverse * gain_ref[0:1, :]).astype(bf16)
            for k in range(group):
                mixed_s[group * j + k] = mixed[k * tok_rows : (k + 1) * tok_rows]
            logits = dot(mixed, router_ref[...])
            marks = jnp.concatenate(
                [
                    named_ref[pl.ds(pl.multiple_of(ring.at(offsets[group * j + k]) * tok_rows, 16), tok_rows)]
                    for k in range(group)
                ],
                axis=0,
            ).astype(f32)
            logits = jnp.where(marks > 0, logits, MASKED)
            powers = jnp.where(
                marks > 0, jnp.exp(logits - jnp.max(logits, axis=-1, keepdims=True)), 0.0
            )
            gates = powers / jnp.sum(powers, axis=-1, keepdims=True)
            if j == 0:
                own_gates[...] = gates[:tok_rows]
            held = jnp.zeros((pair, LANES), f32)
            for x in range(local_experts):
                mine = jnp.sum(
                    jnp.where(lanes == ring.me * local_experts + x, gates, 0.0), axis=-1, keepdims=True
                )
                held = jnp.where(lanes == x, mine, held)
            gate_s[pl.ds(j * pair, pair)] = held
            saves.append(
                pltpu.make_async_copy(
                    mixed_s.at[pl.ds(group * j, group)], mixed_all.at[pl.ds(group * j, group)], save.at[j]
                )
            )
            saves[-1].start()
            advance(steps, 2)

        counts = rows // part
        outgoing = []
        base = n // 2
        for s in range(counts):
            slots = pl.ds(s * group, group)
            part_rows = pl.ds(s * part, part)
            advance(steps, 0 if s < counts - 1 else 64)
            if s == 0:
                own.wait()
            sum_s[part_rows] = jnp.zeros((part, LANES), f32)
            for copy in outgoing:
                copy.wait()
            outgoing = []
            for x in range(local_experts):
                if s == 0:
                    loads[1 + x].wait()
                    if x == 0:
                        loads[1 + local_experts].wait()

                def hidden(t, carry, s=s, x=x, slots=slots, part_rows=part_rows):
                    at = pl.multiple_of(t * tile, tile)
                    mixed = mixed_s[slots].reshape(part, width)
                    back = back_s[slots].reshape(part, width)
                    gate_part = dot(mixed, first_s[x, :, pl.ds(at, tile)])
                    up_part = dot(mixed, first_s[x, :, pl.ds(pl.multiple_of(ff + at, tile), tile)])
                    hidden_back = dot_across(
                        back, second_s[pl.ds(pl.multiple_of(x * ff + at, tile), tile), :]
                    )
                    gate = gate_s[part_rows, x : x + 1]
                    sigmoid = jax.nn.sigmoid(gate_part)
                    swish = gate_part * sigmoid
                    value = swish * up_part
                    out_s[pl.ds(0, part), pl.ds(pl.multiple_of(x * ff + at, tile), tile)] = (
                        value * gate
                    ).astype(bf16)
                    sums = jnp.sum(value * hidden_back, axis=-1, keepdims=True)
                    sum_s[part_rows] = sum_s[part_rows] + jnp.where(lanes == x, sums, 0.0)
                    hidden_back = hidden_back * gate
                    slope = sigmoid * (1.0 + gate_part * (1.0 - sigmoid))
                    up_rows = pl.ds((1 + x) * part, part)
                    out_s[up_rows, pl.ds(at, tile)] = (hidden_back * up_part * slope).astype(bf16)
                    out_s[up_rows, pl.ds(pl.multiple_of(ff + at, tile), tile)] = (
                        hidden_back * swish
                    ).astype(bf16)
                    return carry

                pieces = ff // tile
                lax.fori_loop(0, pieces // 2, hidden, 0)
                advance(steps, 2)
                lax.fori_loop(pieces // 2, pieces, hidden, 0)
                advance(steps, 2)
                outgoing.append(
                    pltpu.make_async_copy(
                        out_s.at[pl.ds((1 + x) * part, part)],
                        up_all.at[x, part_rows],
                        save.at[base + 1 + x],
                    )
                )
                outgoing[-1].start()
            outgoing.append(
                pltpu.make_async_copy(out_s.at[pl.ds(0, part)], gated_all.at[part_rows], save.at[base])
            )
            outgoing[-1].start()
        spread = pltpu.make_async_copy(back_s, back_all, local)
        spread.start()
        for k in range(n):
            gate_back[k] = jnp.transpose(sum_s[pl.ds(k * tok_rows, tok_rows)])[:8]
        for copy in saves + outgoing:
            copy.wait()
        spread.wait()

    return pl.pallas_call(
        body,
        out_shape=(
            jax.ShapeDtypeStruct((n, tok_rows, width), bf16),
            jax.ShapeDtypeStruct((n, tok_rows, width), bf16),
            jax.ShapeDtypeStruct((rows, local_experts * ff), bf16),
            jax.ShapeDtypeStruct((local_experts, rows, 2 * ff), bf16),
            jax.ShapeDtypeStruct((tok_rows, LANES), f32),
            jax.ShapeDtypeStruct((n, 8, LANES), f32),
            jax.ShapeDtypeStruct((tok_rows, width), f32),
        ),
        in_specs=[ANY] * 6 + [VMEM] * 3,
        out_specs=(ANY,) * 4 + (VMEM,) * 3,
        scratch_shapes=[
            pltpu.VMEM(out_all.shape, bf16),
            pltpu.VMEM(first.shape, bf16),
            pltpu.VMEM(second.shape, bf16),
            pltpu.VMEM((n, tok_rows, width), bf16),
            pltpu.VMEM((n, tok_rows, width), bf16),
            pltpu.VMEM((2, pair, width), bf16),
            pltpu.VMEM((pair, width), f32),
            pltpu.VMEM((rows, LANES), f32),
            pltpu.VMEM((rows, LANES), f32),
            sems(2, 2, n // 2),
            sems(2, 2, n // 2),
            sems(2, group, 2),
            sems(2 + local_experts),
            sems(n // 2 + 1 + local_experts),
            pltpu.SemaphoreType.DMA,
        ],
        name="experts_in",
        cost_estimate=pl.CostEstimate(
            flops=2 * rows * width * (width + 3 * ff * local_experts),
            bytes_accessed=60_000_000,
            transcendentals=0,
        ),
        compiler_params=pltpu.CompilerParams(
            collective_id=identity, has_side_effects=True, vmem_limit_bytes=BIG_VMEM
        ),
    )(attend_all, token_all, cotangent, out_all, first, second, gain, router, named)


BIG_VMEM = 60 * 1024 * 1024


def slot_scatter_steps(ring, parts, slots, store, send, receive, need):
    signs = (1, -1)
    half_rows = parts.shape[1] // 2
    f32 = jnp.float32

    def part(offset, half):
        return parts.at[slot_of(offset, ring.n), pl.ds(half * half_rows, half_rows)]

    def copy(way, half, hop, source):
        return remote(
            source,
            slots.at[way, half, hop],
            send.at[way, half, hop],
            receive.at[way, half, hop],
            {"ctx": ring.at(signs[way])},
        )

    started = []
    firsts = [(way, half) for half in (0, 1) for way in (0, 1)]
    firsts.sort(key=lambda one: -slot_of(signs[one[0]] * ring.hops(*one), ring.n))
    for way, half in firsts:
        goal = signs[way] * ring.hops(way, half)
        need(slot_of(goal, ring.n))
        started.append(copy(way, half, 0, part(goal, half)))
        started[-1].start()
    for hop in range(ring.n // 2):
        for way, half in firsts:
            last = ring.hops(way, half) - 1
            if hop <= last:
                slot = slots.at[way, half, hop]
                if hop < last:
                    goal = signs[way] * (last - hop)
                    need(slot_of(goal, ring.n))
                copy(way, half, hop, slot).wait_recv()
                if hop < last:
                    slot[...] = (
                        slot[...].astype(f32) + part(goal, half)[...].astype(f32)
                    ).astype(slot.dtype)
                    started.append(copy(way, half, hop + 1, slot))
                    started[-1].start()
                yield
    need(0)
    for half in (0, 1):
        total = part(0, half)[...].astype(f32)
        for way in (0, 1):
            total = total + slots[way, half, ring.hops(way, half) - 1].astype(f32)
        store(half, total)
    for one in started:
        one.wait_send()


def experts_out(up_all, gated_all, first, second, gate_back, n, identity):
    local_experts, rows, inner = up_all.shape
    width = first.shape[1]
    tok_rows = rows // n
    half_rows = tok_rows // 2
    pair = 2 * tok_rows
    wide = 512
    count = width // wide
    bf16, f32 = jnp.bfloat16, jnp.float32
    offsets = slot_offsets(n)

    def body(
        up_ref,
        gated_ref,
        first_ref,
        second_ref,
        gate_ref,
        row_sum,
        result_all,
        gate_got,
        first_s,
        second_s,
        up_s,
        gated_s,
        part_s,
        result_s,
        slots,
        send,
        receive,
        gate_send,
        gate_receive,
        load,
        first_load,
        other_load,
        save,
    ):
        ring = Ring(n)

        def up_load(j):
            return pltpu.make_async_copy(
                up_ref.at[:, pl.ds(j * pair, pair)], up_s.at[:, pl.ds(j * pair, pair)], load.at[j]
            )

        def weight_load(t):
            return pltpu.make_async_copy(
                first_ref.at[:, pl.ds(t * wide, wide)],
                first_s.at[:, pl.ds(t * wide, wide)],
                first_load.at[t],
            )

        groups = n // 2
        up_load(groups - 1).start()
        for t in range(count):
            weight_load(t).start()
        for j in range(groups - 1):
            up_load(groups - 2 - j).start()
        others = [
            pltpu.make_async_copy(gated_ref, gated_s, other_load.at[0]),
            pltpu.make_async_copy(second_ref, second_s, other_load.at[1]),
        ]
        for copy in others:
            copy.start()
        ring.barrier([{"ctx": ring.at(k)} for k in range(1, n)])
        gate_copies = []
        for k in range(1, n):
            offset = k if k <= n // 2 else k - n
            back = -offset if offset < n // 2 else offset
            gate_copies.append(
                remote(
                    gate_ref.at[slot_of(offset, n)],
                    gate_got.at[slot_of(back, n)],
                    gate_send.at[slot_of(back, n)],
                    gate_receive.at[slot_of(back, n)],
                    {"ctx": ring.at(k)},
                )
            )
            gate_copies[-1].start()
        gate_got[0] = gate_ref[0]

        done = set()

        def product(j):
            rows_j = pl.ds(j * pair, pair)
            up_load(j).wait()

            def columns(t):
                at = pl.ds(pl.multiple_of(t * wide, wide), wide)
                value = dot_across(up_s[0, rows_j], first_s[0, at, :])
                for x in range(1, local_experts):
                    value = value + dot_across(up_s[x, rows_j], first_s[x, at, :])
                value = value.astype(bf16)
                for k in range(2):
                    part_s[2 * j + k, :, at] = value[k * tok_rows : (k + 1) * tok_rows]

            if not done:
                for t in range(count):
                    weight_load(t).wait()
                    columns(t)
            else:

                def step(t, carry):
                    columns(t)
                    return carry

                lax.fori_loop(0, count, step, 0)
            done.add(j)

        def need(slot):
            if slot // 2 not in done:
                product(slot // 2)

        def store(half, total):
            row_sum[pl.ds(half * half_rows, half_rows)] = total

        steps = slot_scatter_steps(ring, part_s, slots, store, send, receive, need)
        for j in reversed(range(groups)):
            need(2 * j)
            advance(steps, 1 if j in (0, groups - 1) else 2)
        for copy in others:
            copy.wait()
        saves = []
        chunk = 2
        for j in range(n // chunk):
            rows_j = pl.ds(j * chunk * tok_rows, chunk * tok_rows)

            def result(t, carry, rows_j=rows_j, j=j):
                at = pl.ds(pl.multiple_of(t * wide, wide), wide)
                value = dot(gated_s[rows_j], second_s[:, at]).astype(bf16)
                for k in range(chunk):
                    result_s[chunk * j + k, :, at] = value[k * tok_rows : (k + 1) * tok_rows]
                return carry

            lax.fori_loop(0, count, result, 0)
            for k in range(chunk):
                slot = chunk * j + k
                device = ring.at(offsets[slot])
                saves.append(
                    pltpu.make_async_copy(
                        result_s.at[slot],
                        result_all.at[pl.ds(pl.multiple_of(device * tok_rows, 16), tok_rows)],
                        save.at[slot],
                    )
                )
                saves[-1].start()
            advance(steps, 2)
        advance(steps, 64)
        for copy in saves:
            copy.wait()
        for copy in gate_copies:
            copy.wait()

    return pl.pallas_call(
        body,
        out_shape=(
            jax.ShapeDtypeStruct((tok_rows, width), f32),
            jax.ShapeDtypeStruct((rows, width), bf16),
            jax.ShapeDtypeStruct(gate_back.shape, f32),
        ),
        in_specs=[ANY] * 4 + [VMEM],
        out_specs=(VMEM, ANY, VMEM),
        scratch_shapes=[
            pltpu.VMEM(first.shape, bf16),
            pltpu.VMEM(second.shape, bf16),
            pltpu.VMEM(up_all.shape, bf16),
            pltpu.VMEM(gated_all.shape, bf16),
            pltpu.VMEM((n, tok_rows, width), bf16),
            pltpu.VMEM((n, tok_rows, width), bf16),
            pltpu.VMEM((2, 2, n // 2, half_rows, width), bf16),
            sems(2, 2, n // 2),
            sems(2, 2, n // 2),
            sems(n),
            sems(n),
            sems(n // 2),
            sems(count),
            sems(2),
            sems(n),
        ],
        name="experts_out",
        cost_estimate=pl.CostEstimate(
            flops=2 * rows * width * 3 * inner // 2 * local_experts,
            bytes_accessed=60_000_000,
            transcendentals=0,
        ),
        compiler_params=pltpu.CompilerParams(
            collective_id=identity, has_side_effects=True, vmem_limit_bytes=BIG_VMEM
        ),
    )(up_all, gated_all, first, second, gate_back)


def exchange_rows(ring, sums, flat, got, send, receive, steps):
    n, rows = ring.n, sums.shape[0]
    for k in range(rows // LANES):
        flat[:, pl.ds(k * LANES, LANES)] = jnp.transpose(sums[pl.ds(k * LANES, LANES)])[:8]
    copies = []
    for k in range(1, n):
        copies.append(
            remote(
                flat,
                got.at[k - 1],
                send.at[k - 1],
                receive.at[k - 1],
                {"ctx": (ring.me + k) % n},
            )
        )
        copies[-1].start()
    advance(steps, 1)
    for copy in copies:
        copy.wait_recv()
    total = flat[...]
    for k in range(n - 1):
        total = total + got[k]
    for k in range(rows // LANES):
        block = total[:, k * LANES : (k + 1) * LANES]
        block = jnp.concatenate([block, jnp.zeros((LANES - 8, LANES), jnp.float32)], axis=0)
        sums[pl.ds(k * LANES, LANES)] = jnp.transpose(block)
    for copy in copies:
        copy.wait_send()


def turn(values, cosine, sine):
    return values * cosine + pltpu.roll(values, HEAD_DIM // 2, 1) * sine


def out_gather_steps(ring, out_ref, chip_ref, out_all, sem):
    own_send, own_receive, ring_send, ring_receive, core_send, core_receive, local = sem
    dp, core, chip, core_chip = partners()
    weight_rows, n, me = out_ref.shape[0], ring.n, ring.me

    def place(group, device):
        return out_all.at[pl.ds(pl.multiple_of((group * n + device) * weight_rows, 16), weight_rows)]

    own = [
        pltpu.make_async_copy(out_ref, place(dp, me), local.at[0]),
        pltpu.make_async_copy(chip_ref, place(chip, me), local.at[1]),
    ]
    copies = [
        remote(out_ref, place(dp, me), own_send.at[0], own_receive.at[0], {"dp": core}),
        remote(chip_ref, place(chip, me), own_send.at[1], own_receive.at[1], {"dp": core}),
    ]
    for copy in own:
        copy.start()

    def arrived(way, half, hop, origin):
        if len(copies) == 2:
            for copy in copies:
                copy.start()
        spot = place(chip if half else dp, origin)
        copies.append(
            remote(
                spot, spot, core_send.at[way, half, hop], core_receive.at[way, half, hop], {"dp": core}
            )
        )
        copies[-1].start()

    yield from gather_steps(
        ring,
        lambda half: chip_ref if half else out_ref,
        lambda device, half: place(chip if half else dp, device),
        ring_send,
        ring_receive,
        arrived,
    )
    for at, group in ((0, core), (1, core_chip)):
        spot = place(group, me)
        remote(spot, spot, own_send.at[at], own_receive.at[at], {"dp": core}).wait_recv()
    for way, sign in ((0, 1), (1, -1)):
        for half in (0, 1):
            for hop in range(ring.hops(way, half)):
                spot = place(core_chip if half else core, ring.at(-sign * (hop + 1)))
                remote(
                    spot,
                    spot,
                    core_send.at[way, half, hop],
                    core_receive.at[way, half, hop],
                    {"dp": core},
                ).wait_recv()
    for copy in copies:
        copy.wait_send()
    for copy in own:
        copy.wait()


def attention_in(
    token_all, in_all, out_rows, out_chip, gain, pair_gains, cosine, sine, bounds, place_row, n, n_dp, identity
):
    rows, width = token_all.shape
    pair = pair_gains.shape[1]
    cols = pair // 2
    heads = cols // HEAD_DIM
    chunk = 256
    weight_rows = out_rows.shape[0]
    bf16, f32 = jnp.bfloat16, jnp.float32
    scale = HEAD_DIM ** (-0.5)

    def body(
        token_ref,
        in_ref,
        out_ref,
        chip_ref,
        gain_ref,
        pair_ref,
        cos_ref,
        sin_ref,
        bound_ref,
        place_ref,
        attend_all,
        out_all,
        probs_all,
        normed_all,
        attend_ref,
        qkv_ref,
        raw_ref,
        inverse_ref,
        probs_s,
        normed_s,
        flat,
        got,
        *sem,
    ):
        out_sem, sem = sem[:7], sem[7:]
        sum_send, sum_receive, ring_send, ring_receive, save = sem
        ring = Ring(n)
        dp, core, chip, core_chip = partners()
        ring.barrier([{"ctx": (ring.me + k) % n} for k in range(1, n)] + [{"dp": core}])
        steps = out_gather_steps(ring, out_ref, chip_ref, out_all, out_sem)
        advance(steps, 1)
        lanes = lax.broadcasted_iota(jnp.int32, (chunk, LANES), 1)

        def chunks(step, count=2):
            total = rows // chunk
            for first in range(0, total, count):
                lax.fori_loop(first, min(first + count, total), step, 0)
                advance(steps, 1)

        def project(j, carry):
            at = pl.ds(pl.multiple_of(j * chunk, chunk), chunk)
            values = token_ref[at].astype(f32)
            inverse = lax.rsqrt(jnp.mean(values * values, axis=-1, keepdims=True) + EPSILON)
            normed = (values * inverse * gain_ref[0:1, :]).astype(bf16)
            normed_s[at] = normed
            projected = dot(normed, in_ref[:, : pair + cols])
            raw_ref[at] = projected[:, :pair]
            qkv_ref[at, pair:] = projected[:, pair:].astype(bf16)
            squares = projected[:, :pair] * projected[:, :pair]
            inverse_ref[at] = jnp.where(
                lanes == 0,
                jnp.sum(squares[:, :cols], axis=-1, keepdims=True),
                jnp.where(lanes == 1, jnp.sum(squares[:, cols:], axis=-1, keepdims=True), 0.0),
            )
            return carry

        chunks(project)
        saves = [pltpu.make_async_copy(normed_s, normed_all, save.at[heads])]
        saves[0].start()
        exchange_rows(ring, inverse_ref, flat, got, sum_send, sum_receive, steps)

        def norm(j, carry):
            at = pl.ds(pl.multiple_of(j * chunk, chunk), chunk)
            inverse = lax.rsqrt(inverse_ref[at] / width + EPSILON)
            inverse_ref[at] = inverse
            for which in range(2):
                for head in range(heads):
                    columns = pl.ds(which * cols + head * HEAD_DIM, HEAD_DIM)
                    values = raw_ref[at, columns] * inverse[:, which : which + 1]
                    values = values * pair_ref[0:1, columns]
                    qkv_ref[at, columns] = turn(values, cos_ref[at], sin_ref[at]).astype(bf16)
            return carry

        chunks(norm)
        for head in range(heads):

            def attend(j, carry, head=head):
                at = pl.ds(pl.multiple_of(j * chunk, chunk), chunk)
                columns = pl.ds(head * HEAD_DIM, HEAD_DIM)
                scores = (
                    dot_across(
                        qkv_ref[at, columns], qkv_ref[:, pl.ds(cols + head * HEAD_DIM, HEAD_DIM)]
                    )
                    * scale
                )
                place = place_ref[0:1, :]
                visible = (place >= bound_ref[at, 0:1]) & (place <= bound_ref[at, 1:2])
                scores = jnp.where(visible, scores, MASKED)
                powers = jnp.where(
                    visible, jnp.exp(scores - jnp.max(scores, axis=-1, keepdims=True)), 0.0
                )
                share = 1.0 / jnp.sum(powers, axis=-1, keepdims=True)
                probs = (powers * share).astype(bf16)
                probs_s[head, at] = probs
                attend_ref[at, columns] = dot(
                    probs, qkv_ref[:, pl.ds(pair + head * HEAD_DIM, HEAD_DIM)]
                ).astype(bf16)
                return carry

            chunks(attend)
            saves.append(pltpu.make_async_copy(probs_s.at[head], probs_all.at[head], save.at[head]))
            saves[-1].start()

        half_rows = rows // 2
        own = pltpu.make_async_copy(
            attend_ref,
            attend_all.at[:, pl.ds(pl.multiple_of(ring.me * cols, LANES), cols)],
            save.at[heads + 1],
        )
        own.start()
        run_steps(
            steps,
            gather_steps(
                ring,
                lambda half: attend_ref.at[pl.ds(half * half_rows, half_rows)],
                lambda device, half: attend_all.at[
                    pl.ds(half * half_rows, half_rows),
                    pl.ds(pl.multiple_of(device * cols, LANES), cols),
                ],
                ring_send,
                ring_receive,
            ),
        )
        own.wait()
        for copy in saves:
            copy.wait()

    return pl.pallas_call(
        body,
        out_shape=(
            jax.ShapeDtypeStruct((rows, width), bf16),
            jax.ShapeDtypeStruct((weight_rows * n * n_dp, width), bf16),
            jax.ShapeDtypeStruct((heads, rows, rows), bf16),
            jax.ShapeDtypeStruct((rows, width), bf16),
            jax.ShapeDtypeStruct((rows, cols), bf16),
            jax.ShapeDtypeStruct((rows, 3 * cols), bf16),
            jax.ShapeDtypeStruct((rows, pair), f32),
            jax.ShapeDtypeStruct((rows, LANES), f32),
        ),
        in_specs=[VMEM, VMEM, ANY, ANY] + [VMEM] * 6,
        out_specs=(ANY,) * 4 + (VMEM,) * 4,
        scratch_shapes=[
            pltpu.VMEM((heads, rows, rows), bf16),
            pltpu.VMEM((rows, width), bf16),
            pltpu.VMEM((8, rows), f32),
            pltpu.VMEM((n - 1, 8, rows), f32),
            sems(2),
            sems(2),
            sems(2, 2, n // 2),
            sems(2, 2, n // 2),
            sems(2, 2, n // 2),
            sems(2, 2, n // 2),
            sems(2),
            sems(n - 1),
            sems(n - 1),
            sems(2, 2, n // 2),
            sems(2, 2, n // 2),
            sems(heads + 2),
        ],
        name="attention_in",
        cost_estimate=pl.CostEstimate(
            flops=2 * rows * width * 3 * cols, bytes_accessed=200_000_000, transcendentals=0
        ),
        compiler_params=pltpu.CompilerParams(
            collective_id=identity, has_side_effects=True, vmem_limit_bytes=BIG_VMEM
        ),
    )(token_all, in_all, out_rows, out_chip, gain, pair_gains, cosine, sine, bounds, place_row)


def gather_with_gradients(block, mixed, up_all, n, n_dp, identity):
    rows, width = block.shape
    half_rows = rows // 2
    count, inner = up_all.shape[0], up_all.shape[2]
    span, tile, piece = width // n_dp, 256, 64
    bf16, f32 = jnp.bfloat16, jnp.float32

    def body(
        block_ref,
        mixed_ref,
        up_ref,
        all_ref,
        near_ref,
        far_ref,
        far_got,
        mixed_s,
        up_s,
        grad_s,
        core_s,
        send,
        receive,
        core_send,
        core_receive,
        local,
        load,
        save,
        far_send,
        far_receive,
    ):
        ring = Ring(n)
        dp, core, chip, core_chip = partners()
        loads = [pltpu.make_async_copy(mixed_ref, mixed_s, load.at[count])]
        for x in range(count):
            loads.append(pltpu.make_async_copy(up_ref.at[x], up_s.at[x], load.at[x]))
        own = pltpu.make_async_copy(
            block_ref, all_ref.at[pl.ds(pl.multiple_of(ring.me * rows, 16), rows)], local
        )
        own.start()
        for copy in loads:
            copy.start()
        ring.barrier(ring.neighbours() + [{"dp": core}, {"dp": chip}])
        steps = gather_steps(
            ring,
            lambda half: block_ref.at[pl.ds(half * half_rows, half_rows)],
            lambda device, half: all_ref.at[
                pl.ds(pl.multiple_of(device * rows + half * half_rows, 16), half_rows)
            ],
            send,
            receive,
        )
        advance(steps, 2)
        loads[0].wait()
        saves, passed = [], []
        for x in range(count):
            loads[1 + x].wait()
            for at, group in enumerate((core_chip, core, chip, dp)):

                def product(j, carry, x=x, at=at, group=group):
                    columns = pl.ds(pl.multiple_of(group * span + j * tile, tile), tile)
                    grad_s[x, at, pl.ds(pl.multiple_of(j * tile, tile), tile)] = lax.dot_general(
                        mixed_s[:, columns],
                        up_s[x],
                        (((0,), (0,)), ((), ())),
                        preferred_element_type=f32,
                    ).astype(bf16)
                    return carry

                lax.fori_loop(0, span // tile, product, 0)
                which = 1 - at % 2
                if at < 2:
                    passed.append(
                        remote(
                            grad_s.at[x, at],
                            core_s.at[x, which],
                            core_send.at[x, which],
                            core_receive.at[x, which],
                            {"dp": core},
                        )
                    )
                    passed[-1].start()
                else:
                    passed[2 * x + at - 2].wait_recv()

                    def add(j, carry, x=x, at=at, which=which):
                        part = pl.ds(pl.multiple_of(j * piece, piece), piece)
                        core_s[x, which, part] = (
                            core_s[x, which, part].astype(f32) + grad_s[x, at, part].astype(f32)
                        ).astype(bf16)
                        return carry

                    lax.fori_loop(0, span // piece, add, 0)
                    if x == 0 and which:
                        across = remote(
                            core_s.at[0, 1, pl.ds(0, PASS_A)], far_got, far_send, far_receive, {"dp": chip}
                        )
                        across.start()
                    saves.append(
                        pltpu.make_async_copy(
                            core_s.at[x, which],
                            (far_ref if which else near_ref).at[x],
                            save.at[x, which],
                        )
                    )
                    saves[-1].start()
                advance(steps, 2)
        advance(steps, 64)
        for copy in passed:
            copy.wait_send()
        across.wait()
        for copy in saves:
            copy.wait()
        own.wait()

    sums = jax.ShapeDtypeStruct((count, span, inner), bf16)
    return pl.pallas_call(
        body,
        out_shape=(
            jax.ShapeDtypeStruct((rows * n, width), block.dtype),
            sums,
            sums,
            jax.ShapeDtypeStruct((PASS_A, inner), bf16),
        ),
        in_specs=[ANY] * 3,
        out_specs=(ANY,) * 4,
        scratch_shapes=[
            pltpu.VMEM(mixed.shape, bf16),
            pltpu.VMEM(up_all.shape, bf16),
            pltpu.VMEM((count, n_dp, span, inner), bf16),
            pltpu.VMEM((count, 2, span, inner), bf16),
            sems(2, 2, n // 2),
            sems(2, 2, n // 2),
            sems(count, 2),
            sems(count, 2),
            pltpu.SemaphoreType.DMA,
            sems(count + 1),
            sems(count, 2),
            pltpu.SemaphoreType.DMA,
            pltpu.SemaphoreType.DMA,
        ],
        name="gather_with_gradients",
        cost_estimate=pl.CostEstimate(
            flops=2 * count * width * inner * mixed.shape[0],
            bytes_accessed=160_000_000,
            transcendentals=0,
        ),
        compiler_params=pltpu.CompilerParams(
            collective_id=identity, has_side_effects=True, vmem_limit_bytes=BIG_VMEM
        ),
    )(block, mixed, up_all)


def attention_back(
    back_all,
    out_all,
    in_all,
    probs,
    attend_low,
    qkv,
    raw,
    inverse,
    pair_gains,
    cosine,
    sine,
    partial,
    far,
    n,
    n_dp,
    identity,
):
    rows, width = back_all.shape
    weight_rows = width // (n * n_dp)
    pair = pair_gains.shape[1]
    cols = pair // 2
    heads = cols // HEAD_DIM
    chunk, wide = 256, 512
    tok_rows = rows // n
    half_rows = tok_rows // 2
    bf16, f32 = jnp.bfloat16, jnp.float32
    scale = HEAD_DIM ** (-0.5)

    def body(
        back_ref,
        out_ref,
        in_ref,
        probs_ref,
        attend_ref,
        qkv_ref,
        raw_ref,
        inverse_ref,
        pair_ref,
        cos_ref,
        sin_ref,
        part_ref,
        far_ref,
        raw_back,
        row_part,
        pair_sum,
        part_sum,
        out_sum,
        far_got,
        next_got,
        out_s,
        in_s,
        probs_s,
        part_s,
        attend_back,
        pair_s,
        value_s,
        sum_s,
        slots,
        flat,
        got,
        sum_send,
        sum_receive,
        ring_send,
        ring_receive,
        load,
        out_p,
        out_core,
        out_chip,
        pass_send,
        pass_receive,
        far_send,
        far_receive,
    ):
        ring = Ring(n)
        dp, core, chip, core_chip = partners()
        loads = [
            pltpu.make_async_copy(part_ref, part_s, load.at[0]),
            pltpu.make_async_copy(
                out_ref.at[pl.ds(pl.multiple_of(ring.me * cols, 16), cols)], out_s, load.at[1]
            ),
            pltpu.make_async_copy(probs_ref, probs_s, load.at[2]),
            pltpu.make_async_copy(in_ref.at[:, pl.ds(0, pair + cols)], in_s, load.at[3]),
        ]
        for copy in loads:
            copy.start()
        ring.barrier(
            [{"ctx": (ring.me + k) % n} for k in range(1, n)] + [{"dp": core}, {"dp": chip}]
        )

        beyond = [
            remote(
                far_ref.at[0, pl.ds(PASS_A, far_got.shape[0])],
                far_got,
                far_send.at[0],
                far_receive.at[0],
                {"dp": chip},
            ),
            remote(
                far_ref.at[1, pl.ds(0, PASS_B)], next_got, far_send.at[1], far_receive.at[1], {"dp": chip}
            ),
        ]
        for copy in beyond:
            copy.start()

        def store(half, total):
            part_sum[pl.ds(half * half_rows, half_rows)] = total

        steps = scatter_steps(
            ring,
            lambda device, half: part_s.at[
                pl.ds(pl.multiple_of(device * tok_rows + half * half_rows, 16), half_rows)
            ],
            slots,
            store,
            ring_send,
            ring_receive,
        )
        loads[0].wait()
        advance(steps, 1)
        lanes = lax.broadcasted_iota(jnp.int32, (chunk, LANES), 1)

        def chunks(step, count=1):
            total = rows // chunk
            for first in range(0, total, count):
                lax.fori_loop(first, min(first + count, total), step, 0)
                advance(steps, 1)

        loads[1].wait()

        def project(j, carry):
            at = pl.ds(pl.multiple_of(j * chunk, chunk), chunk)
            attend_back[at] = dot_across(back_ref[at], out_s[...]).astype(bf16)
            return carry

        chunks(project, 4)

        def out_product(group):
            for t in range(width // wide):
                value = lax.dot_general(
                    attend_ref[:, group * LANES : (group + 1) * LANES],
                    back_ref[:, t * wide : (t + 1) * wide],
                    (((0,), (0,)), ((), ())),
                    preferred_element_type=f32,
                ).astype(bf16)
                for k in range(LANES // weight_rows):
                    out_p[group * LANES // weight_rows + k, :, t * wide : (t + 1) * wide] = value[
                        k * weight_rows : (k + 1) * weight_rows
                    ]

        for group in range(cols // LANES):
            out_product(group)

        def passing(at, source, target, to):
            return remote(source, target, pass_send.at[at], pass_receive.at[at], {"dp": to})

        passed = [
            passing(0, out_p.at[core_chip], out_core.at[1], core),
            passing(1, out_p.at[core], out_core.at[0], core),
        ]
        for copy in passed:
            copy.start()
        loads[2].wait()
        for head in range(heads):
            columns = pl.ds(head * HEAD_DIM, HEAD_DIM)
            key_columns = pl.ds(cols + head * HEAD_DIM, HEAD_DIM)
            value_columns = pl.ds(pair + head * HEAD_DIM, HEAD_DIM)
            pair_s[:, key_columns] = jnp.zeros((rows, HEAD_DIM), f32)
            value_s[:, columns] = jnp.zeros((rows, HEAD_DIM), f32)

            def scores(j, carry, head=head, columns=columns, key_columns=key_columns, value_columns=value_columns):
                at = pl.ds(pl.multiple_of(j * chunk, chunk), chunk)
                back = attend_back[at, columns]
                delta = jnp.sum(
                    back.astype(f32) * attend_ref[at, columns].astype(f32), axis=-1, keepdims=True
                )
                probs_low = probs_s[head, at]
                score_back = (
                    probs_low.astype(f32) * (dot_across(back, qkv_ref[:, value_columns]) - delta)
                ).astype(bf16)
                pair_s[at, columns] = dot(score_back, qkv_ref[:, key_columns])
                over = (((0,), (0,)), ((), ()))
                pair_s[:, key_columns] += lax.dot_general(
                    score_back, qkv_ref[at, columns], over, preferred_element_type=f32
                )
                value_s[:, columns] += lax.dot_general(
                    probs_low, back, over, preferred_element_type=f32
                )
                return carry

            chunks(scores)
        passed[0].wait_recv()
        out_core[1] = (out_core[1].astype(f32) + out_p[chip].astype(f32)).astype(bf16)
        passed.append(passing(2, out_core.at[1], out_chip, chip))
        passed[-1].start()
        pair_sum[...] = jnp.zeros((8, pair), f32)

        def unturn(j, carry):
            at = pl.ds(pl.multiple_of(j * chunk, chunk), chunk)
            held = jnp.zeros((chunk, LANES), f32)
            for which in range(2):
                total = jnp.zeros((chunk, 1), f32)
                for head in range(heads):
                    columns = pl.ds(which * cols + head * HEAD_DIM, HEAD_DIM)
                    back = turn(pair_s[at, columns] * scale, cos_ref[at], -sin_ref[at])
                    normed = raw_ref[at, columns] * inverse_ref[at, which : which + 1]
                    pair_sum[0:1, columns] += jnp.sum(back * normed, axis=0, keepdims=True)
                    back = back * pair_ref[0:1, columns]
                    pair_s[at, columns] = back
                    total = total + jnp.sum(back * normed, axis=-1, keepdims=True)
                held = jnp.where(lanes == which, total, held)
            sum_s[at] = held
            return carry

        chunks(unturn)
        exchange_rows(ring, sum_s, flat, got, sum_send, sum_receive, steps)
        loads[3].wait()

        def finish(j, carry):
            at = pl.ds(pl.multiple_of(j * chunk, chunk), chunk)
            for which in range(2):
                columns = pl.ds(which * cols, cols)
                factor = inverse_ref[at, which : which + 1]
                normed = raw_ref[at, columns] * factor
                mean = sum_s[at, which : which + 1] / width
                raw_back[at, columns] = (factor * (pair_s[at, columns] - normed * mean)).astype(bf16)
            raw_back[at, pl.ds(pair, cols)] = value_s[at].astype(bf16)
            for t in range(width // wide):
                row_part[at, pl.ds(t * wide, wide)] = dot_across(
                    raw_back[at], in_s[pl.ds(t * wide, wide), :]
                ).astype(bf16)
            return carry

        chunks(finish)
        passed[1].wait_recv()
        passed[2].wait_recv()
        out_sum[...] = (
            out_core[0].astype(f32) + out_p[dp].astype(f32) + out_chip[...].astype(f32)
        ).astype(bf16)
        advance(steps, 64)
        for copy in beyond:
            copy.wait()
        for copy in passed:
            copy.wait_send()

    return pl.pallas_call(
        body,
        out_shape=(
            jax.ShapeDtypeStruct((rows, 3 * cols), bf16),
            jax.ShapeDtypeStruct((rows, width), bf16),
            jax.ShapeDtypeStruct((8, pair), f32),
            jax.ShapeDtypeStruct((tok_rows, width), f32),
            jax.ShapeDtypeStruct((weight_rows, width), bf16),
            jax.ShapeDtypeStruct((far.shape[1] - PASS_A, far.shape[2]), bf16),
            jax.ShapeDtypeStruct((PASS_B, far.shape[2]), bf16),
        ),
        in_specs=[VMEM] + [ANY] * 3 + [VMEM] * 7 + [ANY] * 2,
        out_specs=(VMEM,) * 5 + (ANY,) * 2,
        scratch_shapes=[
            pltpu.VMEM((cols, width), bf16),
            pltpu.VMEM((width, pair + cols), bf16),
            pltpu.VMEM((heads, rows, rows), bf16),
            pltpu.VMEM((rows, width), bf16),
            pltpu.VMEM((rows, cols), bf16),
            pltpu.VMEM((rows, pair), f32),
            pltpu.VMEM((rows, cols), f32),
            pltpu.VMEM((rows, LANES), f32),
            pltpu.VMEM((2, 2, n // 2, half_rows, width), bf16),
            pltpu.VMEM((8, rows), f32),
            pltpu.VMEM((n - 1, 8, rows), f32),
            sems(n - 1),
            sems(n - 1),
            sems(2, 2, n // 2),
            sems(2, 2, n // 2),
            sems(4),
            pltpu.VMEM((n_dp, weight_rows, width), bf16),
            pltpu.VMEM((2, weight_rows, width), bf16),
            pltpu.VMEM((weight_rows, width), bf16),
            sems(3),
            sems(3),
            sems(2),
            sems(2),
        ],
        name="attention_back",
        cost_estimate=pl.CostEstimate(
            flops=2 * rows * width * 4 * cols, bytes_accessed=160_000_000, transcendentals=0
        ),
        compiler_params=pltpu.CompilerParams(
            collective_id=identity, has_side_effects=True, vmem_limit_bytes=BIG_VMEM
        ),
    )(
        back_all,
        out_all,
        in_all,
        probs,
        attend_low,
        qkv,
        raw,
        inverse,
        pair_gains,
        cosine,
        sine,
        partial,
        far,
    )


def heads_local(
    tokens,
    document_ids,
    routes,
    norm_gains,
    project_in,
    project_out,
    router_weight,
    expert_in,
    expert_out,
    cotangent,
):
    bf16, f32 = jnp.bfloat16, jnp.float32
    n = lax.axis_size("ctx")
    n_dp = lax.axis_size("dp")
    me = lax.axis_index("ctx")
    tok_rows, width = tokens.shape[1:]
    rows = tok_rows * n
    weight_rows = project_in.shape[0]
    own_heads = HEADS // n
    cols = own_heads * HEAD_DIM
    local_experts = expert_in.shape[0]
    expert_count = local_experts * n
    score_scale = HEAD_DIM ** (-0.5)

    def own(array, size, axis=0):
        return lax.dynamic_slice_in_dim(array, me * size, size, axis)

    named = jnp.any(routes[0][..., None] == jnp.arange(LANES, dtype=jnp.int32), axis=1).astype(bf16)
    small = jnp.concatenate(
        [router_weight, norm_gains, jnp.zeros((weight_rows, LANES - 4 - expert_count), bf16)], axis=1
    )
    in_blocks = project_in.reshape(weight_rows, 3, n, cols).transpose(2, 0, 1, 3)
    in_blocks = jnp.concatenate(
        [
            in_blocks.reshape(n, weight_rows, 3 * cols),
            jnp.broadcast_to(small[None], (n, weight_rows, LANES)),
        ],
        axis=2,
    )
    token_all, named_all, in_all, out_chip = gather_inputs(
        tokens[0], named, in_blocks, project_out, n, n_dp, 1
    )
    named_all = named_all.reshape(rows, LANES)
    in_all = in_all.reshape(width, 3 * cols + LANES)
    small_all = in_all[:, 3 * cols :]
    gains = small_all[:, expert_count : expert_count + 4].astype(f32)
    router_all = small_all[:, :expert_count]
    first = lax.all_gather(expert_in, "dp", axis=1, tiled=True)
    second = lax.all_gather(expert_out, "dp", axis=1, tiled=True).reshape(local_experts * FF, width)

    half_rows = tok_rows // 2

    def dealt(row):
        blocks = row.reshape(2 * n, half_rows)
        return jnp.stack([blocks[:n], blocks[n:][::-1]], axis=1).reshape(rows)

    places = dealt(jnp.arange(rows, dtype=jnp.int32))
    document_row = document_ids[0]
    starts = dealt(document_starts(document_row))
    relative = places - starts
    cosine, sine = rotary_tables(relative, HEAD_DIM)
    cosine = jnp.concatenate([cosine[:, 0], cosine[:, 0]], axis=-1)
    sine = jnp.concatenate([-sine[:, 0], sine[:, 0]], axis=-1)
    bounds = jnp.stack([starts, places], axis=1)
    place_row = places[None]
    pair_gains = own(gains, cols)[:, 1:3].T.reshape(1, 2 * cols)

    attend_gain = gains[:, 0][None]
    attend_all, out_all, probs, attend_in, attend_low, qkv, raw, inverse = attention_in(
        token_all,
        in_all,
        project_out,
        out_chip,
        attend_gain,
        pair_gains,
        cosine,
        sine,
        bounds,
        place_row,
        n,
        n_dp,
        10,
    )

    upstream_all, mixed_all, gated_all, up_all, own_gates, gate_back, own_residual = experts_in(
        attend_all,
        token_all,
        cotangent[0],
        out_all,
        first,
        second,
        gains[:, 3][None],
        small_all,
        named_all,
        n,
        8,
    )
    mixed_slots = mixed_all.reshape(rows, width)
    second_back = jnp.einsum(
        "tf,td->fd", gated_all, upstream_all.reshape(rows, width), preferred_element_type=f32
    ).astype(bf16)
    second_back, up_all = lax.optimization_barrier((second_back, up_all))
    expert_out_gradient = lax.psum_scatter(
        second_back.reshape(local_experts, FF, width), "dp", scatter_dimension=1, tiled=True
    ).astype(f32)
    mixed_back, mixture, gate_back = experts_out(up_all, gated_all, first, second, gate_back, n, 9)
    gate_back = gate_back[:, :local_experts]
    place = ring_place(me, n)
    gate_back = sum(
        jnp.where(
            (jnp.arange(n) == ring_device((place + offset + n) % n, n))[:, None, None],
            gate_back[slot],
            0.0,
        )
        for slot, offset in enumerate(slot_offsets(n))
    )
    gate_back = gate_back.reshape(expert_count, tok_rows).T

    own_gates = own_gates[:, :expert_count]
    own_mixed = mixed_all[0]
    own_mixed_inverse = inverse_rms(own_residual)
    own_mixed_normed = own_residual * own_mixed_inverse
    chosen_back = own_gates * (
        gate_back - jnp.sum(own_gates * gate_back, axis=-1, keepdims=True)
    )
    logit_back = chosen_back.astype(bf16)
    router_part = jnp.einsum("td,te->ed", own_mixed, logit_back, preferred_element_type=f32)
    mixed_back = mixed_back + jnp.einsum(
        "te,de->td", logit_back, router_all, preferred_element_type=f32
    )
    mixed_gain_back = jnp.sum(mixed_back * own_mixed_normed, axis=0)
    residual_back = cotangent[0].astype(f32) + normalize_back(
        mixed_back * gains[:, 3], own_mixed_normed, own_mixed_inverse
    )
    back_all, near, far, got_a = gather_with_gradients(
        residual_back.astype(bf16), mixed_slots, up_all, n, n_dp, 5
    )

    raw_back, row_part, pair_sum, mixture, out_part, got_b, got_c = attention_back(
        back_all,
        out_all,
        in_all,
        probs,
        attend_low,
        qkv,
        raw,
        inverse,
        pair_gains,
        cosine,
        sine,
        mixture,
        far,
        n,
        n_dp,
        11,
    )
    layer_output = (own_residual + mixture).astype(bf16)
    pairs = [(d * n + c, c * n_dp + d) for d in range(n_dp) for c in range(n)]
    project_out_gradient = lax.ppermute(out_part, ("dp", "ctx"), pairs).astype(f32)

    small_rows = -(-(4 + expert_count) // 8) * 8
    small_part = jnp.concatenate(
        [
            jnp.zeros((3, width), f32),
            mixed_gain_back[None],
            router_part,
            jnp.zeros((small_rows - 4 - expert_count, width), f32),
        ],
        axis=0,
    )
    tokens_back, project_in_gradient, small_gradient, got_d = scatter_end(
        row_part,
        attend_in,
        raw_back,
        tokens[0],
        residual_back,
        attend_gain,
        small_part,
        pair_sum,
        far,
        n,
        n_dp,
        6,
    )
    expert_in_gradient = near.astype(f32) + (
        jnp.concatenate([got_a, got_b, got_c, got_d], axis=0).reshape(near.shape).astype(f32)
    )
    per_tile = LANES // weight_rows
    small_gradient = lax.dynamic_slice_in_dim(
        small_gradient, me % per_tile * weight_rows, weight_rows, 1
    ).T
    return (
        layer_output[None],
        tokens_back[None],
        small_gradient[:, :4],
        project_in_gradient,
        project_out_gradient,
        small_gradient[:, 4 : 4 + expert_count],
        expert_in_gradient,
        expert_out_gradient,
    )


def layer(*arrays):
    n, tok_rows, experts = lax.axis_size("ctx"), arrays[0].shape[1], arrays[7].shape[0]
    fits = HEADS % n == 0 and n % 4 == 0 and lax.axis_size("dp") == 4
    fits = fits and tok_rows == LANES and experts == 2 and experts * n + 4 <= LANES
    return (heads_local if fits else gathered_local)(*arrays)


def solution(mesh):
    placed = (
        P("dp", "ctx", None),
        P("dp", None),
        P("dp", "ctx", None),
        P(("dp", "ctx"), None),
        P(("dp", "ctx"), None),
        P(("dp", "ctx"), None),
        P(("dp", "ctx"), None),
        P("ctx", "dp", None),
        P("ctx", "dp", None),
        P("dp", "ctx", None),
    )
    return jax.shard_map(
        layer,
        mesh=mesh,
        in_specs=placed,
        out_specs=(
            P("dp", "ctx", None),
            P("dp", "ctx", None),
            P(("dp", "ctx"), None),
            P(("dp", "ctx"), None),
            P(("dp", "ctx"), None),
            P(("dp", "ctx"), None),
            P("ctx", "dp", None),
            P("ctx", "dp", None),
        ),
        check_vma=False,
    )
```
